32 devices in a mesh: dp: 8 (over y, x, core), mp: 4 (over z).
Axes of the slice: x: 2, y: 2, z: 4, core: 2. Of those that a mesh axis runs over, the one named last changes fastest.
Arguments:
- frames: bfloat16 [16384, 768], P(('dp', 'mp')), may hold values from -6 to 6
- lengths: int32 [16], P('dp'), may hold values from 640 to 1024, as said below
- span_starts: int32 [16, 66], P('dp'), may hold values from 0 to 1014, as said below
- cotangent: bfloat16 [16384, 768], P(('dp', 'mp')), may hold values from -6 to 6
- query_weight: bfloat16 [768, 768], P('dp', 'mp'), may hold values from -0.3125 to 0.3125
- key_weight: bfloat16 [768, 768], P('dp', 'mp'), may hold values from -0.3125 to 0.3125
- value_weight: bfloat16 [768, 768], P('dp', 'mp'), may hold values from -0.21875 to 0.21875
- out_weight: bfloat16 [768, 768], P('mp', 'dp'), may hold values from -0.875 to 0.875
- up_weight: bfloat16 [768, 3072], P('dp', 'mp'), may hold values from -0.21875 to 0.21875
- down_weight: bfloat16 [3072, 768], P('mp', 'dp'), may hold values from -0.15625 to 0.15625
- query_bias: bfloat16 [12, 64], P('mp'), may hold values from -3 to 3
- value_bias: bfloat16 [12, 64], P('mp'), may hold values from -3 to 3
- up_bias: bfloat16 [24, 128], P('mp'), may hold values from -3 to 3
- out_bias: bfloat16 [768], replicated, may hold values from -3 to 3
- down_bias: bfloat16 [768], replicated, may hold values from -3 to 3
- first_gain: bfloat16 [768], replicated, may hold values from 0.25 to 1.75
- first_shift: bfloat16 [768], replicated, may hold values from -2 to 2
- second_gain: bfloat16 [768], replicated, may hold values from 0.25 to 1.75
- second_shift: bfloat16 [768], replicated, may hold values from -2 to 2
- mask_vector: bfloat16 [768], replicated, may hold values from -4 to 4
Outputs:
- out_frames: bfloat16 [16384, 768], P(('dp', 'mp'))
- grad_frames: bfloat16 [16384, 768], P(('dp', 'mp'))
- grad_query_weight: float32 [768, 768], P('dp', 'mp')
- grad_key_weight: float32 [768, 768], P('dp', 'mp')
- grad_value_weight: float32 [768, 768], P('dp', 'mp')
- grad_out_weight: float32 [768, 768], P('mp', 'dp')
- grad_up_weight: float32 [768, 3072], P('dp', 'mp')
- grad_down_weight: float32 [3072, 768], P('mp', 'dp')
- grad_query_bias: float32 [12, 64], P('mp', 'dp')
- grad_value_bias: float32 [12, 64], P('mp', 'dp')
- grad_up_bias: float32 [24, 128], P('mp', 'dp')
- grad_out_bias: float32 [768], P(('dp', 'mp'))
- grad_down_bias: float32 [768], P(('dp', 'mp'))
- grad_first_gain: float32 [768], P(('dp', 'mp'))
- grad_first_shift: float32 [768], P(('dp', 'mp'))
- grad_second_gain: float32 [768], P(('dp', 'mp'))
- grad_second_shift: float32 [768], P(('dp', 'mp'))
- grad_mask_vector: float32 [768], P(('dp', 'mp'))
The draws below stay inside these ranges and needn't reach their ends.
Inputs may be any that keep to these rules, and one draw needn't show every extreme that they name: `lengths`: in each aligned block of 2 clips exactly one clip, drawn from the seed, has 1024 frames, and another has 640. `span_starts`: each start is at most the clip's length minus 10; spans may intersect.
All inputs are finite; a program needn't handle non-finite values.
Results may differ from the reference program's by a relative error of at most 0.022.
Values may be sent and summed in bfloat16 or wider, within the bound.
A program may use at most 128 MiB of HBM per device.

```python
import math
import jax
import jax.numpy as jnp
from jax import lax

D = 768
HEADS = 12
HEAD_DIM = 64
FF = 3072
SPAN = 10
LEN = 1024
CLIPS_DEV = 2
CLIPS = 16
TOKENS = 16384
SPANS = 66


def clip_lengths(key):
    spread_part = jax.random.randint(jax.random.fold_in(key, 11), (CLIPS,), LEN * 5 // 8, LEN + 1)
    chosen = jax.random.randint(jax.random.fold_in(key, 12), (CLIPS // CLIPS_DEV,), 0, CLIPS_DEV)
    slot_index = jnp.arange(CLIPS, dtype=jnp.int32) % CLIPS_DEV
    group_pick = jnp.repeat(chosen, CLIPS_DEV)
    shortest_pick = (group_pick + 1) % CLIPS_DEV
    sizes = jnp.where(slot_index == shortest_pick, LEN * 5 // 8, spread_part)
    return jnp.where(slot_index == group_pick, LEN, sizes).astype(jnp.int32)


def draw_lengths(key, part):
    return clip_lengths(key)


def draw_span_starts(key, part):
    clip_sizes = clip_lengths(key)
    key = jax.random.fold_in(key, 3)
    upper = (clip_sizes - SPAN + 1)[:, None]
    starts = jax.random.randint(key, (CLIPS, SPANS), 0, upper).astype(jnp.int32)
    first_column = (jnp.arange(SPANS, dtype=jnp.int32) == 0)[None, :]
    at_full = (clip_sizes == LEN)[:, None] & first_column
    at_short = (clip_sizes == LEN * 5 // 8)[:, None] & first_column
    starts = jnp.where(at_full, LEN - SPAN, starts)
    starts = jnp.where(at_short, 0, starts)
    return starts.astype(jnp.int32)


def raised(values, key, source, target, blocks, factor):
    owner, partner = [(jnp.arange(values.shape[axis_at]) // (values.shape[axis_at] // blocks)).reshape([-1 if axis == axis_at else 1 for axis in range(values.ndim)]) for axis_at in (source, target)]
    chosen = jax.random.permutation(key, blocks)[partner]
    strong = (owner == chosen) | (owner == (partner + blocks // 2) % blocks)
    return jnp.where(strong, factor * values, values)


def level_of(key, shape, shards, smallest, top_value):
    level = 1.0
    for axis_at, shards_of in shards:
        steps = jax.random.uniform(jax.random.fold_in(jax.random.fold_in(key, 6), axis_at), (shards_of,), jnp.float32, smallest / len(shards), top_value / len(shards))
        level = level * jnp.repeat(jnp.exp(steps), shape[axis_at] // shards_of).reshape((-1,) + (1,) * (len(shape) - 1 - axis_at))
    return level


def scatter_about(key, shape, scale, bound, cuts=(), held_as=jnp.bfloat16):
    entries = jax.random.normal(key, shape, jnp.float32) * scale
    if len(cuts) > 0:
        entries = level_of(key, shape, cuts, -0.22, 0.18) * entries
    return jnp.clip(entries, min=-bound, max=bound).astype(held_as)


def heavy_noise(own_key, extent, spread, bound, split, heavy, kind=jnp.bfloat16):
    entries = spread * jax.random.normal(own_key, extent, jnp.float32)
    if split:
        entries = entries * level_of(own_key, extent, split, -0.22, 0.18)
    return jnp.clip(raised(entries, jax.random.fold_in(own_key, 3), *heavy), -bound, bound).astype(kind)


def setup_inputs(seed: int = 0) -> dict:
    streams_of = jax.random.split(jax.random.key(seed), 21)
    frames = scatter_about(streams_of[0], (TOKENS, D), 1.0, 6.0, ((0, 32),))
    lengths = draw_lengths(jax.random.fold_in(streams_of[20], 71), 0)
    span_starts = draw_span_starts(jax.random.fold_in(streams_of[20], 71), 0)
    cotangent = heavy_noise(streams_of[3], (TOKENS, D), 1.0, 6.0, ((0, 32),), (0, 1, 32, 2.75))
    query_weight = scatter_about(streams_of[4], (D, D), (D // 2) ** -0.5, 0.3125, ((0, 8), (1, 4)))
    key_weight = scatter_about(streams_of[5], (D, D), (D // 2) ** -0.5, 0.3125, ((0, 8), (1, 4)))
    value_weight = scatter_about(streams_of[6], (D, D), D ** -0.5, 0.21875, ((0, 8), (1, 4)))
    out_weight = scatter_about(streams_of[7], (D, D), (D // 16) ** -0.5, 0.875, ((0, 4), (1, 8)))
    up_weight = scatter_about(streams_of[8], (D, FF), D ** -0.5, 0.21875, ((0, 8), (1, 4)))
    down_weight = scatter_about(streams_of[9], (FF, D), (FF // 2) ** -0.5, 0.15625, ((0, 4), (1, 8)))
    query_bias = scatter_about(streams_of[10], (HEADS, HEAD_DIM), 0.5, 3.0, ((0, 4),))
    value_bias = scatter_about(streams_of[11], (HEADS, HEAD_DIM), 0.5, 3.0, ((0, 4),))
    up_bias = scatter_about(streams_of[12], (FF // 128, 128), 0.5, 3.0, ((0, 4),))
    out_bias = scatter_about(streams_of[13], (D,), 0.5, 3.0)
    down_bias = scatter_about(streams_of[14], (D,), 0.5, 3.0)
    first_gain = jnp.clip(1.0 + 0.15 * jax.random.normal(streams_of[15], (D,), jnp.float32), 0.25, 1.75).astype(jnp.bfloat16)
    first_shift = scatter_about(streams_of[16], (D,), 0.3, 2.0)
    second_gain = jnp.clip(1.0 + 0.15 * jax.random.normal(streams_of[17], (D,), jnp.float32), 0.25, 1.75).astype(jnp.bfloat16)
    second_shift = scatter_about(streams_of[18], (D,), 0.3, 2.0)
    mask_vector = scatter_about(streams_of[19], (D,), 1.0, 4.0)
    return dict(frames=frames, lengths=lengths, span_starts=span_starts, cotangent=cotangent, query_weight=query_weight, key_weight=key_weight, value_weight=value_weight, out_weight=out_weight, up_weight=up_weight, down_weight=down_weight, query_bias=query_bias, value_bias=value_bias, up_bias=up_bias, out_bias=out_bias, down_bias=down_bias, first_gain=first_gain, first_shift=first_shift, second_gain=second_gain, second_shift=second_shift, mask_vector=mask_vector)


EPSILON = 1e-05
NEGATIVE = -1e+30

@jax.custom_vjp
def low(v):
    return lax.optimization_barrier(v.astype(jnp.bfloat16)).astype(jnp.float32)

@jax.custom_vjp
def low_back(v):
    return v

def low_keep(v):
    return (low(v), None)

def low_pass(kept, grad):
    return (grad,)

def back_keep(v):
    return (v, None)

def back_low(kept, grad):
    return (low(grad),)
low.defvjp(low_keep, low_pass)
low_back.defvjp(back_keep, back_low)

def matmul(left, right):
    return jnp.dot(left, right, precision=lax.Precision.HIGHEST)

def layer_norm(hidden, gain_vec, shift_vec):
    row_mean = lax.optimization_barrier(jnp.mean(hidden, axis=-1, keepdims=True))
    centered = hidden - row_mean
    variance = lax.optimization_barrier(jnp.mean(centered * centered, axis=-1, keepdims=True))
    return centered * lax.rsqrt(variance + EPSILON) * gain_vec + shift_vec

def by_head(block):
    return block.reshape(LEN, HEADS, HEAD_DIM).transpose(1, 0, 2)

def clip_layer(params, clip_frames, masked, valid_rows):
    query_weight, key_weight, value_weight, out_weight, up_weight, down_weight, query_bias, value_bias, up_bias, out_bias, down_bias, first_gain, first_shift, second_gain, second_shift, mask_vector = params
    inputs = jnp.where(masked[:, None], mask_vector[None, :], clip_frames)
    inputs_low = low(inputs)
    queries = low(low_back(matmul(inputs_low, query_weight) + query_bias.reshape(D)))
    key_rows = low(low_back(matmul(inputs_low, key_weight)))
    values = low(low_back(matmul(inputs_low, value_weight) + value_bias.reshape(D)))
    score_scale = 1.0 / math.sqrt(HEAD_DIM)
    scores = jnp.einsum('hqd,hkd->hqk', by_head(queries), by_head(key_rows), precision=lax.Precision.HIGHEST)
    scores = low_back(scores * score_scale)
    scores = jnp.where(valid_rows[None, None, :] > 0, scores, NEGATIVE)
    attention = jax.nn.softmax(scores, axis=-1)
    attended = jnp.einsum('hqk,hkd->hqd', low(attention), by_head(values), precision=lax.Precision.HIGHEST)
    attended = low(low_back(attended.transpose(1, 0, 2).reshape(LEN, D)))
    attn_branch = low_back(matmul(attended, out_weight))
    normed_one = layer_norm(inputs + attn_branch + out_bias, first_gain, first_shift)
    pre_act = low_back(matmul(low(normed_one), up_weight) + up_bias.reshape(FF))
    acted = low(jax.nn.gelu(pre_act, approximate=False))
    ffn_branch = low_back(matmul(acted, down_weight))
    resid_two = normed_one + ffn_branch + down_bias
    return layer_norm(resid_two, second_gain, second_shift) * valid_rows[:, None]

def reference(frames, lengths, span_starts, cotangent, query_weight, key_weight, value_weight, out_weight, up_weight, down_weight, query_bias, value_bias, up_bias, out_bias, down_bias, first_gain, first_shift, second_gain, second_shift, mask_vector):
    params = tuple((tensor.astype(jnp.float32) for tensor in (query_weight, key_weight, value_weight, out_weight, up_weight, down_weight, query_bias, value_bias, up_bias, out_bias, down_bias, first_gain, first_shift, second_gain, second_shift, mask_vector)))
    positions = jnp.arange(LEN, dtype=jnp.int32)
    valid_rows = (positions[None, :] < lengths[:, None]).astype(jnp.float32)
    covered = (positions[None, None, :] >= span_starts[:, :, None]) & (positions[None, None, :] < span_starts[:, :, None] + SPAN)
    masked = jnp.any(covered, axis=1)
    clip_frames = frames.astype(jnp.float32).reshape(CLIPS, LEN, D)
    clip_grads = cotangent.astype(jnp.float32).reshape(CLIPS, LEN, D)

    def one_clip(totals, pieces):
        frames_in, grads_in, masked_in, valid_in = pieces

        def forward(param_set, frame_set):
            return clip_layer(param_set, frame_set, masked_in, valid_in)
        result, backward = jax.vjp(forward, params, frames_in)
        param_grads, frame_grads = backward(grads_in)
        totals = jax.tree.map(jnp.add, totals, param_grads)
        return (totals, (result.astype(jnp.bfloat16), frame_grads.astype(jnp.bfloat16)))
    zeros = jax.tree.map(jnp.zeros_like, params)
    totals, (outputs, frame_grads) = lax.scan(one_clip, zeros, (clip_frames, clip_grads, masked, valid_rows))
    return (outputs.reshape(TOKENS, D), frame_grads.reshape(TOKENS, D), totals[0], totals[1], totals[2], totals[3], totals[4], totals[5], totals[6], totals[7], totals[8], totals[9], totals[10], totals[11], totals[12], totals[13], totals[14], totals[15])
```

```python
import functools
import math

import jax
import jax.numpy as jnp
from jax import lax
from jax.experimental import pallas as pl
from jax.experimental.pallas import tpu as pltpu
from jax.sharding import PartitionSpec as P

HEAD_DIM = 64
SPAN = 10
LEN = 1024
EPSILON = 1e-05
NEGATIVE = -1e30
SCALE = 1.0 / math.sqrt(HEAD_DIM)

F32 = jnp.float32
BF16 = jnp.bfloat16
MESH = pl.DeviceIdType.MESH
VMEM_LIMIT = 62 * 1024 * 1024

ATT, UP, DOWN = 0, 1, 2
PROJ = 640


def dot(left, right, contract=(1, 0)):
    return lax.dot_general(
        left, right, (((contract[0],), (contract[1],)), ((), ())), preferred_element_type=F32
    )


def hbm():
    return pl.BlockSpec(memory_space=pl.ANY)


def vmem():
    return pl.BlockSpec(memory_space=pltpu.VMEM)


class Place:
    def __init__(self):
        self.dp = lax.axis_index("dp")
        self.z = lax.axis_index("mp")
        self.c = lax.rem(self.dp, 2)
        self.x = lax.rem(self.dp // 2, 2)
        self.y = self.dp // 4
        self.core = (self.dp + 1 - 2 * self.c, self.z)
        self.across_x = (self.dp + 2 - 4 * self.x, self.z)
        self.across_y = (self.dp + 4 - 8 * self.y, self.z)
        self.right = (self.dp, self.z + 1)
        self.left = (self.dp, self.z - 1)
        self.mate = (self.dp, self.z + 1 - 2 * lax.rem(self.z, 2))
        self.far = (self.dp, lax.rem(self.z + 2, 4))

    def greet(self, far):
        barrier = pltpu.get_barrier_semaphore()

        def signal(device):
            pl.semaphore_signal(barrier, inc=1, device_id=device, device_id_type=MESH)

        signal(self.core)
        signal(self.across_x)
        signal(self.across_y)
        if far:
            signal(self.far)
        pl.when(self.z < 3)(lambda: signal(self.right))
        pl.when(self.z > 0)(lambda: signal(self.left))
        ends = jnp.where((self.z == 0) | (self.z == 3), 1, 2)
        pl.semaphore_wait(barrier, (4 if far else 3) + ends)


def remote(src, dst, send, recv, device):
    return pltpu.make_async_remote_copy(
        src_ref=src, dst_ref=dst, send_sem=send, recv_sem=recv, device_id=device, device_id_type=MESH
    )


class Gather:
    def __init__(self, at, blocks, biases, z_send, z_recv, p_send, p_recv):
        self.at, self.blocks, self.biases = at, blocks, biases
        self.z_send, self.z_recv, self.p_send, self.p_recv = z_send, z_recv, p_send, p_recv

    def z_copy(self, kind, m, direction, step):
        at = self.at
        if kind == 3:
            ref = self.biases.at[m]
        else:
            ref = self.blocks.at[kind, m, at.y, at.x, at.c]
        device = at.right if direction == 0 else at.left
        return remote(ref, ref, self.z_send.at[kind, direction, step], self.z_recv.at[kind, m], device)

    def z_step(self, kind, step):
        z = self.at.z
        if step == 0:
            pl.when(z < 3)(lambda: self.z_copy(kind, z, 0, 0).start())
            pl.when(z > 0)(lambda: self.z_copy(kind, z, 1, 0).start())
            return

        @pl.when(z >= step)
        def _():
            self.z_copy(kind, z - step, 0, 0).wait_recv()
            if step < 3:
                pl.when(z < 3)(lambda: self.z_copy(kind, z - step, 0, step).start())

        @pl.when(z + step <= 3)
        def _():
            self.z_copy(kind, z + step, 1, 0).wait_recv()
            if step < 3:
                pl.when(z > 0)(lambda: self.z_copy(kind, z + step, 1, step).start())

    def plane_copy(self, kind, which):
        at, blocks = self.at, self.blocks.at[kind]
        x, y, c = at.x, at.y, at.c
        low, high = pl.ds(0, 48), pl.ds(48, 48)
        ref, device = {
            0: lambda: (blocks.at[:, y, x, c, low], at.across_x),
            1: lambda: (blocks.at[:, y, x, c, high], at.across_y),
            2: lambda: (blocks.at[:, y, :, c, low], at.across_y),
            3: lambda: (blocks.at[:, :, x, c, high], at.across_x),
            4: lambda: (blocks.at[:, y, x, c], at.core),
            5: lambda: (blocks.at[:, y, 1 - x, c, low], at.core),
            6: lambda: (blocks.at[:, 1 - y, x, c, high], at.core),
            7: lambda: (blocks.at[:, 1 - y, :, c, low], at.core),
            8: lambda: (blocks.at[:, :, 1 - x, c, high], at.core),
        }[which]()
        return remote(ref, ref, self.p_send.at[kind, which], self.p_recv.at[kind, which], device)

    def first(self, kind):
        for which in (0, 1, 4):
            self.plane_copy(kind, which).start()

    def second(self, kind):
        self.plane_copy(kind, 0).wait_recv()
        self.plane_copy(kind, 2).start()
        self.plane_copy(kind, 5).start()
        self.plane_copy(kind, 1).wait_recv()
        self.plane_copy(kind, 3).start()
        self.plane_copy(kind, 6).start()

    def third(self, kind):
        self.plane_copy(kind, 2).wait_recv()
        self.plane_copy(kind, 7).start()
        self.plane_copy(kind, 3).wait_recv()
        self.plane_copy(kind, 8).start()

    def last(self, kind):
        for which in range(4, 9):
            self.plane_copy(kind, which).wait_recv()

    def drain(self):
        z = self.at.z
        for kind in range(4):
            for step in range(3):
                pl.when((z < 3) & (z >= step))(
                    lambda k=kind, s=step: self.z_copy(k, z - s, 0, s).wait_send()
                )
                pl.when((z > 0) & (z + step <= 3))(
                    lambda k=kind, s=step: self.z_copy(k, z + s, 1, s).wait_send()
                )
        for kind in range(3):
            for which in range(9):
                self.plane_copy(kind, which).wait_send()


def block_of(blocks, kind, m, low=0, width=768):
    return blocks[kind, m, :, :, :, :, pl.ds(low, width)].reshape(768, width)


def lane_mask(rows, lower):
    lanes = lax.broadcasted_iota(jnp.int32, (rows, 128), 1)
    return (lanes < 64) if lower else (lanes >= 64)


def forward_compute(
    blocks,
    biases,
    xs,
    keybias_ref,
    valid_ref,
    cot_ref,
    vec_ref,
    probs_hbm,
    out_ref,
    recip_ref,
    headout_ref,
    xt_ref,
    qm_ref,
    kt_ref,
    v_ref,
    att_ref,
    acted_ref,
    slope_ref,
    n1t_ref,
    n1_ref,
    rs1_ref,
    gb2_ref,
    gb2t_ref,
    g2_ref,
    sums_ref,
    k_ref,
    vt_ref,
    att_t,
    probs,
    probs_sem,
    total,
    low,
    hooks,
):
    rows = xs.shape[1]
    for side in range(2):
        xt_ref[side] = xs[side].T
    ones_lane = jnp.where(lax.broadcasted_iota(jnp.int32, (rows, 128), 1) == 0, 1.0, 0.0).astype(BF16)

    def probs_copy(head, slot):
        return pltpu.make_async_copy(probs.at[slot], probs_hbm.at[head], probs_sem.at[slot])

    def project(m, _):
        bias = biases[m, 0:1, :].astype(F32)[:, :PROJ]
        own = dot(xs[0], block_of(blocks, ATT, m, 0, PROJ)) + bias
        other = dot(xs[1], block_of(blocks, ATT, m, 128, 512)) + bias[:, 128:]
        k_ref[2 * m, :rows] = own[:, 128:256].astype(BF16)
        k_ref[2 * m, rows:] = other[:, 0:128].astype(BF16)
        v_ref[2 * m, :rows] = own[:, 256:384].astype(BF16)
        v_ref[2 * m, rows:] = other[:, 128:256].astype(BF16)
        k_ref[2 * m + 1, :rows] = own[:, 384:512].astype(BF16)
        k_ref[2 * m + 1, rows:] = other[:, 256:384].astype(BF16)
        v_ref[2 * m + 1, :rows] = own[:, 512:640].astype(BF16)
        v_ref[2 * m + 1, rows:] = other[:, 384:512].astype(BF16)
        lower, upper = lane_mask(rows, True), lane_mask(rows, False)
        pair = own[:, 0:128].astype(BF16).astype(F32) * SCALE
        single = pltpu.roll(own[:, 384:512].astype(BF16).astype(F32) * SCALE, 64, 1)
        qm_ref[3 * m] = jnp.where(lower, pair, 0.0).astype(BF16)
        qm_ref[3 * m + 1] = jnp.where(upper, pair, 0.0).astype(BF16)
        qm_ref[3 * m + 2] = jnp.where(upper, single, 0.0).astype(BF16)
        for tile in range(2):
            kt_ref[2 * m + tile] = k_ref[2 * m + tile].T
            vt_ref[2 * m + tile] = v_ref[2 * m + tile].T
        return 0

    def attend(m, _):
        att_t[0:64, :] = jnp.zeros((64, rows), BF16)
        for j in range(3):
            tile = 2 * m + j // 2
            head = 3 * m + j
            keys = jnp.concatenate([k_ref[tile], keybias_ref[...]], axis=1)
            queries = jnp.concatenate([qm_ref[head], ones_lane], axis=1)
            scores = dot(keys, queries, (1, 1))
            weights = jnp.exp(scores - jnp.max(scores, axis=0, keepdims=True))
            recip = 1.0 / jnp.sum(weights, axis=0, keepdims=True)
            weights = weights.astype(BF16)
            pl.when(m > 0)(lambda h=head, s=j: probs_copy(h, s).wait())
            probs[j] = weights
            probs_copy(head, j).start()
            side = 64 * (j % 2)
            head_out = dot(vt_ref[tile, side : side + 64, :], weights) * recip
            recip_ref[head] = jnp.broadcast_to(recip, (8, rows))
            headout_ref[head] = head_out
            place = (128, 192, 64)[j]
            att_t[place : place + 64, :] = head_out.astype(BF16)
        att_ref[m] = att_t[...].T
        part = dot(att_ref[m], block_of(blocks, ATT, m, 512, 256), (1, 1))

        @pl.when(m == 0)
        def _():
            total[...] = part

        @pl.when(m > 0)
        def _():
            total[...] += part

        hooks.in_attend(m)
        return 0

    hooks.before_project()
    lax.fori_loop(0, 4, project, 0)
    hooks.before_attend()
    lax.fori_loop(0, 4, attend, 0)
    for j in range(3):
        probs_copy(9 + j, j).wait()

    chunk = 64

    def norm_one(i, _):
        r = pl.ds(pl.multiple_of(i * chunk, chunk), chunk)
        resid = xs[0, r, :].astype(F32) + total[r, :] + vec_ref[0:1, :]
        centered = resid - jnp.mean(resid, axis=1, keepdims=True)
        rstd = lax.rsqrt(jnp.mean(centered * centered, axis=1, keepdims=True) + EPSILON)
        unit = centered * rstd
        n1_ref[r, :] = unit
        rs1_ref[r, :] = rstd
        low[r, :] = (unit * vec_ref[2:3, :] + vec_ref[3:4, :]).astype(BF16)
        return 0

    lax.fori_loop(0, rows // chunk, norm_one, 0)
    n1t_ref[...] = low[...].T
    hooks.before_up()

    def feed(m, _):
        pre = dot(low[...], block_of(blocks, UP, m)) + biases[m, 1:2, :].astype(F32)
        phi = 0.5 * (1.0 + lax.erf(pre * (1.0 / math.sqrt(2.0))))
        acted_ref[m] = (pre * phi).astype(BF16)
        slope_ref[m] = (phi + pre * jnp.exp(-0.5 * pre * pre) * (1.0 / math.sqrt(2.0 * math.pi))).astype(BF16)
        hooks.in_feed(m)
        return 0

    lax.fori_loop(0, 4, feed, 0)
    hooks.before_down()

    def down(m, _):
        part = dot(acted_ref[m], block_of(blocks, DOWN, m), (1, 1))

        @pl.when(m == 0)
        def _():
            total[...] = part

        @pl.when(m > 0)
        def _():
            total[...] += part

        return 0

    lax.fori_loop(0, 4, down, 0)

    def norm_two(i, sums):
        r = pl.ds(pl.multiple_of(i * chunk, chunk), chunk)
        normed = n1_ref[r, :] * vec_ref[2:3, :] + vec_ref[3:4, :]
        resid = normed + total[r, :] + vec_ref[1:2, :]
        centered = resid - jnp.mean(resid, axis=1, keepdims=True)
        rstd = lax.rsqrt(jnp.mean(centered * centered, axis=1, keepdims=True) + EPSILON)
        unit = centered * rstd
        valid = valid_ref[r, :]
        out_ref[r, :] = (valid * (unit * vec_ref[4:5, :] + vec_ref[5:6, :])).astype(BF16)
        grad = valid * cot_ref[r, :].astype(F32)
        scaled = grad * vec_ref[4:5, :]
        grad_in = (
            scaled
            - jnp.mean(scaled, axis=1, keepdims=True)
            - unit * jnp.mean(scaled * unit, axis=1, keepdims=True)
        ) * rstd
        g2_ref[r, :] = grad_in
        gb2_ref[r, :] = grad_in.astype(BF16)
        return (
            sums[0] + jnp.sum(grad_in, axis=0, keepdims=True),
            sums[1] + jnp.sum(grad * unit, axis=0, keepdims=True),
            sums[2] + jnp.sum(grad, axis=0, keepdims=True),
        )

    zero = jnp.zeros((1, 768), F32)
    sums = lax.fori_loop(0, rows // chunk, norm_two, (zero, zero, zero))
    sums_ref[...] = jnp.concatenate([*sums, jnp.zeros((5, 768), F32)], axis=0)
    gb2t_ref[...] = gb2_ref[...].T


class NoHooks:
    def before_project(self):
        pass

    def before_attend(self):
        pass

    def in_attend(self, m):
        pass

    def before_up(self):
        pass

    def in_feed(self, m):
        pass

    def before_down(self):
        pass


N_FORWARD_OUTS = 18


def forward_linked(pack_ref, bias_ref, x_ref, *refs):
    keybias, valid, cot, vec = refs[:4]
    blocks_hbm, probs_hbm, *outs = refs[4 : 4 + 2 + N_FORWARD_OUTS - 1]
    scratch = refs[4 + 2 + N_FORWARD_OUTS - 1 :]
    blocks, biases, xs, k_ref, vt_ref, att_t, probs, probs_sem, total, low = scratch[:10]
    z_send, z_recv, p_send, p_recv, x_send, x_recv, keep_sem = scratch[10:]
    at = Place()
    at.greet(False)
    gather = Gather(at, blocks, biases, z_send, z_recv, p_send, p_recv)
    for kind in range(3):
        blocks[kind, at.z, at.y, at.x, at.c] = pack_ref[kind]
    biases[at.z] = bias_ref[...]
    xs[0] = x_ref[...]
    swap = remote(x_ref, xs.at[1], x_send, x_recv, at.mate)
    gather.z_step(ATT, 0)
    gather.z_step(3, 0)
    gather.z_step(ATT, 1)
    gather.z_step(3, 1)
    gather.z_step(ATT, 2)
    gather.z_step(3, 2)
    gather.z_step(ATT, 3)
    gather.z_step(3, 3)
    gather.first(ATT)
    swap.start()
    gather.z_step(UP, 0)
    gather.second(ATT)
    gather.z_step(UP, 1)
    gather.z_step(UP, 2)
    gather.z_step(UP, 3)
    gather.first(UP)
    gather.z_step(DOWN, 0)
    gather.third(ATT)
    gather.second(UP)
    gather.z_step(DOWN, 1)
    gather.z_step(DOWN, 2)
    gather.z_step(DOWN, 3)
    gather.first(DOWN)
    gather.last(ATT)
    swap.wait()
    gather.third(UP)
    gather.second(DOWN)
    gather.last(UP)
    gather.third(DOWN)
    gather.last(DOWN)
    keep = pltpu.make_async_copy(blocks, blocks_hbm, keep_sem)
    keep.start()
    forward_compute(
        blocks, biases, xs, keybias, valid, cot, vec, probs_hbm, *outs,
        k_ref, vt_ref, att_t, probs, probs_sem, total, low, NoHooks(),
    )
    keep.wait()
    gather.drain()


def forward_alone(blocks_in, biases, xs, *refs):
    keybias, valid, cot, vec = refs[:4]
    probs_hbm, *outs = refs[4 : 4 + 1 + N_FORWARD_OUTS - 1]
    scratch = refs[4 + 1 + N_FORWARD_OUTS - 1 :]
    blocks, k_ref, vt_ref, att_t, probs, probs_sem, total, low, keep_sem = scratch
    load = pltpu.make_async_copy(blocks_in, blocks, keep_sem)
    load.start()
    load.wait()
    forward_compute(
        blocks, biases, xs, keybias, valid, cot, vec, probs_hbm, *outs,
        k_ref, vt_ref, att_t, probs, probs_sem, total, low, NoHooks(),
    )


BLOCKS = (3, 4, 2, 2, 2, 96, 768)


def forward_outs(rows):
    def of(shape, dtype):
        return jax.ShapeDtypeStruct(shape, dtype)

    return [
        of((12, LEN, rows), BF16),
        of((rows, 768), BF16),
        of((12, 8, rows), F32),
        of((12, 64, rows), F32),
        of((2, 768, rows), BF16),
        of((12, rows, 128), BF16),
        of((8, 128, LEN), BF16),
        of((8, LEN, 128), BF16),
        of((4, rows, 256), BF16),
        of((4, rows, 768), BF16),
        of((4, rows, 768), BF16),
        of((768, rows), BF16),
        of((rows, 768), F32),
        of((rows, 1), F32),
        of((rows, 768), BF16),
        of((768, rows), BF16),
        of((rows, 768), F32),
        of((8, 768), F32),
    ]


def forward_scratch(rows):
    return [
        pltpu.VMEM((8, LEN, 128), BF16),
        pltpu.VMEM((8, 128, LEN), BF16),
        pltpu.VMEM((256, rows), BF16),
        pltpu.VMEM((3, LEN, rows), BF16),
        pltpu.SemaphoreType.DMA((3,)),
        pltpu.VMEM((rows, 768), F32),
        pltpu.VMEM((rows, 768), BF16),
    ]


def run_forward(linked, weights, bias, x, keybias, valid, cot, vec):
    rows = valid.shape[0]
    outs = forward_outs(rows)
    if linked:
        return pl.pallas_call(
            forward_linked,
            name="forward",
            out_shape=[jax.ShapeDtypeStruct(BLOCKS, BF16), *outs],
            in_specs=[vmem()] * 7,
            out_specs=[hbm(), hbm()] + [vmem()] * (N_FORWARD_OUTS - 1),
            scratch_shapes=[
                pltpu.VMEM(BLOCKS, BF16),
                pltpu.VMEM((4, 16, 768), BF16),
                pltpu.VMEM((2, rows, 768), BF16),
                *forward_scratch(rows),
                pltpu.SemaphoreType.DMA((4, 2, 3)),
                pltpu.SemaphoreType.DMA((4, 4)),
                pltpu.SemaphoreType.DMA((3, 9)),
                pltpu.SemaphoreType.DMA((3, 9)),
                pltpu.SemaphoreType.DMA,
                pltpu.SemaphoreType.DMA,
                pltpu.SemaphoreType.DMA,
            ],
            compiler_params=pltpu.CompilerParams(
                collective_id=0, has_side_effects=True, vmem_limit_bytes=VMEM_LIMIT
            ),
        )(weights, bias, x, keybias, valid, cot, vec)
    outs = pl.pallas_call(
        forward_alone,
        name="forward",
        out_shape=outs,
        in_specs=[hbm()] + [vmem()] * 6,
        out_specs=[hbm()] + [vmem()] * (N_FORWARD_OUTS - 1),
        scratch_shapes=[
            pltpu.VMEM(BLOCKS, BF16),
            *forward_scratch(rows),
            pltpu.SemaphoreType.DMA,
        ],
        compiler_params=pltpu.CompilerParams(vmem_limit_bytes=VMEM_LIMIT),
    )(weights, bias, x, keybias, valid, cot, vec)
    return [weights, *outs]


class Scatter:
    def __init__(self, at, grads, core_in, first_in, second_in, z_in, out, send, recv, z_send, z_recv):
        self.at, self.grads, self.out = at, grads, out
        self.core_in, self.first_in, self.second_in, self.z_in = core_in, first_in, second_in, z_in
        self.send, self.recv, self.z_send, self.z_recv = send, recv, z_send, z_recv

    def copy(self, kind, m, which):
        at, grads = self.at, self.grads.at[kind, m]
        x, y, c = at.x, at.y, at.c
        low, high = pl.ds(0, 48), pl.ds(48, 48)
        src, dst, device = {
            0: lambda: (grads.at[:, :, 1 - c], self.core_in.at[kind, m], at.core),
            1: lambda: (grads.at[:, 1 - x, c, low], self.first_in.at[kind, m, 0], at.across_x),
            2: lambda: (grads.at[1 - y, :, c, high], self.first_in.at[kind, m, 1], at.across_y),
            3: lambda: (grads.at[1 - y, x, c, low], self.second_in.at[kind, m, 0], at.across_y),
            4: lambda: (grads.at[y, 1 - x, c, high], self.second_in.at[kind, m, 1], at.across_x),
        }[which]()
        return remote(src, dst, self.send.at[kind, m, which], self.recv.at[kind, m, which], device)

    def add(self, ref, got):
        ref[...] = (ref[...].astype(F32) + got[...].astype(F32)).astype(BF16)

    def begin(self, kind, m):
        self.copy(kind, m, 0).start()

    def first(self, kind, m):
        at, grads = self.at, self.grads.at[kind, m]
        self.copy(kind, m, 0).wait_recv()
        for y in range(2):
            for x in range(2):
                self.add(grads.at[y, x, at.c], self.core_in.at[kind, m, y, x])
        self.copy(kind, m, 1).start()
        self.copy(kind, m, 2).start()

    def second(self, kind, m):
        at, grads = self.at, self.grads.at[kind, m]
        low, high = pl.ds(0, 48), pl.ds(48, 48)
        self.copy(kind, m, 1).wait_recv()
        for y in range(2):
            self.add(grads.at[y, at.x, at.c, low], self.first_in.at[kind, m, 0, y])
        self.copy(kind, m, 3).start()
        self.copy(kind, m, 2).wait_recv()
        for x in range(2):
            self.add(grads.at[at.y, x, at.c, high], self.first_in.at[kind, m, 1, x])
        self.copy(kind, m, 4).start()

    def third(self, kind, m):
        at = self.at
        grads = self.grads.at[kind, m, at.y, at.x, at.c]
        self.copy(kind, m, 3).wait_recv()
        self.add(grads.at[pl.ds(0, 48)], self.second_in.at[kind, m, 0])
        self.copy(kind, m, 4).wait_recv()
        self.add(grads.at[pl.ds(48, 48)], self.second_in.at[kind, m, 1])

    def z_copy(self, kind, m, direction):
        at = self.at
        src = self.grads.at[kind, m, at.y, at.x, at.c]
        device = at.right if direction == 0 else at.left
        slot = m if direction == 0 else jnp.where(m == at.z - 1, 4, m)
        return remote(src, self.z_in.at[kind, slot], self.z_send.at[kind, m], self.z_recv.at[kind, slot], device)

    def z_landed(self, kind, m, slot, direction):
        at = self.at
        src = self.grads.at[kind, m, at.y, at.x, at.c]
        device = at.right if direction == 0 else at.left
        return remote(src, self.z_in.at[kind, slot], self.z_send.at[kind, m], self.z_recv.at[kind, slot], device)

    def relay(self, kind, m, direction):
        at = self.at
        self.z_landed(kind, m, m, direction).wait_recv()
        self.add(self.grads.at[kind, m, at.y, at.x, at.c], self.z_in.at[kind, m])
        self.z_copy(kind, m, direction).start()

    def z_step(self, kind, step):
        z = self.at.z
        if step == 0:

            @pl.when(z == 0)
            def _():
                for m in (3, 2, 1):
                    self.z_copy(kind, m, 0).start()

            @pl.when(z == 3)
            def _():
                for m in (0, 1, 2):
                    self.z_copy(kind, m, 1).start()

        elif step == 1:

            @pl.when(z == 1)
            def _():
                for m in (3, 2):
                    self.relay(kind, m, 0)

            @pl.when(z == 2)
            def _():
                for m in (0, 1):
                    self.relay(kind, m, 1)

        elif step == 2:
            pl.when(z == 2)(lambda: self.relay(kind, 3, 0))
            pl.when(z == 1)(lambda: self.relay(kind, 0, 1))
        else:
            at = self.at
            self.out[kind] = self.grads[kind, z, at.y, at.x, at.c].astype(F32)

            @pl.when(z > 0)
            def _():
                self.z_landed(kind, z, z, 0).wait_recv()
                self.out[kind] += self.z_in[kind, z].astype(F32)

            @pl.when(z < 3)
            def _():
                self.z_landed(kind, z, 4, 1).wait_recv()
                self.out[kind] += self.z_in[kind, 4].astype(F32)

    def drain(self):
        z = self.at.z
        for kind in range(3):

            def of_index(m, _, kind=kind):
                for which in range(5):
                    self.copy(kind, m, which).wait_send()
                pl.when(m > z)(lambda: self.z_copy(kind, m, 0).wait_send())
                pl.when(m < z)(lambda: self.z_copy(kind, m, 1).wait_send())
                return 0

            lax.fori_loop(0, 4, of_index, 0)


class Totals:
    def __init__(self, at, rows, got, send, recv):
        self.rows, self.got, self.send, self.recv = rows, got, send, recv
        self.partners = (at.core, at.across_x, at.across_y, at.mate, at.far)

    def copy(self, stage):
        return remote(
            self.rows.at[stage], self.got.at[stage], self.send.at[stage], self.recv.at[stage], self.partners[stage]
        )

    def start(self, stage):
        self.copy(stage).start()

    def finish(self, stage):
        self.copy(stage).wait()
        self.rows[stage + 1] = self.rows[stage] + self.got[stage]


def backward_compute(
    blocks_hbm,
    probs_hbm,
    acted_hbm,
    slope_hbm,
    recip_ref,
    headout_ref,
    xt_ref,
    qm_ref,
    kt_ref,
    v_ref,
    att_ref,
    n1t_ref,
    n1_hbm,
    rs1_ref,
    gb2_ref,
    gb2t_ref,
    g2_hbm,
    sums_ref,
    masked_ref,
    vec_ref,
    grads,
    rows_ref,
    weight,
    weight_sem,
    acts,
    acts_sem,
    probs,
    probs_sem,
    gb1,
    gb1t,
    grad_one,
    parts,
    g2_ref,
    state_sem,
    hooks,
):
    rows = g2_ref.shape[0]
    g2_load = pltpu.make_async_copy(g2_hbm, g2_ref, state_sem.at[0])
    n1_load = pltpu.make_async_copy(n1_hbm, grad_one, state_sem.at[1])

    def weight_load(kind, m, slot):
        return pltpu.make_async_copy(blocks_hbm.at[kind, m], weight.at[slot], weight_sem.at[slot])

    def act_loads(m, slot):
        return (
            pltpu.make_async_copy(acted_hbm.at[m], acts.at[slot, 0], acts_sem.at[slot, 0]),
            pltpu.make_async_copy(slope_hbm.at[m], acts.at[slot, 1], acts_sem.at[slot, 1]),
        )

    def probs_load(head, slot):
        return pltpu.make_async_copy(probs_hbm.at[head], probs.at[slot], probs_sem.at[slot])

    def feed_loads(m, slot):
        return (weight_load(DOWN, m, 2 * slot), weight_load(UP, m, 2 * slot + 1), *act_loads(m, slot))

    def begin(copies):
        for copy in copies:
            copy.start()

    def finish(copies):
        for copy in copies:
            copy.wait()

    def block(slot, low=0, width=768):
        return weight[slot, :, :, :, :, pl.ds(low, width)].reshape(768, width)

    def put(kind, m, value, low=0):
        width = value.shape[1]
        grads[kind, m, :, :, :, :, pl.ds(low, width)] = value.astype(BF16).reshape(2, 2, 2, 96, width)

    begin(feed_loads(0, 0))
    begin((g2_load, n1_load))
    for j in range(3):
        probs_load(j, j).start()
    parts[...] = jnp.zeros_like(parts)
    finish((g2_load, n1_load))

    def feed(m, _):
        slot = lax.rem(m, 2)
        pl.when(m < 3)(lambda: begin(feed_loads(m + 1, 1 - slot)))
        finish(feed_loads(m, slot))
        grad_acted = dot(gb2_ref[...], block(2 * slot))
        grad_pre = (grad_acted * acts[slot, 1].astype(F32)).astype(BF16)
        acts[slot, 1] = grad_pre
        parts[m, 0:1, :] = jnp.sum(grad_pre.astype(F32), axis=0, keepdims=True)
        put(DOWN, m, dot(gb2t_ref[...], acts[slot, 0]))
        hooks.down_ready(m)
        put(UP, m, dot(n1t_ref[...], acts[slot, 1]))
        hooks.up_ready(m)
        g2_ref[...] += dot(acts[slot, 1], block(2 * slot + 1), (1, 1))
        return 0

    lax.fori_loop(0, 4, feed, 0)
    for m in range(4):
        weight_load(ATT, m, m).start()

    chunk = 64

    def norm_back(i, sums):
        r = pl.ds(pl.multiple_of(i * chunk, chunk), chunk)
        grad = g2_ref[r, :]
        unit = grad_one[r, :]
        scaled = grad * vec_ref[2:3, :]
        grad_in = (
            scaled
            - jnp.mean(scaled, axis=1, keepdims=True)
            - unit * jnp.mean(scaled * unit, axis=1, keepdims=True)
        ) * rs1_ref[r, :]
        grad_one[r, :] = grad_in
        gb1[r, :] = grad_in.astype(BF16)
        return (
            sums[0] + jnp.sum(grad_in, axis=0, keepdims=True),
            sums[1] + jnp.sum(grad * unit, axis=0, keepdims=True),
            sums[2] + jnp.sum(grad, axis=0, keepdims=True),
        )

    zero = jnp.zeros((1, 768), F32)
    sums = lax.fori_loop(0, rows // chunk, norm_back, (zero, zero, zero))
    rows_ref[0, 0:1, :] = sums[0]
    rows_ref[0, 1:2, :] = sums_ref[0:1, :]
    rows_ref[0, 2:3, :] = sums[1]
    rows_ref[0, 3:4, :] = sums[2]
    rows_ref[0, 4:5, :] = sums_ref[1:2, :]
    rows_ref[0, 5:6, :] = sums_ref[2:3, :]
    gb1t[...] = gb1[...].T
    g2_ref[...] = jnp.zeros_like(g2_ref)

    def attend_back(m, _):
        weight_load(ATT, m, m).wait()
        w_out = block(m, 512, 256)
        grad_att_t = dot(gb1[...], w_out).T
        zeros = jnp.zeros((64, rows), BF16)
        sides = []
        for j in range(3):
            place = (128, 192, 64)[j]
            scaled = (grad_att_t[place : place + 64, :] * recip_ref[3 * m + j, 0:1, :]).astype(BF16)
            sides.append(scaled)
        wide = [
            jnp.concatenate([sides[0], zeros], axis=0),
            jnp.concatenate([zeros, sides[1]], axis=0),
            jnp.concatenate([sides[2], zeros], axis=0),
        ]
        dk, dv, dq = [None, None], [None, None], [None, None]
        for j in range(3):
            t = j // 2
            tile, head = 2 * m + t, 3 * m + j
            shift = jnp.sum(sides[j].astype(F32) * headout_ref[head], axis=0, keepdims=True)
            probs_load(head, j).wait()
            weights = probs[j]
            grad_weights = dot(v_ref[tile], wide[j])
            grad_scores = (weights.astype(F32) * (grad_weights - shift)).astype(BF16)
            grad_v = dot(weights, wide[j].T)
            pl.when(m < 3)(lambda h=head, s=j: probs_load(h + 3, s).start())
            grad_k = dot(grad_scores, qm_ref[head])
            half = 64 * (j % 2) if j < 2 else 64
            grad_q = dot(kt_ref[tile, half : half + 64, :], grad_scores) * SCALE
            dk[t] = grad_k if dk[t] is None else dk[t] + grad_k
            dv[t] = grad_v if dv[t] is None else dv[t] + grad_v
            dq[t] = grad_q if dq[t] is None else jnp.concatenate([dq[t], grad_q], axis=0)
        dq_pair = dq[0].T.astype(BF16)
        dq_single = jnp.concatenate([dq[1], jnp.zeros((64, rows), F32)], axis=0).T.astype(BF16)
        dk = [d.astype(BF16) for d in dk]
        dv = [d.astype(BF16) for d in dv]
        own = acts.at[0, 0, :, pl.ds(0, PROJ)]
        own[:, 0:128] = dq_pair
        own[:, 128:256] = dk[0][:rows]
        own[:, 256:384] = dv[0][:rows]
        own[:, 384:512] = dq_single + dk[1][:rows]
        own[:, 512:640] = dv[1][:rows]
        other = acts.at[0, 1, :, pl.ds(0, PROJ)]
        other[:, 128:256] = dk[0][rows:]
        other[:, 256:384] = dv[0][rows:]
        other[:, 384:512] = dk[1][rows:]
        other[:, 512:640] = dv[1][rows:]
        wide_sum = jnp.sum(own[...].astype(F32), axis=0, keepdims=True)
        narrow_sum = jnp.sum(other[:, 128:640].astype(F32), axis=0, keepdims=True)
        parts[4 + m, 0:1, 0:128] = wide_sum[:, :128]
        parts[4 + m, 0:1, 128:640] = wide_sum[:, 128:] + narrow_sum
        grad_proj = dot(xt_ref[0], own[...])
        grad_other = dot(xt_ref[1], other[:, 128:640])
        grad_out_w = dot(gb1t[...], att_ref[m])
        put(ATT, m, grad_proj[:, :128], 0)
        put(ATT, m, grad_proj[:, 128:512] + grad_other[:, :384], 128)
        put(ATT, m, grad_proj[:, 512:] + grad_other[:, 384:] + grad_out_w[:, :128], 512)
        put(ATT, m, grad_out_w[:, 128:], 640)
        hooks.att_ready(m)
        grad_one[...] += dot(own[...], block(m, 0, PROJ), (1, 1))
        g2_ref[...] += dot(other[:, 128:640], block(m, 128, 512), (1, 1))
        return 0

    lax.fori_loop(0, 4, attend_back, 0)

    def fill(i, total):
        r = pl.ds(pl.multiple_of(i * chunk, chunk), chunk)
        other = g2_ref[r, :]
        gb1[r, :] = other.astype(BF16)
        return total + jnp.sum(
            grad_one[r, :] * masked_ref[0, r, :] + other * masked_ref[1, r, :], axis=0, keepdims=True
        )

    rows_ref[0, 6:7, :] = lax.fori_loop(0, rows // chunk, fill, zero)
    rows_ref[0, 7:8, :] = zero
    for row in range(8):
        rows_ref[0, 8 + row : 9 + row, :] = parts[row, 0:1, :]


def finish_frames(grad_one, got, masked_ref, frames_ref):
    chunk = 64

    def body(i, _):
        r = pl.ds(pl.multiple_of(i * chunk, chunk), chunk)
        total = grad_one[r, :] + got[r, :].astype(F32)
        frames_ref[r, :] = jnp.where(masked_ref[0, r, :] > 0, 0.0, total).astype(BF16)
        return 0

    lax.fori_loop(0, grad_one.shape[0] // chunk, body, 0)


class NoScatter:
    def down_ready(self, m):
        pass

    def up_ready(self, m):
        pass

    def att_ready(self, m):
        pass


N_BACKWARD_INS = 20


def backward_linked(*refs):
    ins = refs[:N_BACKWARD_INS]
    out_ref, rows_out, frames_ref = refs[N_BACKWARD_INS : N_BACKWARD_INS + 3]
    scratch = refs[N_BACKWARD_INS + 3 :]
    grads, rows_ref, weight, weight_sem, acts, acts_sem, probs, probs_sem = scratch[:8]
    gb1, gb1t, grad_one, parts, g2, state_sem = scratch[8:14]
    core_in, first_in, second_in, z_in, rows_in, mate_in = scratch[14:20]
    send, recv, z_send, z_recv, t_send, t_recv, m_send, m_recv = scratch[20:]
    at = Place()
    at.greet(True)
    scatter = Scatter(at, grads, core_in, first_in, second_in, z_in, out_ref, send, recv, z_send, z_recv)
    totals = Totals(at, rows_ref, rows_in, t_send, t_recv)
    backward_compute(
        *ins, grads, rows_ref, weight, weight_sem, acts, acts_sem, probs, probs_sem,
        gb1, gb1t, grad_one, parts, g2, state_sem, NoScatter(),
    )
    swap = remote(gb1, mate_in, m_send, m_recv, at.mate)
    swap.start()
    totals.start(0)

    def each(step, kind):
        def body(m, _):
            step(kind, m)
            return 0

        lax.fori_loop(0, 4, body, 0)

    for kind in range(3):
        each(scatter.begin, kind)
    for kind in range(3):
        each(scatter.first, kind)
    for kind in range(3):
        each(scatter.second, kind)
    for kind in range(3):
        each(scatter.third, kind)
        scatter.z_step(kind, 0)
    for step in range(1, 4):
        for kind in range(3):
            scatter.z_step(kind, step)
    for stage in range(5):
        totals.finish(stage)
        if stage < 4:
            totals.start(stage + 1)
    rows_out[...] = rows_ref[5]
    swap.wait()
    finish_frames(grad_one, mate_in, ins[18], frames_ref)
    scatter.drain()


def backward_alone(*refs):
    ins = refs[:N_BACKWARD_INS]
    grads_out, rows_out, mate_out, grad_one_out = refs[N_BACKWARD_INS : N_BACKWARD_INS + 4]
    scratch = refs[N_BACKWARD_INS + 4 :]
    grads, rows_ref, weight, weight_sem, acts, acts_sem, probs, probs_sem = scratch[:8]
    gb1, gb1t, grad_one, parts, g2, state_sem, keep_sem = scratch[8:]
    backward_compute(
        *ins, grads, rows_ref, weight, weight_sem, acts, acts_sem, probs, probs_sem,
        gb1, gb1t, grad_one, parts, g2, state_sem, NoScatter(),
    )
    keep = pltpu.make_async_copy(grads, grads_out, keep_sem)
    keep.start()
    rows_out[...] = rows_ref[0]
    mate_out[...] = gb1[...]
    grad_one_out[...] = grad_one[...]
    keep.wait()


def backward_scratch(rows):
    return [
        pltpu.VMEM(BLOCKS, BF16),
        pltpu.VMEM((6, 16, 768), F32),
        pltpu.VMEM((4, *BLOCKS[2:]), BF16),
        pltpu.SemaphoreType.DMA((4,)),
        pltpu.VMEM((2, 2, rows, 768), BF16),
        pltpu.SemaphoreType.DMA((2, 2)),
        pltpu.VMEM((3, LEN, rows), BF16),
        pltpu.SemaphoreType.DMA((3,)),
        pltpu.VMEM((rows, 768), BF16),
        pltpu.VMEM((768, rows), BF16),
        pltpu.VMEM((rows, 768), F32),
        pltpu.VMEM((8, 8, 768), F32),
        pltpu.VMEM((rows, 768), F32),
        pltpu.SemaphoreType.DMA((2,)),
    ]


def run_backward(linked, saved, masked, vec):
    blocks, probs, _, recip, headout, xt, qm, kt, v, att, acted, slope, n1t, n1, rs1, gb2, gb2t, g2, sums = saved
    rows = gb2.shape[0]
    ins = (
        blocks, probs, acted, slope, recip, headout, xt, qm, kt, v, att, n1t, n1, rs1, gb2, gb2t, g2, sums, masked, vec
    )
    in_specs = [hbm() if i in (0, 1, 2, 3, 12, 16) else vmem() for i in range(20)]
    if linked:
        return pl.pallas_call(
            backward_linked,
            name="backward",
            out_shape=[
                jax.ShapeDtypeStruct((3, 96, 768), F32),
                jax.ShapeDtypeStruct((16, 768), F32),
                jax.ShapeDtypeStruct((rows, 768), BF16),
            ],
            in_specs=in_specs,
            out_specs=[vmem()] * 3,
            scratch_shapes=[
                *backward_scratch(rows),
                pltpu.VMEM((3, 4, 2, 2, 96, 768), BF16),
                pltpu.VMEM((3, 4, 2, 2, 48, 768), BF16),
                pltpu.VMEM((3, 4, 2, 48, 768), BF16),
                pltpu.VMEM((3, 5, 96, 768), BF16),
                pltpu.VMEM((5, 16, 768), F32),
                pltpu.VMEM((rows, 768), BF16),
                pltpu.SemaphoreType.DMA((3, 4, 5)),
                pltpu.SemaphoreType.DMA((3, 4, 5)),
                pltpu.SemaphoreType.DMA((3, 4)),
                pltpu.SemaphoreType.DMA((3, 5)),
                pltpu.SemaphoreType.DMA((5,)),
                pltpu.SemaphoreType.DMA((5,)),
                pltpu.SemaphoreType.DMA,
                pltpu.SemaphoreType.DMA,
            ],
            compiler_params=pltpu.CompilerParams(
                collective_id=1, has_side_effects=True, vmem_limit_bytes=VMEM_LIMIT
            ),
        )(*ins)
    return pl.pallas_call(
        backward_alone,
        name="backward",
        out_shape=[
            jax.ShapeDtypeStruct(BLOCKS, BF16),
            jax.ShapeDtypeStruct((16, 768), F32),
            jax.ShapeDtypeStruct((rows, 768), BF16),
            jax.ShapeDtypeStruct((rows, 768), F32),
        ],
        in_specs=in_specs,
        out_specs=[hbm()] + [vmem()] * 3,
        scratch_shapes=[*backward_scratch(rows), pltpu.SemaphoreType.DMA],
        compiler_params=pltpu.CompilerParams(vmem_limit_bytes=VMEM_LIMIT),
    )(*ins)


def shards(
    linked,
    frames,
    lengths,
    span_starts,
    cotangent,
    query_weight,
    key_weight,
    value_weight,
    out_weight,
    up_weight,
    down_weight,
    query_bias,
    value_bias,
    up_bias,
    out_bias,
    down_bias,
    first_gain,
    first_shift,
    second_gain,
    second_shift,
    mask_vector,
):
    rows = frames.shape[0]
    dims = query_weight.shape[0]
    z = lax.axis_index("mp")
    clip = z // 2
    half = z % 2
    length = lax.dynamic_index_in_dim(lengths, clip, keepdims=False)
    starts = lax.dynamic_index_in_dim(span_starts, clip, keepdims=False)
    slots = (jnp.arange(LEN, dtype=jnp.int32) + half * rows) % LEN
    valid = slots < length
    masked = jnp.any((slots[:, None] >= starts[None, :]) & (slots[:, None] < starts[None, :] + SPAN), axis=1)
    keybias = jnp.where(
        (jnp.arange(128) == 0)[None, :] & ~valid[:, None], jnp.float32(NEGATIVE), 0.0
    ).astype(BF16)
    valid_rows = valid[:rows].astype(F32)[:, None]
    masked_rows = masked.astype(F32).reshape(2, rows, 1)
    x = jnp.where(masked[:rows, None], mask_vector[None, :], frames)
    out_t = out_weight.T
    pair, single = 2 * HEAD_DIM, 3 * HEAD_DIM
    pack = jnp.stack(
        [
            jnp.concatenate(
                [
                    query_weight[:, :pair], key_weight[:, :pair], value_weight[:, :pair],
                    query_weight[:, pair:], key_weight[:, pair:], value_weight[:, pair:],
                    out_t[:, pair:], out_t[:, :pair],
                ],
                axis=1,
            ),
            up_weight,
            down_weight.T,
        ]
    )
    q_shift, v_shift = query_bias.reshape(-1), value_bias.reshape(-1)
    blank = jnp.zeros((pair,), BF16)
    short = blank[:HEAD_DIM]
    bias = jnp.stack(
        [
            jnp.concatenate([q_shift[:pair], blank, v_shift[:pair], q_shift[pair:], short, v_shift[pair:], short, blank]),
            up_bias.reshape(-1),
        ]
    )
    bias = jnp.pad(bias, ((0, 14), (0, 0)))
    vec = jnp.stack([out_bias, down_bias, first_gain, first_shift, second_gain, second_shift]).astype(F32)
    vec = jnp.pad(vec, ((0, 2), (0, 0)))
    if linked:
        saved = run_forward(True, pack, bias, x, keybias, valid_rows, cotangent, vec)
        grads, totals, grad_frames = run_backward(True, saved, masked_rows, vec)
    else:
        mates = [(0, 1), (1, 0), (2, 3), (3, 2)]
        blocks = lax.all_gather(lax.all_gather(pack, "dp", axis=1, tiled=True), "mp", axis=1)
        biases = lax.all_gather(bias, "mp", axis=0)
        both = jnp.stack([x, lax.ppermute(x, "mp", mates)])
        saved = run_forward(False, blocks.reshape(BLOCKS), biases, both, keybias, valid_rows, cotangent, vec)
        grads, totals, mate, grad_one = run_backward(False, saved, masked_rows, vec)
        grads = grads.reshape(3, 4, 768, 768).astype(F32)
        grads = lax.psum_scatter(grads, "mp", scatter_dimension=1, tiled=False)
        grads = lax.psum_scatter(grads, "dp", scatter_dimension=1, tiled=True)
        totals = lax.psum(totals, ("dp", "mp"))
        grad_frames = grad_one + lax.ppermute(mate, "mp", mates).astype(F32)
        grad_frames = jnp.where(masked[:rows, None], 0.0, grad_frames).astype(BF16)
    out_frames = saved[2]
    att, grad_up, grad_down = grads[0], grads[1], grads[2].T
    grad_query = jnp.concatenate([att[:, 0:128], att[:, 384:448]], axis=1)
    grad_key = jnp.concatenate([att[:, 128:256], att[:, 448:512]], axis=1)
    grad_value = jnp.concatenate([att[:, 256:384], att[:, 512:576]], axis=1)
    grad_out = jnp.concatenate([att[:, 640:768], att[:, 576:640]], axis=1).T
    dp, n_dp = lax.axis_index("dp"), 768 // dims
    part = 768 // (n_dp * 4)
    row_parts = lax.dynamic_slice(totals, (0, (dp * 4 + z) * part), (7, part))
    head_row = lax.dynamic_slice(totals, (12 + z, 0), (1, 768))[0]
    q_row = jnp.concatenate([head_row[0:128], head_row[384:448]]).reshape(3, HEAD_DIM)
    v_row = jnp.concatenate([head_row[256:384], head_row[512:576]]).reshape(3, HEAD_DIM)
    up_row = lax.dynamic_slice(totals, (8 + z, 0), (1, 768)).reshape(6, 128)
    step = HEAD_DIM // n_dp
    grad_query_bias = lax.dynamic_slice(q_row, (0, dp * step), (3, step))
    grad_value_bias = lax.dynamic_slice(v_row, (0, dp * step), (3, step))
    grad_up_bias = lax.dynamic_slice(up_row, (0, dp * 2 * step), (6, 2 * step))
    return (
        out_frames,
        grad_frames,
        grad_query,
        grad_key,
        grad_value,
        grad_out,
        grad_up,
        grad_down,
        grad_query_bias,
        grad_value_bias,
        grad_up_bias,
        *(row_parts[i] for i in range(7)),
    )


def solution(mesh):
    linked = mesh.shape["dp"] == 8 and mesh.shape["mp"] == 4
    split = P(("dp", "mp"))
    return jax.shard_map(
        functools.partial(shards, linked),
        mesh=mesh,
        in_specs=(
            P(("dp", "mp"), None),
            P("dp"),
            P("dp", None),
            P(("dp", "mp"), None),
            P("dp", "mp"),
            P("dp", "mp"),
            P("dp", "mp"),
            P("mp", "dp"),
            P("dp", "mp"),
            P("mp", "dp"),
            P("mp", None),
            P("mp", None),
            P("mp", None),
            *([P()] * 7),
        ),
        out_specs=(
            P(("dp", "mp"), None),
            P(("dp", "mp"), None),
            P("dp", "mp"),
            P("dp", "mp"),
            P("dp", "mp"),
            P("mp", "dp"),
            P("dp", "mp"),
            P("mp", "dp"),
            P("mp", "dp"),
            P("mp", "dp"),
            P("mp", "dp"),
            *([split] * 7),
        ),
        check_vma=False,
    )
```

```python
import functools
import math

import jax
import jax.numpy as jnp
from jax import lax
from jax.experimental import pallas as pl
from jax.experimental.pallas import tpu as pltpu
from jax.sharding import PartitionSpec as P

HEAD_DIM = 64
SPAN = 10
LEN = 1024
EPSILON = 1e-05
NEGATIVE = -1e30
SCALE = 1.0 / math.sqrt(HEAD_DIM)

F32 = jnp.float32
BF16 = jnp.bfloat16
MESH = pl.DeviceIdType.MESH
VMEM_LIMIT = 63 * 1024 * 1024

ATT, UP, DOWN = 0, 1, 2
PROJ = 640


def dot(left, right, contract=(1, 0)):
    return lax.dot_general(
        left, right, (((contract[0],), (contract[1],)), ((), ())), preferred_element_type=F32
    )


def hbm():
    return pl.BlockSpec(memory_space=pl.ANY)


def vmem():
    return pl.BlockSpec(memory_space=pltpu.VMEM)


class Place:
    def __init__(self):
        self.dp = lax.axis_index("dp")
        self.z = lax.axis_index("mp")
        self.c = lax.rem(self.dp, 2)
        self.x = lax.rem(self.dp // 2, 2)
        self.y = self.dp // 4
        self.core = (self.dp + 1 - 2 * self.c, self.z)
        self.across_x = (self.dp + 2 - 4 * self.x, self.z)
        self.across_y = (self.dp + 4 - 8 * self.y, self.z)
        self.right = (self.dp, self.z + 1)
        self.left = (self.dp, self.z - 1)
        self.mate = (self.dp, self.z + 1 - 2 * lax.rem(self.z, 2))
        self.far = (self.dp, lax.rem(self.z + 2, 4))

    def greet(self, far):
        barrier = pltpu.get_barrier_semaphore()

        def signal(device):
            pl.semaphore_signal(barrier, inc=1, device_id=device, device_id_type=MESH)

        signal(self.core)
        signal(self.across_x)
        signal(self.across_y)
        if far:
            signal(self.far)
        pl.when(self.z < 3)(lambda: signal(self.right))
        pl.when(self.z > 0)(lambda: signal(self.left))
        ends = jnp.where((self.z == 0) | (self.z == 3), 1, 2)
        pl.semaphore_wait(barrier, (4 if far else 3) + ends)


def remote(src, dst, send, recv, device):
    return pltpu.make_async_remote_copy(
        src_ref=src, dst_ref=dst, send_sem=send, recv_sem=recv, device_id=device, device_id_type=MESH
    )


class Gather:
    def __init__(self, at, blocks, biases, z_send, z_recv, f_send, f_recv, p_send, p_recv):
        self.at, self.blocks, self.biases = at, blocks, biases
        self.z_send, self.z_recv = z_send, z_recv
        self.f_send, self.f_recv, self.p_send, self.p_recv = f_send, f_recv, p_send, p_recv

    def z_copy(self, kind, m, direction, step):
        at = self.at
        if kind == 3:
            ref = self.biases.at[m]
        else:
            ref = self.blocks.at[kind, m, at.y, at.x, at.c]
        device = at.right if direction == 0 else at.left
        return remote(ref, ref, self.z_send.at[kind, direction, step], self.z_recv.at[kind, m], device)

    def z_step(self, kind, step):
        z = self.at.z
        if step == 0:
            pl.when(z < 3)(lambda: self.z_copy(kind, z, 0, 0).start())
            pl.when(z > 0)(lambda: self.z_copy(kind, z, 1, 0).start())
            self.first(kind, z)
            return

        @pl.when(z >= step)
        def _():
            self.z_copy(kind, z - step, 0, 0).wait_recv()
            if step < 3:
                pl.when(z < 3)(lambda: self.z_copy(kind, z - step, 0, step).start())
            self.first(kind, z - step)

        @pl.when(z + step <= 3)
        def _():
            self.z_copy(kind, z + step, 1, 0).wait_recv()
            if step < 3:
                pl.when(z > 0)(lambda: self.z_copy(kind, z + step, 1, step).start())
            self.first(kind, z + step)

    def first_copy(self, kind, m, which):
        at = self.at
        ref = self.blocks.at[kind, m, at.y, at.x, at.c]
        ref, device = {
            0: lambda: (ref.at[pl.ds(0, 48)], at.across_x),
            1: lambda: (ref.at[pl.ds(48, 48)], at.across_y),
            2: lambda: (ref, at.core),
        }[which]()
        return remote(ref, ref, self.f_send.at[kind, m, which], self.f_recv.at[kind, m, which], device)

    def first(self, kind, m):
        if kind == 3:
            return
        for which in range(3):
            self.first_copy(kind, m, which).start()

    def plane_copy(self, kind, which):
        at, blocks = self.at, self.blocks.at[kind]
        x, y, c = at.x, at.y, at.c
        low, high = pl.ds(0, 48), pl.ds(48, 48)
        ref, device = {
            0: lambda: (blocks.at[:, y, :, c, low], at.across_y),
            1: lambda: (blocks.at[:, :, x, c, high], at.across_x),
            2: lambda: (blocks.at[:, y, 1 - x, c, low], at.core),
            3: lambda: (blocks.at[:, 1 - y, x, c, high], at.core),
            4: lambda: (blocks.at[:, 1 - y, :, c, low], at.core),
            5: lambda: (blocks.at[:, :, 1 - x, c, high], at.core),
        }[which]()
        return remote(ref, ref, self.p_send.at[kind, which], self.p_recv.at[kind, which], device)

    def second(self, kind):
        for m in range(4):
            self.first_copy(kind, m, 0).wait_recv()
        self.plane_copy(kind, 0).start()
        for m in range(4):
            self.first_copy(kind, m, 1).wait_recv()
        self.plane_copy(kind, 1).start()
        self.plane_copy(kind, 2).start()
        self.plane_copy(kind, 3).start()

    def third(self, kind):
        self.plane_copy(kind, 0).wait_recv()
        self.plane_copy(kind, 4).start()
        self.plane_copy(kind, 1).wait_recv()
        self.plane_copy(kind, 5).start()

    def last(self, kind):
        for m in range(4):
            self.first_copy(kind, m, 2).wait_recv()
        for which in range(2, 6):
            self.plane_copy(kind, which).wait_recv()

    def drain(self):
        z = self.at.z
        for kind in range(4):
            for step in range(3):
                pl.when((z < 3) & (z >= step))(
                    lambda k=kind, s=step: self.z_copy(k, z - s, 0, s).wait_send()
                )
                pl.when((z > 0) & (z + step <= 3))(
                    lambda k=kind, s=step: self.z_copy(k, z + s, 1, s).wait_send()
                )
        for kind in range(3):
            for m in range(4):
                for which in range(3):
                    self.first_copy(kind, m, which).wait_send()
            for which in range(6):
                self.plane_copy(kind, which).wait_send()


def block_of(blocks, kind, m, low=0, width=768):
    return blocks[kind, m, :, :, :, :, pl.ds(low, width)].reshape(768, width)


def lane_mask(rows, lower):
    lanes = lax.broadcasted_iota(jnp.int32, (rows, 128), 1)
    return (lanes < 64) if lower else (lanes >= 64)


def forward_compute(
    blocks,
    biases,
    xs,
    keybias_ref,
    valid_ref,
    cot_ref,
    vec_ref,
    probs_hbm,
    out_ref,
    recip_ref,
    headout_ref,
    xt_ref,
    qm_ref,
    kt_ref,
    v_ref,
    att_ref,
    acted_ref,
    slope_ref,
    n1t_ref,
    n1_ref,
    rs1_ref,
    gb2_ref,
    gb2t_ref,
    g2_ref,
    sums_ref,
    k_ref,
    vt_ref,
    att_t,
    probs,
    probs_sem,
    total,
    low,
    hooks,
):
    rows = xs.shape[1]
    for side in range(2):
        xt_ref[side] = xs[side].T
    ones_lane = jnp.where(lax.broadcasted_iota(jnp.int32, (rows, 128), 1) == 0, 1.0, 0.0).astype(BF16)

    def probs_copy(head, slot):
        return pltpu.make_async_copy(probs.at[slot], probs_hbm.at[head], probs_sem.at[slot])

    def project(m, _):
        bias = biases[m, 0:1, :].astype(F32)[:, :PROJ]
        own = dot(xs[0], block_of(blocks, ATT, m, 0, PROJ)) + bias
        other = dot(xs[1], block_of(blocks, ATT, m, 128, 512)) + bias[:, 128:]
        k_ref[2 * m, :rows] = own[:, 128:256].astype(BF16)
        k_ref[2 * m, rows:] = other[:, 0:128].astype(BF16)
        v_ref[2 * m, :rows] = own[:, 256:384].astype(BF16)
        v_ref[2 * m, rows:] = other[:, 128:256].astype(BF16)
        k_ref[2 * m + 1, :rows] = own[:, 384:512].astype(BF16)
        k_ref[2 * m + 1, rows:] = other[:, 256:384].astype(BF16)
        v_ref[2 * m + 1, :rows] = own[:, 512:640].astype(BF16)
        v_ref[2 * m + 1, rows:] = other[:, 384:512].astype(BF16)
        lower, upper = lane_mask(rows, True), lane_mask(rows, False)
        pair = own[:, 0:128].astype(BF16).astype(F32) * SCALE
        single = pltpu.roll(own[:, 384:512].astype(BF16).astype(F32) * SCALE, 64, 1)
        qm_ref[3 * m] = jnp.where(lower, pair, 0.0).astype(BF16)
        qm_ref[3 * m + 1] = jnp.where(upper, pair, 0.0).astype(BF16)
        qm_ref[3 * m + 2] = jnp.where(upper, single, 0.0).astype(BF16)
        for tile in range(2):
            kt_ref[2 * m + tile] = k_ref[2 * m + tile].T
            vt_ref[2 * m + tile] = v_ref[2 * m + tile].T
        return 0

    def attend(m, _):
        att_t[0:64, :] = jnp.zeros((64, rows), BF16)
        for j in range(3):
            tile = 2 * m + j // 2
            head = 3 * m + j
            keys = jnp.concatenate([k_ref[tile], keybias_ref[...]], axis=1)
            queries = jnp.concatenate([qm_ref[head], ones_lane], axis=1)
            scores = dot(keys, queries, (1, 1))
            weights = jnp.exp(scores - jnp.max(scores, axis=0, keepdims=True))
            recip = 1.0 / jnp.sum(weights, axis=0, keepdims=True)
            weights = weights.astype(BF16)
            pl.when(m > 0)(lambda h=head, s=j: probs_copy(h, s).wait())
            probs[j] = weights
            probs_copy(head, j).start()
            side = 64 * (j % 2)
            head_out = dot(vt_ref[tile, side : side + 64, :], weights) * recip
            recip_ref[head] = jnp.broadcast_to(recip, (8, rows))
            headout_ref[head] = head_out
            place = (128, 192, 64)[j]
            att_t[place : place + 64, :] = head_out.astype(BF16)
        att_ref[m] = att_t[...].T
        part = dot(att_ref[m], block_of(blocks, ATT, m, 512, 256), (1, 1))

        @pl.when(m == 0)
        def _():
            total[...] = part

        @pl.when(m > 0)
        def _():
            total[...] += part

        hooks.in_attend(m)
        return 0

    hooks.before_project()
    lax.fori_loop(0, 4, project, 0)
    hooks.before_attend()
    lax.fori_loop(0, 4, attend, 0)
    for j in range(3):
        probs_copy(9 + j, j).wait()

    chunk = 64

    def norm_one(i, _):
        r = pl.ds(pl.multiple_of(i * chunk, chunk), chunk)
        resid = xs[0, r, :].astype(F32) + total[r, :] + vec_ref[0:1, :]
        centered = resid - jnp.mean(resid, axis=1, keepdims=True)
        rstd = lax.rsqrt(jnp.mean(centered * centered, axis=1, keepdims=True) + EPSILON)
        unit = centered * rstd
        n1_ref[r, :] = unit
        rs1_ref[r, :] = rstd
        low[r, :] = (unit * vec_ref[2:3, :] + vec_ref[3:4, :]).astype(BF16)
        return 0

    lax.fori_loop(0, rows // chunk, norm_one, 0)
    n1t_ref[...] = low[...].T
    hooks.before_up()

    def feed(m, _):
        pre = dot(low[...], block_of(blocks, UP, m)) + biases[m, 1:2, :].astype(F32)
        phi = 0.5 * (1.0 + lax.erf(pre * (1.0 / math.sqrt(2.0))))
        acted_ref[m] = (pre * phi).astype(BF16)
        slope_ref[m] = (phi + pre * jnp.exp(-0.5 * pre * pre) * (1.0 / math.sqrt(2.0 * math.pi))).astype(BF16)
        hooks.in_feed(m)
        return 0

    lax.fori_loop(0, 4, feed, 0)
    hooks.before_down()

    def down(m, _):
        part = dot(acted_ref[m], block_of(blocks, DOWN, m), (1, 1))

        @pl.when(m == 0)
        def _():
            total[...] = part

        @pl.when(m > 0)
        def _():
            total[...] += part

        return 0

    lax.fori_loop(0, 4, down, 0)

    def norm_two(i, sums):
        r = pl.ds(pl.multiple_of(i * chunk, chunk), chunk)
        normed = n1_ref[r, :] * vec_ref[2:3, :] + vec_ref[3:4, :]
        resid = normed + total[r, :] + vec_ref[1:2, :]
        centered = resid - jnp.mean(resid, axis=1, keepdims=True)
        rstd = lax.rsqrt(jnp.mean(centered * centered, axis=1, keepdims=True) + EPSILON)
        unit = centered * rstd
        valid = valid_ref[r, :]
        out_ref[r, :] = (valid * (unit * vec_ref[4:5, :] + vec_ref[5:6, :])).astype(BF16)
        grad = valid * cot_ref[r, :].astype(F32)
        scaled = grad * vec_ref[4:5, :]
        grad_in = (
            scaled
            - jnp.mean(scaled, axis=1, keepdims=True)
            - unit * jnp.mean(scaled * unit, axis=1, keepdims=True)
        ) * rstd
        g2_ref[r, :] = grad_in
        gb2_ref[r, :] = grad_in.astype(BF16)
        return (
            sums[0] + jnp.sum(grad_in, axis=0, keepdims=True),
            sums[1] + jnp.sum(grad * unit, axis=0, keepdims=True),
            sums[2] + jnp.sum(grad, axis=0, keepdims=True),
        )

    zero = jnp.zeros((1, 768), F32)
    sums = lax.fori_loop(0, rows // chunk, norm_two, (zero, zero, zero))
    sums_ref[...] = jnp.concatenate([*sums, jnp.zeros((5, 768), F32)], axis=0)
    gb2t_ref[...] = gb2_ref[...].T


class NoHooks:
    def before_project(self):
        pass

    def before_attend(self):
        pass

    def in_attend(self, m):
        pass

    def before_up(self):
        pass

    def in_feed(self, m):
        pass

    def before_down(self):
        pass


class GatherHooks:
    def __init__(self, gather, blocks_out, keep_sem):
        self.gather = gather
        self.keep = [
            pltpu.make_async_copy(gather.blocks.at[kind], blocks_out.at[kind], keep_sem.at[kind]) for kind in range(3)
        ]

    def before_project(self):
        self.gather.last(ATT)
        self.keep[ATT].start()

    def before_attend(self):
        self.gather.second(UP)
        self.gather.z_step(DOWN, 1)

    def in_attend(self, m):
        gather = self.gather
        pl.when(m == 0)(lambda: gather.z_step(DOWN, 2))
        pl.when(m == 1)(lambda: gather.z_step(DOWN, 3))
        pl.when(m == 3)(lambda: gather.third(UP))

    def before_up(self):
        self.gather.last(UP)
        self.keep[UP].start()

    def in_feed(self, m):
        pl.when(m == 0)(lambda: self.gather.second(DOWN))

    def before_down(self):
        self.gather.third(DOWN)
        self.gather.last(DOWN)
        self.keep[DOWN].start()

    def finish(self):
        for copy in self.keep:
            copy.wait()
        self.gather.drain()


N_FORWARD_OUTS = 18


def forward_linked(pack_ref, bias_ref, x_ref, *refs):
    keybias, valid, cot, vec = refs[:4]
    blocks_hbm, probs_hbm, *outs = refs[4 : 4 + 2 + N_FORWARD_OUTS - 1]
    scratch = refs[4 + 2 + N_FORWARD_OUTS - 1 :]
    blocks, biases, xs, k_ref, vt_ref, att_t, probs, probs_sem, total, low = scratch[:10]
    z_send, z_recv, f_send, f_recv, p_send, p_recv, x_send, x_recv, keep_sem = scratch[10:]
    at = Place()
    at.greet(False)
    gather = Gather(at, blocks, biases, z_send, z_recv, f_send, f_recv, p_send, p_recv)
    for kind in range(3):
        blocks[kind, at.z, at.y, at.x, at.c] = pack_ref[kind]
    biases[at.z] = bias_ref[...]
    swap = remote(x_ref, xs.at[1], x_send, x_recv, at.mate)
    gather.z_step(ATT, 0)
    gather.z_step(3, 0)
    xs[0] = x_ref[...]
    gather.z_step(ATT, 1)
    gather.z_step(3, 1)
    gather.z_step(ATT, 2)
    gather.z_step(3, 2)
    gather.z_step(ATT, 3)
    gather.z_step(3, 3)
    gather.z_step(UP, 0)
    swap.start()
    gather.second(ATT)
    gather.z_step(UP, 1)
    gather.z_step(UP, 2)
    gather.z_step(UP, 3)
    gather.third(ATT)
    gather.z_step(DOWN, 0)
    swap.wait()
    hooks = GatherHooks(gather, blocks_hbm, keep_sem)
    forward_compute(
        blocks, biases, xs, keybias, valid, cot, vec, probs_hbm, *outs,
        k_ref, vt_ref, att_t, probs, probs_sem, total, low, hooks,
    )
    hooks.finish()


def forward_alone(blocks_in, biases, xs, *refs):
    keybias, valid, cot, vec = refs[:4]
    probs_hbm, *outs = refs[4 : 4 + 1 + N_FORWARD_OUTS - 1]
    scratch = refs[4 + 1 + N_FORWARD_OUTS - 1 :]
    blocks, k_ref, vt_ref, att_t, probs, probs_sem, total, low, keep_sem = scratch
    load = pltpu.make_async_copy(blocks_in, blocks, keep_sem)
    load.start()
    load.wait()
    forward_compute(
        blocks, biases, xs, keybias, valid, cot, vec, probs_hbm, *outs,
        k_ref, vt_ref, att_t, probs, probs_sem, total, low, NoHooks(),
    )


BLOCKS = (3, 4, 2, 2, 2, 96, 768)


def forward_outs(rows):
    def of(shape, dtype):
        return jax.ShapeDtypeStruct(shape, dtype)

    return [
        of((12, LEN, rows), BF16),
        of((rows, 768), BF16),
        of((12, 8, rows), F32),
        of((12, 64, rows), F32),
        of((2, 768, rows), BF16),
        of((12, rows, 128), BF16),
        of((8, 128, LEN), BF16),
        of((8, LEN, 128), BF16),
        of((4, rows, 256), BF16),
        of((4, rows, 768), BF16),
        of((4, rows, 768), BF16),
        of((768, rows), BF16),
        of((rows, 768), F32),
        of((rows, 1), F32),
        of((rows, 768), BF16),
        of((768, rows), BF16),
        of((rows, 768), F32),
        of((8, 768), F32),
    ]


def forward_scratch(rows):
    return [
        pltpu.VMEM((8, LEN, 128), BF16),
        pltpu.VMEM((8, 128, LEN), BF16),
        pltpu.VMEM((256, rows), BF16),
        pltpu.VMEM((3, LEN, rows), BF16),
        pltpu.SemaphoreType.DMA((3,)),
        pltpu.VMEM((rows, 768), F32),
        pltpu.VMEM((rows, 768), BF16),
    ]


def run_forward(linked, weights, bias, x, keybias, valid, cot, vec):
    rows = valid.shape[0]
    outs = forward_outs(rows)
    if linked:
        return pl.pallas_call(
            forward_linked,
            name="forward",
            out_shape=[jax.ShapeDtypeStruct(BLOCKS, BF16), *outs],
            in_specs=[vmem()] * 7,
            out_specs=[hbm(), hbm()] + [vmem()] * (N_FORWARD_OUTS - 1),
            scratch_shapes=[
                pltpu.VMEM(BLOCKS, BF16),
                pltpu.VMEM((4, 16, 768), BF16),
                pltpu.VMEM((2, rows, 768), BF16),
                *forward_scratch(rows),
                pltpu.SemaphoreType.DMA((4, 2, 3)),
                pltpu.SemaphoreType.DMA((4, 4)),
                pltpu.SemaphoreType.DMA((3, 4, 3)),
                pltpu.SemaphoreType.DMA((3, 4, 3)),
                pltpu.SemaphoreType.DMA((3, 6)),
                pltpu.SemaphoreType.DMA((3, 6)),
                pltpu.SemaphoreType.DMA,
                pltpu.SemaphoreType.DMA,
                pltpu.SemaphoreType.DMA((3,)),
            ],
            compiler_params=pltpu.CompilerParams(
                collective_id=0, has_side_effects=True, vmem_limit_bytes=VMEM_LIMIT
            ),
        )(weights, bias, x, keybias, valid, cot, vec)
    outs = pl.pallas_call(
        forward_alone,
        name="forward",
        out_shape=outs,
        in_specs=[hbm()] + [vmem()] * 6,
        out_specs=[hbm()] + [vmem()] * (N_FORWARD_OUTS - 1),
        scratch_shapes=[
            pltpu.VMEM(BLOCKS, BF16),
            *forward_scratch(rows),
            pltpu.SemaphoreType.DMA,
        ],
        compiler_params=pltpu.CompilerParams(vmem_limit_bytes=VMEM_LIMIT),
    )(weights, bias, x, keybias, valid, cot, vec)
    return [weights, *outs]


def chunk_at(n):
    if isinstance(n, int):
        return (2 - n % 2, n // 2) if n < 8 else (0, n - 8)
    return jnp.where(n < 8, 2 - lax.rem(n, 2), 0), jnp.where(n < 8, n // 2, n - 8)


class Scatter:
    def __init__(self, at, grads, core_in, first_in, second_in, z_in, out, send, recv, z_send, z_recv):
        self.at, self.grads, self.out = at, grads, out
        self.core_in, self.first_in, self.second_in, self.z_in = core_in, first_in, second_in, z_in
        self.send, self.recv, self.z_send, self.z_recv = send, recv, z_send, z_recv

    def copy(self, kind, m, which):
        at, grads = self.at, self.grads.at[kind, m]
        x, y, c = at.x, at.y, at.c
        low, high = pl.ds(0, 48), pl.ds(48, 48)
        src, dst, device = {
            0: lambda: (grads.at[:, :, 1 - c], self.core_in.at[kind, m], at.core),
            1: lambda: (grads.at[:, 1 - x, c, low], self.first_in.at[kind, m, 0], at.across_x),
            2: lambda: (grads.at[1 - y, :, c, high], self.first_in.at[kind, m, 1], at.across_y),
            3: lambda: (grads.at[1 - y, x, c, low], self.second_in.at[kind, m, 0], at.across_y),
            4: lambda: (grads.at[y, 1 - x, c, high], self.second_in.at[kind, m, 1], at.across_x),
        }[which]()
        return remote(src, dst, self.send.at[kind, m, which], self.recv.at[kind, m, which], device)

    def add(self, ref, got):
        ref[...] = (ref[...].astype(F32) + got[...].astype(F32)).astype(BF16)

    def begin(self, kind, m):
        self.copy(kind, m, 0).start()

    def first(self, kind, m):
        at, grads = self.at, self.grads.at[kind, m]
        self.copy(kind, m, 0).wait_recv()
        for y in range(2):
            for x in range(2):
                self.add(grads.at[y, x, at.c], self.core_in.at[kind, m, y, x])
        self.copy(kind, m, 1).start()
        self.copy(kind, m, 2).start()

    def second(self, kind, m):
        at, grads = self.at, self.grads.at[kind, m]
        low, high = pl.ds(0, 48), pl.ds(48, 48)
        self.copy(kind, m, 1).wait_recv()
        for y in range(2):
            self.add(grads.at[y, at.x, at.c, low], self.first_in.at[kind, m, 0, y])
        self.copy(kind, m, 3).start()
        self.copy(kind, m, 2).wait_recv()
        for x in range(2):
            self.add(grads.at[at.y, x, at.c, high], self.first_in.at[kind, m, 1, x])
        self.copy(kind, m, 4).start()

    def third(self, kind, m):
        at = self.at
        grads = self.grads.at[kind, m, at.y, at.x, at.c]
        self.copy(kind, m, 3).wait_recv()
        self.add(grads.at[pl.ds(0, 48)], self.second_in.at[kind, m, 0])
        self.copy(kind, m, 4).wait_recv()
        self.add(grads.at[pl.ds(48, 48)], self.second_in.at[kind, m, 1])

    def z_copy(self, kind, m, direction):
        at = self.at
        src = self.grads.at[kind, m, at.y, at.x, at.c]
        device = at.right if direction == 0 else at.left
        slot = m if direction == 0 else jnp.where(m == at.z - 1, 4, m)
        return remote(src, self.z_in.at[kind, slot], self.z_send.at[kind, m], self.z_recv.at[kind, slot], device)

    def z_landed(self, kind, m, slot, direction):
        at = self.at
        src = self.grads.at[kind, m, at.y, at.x, at.c]
        device = at.right if direction == 0 else at.left
        return remote(src, self.z_in.at[kind, slot], self.z_send.at[kind, m], self.z_recv.at[kind, slot], device)

    def relay(self, kind, m, direction):
        at = self.at
        self.z_landed(kind, m, m, direction).wait_recv()
        self.add(self.grads.at[kind, m, at.y, at.x, at.c], self.z_in.at[kind, m])
        self.z_copy(kind, m, direction).start()

    def z_start(self, kind, m):
        z = self.at.z
        pl.when((z == 0) & (m > 0))(lambda: self.z_copy(kind, m, 0).start())
        pl.when((z == 3) & (m < 3))(lambda: self.z_copy(kind, m, 1).start())

    def z_one(self, kind, m):
        z = self.at.z
        pl.when((z == 1) & (m > 1))(lambda: self.relay(kind, m, 0))
        pl.when((z == 2) & (m < 2))(lambda: self.relay(kind, m, 1))

    def z_two(self, kind, m):
        z = self.at.z
        pl.when((z == 2) & (m == 3))(lambda: self.relay(kind, m, 0))
        pl.when((z == 1) & (m == 0))(lambda: self.relay(kind, m, 1))

    def finish(self, kind):
        at, z = self.at, self.at.z
        self.out[kind] = self.grads[kind, z, at.y, at.x, at.c].astype(F32)

        @pl.when(z > 0)
        def _():
            self.z_landed(kind, z, z, 0).wait_recv()
            self.out[kind] += self.z_in[kind, z].astype(F32)

        @pl.when(z < 3)
        def _():
            self.z_landed(kind, z, 4, 1).wait_recv()
            self.out[kind] += self.z_in[kind, 4].astype(F32)

    def slot(self, n, stages=(0, 1, 2, 3)):
        if 0 in stages:
            self.second(*chunk_at(n))
        if 1 in stages:
            self.third(*chunk_at(n - 1))
            self.z_start(*chunk_at(n - 1))
        if 2 in stages:
            self.z_one(*chunk_at(n - 2))
        if 3 in stages:
            self.z_two(*chunk_at(n - 3))

    def drain(self):
        z = self.at.z
        for kind in range(3):

            def of_index(m, _, kind=kind):
                for which in range(5):
                    self.copy(kind, m, which).wait_send()
                pl.when(m > z)(lambda: self.z_copy(kind, m, 0).wait_send())
                pl.when(m < z)(lambda: self.z_copy(kind, m, 1).wait_send())
                return 0

            lax.fori_loop(0, 4, of_index, 0)


class Totals:
    def __init__(self, at, rows, got, send, recv):
        self.rows, self.got, self.send, self.recv = rows, got, send, recv
        self.partners = (at.core, at.across_x, at.across_y, at.mate, at.far)

    def copy(self, stage):
        return remote(
            self.rows.at[stage], self.got.at[stage], self.send.at[stage], self.recv.at[stage], self.partners[stage]
        )

    def start(self, stage):
        self.copy(stage).start()

    def finish(self, stage):
        self.copy(stage).wait()
        self.rows[stage + 1] = self.rows[stage] + self.got[stage]


def backward_compute(
    blocks_hbm,
    probs_hbm,
    acted_hbm,
    slope_hbm,
    recip_ref,
    headout_hbm,
    xt_hbm,
    qm_hbm,
    kt_hbm,
    v_hbm,
    att_hbm,
    n1t_hbm,
    n1_hbm,
    rs1_ref,
    gb2_hbm,
    gb2t_hbm,
    g2_hbm,
    sums_ref,
    masked_ref,
    vec_ref,
    grads,
    rows_ref,
    weight,
    weight_sem,
    acts,
    acts_sem,
    probs,
    probs_sem,
    gb1,
    gb1t,
    grad_one,
    parts,
    g2_ref,
    state_sem,
    gb2_ref,
    gb2t_ref,
    n1t_ref,
    xt_ref,
    headout_ref,
    qm_ref,
    kt_ref,
    v_ref,
    att_ref,
    head_sem,
    hooks,
):
    rows = g2_ref.shape[0]
    g2_load = pltpu.make_async_copy(g2_hbm, g2_ref, state_sem.at[0])
    n1_load = pltpu.make_async_copy(n1_hbm, grad_one, state_sem.at[1])
    gb2_load = pltpu.make_async_copy(gb2_hbm, gb2_ref, state_sem.at[2])
    gb2t_load = pltpu.make_async_copy(gb2t_hbm, gb2t_ref, state_sem.at[3])
    n1t_load = pltpu.make_async_copy(n1t_hbm, n1t_ref, state_sem.at[4])
    xt_load = pltpu.make_async_copy(xt_hbm, xt_ref, state_sem.at[5])

    def head_loads(m, slot):
        three, two = pl.ds(3 * m, 3), pl.ds(2 * m, 2)
        pairs = (
            (headout_hbm.at[three], headout_ref.at[slot]),
            (qm_hbm.at[three], qm_ref.at[slot]),
            (kt_hbm.at[two], kt_ref.at[slot]),
            (v_hbm.at[two], v_ref.at[slot]),
            (att_hbm.at[m], att_ref.at[slot]),
        )
        return [pltpu.make_async_copy(src, dst, head_sem.at[slot, i]) for i, (src, dst) in enumerate(pairs)]

    def weight_load(kind, m, slot):
        return pltpu.make_async_copy(blocks_hbm.at[kind, m], weight.at[slot], weight_sem.at[slot])

    def act_loads(m, slot):
        return (
            pltpu.make_async_copy(acted_hbm.at[m], acts.at[slot, 0], acts_sem.at[slot, 0]),
            pltpu.make_async_copy(slope_hbm.at[m], acts.at[slot, 1], acts_sem.at[slot, 1]),
        )

    def probs_load(head, slot):
        return pltpu.make_async_copy(probs_hbm.at[head], probs.at[slot], probs_sem.at[slot])

    def feed_loads(m, slot):
        return (weight_load(DOWN, m, 2 * slot), weight_load(UP, m, 2 * slot + 1), *act_loads(m, slot))

    def begin(copies):
        for copy in copies:
            copy.start()

    def finish(copies):
        for copy in copies:
            copy.wait()

    def block(slot, low=0, width=768):
        return weight[slot, :, :, :, :, pl.ds(low, width)].reshape(768, width)

    def put(kind, m, value, low=0):
        width = value.shape[1]
        grads[kind, m, :, :, :, :, pl.ds(low, width)] = value.astype(BF16).reshape(2, 2, 2, 96, width)

    begin((gb2_load,))
    begin(feed_loads(0, 0))
    begin((gb2t_load, n1t_load, g2_load, n1_load, xt_load))
    begin(head_loads(0, 0))
    for j in range(3):
        probs_load(j, j).start()
    parts[...] = jnp.zeros_like(parts)
    finish((gb2_load, gb2t_load, n1t_load, g2_load))

    def feed(m, _):
        slot = lax.rem(m, 2)
        pl.when(m < 3)(lambda: begin(feed_loads(m + 1, 1 - slot)))
        finish(feed_loads(m, slot))
        hooks.feed_begun(m)
        grad_acted = dot(gb2_ref[...], block(2 * slot))
        grad_pre = (grad_acted * acts[slot, 1].astype(F32)).astype(BF16)
        acts[slot, 1] = grad_pre
        parts[m, 0:1, :] = jnp.sum(grad_pre.astype(F32), axis=0, keepdims=True)
        put(DOWN, m, dot(gb2t_ref[...], acts[slot, 0]))
        hooks.down_ready(m)
        put(UP, m, dot(n1t_ref[...], acts[slot, 1]))
        hooks.up_ready(m)
        g2_ref[...] += dot(acts[slot, 1], block(2 * slot + 1), (1, 1))
        hooks.feed_done(m)
        return 0

    lax.fori_loop(0, 4, feed, 0)
    for m in range(4):
        weight_load(ATT, m, m).start()

    chunk = 64

    def norm_back(i, sums):
        r = pl.ds(pl.multiple_of(i * chunk, chunk), chunk)
        grad = g2_ref[r, :]
        unit = grad_one[r, :]
        scaled = grad * vec_ref[2:3, :]
        grad_in = (
            scaled
            - jnp.mean(scaled, axis=1, keepdims=True)
            - unit * jnp.mean(scaled * unit, axis=1, keepdims=True)
        ) * rs1_ref[r, :]
        grad_one[r, :] = grad_in
        gb1[r, :] = grad_in.astype(BF16)
        return (
            sums[0] + jnp.sum(grad_in, axis=0, keepdims=True),
            sums[1] + jnp.sum(grad * unit, axis=0, keepdims=True),
            sums[2] + jnp.sum(grad, axis=0, keepdims=True),
        )

    zero = jnp.zeros((1, 768), F32)
    finish((n1_load, xt_load))
    sums = lax.fori_loop(0, rows // chunk, norm_back, (zero, zero, zero))
    rows_ref[0, 0:1, :] = sums[0]
    rows_ref[0, 1:2, :] = sums_ref[0:1, :]
    rows_ref[0, 2:3, :] = sums[1]
    rows_ref[0, 3:4, :] = sums[2]
    rows_ref[0, 4:5, :] = sums_ref[1:2, :]
    rows_ref[0, 5:6, :] = sums_ref[2:3, :]
    gb1t[...] = gb1[...].T
    hooks.normed()
    g2_ref[...] = jnp.zeros_like(g2_ref)

    def attend_back(m, _):
        slot = lax.rem(m, 2)
        pl.when(m < 3)(lambda: begin(head_loads(m + 1, 1 - slot)))
        weight_load(ATT, m, m).wait()
        finish(head_loads(m, slot))
        w_out = block(m, 512, 256)
        grad_att_t = dot(gb1[...], w_out).T
        zeros = jnp.zeros((64, rows), BF16)
        sides = []
        for j in range(3):
            place = (128, 192, 64)[j]
            scaled = (grad_att_t[place : place + 64, :] * recip_ref[3 * m + j, 0:1, :]).astype(BF16)
            sides.append(scaled)
        wide = [
            jnp.concatenate([sides[0], zeros], axis=0),
            jnp.concatenate([zeros, sides[1]], axis=0),
            jnp.concatenate([sides[2], zeros], axis=0),
        ]
        dk, dv, dq = [None, None], [None, None], [None, None]
        for j in range(3):
            t = j // 2
            head = 3 * m + j
            shift = jnp.sum(sides[j].astype(F32) * headout_ref[slot, j], axis=0, keepdims=True)
            probs_load(head, j).wait()
            weights = probs[j]
            grad_weights = dot(v_ref[slot, t], wide[j])
            grad_scores = (weights.astype(F32) * (grad_weights - shift)).astype(BF16)
            grad_v = dot(weights, wide[j].T)
            pl.when(m < 3)(lambda h=head, s=j: probs_load(h + 3, s).start())
            grad_k = dot(grad_scores, qm_ref[slot, j])
            half = 64 * (j % 2) if j < 2 else 64
            grad_q = dot(kt_ref[slot, t, half : half + 64, :], grad_scores) * SCALE
            dk[t] = grad_k if dk[t] is None else dk[t] + grad_k
            dv[t] = grad_v if dv[t] is None else dv[t] + grad_v
            dq[t] = grad_q if dq[t] is None else jnp.concatenate([dq[t], grad_q], axis=0)
            hooks.head_done(m, j)
        dq_pair = dq[0].T.astype(BF16)
        dq_single = jnp.concatenate([dq[1], jnp.zeros((64, rows), F32)], axis=0).T.astype(BF16)
        dk = [d.astype(BF16) for d in dk]
        dv = [d.astype(BF16) for d in dv]
        own = acts.at[0, 0, :, pl.ds(0, PROJ)]
        own[:, 0:128] = dq_pair
        own[:, 128:256] = dk[0][:rows]
        own[:, 256:384] = dv[0][:rows]
        own[:, 384:512] = dq_single + dk[1][:rows]
        own[:, 512:640] = dv[1][:rows]
        other = acts.at[0, 1, :, pl.ds(0, PROJ)]
        other[:, 128:256] = dk[0][rows:]
        other[:, 256:384] = dv[0][rows:]
        other[:, 384:512] = dk[1][rows:]
        other[:, 512:640] = dv[1][rows:]
        wide_sum = jnp.sum(own[...].astype(F32), axis=0, keepdims=True)
        narrow_sum = jnp.sum(other[:, 128:640].astype(F32), axis=0, keepdims=True)
        parts[4 + m, 0:1, 0:128] = wide_sum[:, :128]
        parts[4 + m, 0:1, 128:640] = wide_sum[:, 128:] + narrow_sum
        grad_proj = dot(xt_ref[0], own[...])
        grad_other = dot(xt_ref[1], other[:, 128:640])
        grad_out_w = dot(gb1t[...], att_ref[slot])
        put(ATT, m, grad_proj[:, :128], 0)
        put(ATT, m, grad_proj[:, 128:512] + grad_other[:, :384], 128)
        put(ATT, m, grad_proj[:, 512:] + grad_other[:, 384:] + grad_out_w[:, :128], 512)
        put(ATT, m, grad_out_w[:, 128:], 640)
        hooks.att_ready(m)
        grad_one[...] += dot(own[...], block(m, 0, PROJ), (1, 1))
        g2_ref[...] += dot(other[:, 128:640], block(m, 128, 512), (1, 1))
        return 0

    lax.fori_loop(0, 4, attend_back, 0)

    def fill(i, total):
        r = pl.ds(pl.multiple_of(i * chunk, chunk), chunk)
        other = g2_ref[r, :]
        gb1[r, :] = other.astype(BF16)
        return total + jnp.sum(
            grad_one[r, :] * masked_ref[0, r, :] + other * masked_ref[1, r, :], axis=0, keepdims=True
        )

    rows_ref[0, 6:7, :] = lax.fori_loop(0, rows // chunk, fill, zero)
    rows_ref[0, 7:8, :] = zero
    for row in range(8):
        rows_ref[0, 8 + row : 9 + row, :] = parts[row, 0:1, :]


def finish_frames(grad_one, got, masked_ref, frames_ref):
    chunk = 64

    def body(i, _):
        r = pl.ds(pl.multiple_of(i * chunk, chunk), chunk)
        total = grad_one[r, :] + got[r, :].astype(F32)
        frames_ref[r, :] = jnp.where(masked_ref[0, r, :] > 0, 0.0, total).astype(BF16)
        return 0

    lax.fori_loop(0, grad_one.shape[0] // chunk, body, 0)


class NoScatter:
    def feed_begun(self, m):
        pass

    def down_ready(self, m):
        pass

    def up_ready(self, m):
        pass

    def feed_done(self, m):
        pass

    def normed(self):
        pass

    def head_done(self, m, j):
        pass

    def att_ready(self, m):
        pass


class ScatterHooks:
    def __init__(self, scatter):
        self.scatter = scatter

    def feed_begun(self, m):
        pl.when(m > 0)(lambda: self.scatter.first(UP, m - 1))

    def down_ready(self, m):
        self.scatter.begin(DOWN, m)

    def up_ready(self, m):
        self.scatter.first(DOWN, m)
        self.scatter.begin(UP, m)

    def feed_done(self, m):
        pl.when(m == 1)(lambda: self.scatter.slot(0, (0,)))
        pl.when(m == 2)(lambda: self.scatter.slot(1, (0, 1)))
        pl.when(m == 3)(lambda: self.scatter.slot(2, (0, 1, 2)))

    def normed(self):
        self.scatter.first(UP, 3)
        self.scatter.slot(3)

    def head_done(self, m, j):
        if j == 0:
            pl.when(m > 0)(lambda: self.scatter.first(ATT, m - 1))
        if j == 2:
            self.scatter.slot(m + 4)

    def att_ready(self, m):
        self.scatter.begin(ATT, m)


N_BACKWARD_INS = 20
N_BACKWARD_SCRATCH = 24


def backward_linked(*refs):
    ins = refs[:N_BACKWARD_INS]
    out_ref, rows_out, frames_ref = refs[N_BACKWARD_INS : N_BACKWARD_INS + 3]
    scratch = refs[N_BACKWARD_INS + 3 :]
    scratch, links = scratch[:N_BACKWARD_SCRATCH], scratch[N_BACKWARD_SCRATCH:]
    grads, rows_ref, gb1, grad_one = scratch[0], scratch[1], scratch[8], scratch[10]
    core_in, first_in, second_in, z_in, rows_in, mate_in = links[:6]
    send, recv, z_send, z_recv, t_send, t_recv, m_send, m_recv = links[6:]
    at = Place()
    at.greet(True)
    scatter = Scatter(at, grads, core_in, first_in, second_in, z_in, out_ref, send, recv, z_send, z_recv)
    totals = Totals(at, rows_ref, rows_in, t_send, t_recv)
    backward_compute(*ins, *scratch, ScatterHooks(scatter))
    swap = remote(gb1, mate_in, m_send, m_recv, at.mate)
    swap.start()
    totals.start(0)

    scatter.first(ATT, 3)

    def rest(n, _):
        scatter.slot(n)
        return 0

    lax.fori_loop(8, 12, rest, 0)
    totals.finish(0)
    totals.start(1)
    scatter.slot(12, (1, 2, 3))
    totals.finish(1)
    totals.start(2)
    scatter.finish(DOWN)
    scatter.finish(UP)
    totals.finish(2)
    totals.start(3)
    scatter.slot(13, (2, 3))
    totals.finish(3)
    totals.start(4)
    swap.wait()
    finish_frames(grad_one, mate_in, ins[18], frames_ref)
    scatter.slot(14, (3,))
    totals.finish(4)
    rows_out[...] = rows_ref[5]
    scatter.finish(ATT)
    scatter.drain()


def backward_alone(*refs):
    ins = refs[:N_BACKWARD_INS]
    grads_out, rows_out, mate_out, grad_one_out = refs[N_BACKWARD_INS : N_BACKWARD_INS + 4]
    scratch = refs[N_BACKWARD_INS + 4 :]
    *scratch, keep_sem = scratch
    grads, rows_ref, gb1, grad_one = scratch[0], scratch[1], scratch[8], scratch[10]
    backward_compute(*ins, *scratch, NoScatter())
    keep = pltpu.make_async_copy(grads, grads_out, keep_sem)
    keep.start()
    rows_out[...] = rows_ref[0]
    mate_out[...] = gb1[...]
    grad_one_out[...] = grad_one[...]
    keep.wait()


def backward_scratch(rows):
    return [
        pltpu.VMEM(BLOCKS, BF16),
        pltpu.VMEM((6, 16, 768), F32),
        pltpu.VMEM((4, *BLOCKS[2:]), BF16),
        pltpu.SemaphoreType.DMA((4,)),
        pltpu.VMEM((2, 2, rows, 768), BF16),
        pltpu.SemaphoreType.DMA((2, 2)),
        pltpu.VMEM((3, LEN, rows), BF16),
        pltpu.SemaphoreType.DMA((3,)),
        pltpu.VMEM((rows, 768), BF16),
        pltpu.VMEM((768, rows), BF16),
        pltpu.VMEM((rows, 768), F32),
        pltpu.VMEM((8, 8, 768), F32),
        pltpu.VMEM((rows, 768), F32),
        pltpu.SemaphoreType.DMA((6,)),
        pltpu.VMEM((rows, 768), BF16),
        pltpu.VMEM((768, rows), BF16),
        pltpu.VMEM((768, rows), BF16),
        pltpu.VMEM((2, 768, rows), BF16),
        pltpu.VMEM((2, 3, 64, rows), F32),
        pltpu.VMEM((2, 3, rows, 128), BF16),
        pltpu.VMEM((2, 2, 128, LEN), BF16),
        pltpu.VMEM((2, 2, LEN, 128), BF16),
        pltpu.VMEM((2, rows, 256), BF16),
        pltpu.SemaphoreType.DMA((2, 5)),
    ]


def run_backward(linked, saved, masked, vec):
    blocks, probs, _, recip, headout, xt, qm, kt, v, att, acted, slope, n1t, n1, rs1, gb2, gb2t, g2, sums = saved
    rows = gb2.shape[0]
    ins = (
        blocks, probs, acted, slope, recip, headout, xt, qm, kt, v, att, n1t, n1, rs1, gb2, gb2t, g2, sums, masked, vec
    )
    in_specs = [vmem() if i in (4, 13, 17, 18, 19) else hbm() for i in range(20)]
    if linked:
        return pl.pallas_call(
            backward_linked,
            name="backward",
            out_shape=[
                jax.ShapeDtypeStruct((3, 96, 768), F32),
                jax.ShapeDtypeStruct((16, 768), F32),
                jax.ShapeDtypeStruct((rows, 768), BF16),
            ],
            in_specs=in_specs,
            out_specs=[vmem()] * 3,
            scratch_shapes=[
                *backward_scratch(rows),
                pltpu.VMEM((3, 4, 2, 2, 96, 768), BF16),
                pltpu.VMEM((3, 4, 2, 2, 48, 768), BF16),
                pltpu.VMEM((3, 4, 2, 48, 768), BF16),
                pltpu.VMEM((3, 5, 96, 768), BF16),
                pltpu.VMEM((5, 16, 768), F32),
                pltpu.VMEM((rows, 768), BF16),
                pltpu.SemaphoreType.DMA((3, 4, 5)),
                pltpu.SemaphoreType.DMA((3, 4, 5)),
                pltpu.SemaphoreType.DMA((3, 4)),
                pltpu.SemaphoreType.DMA((3, 5)),
                pltpu.SemaphoreType.DMA((5,)),
                pltpu.SemaphoreType.DMA((5,)),
                pltpu.SemaphoreType.DMA,
                pltpu.SemaphoreType.DMA,
            ],
            compiler_params=pltpu.CompilerParams(
                collective_id=1, has_side_effects=True, vmem_limit_bytes=VMEM_LIMIT
            ),
        )(*ins)
    return pl.pallas_call(
        backward_alone,
        name="backward",
        out_shape=[
            jax.ShapeDtypeStruct(BLOCKS, BF16),
            jax.ShapeDtypeStruct((16, 768), F32),
            jax.ShapeDtypeStruct((rows, 768), BF16),
            jax.ShapeDtypeStruct((rows, 768), F32),
        ],
        in_specs=in_specs,
        out_specs=[hbm()] + [vmem()] * 3,
        scratch_shapes=[*backward_scratch(rows), pltpu.SemaphoreType.DMA],
        compiler_params=pltpu.CompilerParams(vmem_limit_bytes=VMEM_LIMIT),
    )(*ins)


def shards(
    linked,
    frames,
    lengths,
    span_starts,
    cotangent,
    query_weight,
    key_weight,
    value_weight,
    out_weight,
    up_weight,
    down_weight,
    query_bias,
    value_bias,
    up_bias,
    out_bias,
    down_bias,
    first_gain,
    first_shift,
    second_gain,
    second_shift,
    mask_vector,
):
    rows = frames.shape[0]
    dims = query_weight.shape[0]
    z = lax.axis_index("mp")
    clip = z // 2
    half = z % 2
    length = lax.dynamic_index_in_dim(lengths, clip, keepdims=False)
    starts = lax.dynamic_index_in_dim(span_starts, clip, keepdims=False)
    slots = (jnp.arange(LEN, dtype=jnp.int32) + half * rows) % LEN
    valid = slots < length
    masked = jnp.any((slots[:, None] >= starts[None, :]) & (slots[:, None] < starts[None, :] + SPAN), axis=1)
    keybias = jnp.where(
        (jnp.arange(128) == 0)[None, :] & ~valid[:, None], jnp.float32(NEGATIVE), 0.0
    ).astype(BF16)
    valid_rows = valid[:rows].astype(F32)[:, None]
    masked_rows = masked.astype(F32).reshape(2, rows, 1)
    x = jnp.where(masked[:rows, None], mask_vector[None, :], frames)
    out_t = out_weight.T
    pair, single = 2 * HEAD_DIM, 3 * HEAD_DIM
    pack = jnp.stack(
        [
            jnp.concatenate(
                [
                    query_weight[:, :pair], key_weight[:, :pair], value_weight[:, :pair],
                    query_weight[:, pair:], key_weight[:, pair:], value_weight[:, pair:],
                    out_t[:, pair:], out_t[:, :pair],
                ],
                axis=1,
            ),
            up_weight,
            down_weight.T,
        ]
    )
    q_shift, v_shift = query_bias.reshape(-1), value_bias.reshape(-1)
    blank = jnp.zeros((pair,), BF16)
    short = blank[:HEAD_DIM]
    bias = jnp.stack(
        [
            jnp.concatenate([q_shift[:pair], blank, v_shift[:pair], q_shift[pair:], short, v_shift[pair:], short, blank]),
            up_bias.reshape(-1),
        ]
    )
    bias = jnp.pad(bias, ((0, 14), (0, 0)))
    vec = jnp.stack([out_bias, down_bias, first_gain, first_shift, second_gain, second_shift]).astype(F32)
    vec = jnp.pad(vec, ((0, 2), (0, 0)))
    if linked:
        saved = run_forward(True, pack, bias, x, keybias, valid_rows, cotangent, vec)
        grads, totals, grad_frames = run_backward(True, saved, masked_rows, vec)
    else:
        mates = [(0, 1), (1, 0), (2, 3), (3, 2)]
        blocks = lax.all_gather(lax.all_gather(pack, "dp", axis=1, tiled=True), "mp", axis=1)
        biases = lax.all_gather(bias, "mp", axis=0)
        both = jnp.stack([x, lax.ppermute(x, "mp", mates)])
        saved = run_forward(False, blocks.reshape(BLOCKS), biases, both, keybias, valid_rows, cotangent, vec)
        grads, totals, mate, grad_one = run_backward(False, saved, masked_rows, vec)
        grads = grads.reshape(3, 4, 768, 768).astype(F32)
        grads = lax.psum_scatter(grads, "mp", scatter_dimension=1, tiled=False)
        grads = lax.psum_scatter(grads, "dp", scatter_dimension=1, tiled=True)
        totals = lax.psum(totals, ("dp", "mp"))
        grad_frames = grad_one + lax.ppermute(mate, "mp", mates).astype(F32)
        grad_frames = jnp.where(masked[:rows, None], 0.0, grad_frames).astype(BF16)
    out_frames = saved[2]
    att, grad_up, grad_down = grads[0], grads[1], grads[2].T
    grad_query = jnp.concatenate([att[:, 0:128], att[:, 384:448]], axis=1)
    grad_key = jnp.concatenate([att[:, 128:256], att[:, 448:512]], axis=1)
    grad_value = jnp.concatenate([att[:, 256:384], att[:, 512:576]], axis=1)
    grad_out = jnp.concatenate([att[:, 640:768], att[:, 576:640]], axis=1).T
    dp, n_dp = lax.axis_index("dp"), 768 // dims
    part = 768 // (n_dp * 4)
    row_parts = lax.dynamic_slice(totals, (0, (dp * 4 + z) * part), (7, part))
    head_row = lax.dynamic_slice(totals, (12 + z, 0), (1, 768))[0]
    q_row = jnp.concatenate([head_row[0:128], head_row[384:448]]).reshape(3, HEAD_DIM)
    v_row = jnp.concatenate([head_row[256:384], head_row[512:576]]).reshape(3, HEAD_DIM)
    up_row = lax.dynamic_slice(totals, (8 + z, 0), (1, 768)).reshape(6, 128)
    step = HEAD_DIM // n_dp
    grad_query_bias = lax.dynamic_slice(q_row, (0, dp * step), (3, step))
    grad_value_bias = lax.dynamic_slice(v_row, (0, dp * step), (3, step))
    grad_up_bias = lax.dynamic_slice(up_row, (0, dp * 2 * step), (6, 2 * step))
    return (
        out_frames,
        grad_frames,
        grad_query,
        grad_key,
        grad_value,
        grad_out,
        grad_up,
        grad_down,
        grad_query_bias,
        grad_value_bias,
        grad_up_bias,
        *(row_parts[i] for i in range(7)),
    )


def solution(mesh):
    linked = mesh.shape["dp"] == 8 and mesh.shape["mp"] == 4
    split = P(("dp", "mp"))
    return jax.shard_map(
        functools.partial(shards, linked),
        mesh=mesh,
        in_specs=(
            P(("dp", "mp"), None),
            P("dp"),
            P("dp", None),
            P(("dp", "mp"), None),
            P("dp", "mp"),
            P("dp", "mp"),
            P("dp", "mp"),
            P("mp", "dp"),
            P("dp", "mp"),
            P("mp", "dp"),
            P("mp", None),
            P("mp", None),
            P("mp", None),
            *([P()] * 7),
        ),
        out_specs=(
            P(("dp", "mp"), None),
            P(("dp", "mp"), None),
            P("dp", "mp"),
            P("dp", "mp"),
            P("dp", "mp"),
            P("mp", "dp"),
            P("dp", "mp"),
            P("mp", "dp"),
            P("mp", "dp"),
            P("mp", "dp"),
            P("mp", "dp"),
            *([split] * 7),
        ),
        check_vma=False,
    )
```

```python
import functools
import math

import jax
import jax.numpy as jnp
from jax import lax
from jax.experimental import pallas as pl
from jax.experimental.pallas import tpu as pltpu
from jax.sharding import PartitionSpec as P

HEAD_DIM = 64
SPAN = 10
LEN = 1024
EPSILON = 1e-05
NEGATIVE = -1e30
SCALE = 1.0 / math.sqrt(HEAD_DIM)

F32 = jnp.float32
BF16 = jnp.bfloat16
MESH = pl.DeviceIdType.MESH
VMEM_LIMIT = 63 * 1024 * 1024

ATT, UP, DOWN = 0, 1, 2
PROJ = 640


def dot(left, right, contract=(1, 0)):
    return lax.dot_general(
        left, right, (((contract[0],), (contract[1],)), ((), ())), preferred_element_type=F32
    )


def hbm():
    return pl.BlockSpec(memory_space=pl.ANY)


def vmem():
    return pl.BlockSpec(memory_space=pltpu.VMEM)


class Place:
    def __init__(self):
        self.dp = lax.axis_index("dp")
        self.z = lax.axis_index("mp")
        self.c = lax.rem(self.dp, 2)
        self.x = lax.rem(self.dp // 2, 2)
        self.y = self.dp // 4
        self.core = (self.dp + 1 - 2 * self.c, self.z)
        self.across_x = (self.dp + 2 - 4 * self.x, self.z)
        self.across_y = (self.dp + 4 - 8 * self.y, self.z)
        self.right = (self.dp, self.z + 1)
        self.left = (self.dp, self.z - 1)
        self.mate = (self.dp, self.z + 1 - 2 * lax.rem(self.z, 2))
        self.far = (self.dp, lax.rem(self.z + 2, 4))

    def greet(self, far):
        barrier = pltpu.get_barrier_semaphore()

        def signal(device):
            pl.semaphore_signal(barrier, inc=1, device_id=device, device_id_type=MESH)

        signal(self.core)
        signal(self.across_x)
        signal(self.across_y)
        if far:
            signal(self.far)
        pl.when(self.z < 3)(lambda: signal(self.right))
        pl.when(self.z > 0)(lambda: signal(self.left))
        ends = jnp.where((self.z == 0) | (self.z == 3), 1, 2)
        pl.semaphore_wait(barrier, (4 if far else 3) + ends)


def remote(src, dst, send, recv, device):
    return pltpu.make_async_remote_copy(
        src_ref=src, dst_ref=dst, send_sem=send, recv_sem=recv, device_id=device, device_id_type=MESH
    )


class Gather:
    def __init__(self, at, blocks, biases, z_send, z_recv, p_send, p_recv):
        self.at, self.blocks, self.biases = at, blocks, biases
        self.z_send, self.z_recv, self.p_send, self.p_recv = z_send, z_recv, p_send, p_recv

    def z_copy(self, kind, m, direction, step):
        at = self.at
        if kind == 3:
            ref = self.biases.at[m]
        else:
            ref = self.blocks.at[kind, m, at.y, at.x, at.c]
        device = at.right if direction == 0 else at.left
        return remote(ref, ref, self.z_send.at[kind, direction, step], self.z_recv.at[kind, m], device)

    def z_step(self, kind, step):
        z = self.at.z
        if step == 0:
            pl.when(z < 3)(lambda: self.z_copy(kind, z, 0, 0).start())
            pl.when(z > 0)(lambda: self.z_copy(kind, z, 1, 0).start())
            return

        @pl.when(z >= step)
        def _():
            self.z_copy(kind, z - step, 0, 0).wait_recv()
            if step < 3:
                pl.when(z < 3)(lambda: self.z_copy(kind, z - step, 0, step).start())
            self.first(kind, z - step)

        @pl.when(z + step <= 3)
        def _():
            self.z_copy(kind, z + step, 1, 0).wait_recv()
            if step < 3:
                pl.when(z > 0)(lambda: self.z_copy(kind, z + step, 1, step).start())
            self.first(kind, z + step)

    def plane_copy(self, kind, m, which):
        at, block = self.at, self.blocks.at[kind, m]
        x, y, c = at.x, at.y, at.c
        low, high = pl.ds(0, 48), pl.ds(48, 48)
        ref, device = {
            0: lambda: (block.at[y, x, c, low], at.across_x),
            1: lambda: (block.at[y, x, c, high], at.across_y),
            2: lambda: (block.at[y, :, c, low], at.across_y),
            3: lambda: (block.at[:, x, c, high], at.across_x),
            4: lambda: (block.at[:, :, c], at.core),
        }[which]()
        return remote(ref, ref, self.p_send.at[kind, m, which], self.p_recv.at[kind, m, which], device)

    def at_step(self, step, act):
        z = self.at.z
        if step == 0:
            act(z)
            return
        pl.when(z >= step)(lambda: act(z - step))
        pl.when(z + step <= 3)(lambda: act(z + step))

    def first(self, kind, m):
        if kind < 3:
            self.plane_copy(kind, m, 0).start()
            self.plane_copy(kind, m, 1).start()

    def second(self, kind, step):
        def act(m):
            self.plane_copy(kind, m, 0).wait_recv()
            self.plane_copy(kind, m, 2).start()
            self.plane_copy(kind, m, 1).wait_recv()
            self.plane_copy(kind, m, 3).start()

        self.at_step(step, act)

    def third(self, kind, step):
        def act(m):
            self.plane_copy(kind, m, 2).wait_recv()
            self.plane_copy(kind, m, 3).wait_recv()
            self.plane_copy(kind, m, 4).start()

        self.at_step(step, act)

    def last(self, kind):
        for m in range(4):
            self.plane_copy(kind, m, 4).wait_recv()

    def drain(self):
        z = self.at.z
        for kind in range(4):
            for step in range(3):
                pl.when((z < 3) & (z >= step))(
                    lambda k=kind, s=step: self.z_copy(k, z - s, 0, s).wait_send()
                )
                pl.when((z > 0) & (z + step <= 3))(
                    lambda k=kind, s=step: self.z_copy(k, z + s, 1, s).wait_send()
                )
        for kind in range(3):
            for m in range(4):
                for which in range(5):
                    self.plane_copy(kind, m, which).wait_send()


def block_of(blocks, kind, m, low=0, width=768):
    return blocks[kind, m, :, :, :, :, pl.ds(low, width)].reshape(768, width)


def lane_mask(rows, lower):
    lanes = lax.broadcasted_iota(jnp.int32, (rows, 128), 1)
    return (lanes < 64) if lower else (lanes >= 64)


def forward_compute(
    blocks,
    biases,
    xs,
    keybias_ref,
    valid_ref,
    cot_ref,
    vec_ref,
    probs_hbm,
    out_ref,
    outs_hbm,
    outs_ref,
    outs_sem,
    k_ref,
    vt_ref,
    att_t,
    probs,
    probs_sem,
    total,
    low,
    stats,
    hooks,
):
    rows = xs.shape[1]
    (recip_ref, headout_ref, xt_ref, qm_ref, kt_ref, v_ref, att_ref, acted_ref, slope_ref, n1t_ref, n1_ref, rs1_ref,
     gb2_ref, gb2t_ref, g2_ref, sums_ref) = outs_ref
    keeps = [
        pltpu.make_async_copy(ref, to, outs_sem.at[i]) for i, (ref, to) in enumerate(zip(outs_ref, outs_hbm, strict=True))
    ]

    def keep(*which):
        for i in which:
            keeps[i].start()

    xt_ref[0] = xs[0].T
    ones_lane = jnp.where(lax.broadcasted_iota(jnp.int32, (rows, 128), 1) == 0, 1.0, 0.0).astype(BF16)

    def probs_copy(head, side, slot):
        return pltpu.make_async_copy(
            probs.at[slot], probs_hbm.at[head, pl.ds(side * rows, rows)], probs_sem.at[slot]
        )

    own_rows, other_rows = pl.ds(0, rows), pl.ds(rows, rows)

    def project(m, _):
        bias = biases[m, 0:1, :].astype(F32)[:, :PROJ]
        own = dot(xs[0], block_of(blocks, ATT, m, 0, PROJ)) + bias
        k_ref[2 * m, own_rows] = own[:, 128:256].astype(BF16)
        v_ref[2 * m, own_rows] = own[:, 256:384].astype(BF16)
        k_ref[2 * m + 1, own_rows] = own[:, 384:512].astype(BF16)
        v_ref[2 * m + 1, own_rows] = own[:, 512:640].astype(BF16)
        lower, upper = lane_mask(rows, True), lane_mask(rows, False)
        pair = own[:, 0:128].astype(BF16).astype(F32) * SCALE
        single = pltpu.roll(own[:, 384:512].astype(BF16).astype(F32) * SCALE, 64, 1)
        qm_ref[3 * m] = jnp.where(lower, pair, 0.0).astype(BF16)
        qm_ref[3 * m + 1] = jnp.where(upper, pair, 0.0).astype(BF16)
        qm_ref[3 * m + 2] = jnp.where(upper, single, 0.0).astype(BF16)
        for tile in range(2):
            kt_ref[2 * m + tile, :, own_rows] = k_ref[2 * m + tile, own_rows].T
            vt_ref[2 * m + tile, :, own_rows] = v_ref[2 * m + tile, own_rows].T
        hooks.in_project(m)
        return 0

    def project_other(m, _):
        bias = biases[m, 0:1, :].astype(F32)[:, 128:PROJ]
        other = dot(xs[1], block_of(blocks, ATT, m, 128, 512)) + bias
        k_ref[2 * m, other_rows] = other[:, 0:128].astype(BF16)
        v_ref[2 * m, other_rows] = other[:, 128:256].astype(BF16)
        k_ref[2 * m + 1, other_rows] = other[:, 256:384].astype(BF16)
        v_ref[2 * m + 1, other_rows] = other[:, 384:512].astype(BF16)
        for tile in range(2):
            kt_ref[2 * m + tile, :, other_rows] = k_ref[2 * m + tile, other_rows].T
            vt_ref[2 * m + tile, :, other_rows] = v_ref[2 * m + tile, other_rows].T
        return 0

    def attend_half(m, j, side):
        tile, head = 2 * m + j // 2, 3 * m + j
        half = own_rows if side == 0 else other_rows
        keys = jnp.concatenate([k_ref[tile, half], keybias_ref[half, :]], axis=1)
        queries = jnp.concatenate([qm_ref[head], ones_lane], axis=1)
        scores = dot(keys, queries, (1, 1))
        top = jnp.max(scores, axis=0, keepdims=True)
        weights = jnp.exp(scores - top)
        total_weight = jnp.sum(weights, axis=0, keepdims=True)
        weights = weights.astype(BF16)
        if side == 0:
            pl.when(m > 0)(lambda: probs_copy(head, side, j).wait())
        else:
            probs_copy(head, side, j).wait()
        probs[j] = weights
        probs_copy(head, side, j).start()
        lane = 64 * (j % 2)
        head_out = dot(vt_ref[tile, lane : lane + 64, half], weights)
        headout_ref[head, side] = head_out
        return top, total_weight, head_out

    def attend_own(m, _):
        for j in range(3):
            top, total_weight, _ = attend_half(m, j, 0)
            stats[3 * m + j, 0:1, :] = top
            stats[3 * m + j, 1:2, :] = total_weight
            hooks.in_own(m, j)
        return 0

    def attend(m, _):
        att_t[0:64, :] = jnp.zeros((64, rows), BF16)
        for j in range(3):
            head = 3 * m + j
            top, total_weight, head_out = attend_half(m, j, 1)
            top_own = stats[head, 0:1, :]
            top_all = jnp.maximum(top, top_own)
            factor, factor_own = jnp.exp(top - top_all), jnp.exp(top_own - top_all)
            recip = 1.0 / (factor_own * stats[head, 1:2, :] + factor * total_weight)
            factor, factor_own = factor * recip, factor_own * recip
            recip_ref[head] = jnp.concatenate(
                [factor_own, factor, jnp.zeros((6, rows), F32)], axis=0
            )
            place = (128, 192, 64)[j]
            att_t[place : place + 64, :] = (headout_ref[head, 0] * factor_own + head_out * factor).astype(BF16)
            hooks.in_attend(m, j)
        att_ref[m] = att_t[...].T
        part = dot(att_ref[m], block_of(blocks, ATT, m, 512, 256), (1, 1))

        @pl.when(m == 0)
        def _():
            total[...] = part

        @pl.when(m > 0)
        def _():
            total[...] += part

        return 0

    hooks.before_project()
    lax.fori_loop(0, 4, project, 0)
    lax.fori_loop(0, 4, attend_own, 0)
    hooks.before_other()
    xt_ref[1] = xs[1].T
    lax.fori_loop(0, 4, project_other, 0)
    keep(2, 3, 4, 5)
    lax.fori_loop(0, 4, attend, 0)
    keep(0, 1, 6)
    for j in range(3):
        probs_copy(9 + j, 1, j).wait()

    chunk = 64

    def norm_one(i, _):
        r = pl.ds(pl.multiple_of(i * chunk, chunk), chunk)
        resid = xs[0, r, :].astype(F32) + total[r, :] + vec_ref[0:1, :]
        centered = resid - jnp.mean(resid, axis=1, keepdims=True)
        rstd = lax.rsqrt(jnp.mean(centered * centered, axis=1, keepdims=True) + EPSILON)
        unit = centered * rstd
        n1_ref[r, :] = unit
        rs1_ref[r, :] = rstd
        low[r, :] = (unit * vec_ref[2:3, :] + vec_ref[3:4, :]).astype(BF16)
        return 0

    lax.fori_loop(0, rows // chunk, norm_one, 0)
    n1t_ref[...] = low[...].T
    keep(9, 10, 11)
    hooks.before_up()

    def feed(m, _):
        pre = dot(low[...], block_of(blocks, UP, m)) + biases[m, 1:2, :].astype(F32)
        phi = 0.5 * (1.0 + lax.erf(pre * (1.0 / math.sqrt(2.0))))
        acted_ref[m] = (pre * phi).astype(BF16)
        slope_ref[m] = (phi + pre * jnp.exp(-0.5 * pre * pre) * (1.0 / math.sqrt(2.0 * math.pi))).astype(BF16)
        hooks.in_feed(m)
        return 0

    lax.fori_loop(0, 4, feed, 0)
    keep(7, 8)
    hooks.before_down()

    def down(m, _):
        part = dot(acted_ref[m], block_of(blocks, DOWN, m), (1, 1))

        @pl.when(m == 0)
        def _():
            total[...] = part

        @pl.when(m > 0)
        def _():
            total[...] += part

        return 0

    lax.fori_loop(0, 4, down, 0)

    def norm_two(i, sums):
        r = pl.ds(pl.multiple_of(i * chunk, chunk), chunk)
        normed = n1_ref[r, :] * vec_ref[2:3, :] + vec_ref[3:4, :]
        resid = normed + total[r, :] + vec_ref[1:2, :]
        centered = resid - jnp.mean(resid, axis=1, keepdims=True)
        rstd = lax.rsqrt(jnp.mean(centered * centered, axis=1, keepdims=True) + EPSILON)
        unit = centered * rstd
        valid = valid_ref[r, :]
        out_ref[r, :] = (valid * (unit * vec_ref[4:5, :] + vec_ref[5:6, :])).astype(BF16)
        grad = valid * cot_ref[r, :].astype(F32)
        scaled = grad * vec_ref[4:5, :]
        grad_in = (
            scaled
            - jnp.mean(scaled, axis=1, keepdims=True)
            - unit * jnp.mean(scaled * unit, axis=1, keepdims=True)
        ) * rstd
        g2_ref[r, :] = grad_in
        gb2_ref[r, :] = grad_in.astype(BF16)
        return (
            sums[0] + jnp.sum(grad_in, axis=0, keepdims=True),
            sums[1] + jnp.sum(grad * unit, axis=0, keepdims=True),
            sums[2] + jnp.sum(grad, axis=0, keepdims=True),
        )

    zero = jnp.zeros((1, 768), F32)
    sums = lax.fori_loop(0, rows // chunk, norm_two, (zero, zero, zero))
    sums_ref[...] = jnp.concatenate([*sums, jnp.zeros((5, 768), F32)], axis=0)
    keep(12, 14, 15)
    gb2t_ref[...] = gb2_ref[...].T
    keep(13)
    for copy in keeps:
        copy.wait()


class NoHooks:
    def before_project(self):
        pass

    def in_project(self, m):
        pass

    def before_other(self):
        pass

    def in_own(self, m, j):
        pass

    def in_attend(self, m, j):
        pass

    def before_up(self):
        pass

    def in_feed(self, m):
        pass

    def before_down(self):
        pass


class GatherHooks:
    IN_PROJECT = {
        1: (("second", UP, 0),),
        3: (("second", DOWN, 0),),
    }
    IN_OWN = {
        (0, 2): (("second", UP, 1),),
        (1, 2): (("z_step", UP, 2), ("third", UP, 0)),
        (3, 2): (("third", UP, 1),),
    }
    BEFORE_OTHER = (("third", DOWN, 0),)
    IN_ATTEND = {
        (0, 0): (("z_step", DOWN, 1),),
        (0, 2): (("second", UP, 2),),
        (1, 1): (("z_step", UP, 3),),
        (1, 2): (("second", DOWN, 1),),
        (2, 1): (("z_step", DOWN, 2), ("third", UP, 2)),
        (3, 0): (("second", UP, 3),),
    }
    BEFORE_UP = (("z_step", DOWN, 3), ("third", UP, 3), ("second", DOWN, 2))
    IN_FEED = {
        1: (("third", DOWN, 1),),
        2: (("second", DOWN, 3),),
    }

    def __init__(self, gather, swap, blocks_out, keep_sem):
        self.gather, self.swap = gather, swap
        self.keep = [
            pltpu.make_async_copy(gather.blocks.at[kind], blocks_out.at[kind], keep_sem.at[kind]) for kind in range(3)
        ]

    def run(self, events):
        for name, kind, step in events:
            getattr(self.gather, name)(kind, step)

    def before_project(self):
        self.gather.last(ATT)
        self.keep[ATT].start()

    def in_project(self, m):
        self.on(self.IN_PROJECT, m)

    def before_other(self):
        self.run(self.BEFORE_OTHER)
        self.swap.wait()

    def on(self, table, m, j=None):
        for key, events in table.items():
            index, head = (key, None) if j is None else key
            if head == j:
                pl.when(m == index)(functools.partial(self.run, events))

    def in_own(self, m, j):
        self.on(self.IN_OWN, m, j)

    def in_attend(self, m, j):
        self.on(self.IN_ATTEND, m, j)

    def before_up(self):
        self.run(self.BEFORE_UP)
        self.gather.last(UP)
        self.keep[UP].start()

    def in_feed(self, m):
        self.on(self.IN_FEED, m)

    def before_down(self):
        self.run((("third", DOWN, 2), ("third", DOWN, 3)))
        self.gather.last(DOWN)
        self.keep[DOWN].start()

    def finish(self):
        for copy in self.keep:
            copy.wait()
        self.gather.drain()


N_KEPT = 16


def pack_weights(query, key, value, out_t, up, down_t):
    pair, single = 2 * HEAD_DIM, 3 * HEAD_DIM
    att = jnp.concatenate(
        [
            query[:, :pair], key[:, :pair], value[:, :pair],
            query[:, pair:single], key[:, pair:single],
            value[:, pair:single], out_t[:, pair:single], out_t[:, :pair],
        ],
        axis=1,
    )
    return att, up, down_t


def pack_biases(query_bias, value_bias, up_bias):
    def row(i, bias):
        return bias[i : i + 1, :]

    blank = jnp.zeros((1, HEAD_DIM), BF16)
    pieces = [
        row(0, query_bias), row(1, query_bias), blank, blank, row(0, value_bias), row(1, value_bias),
        row(2, query_bias), blank, row(2, value_bias), blank, blank, blank,
    ]
    ups = jnp.concatenate([row(i, up_bias) for i in range(6)], axis=1)
    return jnp.concatenate([jnp.concatenate(pieces, axis=1), ups, jnp.zeros((14, 768), BF16)], axis=0)


def fill_vectors(vec, vecs):
    for i, ref in enumerate(vecs):
        vec[i : i + 1, :] = ref[...].astype(F32).reshape(1, 768)


def transposed(block):
    wide = jnp.concatenate([block, jnp.zeros((block.shape[0], 128 - block.shape[1]), block.dtype)], axis=1)
    return wide.T[: block.shape[1]]


def forward_linked(*refs):
    (lengths, starts, frames, cot, query, key, value, out_w, up, down, query_bias, value_bias, up_bias) = refs[:13]
    vecs, refs = refs[13:20], refs[20:]
    blocks_hbm, probs_hbm, out_ref, masked_ref, *outs = refs[: 4 + N_KEPT]
    blocks, biases, xs, keybias, valid, vec, *scratch = refs[4 + N_KEPT :]
    scratch, links = scratch[:N_FORWARD_SCRATCH], scratch[N_FORWARD_SCRATCH:]
    z_send, z_recv, p_send, p_recv, x_send, x_recv, keep_sem = links
    at = Place()
    at.greet(False)
    gather = Gather(at, blocks, biases, z_send, z_recv, p_send, p_recv)
    packs = pack_weights(
        query[...], key[...], value[...], transposed(out_w[...]), up[...], down[...]
    )
    for kind in range(3):
        blocks[kind, at.z, at.y, at.x, at.c] = packs[kind]
        if kind == 0:
            gather.z_step(ATT, 0)
            gather.first(ATT, at.z)
    biases[at.z] = pack_biases(query_bias[...], value_bias[...], up_bias[...])
    gather.z_step(3, 0)
    fill_vectors(vec, vecs)
    rows = frames.shape[0]
    clip, half = at.z // 2, lax.rem(at.z, 2)
    length = lengths[clip]
    start = starts[pl.ds(clip, 1), :]
    for side in range(2):
        first = rows * (half if side == 0 else 1 - half)
        slots = first + lax.broadcasted_iota(jnp.int32, (rows, start.shape[1]), 0)
        covered = jnp.where((slots >= start) & (slots < start + SPAN), 1.0, 0.0)
        masked_ref[side] = jnp.max(covered, axis=1, keepdims=True)
        slots = first + lax.broadcasted_iota(jnp.int32, (rows, 128), 0)
        lanes = lax.broadcasted_iota(jnp.int32, (rows, 128), 1)
        here = pl.ds(side * rows, rows)
        keybias[here, :] = jnp.where((slots >= length) & (lanes == 0), NEGATIVE, 0.0).astype(BF16)
        if side == 0:
            valid[...] = jnp.where(slots[:, 0:1] < length, 1.0, 0.0)
    xs[0] = jnp.where(masked_ref[0] > 0, vec[6:7, :], frames[...].astype(F32)).astype(BF16)
    swap = remote(xs.at[0], xs.at[1], x_send, x_recv, at.mate)
    gather.z_step(ATT, 1)
    gather.z_step(3, 1)
    gather.second(ATT, 0)
    gather.z_step(ATT, 2)
    gather.z_step(3, 2)
    gather.z_step(UP, 0)
    gather.second(ATT, 1)
    gather.third(ATT, 0)
    gather.z_step(ATT, 3)
    gather.z_step(3, 3)
    gather.second(ATT, 2)
    gather.third(ATT, 1)
    gather.second(ATT, 3)
    gather.first(UP, at.z)
    gather.z_step(UP, 1)
    swap.start()
    gather.z_step(DOWN, 0)
    gather.first(DOWN, at.z)
    gather.third(ATT, 2)
    gather.third(ATT, 3)
    hooks = GatherHooks(gather, swap, blocks_hbm, keep_sem)
    forward_compute(blocks, biases, xs, keybias, valid, cot, vec, probs_hbm, out_ref, outs, *scratch, hooks)
    hooks.finish()


def forward_alone(blocks_in, biases, xs, keybias, valid, cot, *refs):
    vecs, (probs_hbm, out_ref, *outs), scratch = refs[:7], refs[7 : 9 + N_KEPT], refs[9 + N_KEPT :]
    blocks, vec, *scratch, keep_sem = scratch
    fill_vectors(vec, vecs)
    load = pltpu.make_async_copy(blocks_in, blocks, keep_sem)
    load.start()
    load.wait()
    forward_compute(
        blocks, biases, xs, keybias, valid, cot, vec, probs_hbm, out_ref, outs, *scratch, NoHooks()
    )


BLOCKS = (3, 4, 2, 2, 2, 96, 768)


def forward_outs(rows):
    def of(shape, dtype):
        return jax.ShapeDtypeStruct(shape, dtype)

    return [
        of((12, 8, rows), F32),
        of((12, 2, 64, rows), F32),
        of((2, 768, rows), BF16),
        of((12, rows, 128), BF16),
        of((8, 128, LEN), BF16),
        of((8, LEN, 128), BF16),
        of((4, rows, 256), BF16),
        of((4, rows, 768), BF16),
        of((4, rows, 768), BF16),
        of((768, rows), BF16),
        of((rows, 768), F32),
        of((rows, 1), F32),
        of((rows, 768), BF16),
        of((768, rows), BF16),
        of((rows, 768), F32),
        of((8, 768), F32),
    ]


N_FORWARD_SCRATCH = 10


def forward_scratch(rows):
    return [
        [pltpu.VMEM(out.shape, out.dtype) for out in forward_outs(rows)],
        pltpu.SemaphoreType.DMA((N_KEPT,)),
        pltpu.VMEM((8, LEN, 128), BF16),
        pltpu.VMEM((8, 128, LEN), BF16),
        pltpu.VMEM((256, rows), BF16),
        pltpu.VMEM((3, rows, rows), BF16),
        pltpu.SemaphoreType.DMA((3,)),
        pltpu.VMEM((rows, 768), F32),
        pltpu.VMEM((rows, 768), BF16),
        pltpu.VMEM((12, 8, rows), F32),
    ]


def run_forward_linked(rows, *ins):
    outs = forward_outs(rows)
    probs = jax.ShapeDtypeStruct((12, LEN, rows), BF16)
    frames = jax.ShapeDtypeStruct((rows, 768), BF16)
    masked = jax.ShapeDtypeStruct((2, rows, 1), F32)
    blocks, probs, frames, masked, *kept = pl.pallas_call(
        forward_linked,
        name="forward",
        out_shape=[jax.ShapeDtypeStruct(BLOCKS, BF16), probs, frames, masked, *outs],
        in_specs=[pl.BlockSpec(memory_space=pltpu.SMEM)] + [vmem()] * 19,
        out_specs=[hbm(), hbm(), vmem(), vmem()] + [hbm()] * N_KEPT,
        scratch_shapes=[
            pltpu.VMEM(BLOCKS, BF16),
            pltpu.VMEM((4, 16, 768), BF16),
            pltpu.VMEM((2, rows, 768), BF16),
            pltpu.VMEM((LEN, 128), BF16),
            pltpu.VMEM((rows, 1), F32),
            pltpu.VMEM((8, 768), F32),
            *forward_scratch(rows),
            pltpu.SemaphoreType.DMA((4, 2, 3)),
            pltpu.SemaphoreType.DMA((4, 4)),
            pltpu.SemaphoreType.DMA((3, 4, 5)),
            pltpu.SemaphoreType.DMA((3, 4, 5)),
            pltpu.SemaphoreType.DMA,
            pltpu.SemaphoreType.DMA,
            pltpu.SemaphoreType.DMA((3,)),
        ],
        compiler_params=pltpu.CompilerParams(
            collective_id=0, has_side_effects=True, vmem_limit_bytes=VMEM_LIMIT
        ),
    )(*ins)
    return blocks, probs, frames, masked, kept


def run_forward_alone(rows, *ins):
    probs = jax.ShapeDtypeStruct((12, LEN, rows), BF16)
    frames = jax.ShapeDtypeStruct((rows, 768), BF16)
    probs, frames, *kept = pl.pallas_call(
        forward_alone,
        name="forward",
        out_shape=[probs, frames, *forward_outs(rows)],
        in_specs=[hbm()] + [vmem()] * 12,
        out_specs=[hbm(), vmem()] + [hbm()] * N_KEPT,
        scratch_shapes=[pltpu.VMEM(BLOCKS, BF16), pltpu.VMEM((8, 768), F32), *forward_scratch(rows), pltpu.SemaphoreType.DMA],
        compiler_params=pltpu.CompilerParams(vmem_limit_bytes=VMEM_LIMIT),
    )(*ins)
    return probs, frames, kept


def chunk_at(n):
    return (2 - n % 2, n // 2) if n < 8 else (0, n - 8)


class Scatter:
    def __init__(self, at, grads, core_in, first_in, second_in, z_in, out, send, recv, z_send, z_recv):
        self.at, self.grads, self.out = at, grads, out
        self.core_in, self.first_in, self.second_in, self.z_in = core_in, first_in, second_in, z_in
        self.send, self.recv, self.z_send, self.z_recv = send, recv, z_send, z_recv

    def copy(self, kind, m, which):
        at, grads = self.at, self.grads.at[kind, m]
        x, y, c = at.x, at.y, at.c
        low, high = pl.ds(0, 48), pl.ds(48, 48)
        src, dst, device = {
            0: lambda: (grads.at[:, :, 1 - c], self.core_in.at[kind, m], at.core),
            1: lambda: (grads.at[:, 1 - x, c, low], self.first_in.at[kind, m, 0], at.across_x),
            2: lambda: (grads.at[1 - y, :, c, high], self.first_in.at[kind, m, 1], at.across_y),
            3: lambda: (grads.at[1 - y, x, c, low], self.second_in.at[kind, m, 0], at.across_y),
            4: lambda: (grads.at[y, 1 - x, c, high], self.second_in.at[kind, m, 1], at.across_x),
        }[which]()
        return remote(src, dst, self.send.at[kind, m, which], self.recv.at[kind, m, which], device)

    def add(self, ref, got):
        ref[...] = (ref[...].astype(F32) + got[...].astype(F32)).astype(BF16)

    def begin(self, kind, m):
        self.copy(kind, m, 0).start()

    def first(self, kind, m):
        at, grads = self.at, self.grads.at[kind, m]
        self.copy(kind, m, 0).wait_recv()
        for y in range(2):
            for x in range(2):
                self.add(grads.at[y, x, at.c], self.core_in.at[kind, m, y, x])
        self.copy(kind, m, 1).start()
        self.copy(kind, m, 2).start()

    def second(self, kind, m):
        at, grads = self.at, self.grads.at[kind, m]
        low, high = pl.ds(0, 48), pl.ds(48, 48)
        self.copy(kind, m, 1).wait_recv()
        for y in range(2):
            self.add(grads.at[y, at.x, at.c, low], self.first_in.at[kind, m, 0, y])
        self.copy(kind, m, 3).start()
        self.copy(kind, m, 2).wait_recv()
        for x in range(2):
            self.add(grads.at[at.y, x, at.c, high], self.first_in.at[kind, m, 1, x])
        self.copy(kind, m, 4).start()

    def third(self, kind, m):
        at = self.at
        grads = self.grads.at[kind, m, at.y, at.x, at.c]
        self.copy(kind, m, 3).wait_recv()
        self.add(grads.at[pl.ds(0, 48)], self.second_in.at[kind, m, 0])
        self.copy(kind, m, 4).wait_recv()
        self.add(grads.at[pl.ds(48, 48)], self.second_in.at[kind, m, 1])
        self.z_start(kind, m)

    def z_copy(self, kind, m, direction):
        at = self.at
        src = self.grads.at[kind, m, at.y, at.x, at.c]
        device = at.right if direction == 0 else at.left
        slot = m if direction == 0 else jnp.where(m == at.z - 1, 4, m)
        return remote(src, self.z_in.at[kind, slot], self.z_send.at[kind, m], self.z_recv.at[kind, slot], device)

    def z_landed(self, kind, m, slot, direction):
        at = self.at
        src = self.grads.at[kind, m, at.y, at.x, at.c]
        device = at.right if direction == 0 else at.left
        return remote(src, self.z_in.at[kind, slot], self.z_send.at[kind, m], self.z_recv.at[kind, slot], device)

    def relay(self, kind, m, direction):
        at = self.at
        self.z_landed(kind, m, m, direction).wait_recv()
        self.add(self.grads.at[kind, m, at.y, at.x, at.c], self.z_in.at[kind, m])
        self.z_copy(kind, m, direction).start()

    def z_start(self, kind, m):
        z = self.at.z
        if m > 0:
            pl.when(z == 0)(lambda: self.z_copy(kind, m, 0).start())
        if m < 3:
            pl.when(z == 3)(lambda: self.z_copy(kind, m, 1).start())

    def z_one(self, kind, m):
        z = self.at.z
        if m > 1:
            pl.when(z == 1)(lambda: self.relay(kind, m, 0))
        else:
            pl.when(z == 2)(lambda: self.relay(kind, m, 1))

    def z_two(self, kind, m):
        z = self.at.z
        if m == 3:
            pl.when(z == 2)(lambda: self.relay(kind, m, 0))
        if m == 0:
            pl.when(z == 1)(lambda: self.relay(kind, m, 1))

    def finish(self, kind):
        at, z = self.at, self.at.z
        self.out[kind] = self.grads[kind, z, at.y, at.x, at.c].astype(F32)

        @pl.when(z > 0)
        def _():
            self.z_landed(kind, z, z, 0).wait_recv()
            self.out[kind] += self.z_in[kind, z].astype(F32)

        @pl.when(z < 3)
        def _():
            self.z_landed(kind, z, 4, 1).wait_recv()
            self.out[kind] += self.z_in[kind, 4].astype(F32)

    def run(self, **steps):
        for name, places in steps.items():
            for n in places:
                getattr(self, name)(*chunk_at(n))

    def drain(self):
        z = self.at.z
        for kind in range(3):

            def of_index(m, _, kind=kind):
                for which in range(5):
                    self.copy(kind, m, which).wait_send()
                pl.when(m > z)(lambda: self.z_copy(kind, m, 0).wait_send())
                pl.when(m < z)(lambda: self.z_copy(kind, m, 1).wait_send())
                return 0

            lax.fori_loop(0, 4, of_index, 0)


class Totals:
    def __init__(self, at, rows, got, send, recv):
        self.rows, self.got, self.send, self.recv = rows, got, send, recv
        self.partners = (at.core, at.across_x, at.across_y, at.mate, at.far)

    def copy(self, stage):
        return remote(
            self.rows.at[stage], self.got.at[stage], self.send.at[stage], self.recv.at[stage], self.partners[stage]
        )

    def start(self, stage):
        self.copy(stage).start()

    def finish(self, stage):
        self.copy(stage).wait()
        self.rows[stage + 1] = self.rows[stage] + self.got[stage]


def backward_compute(
    blocks_hbm,
    probs_hbm,
    acted_hbm,
    slope_hbm,
    recip_ref,
    headout_hbm,
    xt_hbm,
    qm_hbm,
    kt_hbm,
    v_hbm,
    att_hbm,
    n1t_hbm,
    n1_hbm,
    rs1_ref,
    gb2_hbm,
    gb2t_hbm,
    g2_hbm,
    sums_ref,
    masked_ref,
    gain_ref,
    grads,
    rows_ref,
    weight,
    weight_sem,
    acts,
    acts_sem,
    probs,
    probs_sem,
    gb1,
    gb1t,
    grad_one,
    parts,
    g2_ref,
    state_sem,
    gb2_ref,
    gb2t_ref,
    n1t_ref,
    xt_ref,
    headout_ref,
    qm_ref,
    kt_ref,
    v_ref,
    att_ref,
    head_sem,
    own,
    sides,
    shifts,
    shares,
    hooks,
):
    rows = g2_ref.shape[0]
    g2_load = pltpu.make_async_copy(g2_hbm, g2_ref, state_sem.at[0])
    n1_load = pltpu.make_async_copy(n1_hbm, grad_one, state_sem.at[1])
    gb2_load = pltpu.make_async_copy(gb2_hbm, gb2_ref, state_sem.at[2])
    gb2t_load = pltpu.make_async_copy(gb2t_hbm, gb2t_ref, state_sem.at[3])
    n1t_load = pltpu.make_async_copy(n1t_hbm, n1t_ref, state_sem.at[4])
    xt_load = pltpu.make_async_copy(xt_hbm, xt_ref, state_sem.at[5])

    def head_loads(m, slot, side):
        three, two, half = pl.ds(3 * m, 3), pl.ds(2 * m, 2), pl.ds(side * rows, rows)
        pairs = [
            (qm_hbm.at[three], qm_ref.at[slot]),
            (kt_hbm.at[two, :, half], kt_ref.at[slot]),
            (v_hbm.at[two, half], v_ref.at[slot]),
            (headout_hbm.at[three], headout_ref.at[slot]) if side else (att_hbm.at[m], att_ref.at[slot]),
        ]
        return [
            pltpu.make_async_copy(src, dst, head_sem.at[slot, i if i < 3 else 4 - side])
            for i, (src, dst) in enumerate(pairs)
        ]

    def weight_load(kind, m, slot):
        return pltpu.make_async_copy(blocks_hbm.at[kind, m], weight.at[slot], weight_sem.at[slot])

    def act_loads(m, slot):
        return (
            pltpu.make_async_copy(acted_hbm.at[m], acts.at[slot, 0], acts_sem.at[slot, 0]),
            pltpu.make_async_copy(slope_hbm.at[m], acts.at[slot, 1], acts_sem.at[slot, 1]),
        )

    def probs_load(head, side, slot):
        return pltpu.make_async_copy(
            probs_hbm.at[head, pl.ds(side * rows, rows)], probs.at[slot], probs_sem.at[slot]
        )

    def feed_loads(m, slot):
        return (weight_load(DOWN, m, 2 * slot), weight_load(UP, m, 2 * slot + 1), *act_loads(m, slot))

    def begin(copies):
        for copy in copies:
            copy.start()

    def finish(copies):
        for copy in copies:
            copy.wait()

    def block(slot, low=0, width=768):
        return weight[slot, :, :, :, :, pl.ds(low, width)].reshape(768, width)

    def put(kind, m, value, low=0):
        width = value.shape[1]
        grads[kind, m, :, :, :, :, pl.ds(low, width)] = value.astype(BF16).reshape(2, 2, 2, 96, width)

    begin((gb2_load,))
    begin(feed_loads(0, 0))
    begin((gb2t_load, n1t_load, g2_load, n1_load, xt_load))
    begin(head_loads(0, 0, 1))
    for j in range(3):
        probs_load(j, 1, j).start()
    parts[...] = jnp.zeros_like(parts)
    finish((gb2_load, gb2t_load, n1t_load, g2_load))

    def feed(m, _):
        slot = lax.rem(m, 2)
        pl.when(m < 3)(lambda: begin(feed_loads(m + 1, 1 - slot)))
        finish(feed_loads(m, slot))
        grad_acted = dot(gb2_ref[...], block(2 * slot))
        grad_pre = (grad_acted * acts[slot, 1].astype(F32)).astype(BF16)
        acts[slot, 1] = grad_pre
        hooks.after("grad_pre", m)
        parts[m, 0:1, :] = jnp.sum(grad_pre.astype(F32), axis=0, keepdims=True)
        put(DOWN, m, dot(gb2t_ref[...], acts[slot, 0]))
        hooks.ready(DOWN, m)
        hooks.after("down", m)
        put(UP, m, dot(n1t_ref[...], acts[slot, 1]))
        hooks.ready(UP, m)
        g2_ref[...] += dot(acts[slot, 1], block(2 * slot + 1), (1, 1))
        hooks.after("feed", m)
        return 0

    lax.fori_loop(0, 4, feed, 0)
    for m in range(4):
        weight_load(ATT, m, m).start()

    chunk = 64

    def norm_back(i, sums):
        r = pl.ds(pl.multiple_of(i * chunk, chunk), chunk)
        grad = g2_ref[r, :]
        unit = grad_one[r, :]
        scaled = grad * gain
        grad_in = (
            scaled
            - jnp.mean(scaled, axis=1, keepdims=True)
            - unit * jnp.mean(scaled * unit, axis=1, keepdims=True)
        ) * rs1_ref[r, :]
        grad_one[r, :] = grad_in
        gb1[r, :] = grad_in.astype(BF16)
        return (
            sums[0] + jnp.sum(grad_in, axis=0, keepdims=True),
            sums[1] + jnp.sum(grad * unit, axis=0, keepdims=True),
            sums[2] + jnp.sum(grad, axis=0, keepdims=True),
        )

    zero = jnp.zeros((1, 768), F32)
    finish((n1_load, xt_load))
    gain = gain_ref[...].astype(F32).reshape(1, 768)
    sums = lax.fori_loop(0, rows // chunk, norm_back, (zero, zero, zero))
    rows_ref[0, 0:1, :] = sums[0]
    rows_ref[0, 1:2, :] = sums_ref[0:1, :]
    rows_ref[0, 2:3, :] = sums[1]
    rows_ref[0, 3:4, :] = sums[2]
    rows_ref[0, 4:5, :] = sums_ref[1:2, :]
    rows_ref[0, 5:6, :] = sums_ref[2:3, :]
    gb1t[...] = gb1[...].T
    hooks.after("norm")
    g2_ref[...] = jnp.zeros_like(g2_ref)

    def wide(m, j, side):
        zeros = jnp.zeros((64, rows), BF16)
        return jnp.concatenate([zeros, side] if j == 1 else [side, zeros], axis=0)

    def half_back(slot, m, j, side, shift, next_load):
        t = j // 2
        side = wide(m, j, side)
        probs_load(0, 0, j).wait()
        weights = probs[j]
        grad_weights = dot(v_ref[slot, t], side)
        grad_scores = (weights.astype(F32) * (grad_weights - shift)).astype(BF16)
        grad_v = dot(weights, side.T)
        next_load()
        grad_k = dot(grad_scores, qm_ref[slot, j])
        lane = 0 if j == 0 else 64
        grad_q = dot(kt_ref[slot, t, lane : lane + 64, :], grad_scores)
        return grad_k, grad_v, grad_q

    def join(parts):
        return [parts[0] + parts[1], parts[2]]

    def back_other(m, _):
        slot = lax.rem(m, 2)
        pl.when(m < 3)(lambda: begin(head_loads(m + 1, 1 - slot, 1)))
        pl.when(m == 3)(lambda: begin(head_loads(0, 0, 0)))
        weight_load(ATT, m, m).wait()
        finish(head_loads(m, slot, 1))
        grad_att_t = dot(gb1[...], block(m, 512, 256)).T
        grads_k, grads_v = [], []
        for j in range(3):
            head = 3 * m + j
            place = (128, 192, 64)[j]
            grad_att = grad_att_t[place : place + 64, :]
            own = (grad_att * recip_ref[head, 0:1, :]).astype(BF16)
            other = (grad_att * recip_ref[head, 1:2, :]).astype(BF16)
            row_sum = jnp.sum(
                own.astype(F32) * headout_ref[slot, j, 0] + other.astype(F32) * headout_ref[slot, j, 1],
                axis=0,
                keepdims=True,
            )
            sides[head] = own
            shifts[head, 0:1, :] = row_sum * recip_ref[head, 0:1, :]

            def next_load(j=j, head=head):
                pl.when(m < 3)(lambda: probs_load(head + 3, 1, j).start())
                pl.when(m == 3)(lambda: probs_load(j, 0, j).start())

            grad_k, grad_v, grad_q = half_back(
                slot, m, j, other, row_sum * recip_ref[head, 1:2, :], next_load
            )
            grads_k.append(grad_k)
            grads_v.append(grad_v)
            shares[head] = grad_q
            hooks.after(f"other{j}", m)
        grads_k, grads_v = join(grads_k), join(grads_v)
        tile = acts.at[m // 2, lax.rem(m, 2)]
        tile[:, 128:256] = grads_k[0].astype(BF16)
        tile[:, 256:384] = grads_v[0].astype(BF16)
        tile[:, 384:512] = grads_k[1].astype(BF16)
        tile[:, 512:640] = grads_v[1].astype(BF16)
        parts[4 + m, 0:1, 128:640] = jnp.sum(tile[:, 128:640].astype(F32), axis=0, keepdims=True)
        g2_ref[...] += dot(tile[:, 128:640], block(m, 128, 512), (1, 1))
        return 0

    lax.fori_loop(0, 4, back_other, 0)

    def fill_other(i, total):
        r = pl.ds(pl.multiple_of(i * chunk, chunk), chunk)
        other = g2_ref[r, :]
        gb1[r, :] = other.astype(BF16)
        return total + jnp.sum(other * masked_ref[1, r, :], axis=0, keepdims=True)

    fill = lax.fori_loop(0, rows // chunk, fill_other, zero)
    hooks.after("mate")

    def back_own(m, _):
        slot = lax.rem(m, 2)
        pl.when(m < 3)(lambda: begin(head_loads(m + 1, 1 - slot, 0)))
        finish(head_loads(m, slot, 0))
        grads_k, grads_v, grads_q = [], [], []
        for j in range(3):
            head = 3 * m + j

            def next_load(j=j, head=head):
                pl.when(m < 3)(lambda: probs_load(head + 3, 0, j).start())

            grad_k, grad_v, grad_q = half_back(slot, m, j, sides[head], shifts[head, 0:1, :], next_load)
            grads_k.append(grad_k)
            grads_v.append(grad_v)
            grads_q.append((grad_q + shares[head]) * SCALE)
            hooks.after(f"own{j}", m)
        grads_k, grads_v = join(grads_k), join(grads_v)
        single = jnp.concatenate([grads_q[2], jnp.zeros((64, rows), F32)], axis=0).T
        own[:, 0:128] = jnp.concatenate(grads_q[:2], axis=0).T.astype(BF16)
        own[:, 128:256] = grads_k[0].astype(BF16)
        own[:, 256:384] = grads_v[0].astype(BF16)
        own[:, 384:512] = (grads_k[1] + single).astype(BF16)
        own[:, 512:640] = grads_v[1].astype(BF16)
        parts[4 + m, 0:1, 0:PROJ] += jnp.sum(own[...].astype(F32), axis=0, keepdims=True)
        other = acts[m // 2, lax.rem(m, 2), :, 128:640]
        grad_proj = dot(xt_ref[0], own[...])
        grad_other = dot(xt_ref[1], other)
        grad_out_w = dot(gb1t[...], att_ref[slot])
        put(ATT, m, grad_proj[:, :128], 0)
        put(ATT, m, grad_proj[:, 128:512] + grad_other[:, :384], 128)
        put(ATT, m, grad_proj[:, 512:] + grad_other[:, 384:] + grad_out_w[:, :128], 512)
        put(ATT, m, grad_out_w[:, 128:], 640)
        hooks.ready(ATT, m)
        grad_one[...] += dot(own[...], block(m, 0, PROJ), (1, 1))
        hooks.after("own", m)
        return 0

    lax.fori_loop(0, 4, back_own, 0)

    def fill_own(i, total):
        r = pl.ds(pl.multiple_of(i * chunk, chunk), chunk)
        return total + jnp.sum(grad_one[r, :] * masked_ref[0, r, :], axis=0, keepdims=True)

    rows_ref[0, 6:7, :] = lax.fori_loop(0, rows // chunk, fill_own, fill)
    rows_ref[0, 7:8, :] = zero
    for row in range(8):
        rows_ref[0, 8 + row : 9 + row, :] = parts[row, 0:1, :]


def finish_frames(grad_one, got, masked_ref, frames_ref):
    chunk = 64

    def body(i, _):
        r = pl.ds(pl.multiple_of(i * chunk, chunk), chunk)
        total = grad_one[r, :] + got[r, :].astype(F32)
        frames_ref[r, :] = jnp.where(masked_ref[0, r, :] > 0, 0.0, total).astype(BF16)
        return 0

    lax.fori_loop(0, grad_one.shape[0] // chunk, body, 0)


class NoScatter:
    def after(self, point, m=0):
        pass

    def ready(self, kind, m):
        pass


class ScatterHooks:
    PLAN = {
        ("feed", 0): dict(first=(0,)),
        ("grad_pre", 1): dict(first=(1,)),
        ("feed", 1): dict(second=(0,), first=(2,)),
        ("down", 2): dict(second=(1,), first=(3,)),
        ("feed", 3): dict(second=(2,), first=(4,), third=(0,)),
        ("norm", 0): dict(second=(3,), first=(5,), third=(1,)),
        ("other1", 1): dict(second=(4,), first=(6,), third=(2,), z_one=(0,)),
        ("other1", 2): dict(second=(5,), first=(7,), third=(3,), z_one=(1,)),
        ("other2", 3): dict(second=(6,), third=(4,), z_one=(2,), z_two=(0,)),
        ("mate", 0): dict(swap=(0,)),
        ("own0", 0): dict(swap=(1,)),
        ("own", 0): dict(second=(7,), third=(5,), z_one=(3,), z_two=(1,), swap=(2,)),
        ("own0", 1): dict(first=(8,)),
        ("own1", 1): dict(swap=(3,)),
        ("own", 1): dict(second=(8,), third=(6, 7), z_one=(4,), z_two=(2,)),
        ("own0", 2): dict(first=(9,)),
        ("own", 2): dict(second=(9,), third=(8,), z_one=(5,), z_two=(3,)),
        ("own0", 3): dict(first=(10,)),
        ("own", 3): dict(second=(10,), third=(9,), z_one=(6, 7), z_two=(4, 5)),
    }

    def __init__(self, scatter, swaps):
        self.scatter, self.swaps = scatter, swaps

    def ready(self, kind, m):
        self.scatter.begin(kind, m)

    def run(self, swap=(), **steps):
        self.scatter.run(**steps)
        for piece in swap:
            self.swaps[piece].start()

    def after(self, point, m=0):
        for (name, index), steps in self.PLAN.items():
            if name == point:
                if isinstance(m, int):
                    self.run(**steps)
                else:
                    pl.when(m == index)(functools.partial(self.run, **steps))


N_BACKWARD_INS = 20
N_BACKWARD_SCRATCH = 28


def backward_linked(*refs):
    ins = refs[:N_BACKWARD_INS]
    out_ref, rows_out, frames_ref = refs[N_BACKWARD_INS : N_BACKWARD_INS + 3]
    scratch = refs[N_BACKWARD_INS + 3 :]
    scratch, links = scratch[:N_BACKWARD_SCRATCH], scratch[N_BACKWARD_SCRATCH:]
    grads, rows_ref, gb1, grad_one = scratch[0], scratch[1], scratch[8], scratch[10]
    core_in, first_in, second_in, z_in, rows_in, mate_in = links[:6]
    send, recv, z_send, z_recv, t_send, t_recv, m_send, m_recv = links[6:]
    at = Place()
    at.greet(True)
    scatter = Scatter(at, grads, core_in, first_in, second_in, z_in, out_ref, send, recv, z_send, z_recv)
    totals = Totals(at, rows_ref, rows_in, t_send, t_recv)
    piece = gb1.shape[0] // 4
    swaps = [
        remote(
            gb1.at[pl.ds(i * piece, piece)], mate_in.at[pl.ds(i * piece, piece)], m_send.at[i], m_recv.at[i], at.mate
        )
        for i in range(4)
    ]
    backward_compute(*ins, *scratch, ScatterHooks(scatter, swaps))
    totals.start(0)
    scatter.run(first=(11,))
    totals.finish(0)
    totals.start(1)
    scatter.run(third=(10,), z_one=(8,), z_two=(6,))
    scatter.run(second=(11,))
    totals.finish(1)
    totals.start(2)
    scatter.run(z_one=(9,), z_two=(7,))
    scatter.run(third=(11,))
    totals.finish(2)
    totals.start(3)
    scatter.finish(DOWN)
    scatter.finish(UP)
    scatter.run(z_one=(10,), z_two=(8,))
    totals.finish(3)
    totals.start(4)
    scatter.run(z_one=(11,), z_two=(9, 10))
    for swap in swaps:
        swap.wait()
    finish_frames(grad_one, mate_in, ins[18], frames_ref)
    totals.finish(4)
    rows_out[...] = rows_ref[5]
    scatter.run(z_two=(11,))
    scatter.finish(ATT)
    scatter.drain()


def backward_alone(*refs):
    ins = refs[:N_BACKWARD_INS]
    grads_out, rows_out, mate_out, grad_one_out = refs[N_BACKWARD_INS : N_BACKWARD_INS + 4]
    scratch = refs[N_BACKWARD_INS + 4 :]
    *scratch, keep_sem = scratch
    grads, rows_ref, gb1, grad_one = scratch[0], scratch[1], scratch[8], scratch[10]
    backward_compute(*ins, *scratch, NoScatter())
    keep = pltpu.make_async_copy(grads, grads_out, keep_sem)
    keep.start()
    rows_out[...] = rows_ref[0]
    mate_out[...] = gb1[...]
    grad_one_out[...] = grad_one[...]
    keep.wait()


def backward_scratch(rows):
    return [
        pltpu.VMEM(BLOCKS, BF16),
        pltpu.VMEM((6, 16, 768), F32),
        pltpu.VMEM((4, *BLOCKS[2:]), BF16),
        pltpu.SemaphoreType.DMA((4,)),
        pltpu.VMEM((2, 2, rows, 768), BF16),
        pltpu.SemaphoreType.DMA((2, 2)),
        pltpu.VMEM((3, rows, rows), BF16),
        pltpu.SemaphoreType.DMA((3,)),
        pltpu.VMEM((rows, 768), BF16),
        pltpu.VMEM((768, rows), BF16),
        pltpu.VMEM((rows, 768), F32),
        pltpu.VMEM((8, 8, 768), F32),
        pltpu.VMEM((rows, 768), F32),
        pltpu.SemaphoreType.DMA((6,)),
        pltpu.VMEM((rows, 768), BF16),
        pltpu.VMEM((768, rows), BF16),
        pltpu.VMEM((768, rows), BF16),
        pltpu.VMEM((2, 768, rows), BF16),
        pltpu.VMEM((2, 3, 2, 64, rows), F32),
        pltpu.VMEM((2, 3, rows, 128), BF16),
        pltpu.VMEM((2, 2, 128, rows), BF16),
        pltpu.VMEM((2, 2, rows, 128), BF16),
        pltpu.VMEM((2, rows, 256), BF16),
        pltpu.SemaphoreType.DMA((2, 5)),
        pltpu.VMEM((rows, PROJ), BF16),
        pltpu.VMEM((12, 64, rows), BF16),
        pltpu.VMEM((12, 8, rows), F32),
        pltpu.VMEM((12, 64, rows), F32),
    ]


def run_backward(linked, blocks, probs, kept, masked, gain):
    recip, headout, xt, qm, kt, v, att, acted, slope, n1t, n1, rs1, gb2, gb2t, g2, sums = kept
    rows = gb2.shape[0]
    ins = (
        blocks, probs, acted, slope, recip, headout, xt, qm, kt, v, att, n1t, n1, rs1, gb2, gb2t, g2, sums, masked, gain
    )
    in_specs = [vmem() if i in (4, 13, 17, 18, 19) else hbm() for i in range(20)]
    if linked:
        return pl.pallas_call(
            backward_linked,
            name="backward",
            out_shape=[
                jax.ShapeDtypeStruct((3, 96, 768), F32),
                jax.ShapeDtypeStruct((16, 768), F32),
                jax.ShapeDtypeStruct((rows, 768), BF16),
            ],
            in_specs=in_specs,
            out_specs=[vmem()] * 3,
            scratch_shapes=[
                *backward_scratch(rows),
                pltpu.VMEM((3, 4, 2, 2, 96, 768), BF16),
                pltpu.VMEM((3, 4, 2, 2, 48, 768), BF16),
                pltpu.VMEM((3, 4, 2, 48, 768), BF16),
                pltpu.VMEM((3, 5, 96, 768), BF16),
                pltpu.VMEM((5, 16, 768), F32),
                pltpu.VMEM((rows, 768), BF16),
                pltpu.SemaphoreType.DMA((3, 4, 5)),
                pltpu.SemaphoreType.DMA((3, 4, 5)),
                pltpu.SemaphoreType.DMA((3, 4)),
                pltpu.SemaphoreType.DMA((3, 5)),
                pltpu.SemaphoreType.DMA((5,)),
                pltpu.SemaphoreType.DMA((5,)),
                pltpu.SemaphoreType.DMA((4,)),
                pltpu.SemaphoreType.DMA((4,)),
            ],
            compiler_params=pltpu.CompilerParams(
                collective_id=1, has_side_effects=True, vmem_limit_bytes=VMEM_LIMIT
            ),
        )(*ins)
    return pl.pallas_call(
        backward_alone,
        name="backward",
        out_shape=[
            jax.ShapeDtypeStruct(BLOCKS, BF16),
            jax.ShapeDtypeStruct((16, 768), F32),
            jax.ShapeDtypeStruct((rows, 768), BF16),
            jax.ShapeDtypeStruct((rows, 768), F32),
        ],
        in_specs=in_specs,
        out_specs=[hbm()] + [vmem()] * 3,
        scratch_shapes=[*backward_scratch(rows), pltpu.SemaphoreType.DMA],
        compiler_params=pltpu.CompilerParams(vmem_limit_bytes=VMEM_LIMIT),
    )(*ins)


def finish_kernel(parts, grads, totals, out_in, frames_in, out, frames, *outs):
    n_dp, n_mp = parts
    query, key, value, out_w, up, down, query_bias, value_bias, up_bias, *vectors = outs
    out[...] = out_in[...]
    frames[...] = frames_in[...]
    att = grads[0]
    query[...] = jnp.concatenate([att[:, 0:128], att[:, 384:448]], axis=1)
    key[...] = jnp.concatenate([att[:, 128:256], att[:, 448:512]], axis=1)
    value[...] = jnp.concatenate([att[:, 256:384], att[:, 512:576]], axis=1)
    out_w[...] = jnp.concatenate([att[:, 640:768], att[:, 576:640]], axis=1).T
    up[...] = grads[1]
    down[...] = grads[2]
    dp, z = lax.axis_index("dp"), lax.axis_index("mp")
    rows = totals[...]
    row_at = lax.broadcasted_iota(jnp.int32, rows.shape, 0)

    def shifted(block, by):
        return pltpu.roll(block, lax.rem(768 - by, 768), 1)

    def row_of(index):
        return jnp.broadcast_to(jnp.sum(jnp.where(row_at == index, rows, 0.0), axis=0, keepdims=True), (8, 768))

    part = 768 // (n_dp * n_mp)
    mine = shifted(rows[0:8], (dp * n_mp + z) * part)
    for i, ref in enumerate(vectors):
        ref[...] = mine[i : i + 1, :part]
    step = HEAD_DIM // n_dp
    heads = shifted(row_of(12 + z), dp * step)
    for head, (q_lane, v_lane) in enumerate(((0, 256), (64, 320), (384, 512))):
        query_bias[head : head + 1, :] = heads[0:1, q_lane : q_lane + step]
        value_bias[head : head + 1, :] = heads[0:1, v_lane : v_lane + step]
    ups = shifted(row_of(8 + z), dp * 2 * step)
    for i in range(6):
        up_bias[i : i + 1, :] = ups[0:1, 128 * i : 128 * i + 2 * step]


def run_finish(n_dp, n_mp, grads, totals, out, frames):
    def of(shape, dtype=F32):
        return jax.ShapeDtypeStruct(shape, dtype)

    d, step, part = grads.shape[1], HEAD_DIM // n_dp, 768 // (n_dp * n_mp)
    *outs, = pl.pallas_call(
        functools.partial(finish_kernel, (n_dp, n_mp)),
        name="finish",
        out_shape=[
            of(out.shape, BF16), of(frames.shape, BF16), of((d, 192)), of((d, 192)), of((d, 192)), of((192, d)),
            of((d, 768)), of((d, 768)), of((3, step)), of((3, step)), of((6, 2 * step)), *[of((1, part))] * 7,
        ],
        in_specs=[vmem()] * 4,
        out_specs=[vmem()] * 18,
        compiler_params=pltpu.CompilerParams(vmem_limit_bytes=VMEM_LIMIT),
    )(grads, totals, out, frames)
    return (*outs[:7], outs[7].T, *outs[8:11], *(row.reshape(part) for row in outs[11:]))


def shards(
    linked,
    frames,
    lengths,
    span_starts,
    cotangent,
    query_weight,
    key_weight,
    value_weight,
    out_weight,
    up_weight,
    down_weight,
    query_bias,
    value_bias,
    up_bias,
    out_bias,
    down_bias,
    first_gain,
    first_shift,
    second_gain,
    second_shift,
    mask_vector,
):
    rows = frames.shape[0]
    n_dp = 768 // query_weight.shape[0]
    n_mp = 768 // query_weight.shape[1]
    vecs = (out_bias, down_bias, first_gain, first_shift, second_gain, second_shift, mask_vector)
    if linked:
        blocks, probs, out, masked, kept = run_forward_linked(
            rows, lengths, span_starts, frames, cotangent, query_weight, key_weight, value_weight, out_weight,
            up_weight, down_weight.T, query_bias, value_bias, up_bias, *vecs,
        )
        grads, totals, grad_frames = run_backward(True, blocks, probs, kept, masked, first_gain)
        return run_finish(n_dp, n_mp, grads, totals, out, grad_frames)
    z = lax.axis_index("mp")
    half = z % 2
    length = lax.dynamic_index_in_dim(lengths, z // 2, keepdims=False)
    starts = lax.dynamic_index_in_dim(span_starts, z // 2, keepdims=False)
    slots = (jnp.arange(LEN, dtype=jnp.int32) + half * rows) % LEN
    valid = slots < length
    masked = jnp.any((slots[:, None] >= starts[None, :]) & (slots[:, None] < starts[None, :] + SPAN), axis=1)
    keybias = jnp.where(
        (jnp.arange(128) == 0)[None, :] & ~valid[:, None], jnp.float32(NEGATIVE), 0.0
    ).astype(BF16)
    valid_rows = valid[:rows].astype(F32)[:, None]
    masked_rows = masked.astype(F32).reshape(2, rows, 1)
    x = jnp.where(masked[:rows, None], mask_vector[None, :], frames)
    pack = jnp.stack(pack_weights(query_weight, key_weight, value_weight, out_weight.T, up_weight, down_weight.T))
    bias = pack_biases(query_bias, value_bias, up_bias)
    mates = [(0, 1), (1, 0), (2, 3), (3, 2)]
    blocks = lax.all_gather(lax.all_gather(pack, "dp", axis=1, tiled=True), "mp", axis=1).reshape(BLOCKS)
    biases = lax.all_gather(bias, "mp", axis=0)
    both = jnp.stack([x, lax.ppermute(x, "mp", mates)])
    probs, out, kept = run_forward_alone(rows, blocks, biases, both, keybias, valid_rows, cotangent, *vecs)
    grads, totals, mate, grad_one = run_backward(False, blocks, probs, kept, masked_rows, first_gain)
    grads = grads.reshape(3, 4, 768, 768).astype(F32)
    grads = lax.psum_scatter(grads, "mp", scatter_dimension=1, tiled=False)
    grads = lax.psum_scatter(grads, "dp", scatter_dimension=1, tiled=True)
    totals = lax.psum(totals, ("dp", "mp"))
    grad_frames = grad_one + lax.ppermute(mate, "mp", mates).astype(F32)
    grad_frames = jnp.where(masked[:rows, None], 0.0, grad_frames).astype(BF16)
    return run_finish(n_dp, n_mp, grads, totals, out, grad_frames)


def solution(mesh):
    linked = mesh.shape["dp"] == 8 and mesh.shape["mp"] == 4
    split = P(("dp", "mp"))
    return jax.shard_map(
        functools.partial(shards, linked),
        mesh=mesh,
        in_specs=(
            P(("dp", "mp"), None),
            P("dp"),
            P("dp", None),
            P(("dp", "mp"), None),
            P("dp", "mp"),
            P("dp", "mp"),
            P("dp", "mp"),
            P("mp", "dp"),
            P("dp", "mp"),
            P("mp", "dp"),
            P("mp", None),
            P("mp", None),
            P("mp", None),
            *([P()] * 7),
        ),
        out_specs=(
            P(("dp", "mp"), None),
            P(("dp", "mp"), None),
            P("dp", "mp"),
            P("dp", "mp"),
            P("dp", "mp"),
            P("mp", "dp"),
            P("dp", "mp"),
            P("mp", "dp"),
            P("mp", "dp"),
            P("mp", "dp"),
            P("mp", "dp"),
            *([split] * 7),
        ),
        check_vma=False,
    )
```

```python
import functools
import math

import jax
import jax.numpy as jnp
from jax import lax
from jax.experimental import pallas as pl
from jax.experimental.pallas import tpu as pltpu
from jax.sharding import PartitionSpec as P

HEAD_DIM = 64
SPAN = 10
LEN = 1024
EPSILON = 1e-05
NEGATIVE = -1e30
SCALE = 1.0 / math.sqrt(HEAD_DIM)

F32 = jnp.float32
BF16 = jnp.bfloat16
MESH = pl.DeviceIdType.MESH
VMEM_LIMIT = 63 * 1024 * 1024

ATT, UP, DOWN = 0, 1, 2
PROJ = 640


def dot(left, right, contract=(1, 0)):
    return lax.dot_general(
        left, right, (((contract[0],), (contract[1],)), ((), ())), preferred_element_type=F32
    )


def hbm():
    return pl.BlockSpec(memory_space=pl.ANY)


def vmem():
    return pl.BlockSpec(memory_space=pltpu.VMEM)


class Place:
    def __init__(self):
        self.dp = lax.axis_index("dp")
        self.z = lax.axis_index("mp")
        self.c = lax.rem(self.dp, 2)
        self.x = lax.rem(self.dp // 2, 2)
        self.y = self.dp // 4
        self.core = (self.dp + 1 - 2 * self.c, self.z)
        self.across_x = (self.dp + 2 - 4 * self.x, self.z)
        self.across_y = (self.dp + 4 - 8 * self.y, self.z)
        self.right = (self.dp, self.z + 1)
        self.left = (self.dp, self.z - 1)
        self.mate = (self.dp, self.z + 1 - 2 * lax.rem(self.z, 2))
        self.far = (self.dp, lax.rem(self.z + 2, 4))

    def hello(self, far):
        barrier = pltpu.get_barrier_semaphore()

        def signal(device):
            pl.semaphore_signal(barrier, inc=1, device_id=device, device_id_type=MESH)

        signal(self.core)
        signal(self.across_x)
        signal(self.across_y)
        if far:
            signal(self.far)
        pl.when(self.z < 3)(lambda: signal(self.right))
        pl.when(self.z > 0)(lambda: signal(self.left))

    def meet(self, far):
        ends = jnp.where((self.z == 0) | (self.z == 3), 1, 2)
        pl.semaphore_wait(pltpu.get_barrier_semaphore(), (4 if far else 3) + ends)


def remote(src, dst, send, recv, device):
    return pltpu.make_async_remote_copy(
        src_ref=src, dst_ref=dst, send_sem=send, recv_sem=recv, device_id=device, device_id_type=MESH
    )


class Gather:
    def __init__(self, at, blocks, biases, z_send, z_recv, p_send, p_recv):
        self.at, self.blocks, self.biases = at, blocks, biases
        self.z_send, self.z_recv, self.p_send, self.p_recv = z_send, z_recv, p_send, p_recv

    def z_copy(self, kind, m, direction, step):
        at = self.at
        if kind == 3:
            ref = self.biases.at[m]
        else:
            ref = self.blocks.at[kind, m, at.y, at.x, at.c]
        device = at.right if direction == 0 else at.left
        return remote(ref, ref, self.z_send.at[kind, direction, step], self.z_recv.at[kind, m], device)

    def z_step(self, kind, step):
        z = self.at.z
        if step == 0:
            pl.when((z > 0) & (z < 2))(lambda: self.z_copy(kind, z, 1, 0).start())
            pl.when(z < 3)(lambda: self.z_copy(kind, z, 0, 0).start())
            pl.when(z >= 2)(lambda: self.z_copy(kind, z, 1, 0).start())
            return

        def from_left():
            @pl.when(z >= step)
            def _():
                self.z_copy(kind, z - step, 0, 0).wait_recv()
                if step < 3:
                    pl.when(z < 3)(lambda: self.z_copy(kind, z - step, 0, step).start())
                self.first(kind, z - step)

        def from_right():
            @pl.when(z + step <= 3)
            def _():
                self.z_copy(kind, z + step, 1, 0).wait_recv()
                if step < 3:
                    pl.when(z > 0)(lambda: self.z_copy(kind, z + step, 1, step).start())
                self.first(kind, z + step)

        pl.when(z < 2)(from_right)
        from_left()
        pl.when(z >= 2)(from_right)

    def plane_copy(self, kind, m, which):
        at, block = self.at, self.blocks.at[kind, m]
        x, y, c = at.x, at.y, at.c
        low, high = pl.ds(0, 48), pl.ds(48, 48)
        ref, device = {
            0: lambda: (block.at[y, x, c, low], at.across_x),
            1: lambda: (block.at[y, x, c, high], at.across_y),
            2: lambda: (block.at[y, :, c, low], at.across_y),
            3: lambda: (block.at[:, x, c, high], at.across_x),
            4: lambda: (block.at[:, :, c], at.core),
        }[which]()
        return remote(ref, ref, self.p_send.at[kind, m, which], self.p_recv.at[kind, m, which], device)

    def at_step(self, step, act):
        z = self.at.z
        if step == 0:
            act(z)
            return
        pl.when(z >= step)(lambda: act(z - step))
        pl.when(z + step <= 3)(lambda: act(z + step))

    def order(self, step):
        z = self.at.z
        from_low = jnp.where(z == 1, jnp.where(step < 2, 1 - step, step), step)
        mirrored = 3 - z
        from_high = jnp.where(mirrored == 1, jnp.where(step < 2, 1 - step, step), step)
        return jnp.where(z < 2, from_low, 3 - from_high)

    def first(self, kind, m):
        if kind < 3:
            self.plane_copy(kind, m, 0).start()
            self.plane_copy(kind, m, 1).start()

    def second(self, kind, step):
        def act(m):
            self.plane_copy(kind, m, 0).wait_recv()
            self.plane_copy(kind, m, 2).start()
            self.plane_copy(kind, m, 1).wait_recv()
            self.plane_copy(kind, m, 3).start()

        self.at_step(step, act)

    def third(self, kind, step):
        def act(m):
            self.plane_copy(kind, m, 2).wait_recv()
            self.plane_copy(kind, m, 3).wait_recv()
            self.plane_copy(kind, m, 4).start()

        self.at_step(step, act)

    def last(self, kind):
        for m in range(4):
            self.plane_copy(kind, m, 4).wait_recv()

    def drain(self):
        z = self.at.z
        for kind in range(4):
            for step in range(3):
                pl.when((z < 3) & (z >= step))(
                    lambda k=kind, s=step: self.z_copy(k, z - s, 0, s).wait_send()
                )
                pl.when((z > 0) & (z + step <= 3))(
                    lambda k=kind, s=step: self.z_copy(k, z + s, 1, s).wait_send()
                )
        for kind in range(3):
            for m in range(4):
                for which in range(5):
                    self.plane_copy(kind, m, which).wait_send()


def block_of(blocks, kind, m, low=0, width=768):
    return blocks[kind, m, :, :, :, :, pl.ds(low, width)].reshape(768, width)


def lane_mask(rows, lower):
    lanes = lax.broadcasted_iota(jnp.int32, (rows, 128), 1)
    return (lanes < 64) if lower else (lanes >= 64)


def forward_compute(
    blocks,
    biases,
    xs,
    keybias_ref,
    valid_ref,
    cot_ref,
    vec_ref,
    probs_hbm,
    out_hbm,
    outs_hbm,
    outs_ref,
    outs_sem,
    k_ref,
    vt_ref,
    probs,
    probs_sem,
    total,
    low,
    stats,
    out_ref,
    out_sem,
    hooks,
):
    rows = xs.shape[1]
    (recip_ref, headout_ref, xt_ref, qm_ref, kt_ref, v_ref, att_ref, acted_ref, slope_ref, n1t_ref, n1_ref, rs1_ref,
     gb2_ref, gb2t_ref, g2_ref, sums_ref) = outs_ref
    keeps = [
        pltpu.make_async_copy(ref, to, outs_sem.at[i]) for i, (ref, to) in enumerate(zip(outs_ref, outs_hbm, strict=True))
    ]

    def keep(*which):
        for i in which:
            keeps[i].start()

    xt_ref[0] = xs[0].T
    ones_lane = jnp.where(lax.broadcasted_iota(jnp.int32, (rows, 128), 1) == 0, 1.0, 0.0).astype(BF16)

    def probs_copy(head, side, slot):
        return pltpu.make_async_copy(
            probs.at[slot], probs_hbm.at[head, pl.ds(side * rows, rows)], probs_sem.at[slot]
        )

    own_rows, other_rows = pl.ds(0, rows), pl.ds(rows, rows)

    def project(m, _):
        bias = biases[m, 0:1, :].astype(F32)[:, :PROJ]
        own = dot(xs[0], block_of(blocks, ATT, m, 0, PROJ)) + bias
        k_ref[2 * m, own_rows] = own[:, 128:256].astype(BF16)
        v_ref[2 * m, own_rows] = own[:, 256:384].astype(BF16)
        k_ref[2 * m + 1, own_rows] = own[:, 384:512].astype(BF16)
        v_ref[2 * m + 1, own_rows] = own[:, 512:640].astype(BF16)
        lower, upper = lane_mask(rows, True), lane_mask(rows, False)
        pair = own[:, 0:128].astype(BF16).astype(F32) * SCALE
        single = pltpu.roll(own[:, 384:512].astype(BF16).astype(F32) * SCALE, 64, 1)
        qm_ref[3 * m] = jnp.where(lower, pair, 0.0).astype(BF16)
        qm_ref[3 * m + 1] = jnp.where(upper, pair, 0.0).astype(BF16)
        qm_ref[3 * m + 2] = jnp.where(upper, single, 0.0).astype(BF16)
        for tile in range(2):
            kt_ref[2 * m + tile, :, own_rows] = k_ref[2 * m + tile, own_rows].T
            vt_ref[2 * m + tile, :, own_rows] = v_ref[2 * m + tile, own_rows].T
        hooks.after("project", m)
        return 0

    def project_other(m, _):
        bias = biases[m, 0:1, :].astype(F32)[:, 128:PROJ]
        other = dot(xs[1], block_of(blocks, ATT, m, 128, 512)) + bias
        k_ref[2 * m, other_rows] = other[:, 0:128].astype(BF16)
        v_ref[2 * m, other_rows] = other[:, 128:256].astype(BF16)
        k_ref[2 * m + 1, other_rows] = other[:, 256:384].astype(BF16)
        v_ref[2 * m + 1, other_rows] = other[:, 384:512].astype(BF16)
        for tile in range(2):
            kt_ref[2 * m + tile, :, other_rows] = k_ref[2 * m + tile, other_rows].T
            vt_ref[2 * m + tile, :, other_rows] = v_ref[2 * m + tile, other_rows].T
        return 0

    def attend_half(m, side):
        half = own_rows if side == 0 else other_rows

        def free():
            for j in range(3):
                probs_copy(3 * m + j, side, j).wait()

        if side == 0:
            pl.when(m > 0)(free)
        else:
            free()
        scores, tops, sums, outs = [], [], [], []
        for j in range(3):
            keys = jnp.concatenate([k_ref[2 * m + j // 2, half], keybias_ref[half, :]], axis=1)
            queries = jnp.concatenate([qm_ref[3 * m + j], ones_lane], axis=1)
            scores.append(dot(keys, queries, (1, 1)))
        for j in range(3):
            top = jnp.max(scores[j], axis=0, keepdims=True)
            weights = jnp.exp(scores[j] - top)
            tops.append(top)
            sums.append(jnp.sum(weights, axis=0, keepdims=True))
            probs[j] = weights.astype(BF16)
            lane = 64 * (j % 2)
            outs.append(dot(vt_ref[2 * m + j // 2, lane : lane + 64, half], probs[j]))
            headout_ref[3 * m + j, side] = outs[j]
        return tops, sums, outs

    def send_probs(m, side):
        for j in range(3):
            probs_copy(3 * m + j, side, j).start()

    def attend_own(m, _):
        tops, sums, _ = attend_half(m, 0)
        for j in range(3):
            stats[3 * m + j, 0:1, :] = tops[j]
            stats[3 * m + j, 1:2, :] = sums[j]
        send_probs(m, 0)
        hooks.after("own", m)
        return 0

    def attend(m, _):
        tops, sums, outs = attend_half(m, 1)
        pieces = [jnp.zeros((64, rows), BF16), None, None, None]
        for j in range(3):
            head = 3 * m + j
            top_own = stats[head, 0:1, :]
            top_all = jnp.maximum(tops[j], top_own)
            factor, factor_own = jnp.exp(tops[j] - top_all), jnp.exp(top_own - top_all)
            recip = 1.0 / (factor_own * stats[head, 1:2, :] + factor * sums[j])
            factor, factor_own = factor * recip, factor_own * recip
            recip_ref[head] = jnp.concatenate([factor_own, factor, jnp.zeros((6, rows), F32)], axis=0)
            pieces[(2, 3, 1)[j]] = (headout_ref[head, 0] * factor_own + outs[j] * factor).astype(BF16)
        att_ref[m] = jnp.concatenate(pieces, axis=0).T
        send_probs(m, 1)
        hooks.after("other", m)
        return 0

    hooks.before("project")
    lax.fori_loop(0, 4, project, 0)
    lax.fori_loop(0, 4, attend_own, 0)
    hooks.before("other")
    xt_ref[1] = xs[1].T
    lax.fori_loop(0, 4, project_other, 0)
    keep(2, 3, 4, 5)
    hooks.after("swapped")
    lax.fori_loop(0, 4, attend, 0)
    keep(0, 1, 6)
    branch = [dot(att_ref[m], block_of(blocks, ATT, m, 512, 256), (1, 1)) for m in range(4)]
    total[...] = (branch[0] + branch[1]) + (branch[2] + branch[3])
    for j in range(3):
        probs_copy(9 + j, 1, j).wait()

    chunk = 64

    def norm_one(i, _):
        r = pl.ds(pl.multiple_of(i * chunk, chunk), chunk)
        resid = xs[0, r, :].astype(F32) + total[r, :] + vec_ref[0:1, :]
        centered = resid - jnp.mean(resid, axis=1, keepdims=True)
        rstd = lax.rsqrt(jnp.mean(centered * centered, axis=1, keepdims=True) + EPSILON)
        unit = centered * rstd
        n1_ref[r, :] = unit
        rs1_ref[r, :] = rstd
        low[r, :] = (unit * vec_ref[2:3, :] + vec_ref[3:4, :]).astype(BF16)
        return 0

    lax.fori_loop(0, rows // chunk, norm_one, 0)
    n1t_ref[...] = low[...].T
    keep(9, 10, 11)
    hooks.after("norm")
    hooks.before("feed")

    def feed(m, _):
        pre = dot(low[...], block_of(blocks, UP, m)) + biases[m, 1:2, :].astype(F32)
        phi = 0.5 * (1.0 + lax.erf(pre * (1.0 / math.sqrt(2.0))))
        acted_ref[m] = (pre * phi).astype(BF16)
        slope_ref[m] = (phi + pre * jnp.exp(-0.5 * pre * pre) * (1.0 / math.sqrt(2.0 * math.pi))).astype(BF16)
        hooks.after("feed", m)
        return 0

    lax.fori_loop(0, 4, feed, 0)
    keep(7, 8)
    hooks.before("down")

    def down(step, _):
        m = hooks.order(step)
        hooks.landed(DOWN, m)
        part = dot(acted_ref[m], block_of(blocks, DOWN, m), (1, 1))

        @pl.when(step == 0)
        def _():
            total[...] = part

        @pl.when(step > 0)
        def _():
            total[...] += part

        return 0

    lax.fori_loop(0, 4, down, 0)
    hooks.all_landed()

    def norm_two(i, sums):
        r = pl.ds(pl.multiple_of(i * chunk, chunk), chunk)
        normed = n1_ref[r, :] * vec_ref[2:3, :] + vec_ref[3:4, :]
        resid = normed + total[r, :] + vec_ref[1:2, :]
        centered = resid - jnp.mean(resid, axis=1, keepdims=True)
        rstd = lax.rsqrt(jnp.mean(centered * centered, axis=1, keepdims=True) + EPSILON)
        unit = centered * rstd
        valid = valid_ref[r, :]
        out_ref[r, :] = (valid * (unit * vec_ref[4:5, :] + vec_ref[5:6, :])).astype(BF16)
        grad = valid * cot_ref[r, :].astype(F32)
        scaled = grad * vec_ref[4:5, :]
        grad_in = (
            scaled
            - jnp.mean(scaled, axis=1, keepdims=True)
            - unit * jnp.mean(scaled * unit, axis=1, keepdims=True)
        ) * rstd
        g2_ref[r, :] = grad_in
        gb2_ref[r, :] = grad_in.astype(BF16)
        for i, (ref, to) in enumerate(((out_ref, out_hbm), (g2_ref, outs_hbm[14]), (gb2_ref, outs_hbm[12]))):
            pltpu.make_async_copy(ref.at[r], to.at[r], out_sem.at[i]).start()
        return (
            sums[0] + jnp.sum(grad_in, axis=0, keepdims=True),
            sums[1] + jnp.sum(grad * unit, axis=0, keepdims=True),
            sums[2] + jnp.sum(grad, axis=0, keepdims=True),
        )

    zero = jnp.zeros((1, 768), F32)
    sums = lax.fori_loop(0, rows // chunk, norm_two, (zero, zero, zero))
    sums_ref[...] = jnp.concatenate([*sums, jnp.zeros((5, 768), F32)], axis=0)
    keep(15)
    gb2t_ref[...] = gb2_ref[...].T
    keep(13)
    hooks.finish()
    for i, copy in enumerate(keeps):
        if i not in (12, 14):
            copy.wait()
    for i, (ref, to) in enumerate(((out_ref, out_hbm), (g2_ref, outs_hbm[14]), (gb2_ref, outs_hbm[12]))):
        pltpu.make_async_copy(ref, to, out_sem.at[i]).wait()


class NoHooks:
    def after(self, point, m=0):
        pass

    def before(self, point):
        pass

    def order(self, step):
        return step

    def landed(self, kind, m):
        pass

    def all_landed(self):
        pass

    def finish(self):
        pass


class GatherHooks:
    MIDDLE = {
        ("project", 1): (("z_step", DOWN, 1),),
        ("project", 3): (("second", UP, 0), ("second", UP, 1)),
        ("own", 0): (("second", UP, 2),),
        ("own", 1): (("z_step", DOWN, 2), ("second", DOWN, 0), ("third", UP, 0)),
        ("own", 3): (("second", DOWN, 1),),
        ("swapped", 0): (("third", UP, 1),),
        ("other", 0): (("second", DOWN, 2), ("third", UP, 2)),
        ("other", 1): (("third", DOWN, 0),),
        ("other", 3): (("third", DOWN, 1),),
        ("feed", 0): (("third", DOWN, 2),),
    }
    END = {
        ("project", 1): (("second", UP, 0),),
        ("project", 3): (("second", UP, 1),),
        ("own", 0): (("second", DOWN, 0),),
        ("own", 1): (("third", UP, 0),),
        ("own", 2): (("third", UP, 1),),
        ("own", 3): (("z_step", UP, 2),),
        ("swapped", 0): (("z_step", UP, 3), ("third", DOWN, 0)),
        ("other", 0): (("second", UP, 2), ("z_step", DOWN, 1)),
        ("other", 1): (("second", UP, 3), ("z_step", DOWN, 2)),
        ("other", 2): (("second", DOWN, 1), ("third", UP, 2)),
        ("other", 3): (("z_step", DOWN, 3), ("second", DOWN, 2)),
        ("norm", 0): (("third", UP, 3),),
        ("feed", 0): (("second", DOWN, 3),),
        ("feed", 1): (("third", DOWN, 1),),
        ("feed", 3): (("third", DOWN, 2),),
        ("down", 0): (("third", DOWN, 3),),
    }

    def __init__(self, gather, swap, blocks_out, keep_sem):
        self.gather, self.swap = gather, swap
        z = gather.at.z
        self.at_end = (z == 0) | (z == 3)
        self.keep = [
            pltpu.make_async_copy(gather.blocks.at[kind], blocks_out.at[kind], keep_sem.at[kind]) for kind in range(3)
        ]

    def after(self, point, m=0):
        for table, here in ((self.MIDDLE, ~self.at_end), (self.END, self.at_end)):
            for (name, index), events in table.items():
                if name == point:

                    def act(events=events):
                        for step, *which in events:
                            getattr(self.gather, step)(*which)

                    pl.when(here if isinstance(m, int) else here & (m == index))(act)

    def before(self, point):
        if point == "project":
            self.gather.last(ATT)
            self.keep[ATT].start()
        if point == "other":
            self.swap.wait()
        if point == "feed":
            self.gather.last(UP)
            self.keep[UP].start()
        if point == "down":
            self.after("down")

    def order(self, step):
        return self.gather.order(step)

    def landed(self, kind, m):
        self.gather.plane_copy(kind, m, 4).wait_recv()

    def all_landed(self):
        self.keep[DOWN].start()

    def finish(self):
        for copy in self.keep:
            copy.wait()
        self.gather.drain()


N_KEPT = 16


def pack_weights(query, key, value, out_t, up, down_t):
    pair, single = 2 * HEAD_DIM, 3 * HEAD_DIM
    att = jnp.concatenate(
        [
            query[:, :pair], key[:, :pair], value[:, :pair],
            query[:, pair:single], key[:, pair:single],
            value[:, pair:single], out_t[:, pair:single], out_t[:, :pair],
        ],
        axis=1,
    )
    return att, up, down_t


def pack_biases(query_bias, value_bias, up_bias):
    def row(i, bias):
        return bias[i : i + 1, :]

    blank = jnp.zeros((1, HEAD_DIM), BF16)
    pieces = [
        row(0, query_bias), row(1, query_bias), blank, blank, row(0, value_bias), row(1, value_bias),
        row(2, query_bias), blank, row(2, value_bias), blank, blank, blank,
    ]
    ups = jnp.concatenate([row(i, up_bias) for i in range(6)], axis=1)
    return jnp.concatenate([jnp.concatenate(pieces, axis=1), ups, jnp.zeros((14, 768), BF16)], axis=0)


def fill_vectors(vec, vecs):
    for i, ref in enumerate(vecs):
        vec[i : i + 1, :] = ref[...].astype(F32).reshape(1, 768)


def transposed(block):
    wide = jnp.concatenate([block, jnp.zeros((block.shape[0], 128 - block.shape[1]), block.dtype)], axis=1)
    return wide.T[: block.shape[1]]


def forward_linked(*refs):
    (lengths, starts, frames, cot, query, key, value, out_w, up, down, query_bias, value_bias, up_bias) = refs[:13]
    vecs, refs = refs[13:20], refs[20:]
    blocks_hbm, probs_hbm, out_hbm, masked_hbm, *outs = refs[: 4 + N_KEPT]
    blocks, biases, xs, keybias, valid, vec, masked_ref, masked_sem, *scratch = refs[4 + N_KEPT :]
    scratch, links = scratch[:N_FORWARD_SCRATCH], scratch[N_FORWARD_SCRATCH:]
    z_send, z_recv, p_send, p_recv, x_send, x_recv, keep_sem = links
    at = Place()
    at.hello(False)
    at.meet(False)
    gather = Gather(at, blocks, biases, z_send, z_recv, p_send, p_recv)
    packs = pack_weights(
        query[...], key[...], value[...], transposed(out_w[...]), up[...], down[...]
    )
    for kind in range(3):
        blocks[kind, at.z, at.y, at.x, at.c] = packs[kind]
        if kind == 0:
            gather.z_step(ATT, 0)
            gather.first(ATT, at.z)
    biases[at.z] = pack_biases(query_bias[...], value_bias[...], up_bias[...])
    gather.z_step(3, 0)
    at_end = (at.z == 0) | (at.z == 3)

    @pl.when(at_end)
    def _():
        gather.z_step(UP, 0)
        gather.z_step(DOWN, 0)

    fill_vectors(vec, vecs)
    rows = frames.shape[0]
    clip, half = at.z // 2, lax.rem(at.z, 2)
    length = lengths[clip]
    start = starts[pl.ds(clip, 1), :]
    for side in range(2):
        first = rows * (half if side == 0 else 1 - half)
        slots = first + lax.broadcasted_iota(jnp.int32, (rows, start.shape[1]), 0)
        covered = jnp.where((slots >= start) & (slots < start + SPAN), 1.0, 0.0)
        masked_ref[side] = jnp.max(covered, axis=1, keepdims=True)
        slots = first + lax.broadcasted_iota(jnp.int32, (rows, 128), 0)
        lanes = lax.broadcasted_iota(jnp.int32, (rows, 128), 1)
        here = pl.ds(side * rows, rows)
        keybias[here, :] = jnp.where((slots >= length) & (lanes == 0), NEGATIVE, 0.0).astype(BF16)
        if side == 0:
            valid[...] = jnp.where(slots[:, 0:1] < length, 1.0, 0.0)
    masked_copy = pltpu.make_async_copy(masked_ref, masked_hbm, masked_sem)
    masked_copy.start()
    xs[0] = jnp.where(masked_ref[0] > 0, vec[6:7, :], frames[...].astype(F32)).astype(BF16)
    swap = remote(xs.at[0], xs.at[1], x_send, x_recv, at.mate)
    pl.when(at_end)(swap.start)
    gather.z_step(ATT, 1)
    gather.z_step(3, 1)
    gather.second(ATT, 0)
    gather.z_step(ATT, 2)
    gather.z_step(3, 2)

    @pl.when(~at_end)
    def _():
        gather.z_step(UP, 0)
        swap.start()

    gather.second(ATT, 1)
    gather.third(ATT, 0)
    gather.z_step(ATT, 3)
    gather.z_step(3, 3)
    gather.second(ATT, 2)
    gather.z_step(UP, 1)
    gather.third(ATT, 1)
    gather.second(ATT, 3)
    gather.first(UP, at.z)
    gather.third(ATT, 2)

    @pl.when(~at_end)
    def _():
        gather.z_step(UP, 2)
        gather.z_step(DOWN, 0)

    gather.first(DOWN, at.z)
    gather.third(ATT, 3)
    hooks = GatherHooks(gather, swap, blocks_hbm, keep_sem)
    forward_compute(blocks, biases, xs, keybias, valid, cot, vec, probs_hbm, out_hbm, outs, *scratch, hooks)
    masked_copy.wait()


def forward_alone(blocks_in, biases, xs, keybias, valid, cot, *refs):
    vecs, (probs_hbm, out_hbm, *outs), scratch = refs[:7], refs[7 : 9 + N_KEPT], refs[9 + N_KEPT :]
    blocks, vec, *scratch, keep_sem = scratch
    fill_vectors(vec, vecs)
    load = pltpu.make_async_copy(blocks_in, blocks, keep_sem)
    load.start()
    load.wait()
    forward_compute(
        blocks, biases, xs, keybias, valid, cot, vec, probs_hbm, out_hbm, outs, *scratch, NoHooks()
    )


BLOCKS = (3, 4, 2, 2, 2, 96, 768)


def forward_outs(rows):
    def of(shape, dtype):
        return jax.ShapeDtypeStruct(shape, dtype)

    return [
        of((12, 8, rows), F32),
        of((12, 2, 64, rows), F32),
        of((2, 768, rows), BF16),
        of((12, rows, 128), BF16),
        of((8, 128, LEN), BF16),
        of((8, LEN, 128), BF16),
        of((4, rows, 256), BF16),
        of((4, rows, 768), BF16),
        of((4, rows, 768), BF16),
        of((768, rows), BF16),
        of((rows, 768), F32),
        of((rows, 1), F32),
        of((rows, 768), BF16),
        of((768, rows), BF16),
        of((rows, 768), F32),
        of((8, 768), F32),
    ]


N_FORWARD_SCRATCH = 11


def forward_scratch(rows):
    return [
        [pltpu.VMEM(out.shape, out.dtype) for out in forward_outs(rows)],
        pltpu.SemaphoreType.DMA((N_KEPT,)),
        pltpu.VMEM((8, LEN, 128), BF16),
        pltpu.VMEM((8, 128, LEN), BF16),
        pltpu.VMEM((3, rows, rows), BF16),
        pltpu.SemaphoreType.DMA((3,)),
        pltpu.VMEM((rows, 768), F32),
        pltpu.VMEM((rows, 768), BF16),
        pltpu.VMEM((12, 8, rows), F32),
        pltpu.VMEM((rows, 768), BF16),
        pltpu.SemaphoreType.DMA((3,)),
    ]


def run_forward_linked(rows, *ins):
    outs = forward_outs(rows)
    probs = jax.ShapeDtypeStruct((12, LEN, rows), BF16)
    frames = jax.ShapeDtypeStruct((rows, 768), BF16)
    masked = jax.ShapeDtypeStruct((2, rows, 1), F32)
    blocks, probs, frames, masked, *kept = pl.pallas_call(
        forward_linked,
        name="forward",
        out_shape=[jax.ShapeDtypeStruct(BLOCKS, BF16), probs, frames, masked, *outs],
        in_specs=[pl.BlockSpec(memory_space=pltpu.SMEM)] + [vmem()] * 19,
        out_specs=[hbm()] * (4 + N_KEPT),
        scratch_shapes=[
            pltpu.VMEM(BLOCKS, BF16),
            pltpu.VMEM((4, 16, 768), BF16),
            pltpu.VMEM((2, rows, 768), BF16),
            pltpu.VMEM((LEN, 128), BF16),
            pltpu.VMEM((rows, 1), F32),
            pltpu.VMEM((8, 768), F32),
            pltpu.VMEM((2, rows, 1), F32),
            pltpu.SemaphoreType.DMA,
            *forward_scratch(rows),
            pltpu.SemaphoreType.DMA((4, 2, 3)),
            pltpu.SemaphoreType.DMA((4, 4)),
            pltpu.SemaphoreType.DMA((3, 4, 5)),
            pltpu.SemaphoreType.DMA((3, 4, 5)),
            pltpu.SemaphoreType.DMA,
            pltpu.SemaphoreType.DMA,
            pltpu.SemaphoreType.DMA((3,)),
        ],
        compiler_params=pltpu.CompilerParams(
            collective_id=0, has_side_effects=True, vmem_limit_bytes=VMEM_LIMIT
        ),
    )(*ins)
    return blocks, probs, frames, masked, kept


def run_forward_alone(rows, *ins):
    probs = jax.ShapeDtypeStruct((12, LEN, rows), BF16)
    frames = jax.ShapeDtypeStruct((rows, 768), BF16)
    probs, frames, *kept = pl.pallas_call(
        forward_alone,
        name="forward",
        out_shape=[probs, frames, *forward_outs(rows)],
        in_specs=[hbm()] + [vmem()] * 12,
        out_specs=[hbm()] * (2 + N_KEPT),
        scratch_shapes=[pltpu.VMEM(BLOCKS, BF16), pltpu.VMEM((8, 768), F32), *forward_scratch(rows), pltpu.SemaphoreType.DMA],
        compiler_params=pltpu.CompilerParams(vmem_limit_bytes=VMEM_LIMIT),
    )(*ins)
    return probs, frames, kept


ATT_ORDER = (0, 3, 1, 2)


def att_order(place):
    return jnp.where(place == 0, 0, jnp.where(place == 1, 3, place - 1))


def chunk_at(n):
    return (DOWN, n) if n < 4 else (UP, n - 4) if n < 8 else (ATT, ATT_ORDER[n - 8])


class Scatter:
    def __init__(self, at, grads, core_in, first_in, second_in, z_in, out, send, recv, z_send, z_recv):
        self.at, self.grads, self.out = at, grads, out
        self.core_in, self.first_in, self.second_in, self.z_in = core_in, first_in, second_in, z_in
        self.send, self.recv, self.z_send, self.z_recv = send, recv, z_send, z_recv

    def copy(self, kind, m, which):
        at, grads = self.at, self.grads.at[kind, m]
        x, y, c = at.x, at.y, at.c
        low, high = pl.ds(0, 48), pl.ds(48, 48)
        src, dst, device = {
            0: lambda: (grads.at[:, :, 1 - c], self.core_in.at[kind, m], at.core),
            1: lambda: (grads.at[:, 1 - x, c, low], self.first_in.at[kind, m, 0], at.across_x),
            2: lambda: (grads.at[1 - y, :, c, high], self.first_in.at[kind, m, 1], at.across_y),
            3: lambda: (grads.at[1 - y, x, c, low], self.second_in.at[kind, m, 0], at.across_y),
            4: lambda: (grads.at[y, 1 - x, c, high], self.second_in.at[kind, m, 1], at.across_x),
        }[which]()
        return remote(src, dst, self.send.at[kind, m, which], self.recv.at[kind, m, which], device)

    def add(self, ref, got):
        ref[...] = (ref[...].astype(F32) + got[...].astype(F32)).astype(BF16)

    def begin(self, kind, m):
        self.copy(kind, m, 0).start()

    def first(self, kind, m):
        at, grads = self.at, self.grads.at[kind, m]
        self.copy(kind, m, 0).wait_recv()
        for y in range(2):
            for x in range(2):
                self.add(grads.at[y, x, at.c], self.core_in.at[kind, m, y, x])
        self.copy(kind, m, 1).start()
        self.copy(kind, m, 2).start()

    def second(self, kind, m):
        at, grads = self.at, self.grads.at[kind, m]
        low, high = pl.ds(0, 48), pl.ds(48, 48)
        self.copy(kind, m, 1).wait_recv()
        for y in range(2):
            self.add(grads.at[y, at.x, at.c, low], self.first_in.at[kind, m, 0, y])
        self.copy(kind, m, 3).start()
        self.copy(kind, m, 2).wait_recv()
        for x in range(2):
            self.add(grads.at[at.y, x, at.c, high], self.first_in.at[kind, m, 1, x])
        self.copy(kind, m, 4).start()

    def third(self, kind, m):
        at = self.at
        grads = self.grads.at[kind, m, at.y, at.x, at.c]
        self.copy(kind, m, 3).wait_recv()
        self.add(grads.at[pl.ds(0, 48)], self.second_in.at[kind, m, 0])
        self.copy(kind, m, 4).wait_recv()
        self.add(grads.at[pl.ds(48, 48)], self.second_in.at[kind, m, 1])
        self.z_start(kind, m)

    def z_copy(self, kind, m, direction):
        at = self.at
        src = self.grads.at[kind, m, at.y, at.x, at.c]
        device = at.right if direction == 0 else at.left
        slot = m if direction == 0 else jnp.where(m == at.z - 1, 4, m)
        return remote(src, self.z_in.at[kind, slot], self.z_send.at[kind, m], self.z_recv.at[kind, slot], device)

    def z_landed(self, kind, m, slot, direction):
        at = self.at
        src = self.grads.at[kind, m, at.y, at.x, at.c]
        device = at.right if direction == 0 else at.left
        return remote(src, self.z_in.at[kind, slot], self.z_send.at[kind, m], self.z_recv.at[kind, slot], device)

    def relay(self, kind, m, direction):
        at = self.at
        self.z_landed(kind, m, m, direction).wait_recv()
        self.add(self.grads.at[kind, m, at.y, at.x, at.c], self.z_in.at[kind, m])
        self.z_copy(kind, m, direction).start()

    def z_start(self, kind, m):
        z = self.at.z
        if m > 0:
            pl.when(z == 0)(lambda: self.z_copy(kind, m, 0).start())
        if m < 3:
            pl.when(z == 3)(lambda: self.z_copy(kind, m, 1).start())

    def z_one(self, kind, m):
        z = self.at.z
        if m > 1:
            pl.when(z == 1)(lambda: self.relay(kind, m, 0))
        else:
            pl.when(z == 2)(lambda: self.relay(kind, m, 1))

    def z_two(self, kind, m):
        z = self.at.z
        if m == 3:
            pl.when(z == 2)(lambda: self.relay(kind, m, 0))
        if m == 0:
            pl.when(z == 1)(lambda: self.relay(kind, m, 1))

    def finish(self, kind):
        at, z = self.at, self.at.z
        self.out[kind] = self.grads[kind, z, at.y, at.x, at.c].astype(F32)

        @pl.when(z > 0)
        def _():
            self.z_landed(kind, z, z, 0).wait_recv()
            self.out[kind] += self.z_in[kind, z].astype(F32)

        @pl.when(z < 3)
        def _():
            self.z_landed(kind, z, 4, 1).wait_recv()
            self.out[kind] += self.z_in[kind, 4].astype(F32)

    def run(self, **steps):
        for name, places in steps.items():
            for n in places:
                getattr(self, name)(*chunk_at(n))

    def drain(self):
        z = self.at.z
        for kind in range(3):

            def of_index(m, _, kind=kind):
                for which in range(5):
                    self.copy(kind, m, which).wait_send()
                pl.when(m > z)(lambda: self.z_copy(kind, m, 0).wait_send())
                pl.when(m < z)(lambda: self.z_copy(kind, m, 1).wait_send())
                return 0

            lax.fori_loop(0, 4, of_index, 0)


class Totals:
    def __init__(self, at, rows, got, send, recv):
        self.rows, self.got, self.send, self.recv = rows, got, send, recv
        self.partners = (at.core, at.across_x, at.across_y, at.mate, at.far)

    def copy(self, stage):
        return remote(
            self.rows.at[stage], self.got.at[stage], self.send.at[stage], self.recv.at[stage], self.partners[stage]
        )

    def start(self, stage):
        self.copy(stage).start()

    def finish(self, stage):
        self.copy(stage).wait()
        self.rows[stage + 1] = self.rows[stage] + self.got[stage]


def backward_compute(
    blocks_hbm,
    probs_hbm,
    acted_hbm,
    slope_hbm,
    recip_hbm,
    headout_hbm,
    xt_hbm,
    qm_hbm,
    kt_hbm,
    v_hbm,
    att_hbm,
    n1t_hbm,
    n1_hbm,
    rs1_hbm,
    gb2_hbm,
    gb2t_hbm,
    g2_hbm,
    sums_hbm,
    masked_hbm,
    gain_ref,
    grads,
    rows_ref,
    weight,
    weight_sem,
    acts,
    acts_sem,
    probs,
    probs_sem,
    gb1,
    gb1t,
    grad_one,
    parts,
    g2_ref,
    state_sem,
    gb2_ref,
    gb2t_ref,
    n1t_ref,
    xt_ref,
    headout_ref,
    qm_ref,
    kt_ref,
    v_ref,
    att_ref,
    head_sem,
    own,
    sides,
    shifts,
    shares,
    recip_ref,
    rs1_ref,
    sums_ref,
    masked_ref,
    small_sem,
    hooks,
):
    rows = g2_ref.shape[0]
    g2_load = pltpu.make_async_copy(g2_hbm, g2_ref, state_sem.at[0])
    n1_load = pltpu.make_async_copy(n1_hbm, grad_one, state_sem.at[1])
    gb2_load = pltpu.make_async_copy(gb2_hbm, gb2_ref, state_sem.at[2])
    gb2t_load = pltpu.make_async_copy(gb2t_hbm, gb2t_ref, state_sem.at[3])
    n1t_load = pltpu.make_async_copy(n1t_hbm, n1t_ref, state_sem.at[4])
    xt_load = pltpu.make_async_copy(xt_hbm, xt_ref, state_sem.at[5])

    small_loads = [
        pltpu.make_async_copy(src, dst, small_sem.at[i])
        for i, (src, dst) in enumerate(
            ((recip_hbm, recip_ref), (rs1_hbm, rs1_ref), (sums_hbm, sums_ref), (masked_hbm, masked_ref))
        )
    ]

    def head_loads(m, slot, side):
        three, two, half = pl.ds(3 * m, 3), pl.ds(2 * m, 2), pl.ds(side * rows, rows)
        pairs = [
            (qm_hbm.at[three], qm_ref.at[slot]),
            (kt_hbm.at[two, :, half], kt_ref.at[slot]),
            (v_hbm.at[two, half], v_ref.at[slot]),
            (headout_hbm.at[three], headout_ref.at[slot]) if side else (att_hbm.at[m], att_ref.at[slot]),
        ]
        return [
            pltpu.make_async_copy(src, dst, head_sem.at[slot, i if i < 3 else 4 - side])
            for i, (src, dst) in enumerate(pairs)
        ]

    def weight_load(kind, m, slot):
        return pltpu.make_async_copy(blocks_hbm.at[kind, m], weight.at[slot], weight_sem.at[slot])

    def act_loads(m, slot):
        return (
            pltpu.make_async_copy(acted_hbm.at[m], acts.at[slot, 0], acts_sem.at[slot, 0]),
            pltpu.make_async_copy(slope_hbm.at[m], acts.at[slot, 1], acts_sem.at[slot, 1]),
        )

    def probs_loads(m, slot, side):
        half = pl.ds(side * rows, rows)
        return [
            pltpu.make_async_copy(probs_hbm.at[3 * m + j, half], probs.at[slot, j], probs_sem.at[slot, j])
            for j in range(3)
        ]

    def feed_loads(m, slot):
        return (weight_load(DOWN, m, 2 * slot), weight_load(UP, m, 2 * slot + 1), act_loads(m, slot)[1])

    def begin(copies):
        for copy in copies:
            copy.start()

    def finish(copies):
        for copy in copies:
            copy.wait()

    def block(slot, low=0, width=768):
        return weight[slot, :, :, :, :, pl.ds(low, width)].reshape(768, width)

    def put(kind, m, value, low=0):
        width = value.shape[1]
        grads[kind, m, :, :, :, :, pl.ds(low, width)] = value.astype(BF16).reshape(2, 2, 2, 96, width)

    begin((gb2t_load, act_loads(0, 0)[0], act_loads(1, 1)[0]))
    parts[...] = jnp.zeros_like(parts)
    hooks.after("start")
    finish((gb2t_load,))

    def feed_down(m, _):
        slot = lax.rem(m, 2)
        finish(act_loads(m, slot)[:1])
        put(DOWN, m, dot(gb2t_ref[...], acts[slot, 0]))
        hooks.ready(DOWN, m)
        pl.when(m < 2)(lambda: begin(act_loads(m + 2, slot)[:1]))

        @pl.when(m == 0)
        def _():
            begin((gb2_load, *feed_loads(0, 0)))
            begin((n1t_load, g2_load, n1_load, *small_loads, xt_load))
            begin(head_loads(0, 0, 1))
            begin(probs_loads(0, 0, 1))

        hooks.after("down", m)
        return 0

    lax.fori_loop(0, 4, feed_down, 0)
    finish((gb2_load, n1t_load, g2_load))

    def feed(m, _):
        slot = lax.rem(m, 2)
        pl.when(m < 3)(lambda: begin(feed_loads(m + 1, 1 - slot)))
        finish(feed_loads(m, slot))
        grad_acted = dot(gb2_ref[...], block(2 * slot))
        grad_pre = (grad_acted * acts[slot, 1].astype(F32)).astype(BF16)
        parts[m, 0:1, :] = jnp.sum(grad_pre.astype(F32), axis=0, keepdims=True)
        put(UP, m, dot(n1t_ref[...], grad_pre))
        g2_ref[...] += dot(grad_pre, block(2 * slot + 1), (1, 1))
        hooks.ready(UP, m)
        hooks.after("feed", m)
        return 0

    lax.fori_loop(0, 4, feed, 0)
    for m in range(4):
        weight_load(ATT, m, m).start()

    chunk = 64

    def norm_back(i, sums):
        r = pl.ds(pl.multiple_of(i * chunk, chunk), chunk)
        grad = g2_ref[r, :]
        unit = grad_one[r, :]
        scaled = grad * gain
        grad_in = (
            scaled
            - jnp.mean(scaled, axis=1, keepdims=True)
            - unit * jnp.mean(scaled * unit, axis=1, keepdims=True)
        ) * rs1_ref[r, :]
        grad_one[r, :] = grad_in
        gb1[r, :] = grad_in.astype(BF16)
        return (
            sums[0] + jnp.sum(grad_in, axis=0, keepdims=True),
            sums[1] + jnp.sum(grad * unit, axis=0, keepdims=True),
            sums[2] + jnp.sum(grad, axis=0, keepdims=True),
        )

    zero = jnp.zeros((1, 768), F32)
    finish((n1_load, xt_load))
    finish(small_loads)
    gain = gain_ref[...].astype(F32).reshape(1, 768)
    sums = lax.fori_loop(0, rows // chunk, norm_back, (zero, zero, zero))
    rows_ref[0, 0:1, :] = sums[0]
    rows_ref[0, 1:2, :] = sums_ref[0:1, :]
    rows_ref[0, 2:3, :] = sums[1]
    rows_ref[0, 3:4, :] = sums[2]
    rows_ref[0, 4:5, :] = sums_ref[1:2, :]
    rows_ref[0, 5:6, :] = sums_ref[2:3, :]
    gb1t[...] = gb1[...].T
    hooks.after("norm")
    g2_ref[...] = jnp.zeros_like(g2_ref)

    def wide(j, side):
        zeros = jnp.zeros((64, rows), BF16)
        return jnp.concatenate([zeros, side] if j == 1 else [side, zeros], axis=0)

    def half_back(slot, sides_here, shifts_here):
        grads_k, grads_v, grads_q = [], [], []
        wides = [wide(j, sides_here[j]) for j in range(3)]
        grad_weights = [dot(v_ref[slot, j // 2], wides[j]) for j in range(3)]
        for j in range(3):
            weights = probs[slot, j]
            grad_scores = (weights.astype(F32) * (grad_weights[j] - shifts_here[j])).astype(BF16)
            grads_v.append(dot(weights, wides[j].T))
            grads_k.append(dot(grad_scores, qm_ref[slot, j]))
            lane = 0 if j == 0 else 64
            grads_q.append(dot(kt_ref[slot, j // 2, lane : lane + 64, :], grad_scores))
        return [grads_k[0] + grads_k[1], grads_k[2]], [grads_v[0] + grads_v[1], grads_v[2]], grads_q

    def back_other(m, _):
        slot = lax.rem(m, 2)
        pl.when(m < 3)(lambda: begin([*head_loads(m + 1, 1 - slot, 1), *probs_loads(m + 1, 1 - slot, 1)]))
        pl.when(m == 3)(lambda: begin([*head_loads(0, 0, 0), *probs_loads(0, 0, 0)]))
        weight_load(ATT, m, m).wait()
        finish(head_loads(m, slot, 1))
        finish(probs_loads(m, slot, 1))
        grad_att_t = dot(gb1[...], block(m, 512, 256)).T
        others, shifts_here = [], []
        for j in range(3):
            head = 3 * m + j
            place = (128, 192, 64)[j]
            grad_att = grad_att_t[place : place + 64, :]
            factor_own, factor = recip_ref[head, 0:1, :], recip_ref[head, 1:2, :]
            own_side = (grad_att * factor_own).astype(BF16)
            others.append((grad_att * factor).astype(BF16))
            row_sum = jnp.sum(
                own_side.astype(F32) * headout_ref[slot, j, 0] + others[j].astype(F32) * headout_ref[slot, j, 1],
                axis=0,
                keepdims=True,
            )
            sides[head] = own_side
            shifts[head, 0:1, :] = row_sum * factor_own
            shifts_here.append(row_sum * factor)
        grads_k, grads_v, grads_q = half_back(slot, others, shifts_here)
        for j in range(3):
            shares[3 * m + j] = grads_q[j]
        tile = acts.at[m // 2, lax.rem(m, 2)]
        tile[:, 128:256] = grads_k[0].astype(BF16)
        tile[:, 256:384] = grads_v[0].astype(BF16)
        tile[:, 384:512] = grads_k[1].astype(BF16)
        tile[:, 512:640] = grads_v[1].astype(BF16)
        parts[4 + m, 0:1, 128:640] = jnp.sum(tile[:, 128:640].astype(F32), axis=0, keepdims=True)
        g2_ref[...] += dot(tile[:, 128:640], block(m, 128, 512), (1, 1))
        hooks.after("other", m)
        return 0

    lax.fori_loop(0, 4, back_other, 0)

    def fill_other(i, total):
        r = pl.ds(pl.multiple_of(i * chunk, chunk), chunk)
        other = g2_ref[r, :]
        gb1[r, :] = other.astype(BF16)
        return total + jnp.sum(other * masked_ref[1, r, :], axis=0, keepdims=True)

    fill = lax.fori_loop(0, rows // chunk, fill_other, zero)
    hooks.after("mate")

    def back_own(place, _):
        slot = lax.rem(place, 2)
        m = att_order(place)

        @pl.when(place < 3)
        def _():
            after = att_order(place + 1)
            begin([*head_loads(after, 1 - slot, 0), *probs_loads(after, 1 - slot, 0)])

        finish(head_loads(m, slot, 0))
        finish(probs_loads(m, slot, 0))
        grads_k, grads_v, grads_q = half_back(
            slot, [sides[3 * m + j] for j in range(3)], [shifts[3 * m + j, 0:1, :] for j in range(3)]
        )
        grads_q = [(grads_q[j] + shares[3 * m + j]) * SCALE for j in range(3)]
        single = jnp.concatenate([grads_q[2], jnp.zeros((64, rows), F32)], axis=0).T
        own[:, 0:128] = jnp.concatenate(grads_q[:2], axis=0).T.astype(BF16)
        own[:, 128:256] = grads_k[0].astype(BF16)
        own[:, 256:384] = grads_v[0].astype(BF16)
        own[:, 384:512] = (grads_k[1] + single).astype(BF16)
        own[:, 512:640] = grads_v[1].astype(BF16)
        parts[4 + m, 0:1, 0:PROJ] += jnp.sum(own[...].astype(F32), axis=0, keepdims=True)
        hooks.after("middle", place)
        other = acts[m // 2, lax.rem(m, 2), :, 128:640]
        grad_proj = dot(xt_ref[0], own[...])
        grad_other = dot(xt_ref[1], other)
        grad_out_w = dot(gb1t[...], att_ref[slot])
        put(ATT, m, grad_proj[:, :128], 0)
        put(ATT, m, grad_proj[:, 128:512] + grad_other[:, :384], 128)
        put(ATT, m, grad_proj[:, 512:] + grad_other[:, 384:] + grad_out_w[:, :128], 512)
        put(ATT, m, grad_out_w[:, 128:], 640)
        grad_one[...] += dot(own[...], block(m, 0, PROJ), (1, 1))
        hooks.ready(ATT, m)
        hooks.after("own", place)
        return 0

    lax.fori_loop(0, 4, back_own, 0)

    def fill_own(i, total):
        r = pl.ds(pl.multiple_of(i * chunk, chunk), chunk)
        return total + jnp.sum(grad_one[r, :] * masked_ref[0, r, :], axis=0, keepdims=True)

    rows_ref[0, 6:7, :] = lax.fori_loop(0, rows // chunk, fill_own, fill)
    rows_ref[0, 7:8, :] = zero
    for row in range(8):
        rows_ref[0, 8 + row : 9 + row, :] = parts[row, 0:1, :]


def finish_frames(grad_one, got, masked_ref, frames_ref):
    chunk = 64

    def body(i, _):
        r = pl.ds(pl.multiple_of(i * chunk, chunk), chunk)
        total = grad_one[r, :] + got[r, :].astype(F32)
        frames_ref[r, :] = jnp.where(masked_ref[0, r, :] > 0, 0.0, total).astype(BF16)
        return 0

    lax.fori_loop(0, grad_one.shape[0] // chunk, body, 0)


class NoScatter:
    def after(self, point, m=0):
        pass

    def ready(self, kind, m):
        pass


class ScatterHooks:
    PLAN = {
        ("down", 2): dict(first=(0,)),
        ("down", 3): dict(first=(1,)),
        ("feed", 0): dict(first=(2,)),
        ("feed", 1): dict(second=(0, 1), first=(3,)),
        ("feed", 3): dict(second=(2,), first=(4, 5), third=(0,)),
        ("norm", 0): dict(third=(1,)),
        ("other", 0): dict(second=(3,), first=(6,)),
        ("other", 1): dict(third=(2,), z_one=(0,)),
        ("other", 2): dict(second=(4,), first=(7,), z_one=(1,)),
        ("other", 3): dict(second=(5,), third=(3,), z_one=(2,), z_two=(0,)),
        ("mate", 0): dict(swap=(0,)),
        ("own", 0): dict(second=(6,), third=(4,), z_one=(3,)),
        ("middle", 1): dict(first=(8,), second=(7,), swap=(1,)),
        ("own", 1): dict(third=(5,), z_one=(4,), z_two=(3,)),
        ("middle", 2): dict(first=(9,), third=(6,), swap=(2,)),
        ("own", 2): dict(z_one=(5,)),
        ("middle", 3): dict(second=(8,), first=(10,), third=(7,), swap=(3,)),
        ("own", 3): dict(z_one=(6,), z_two=(4,)),
    }

    def __init__(self, at, scatter, swaps):
        self.at, self.scatter, self.swaps = at, scatter, swaps

    def ready(self, kind, m):
        self.scatter.begin(kind, m)

    def run(self, swap=(), **steps):
        self.scatter.run(**steps)
        for piece in swap:
            self.swaps[piece].start()

    def after(self, point, m=0):
        if point == "start":
            self.at.meet(True)
        for (name, index), steps in self.PLAN.items():
            if name == point:
                if isinstance(m, int):
                    self.run(**steps)
                else:
                    pl.when(m == index)(functools.partial(self.run, **steps))


N_BACKWARD_INS = 20
N_BACKWARD_SCRATCH = 33


def backward_linked(*refs):
    ins = refs[:N_BACKWARD_INS]
    out_ref, rows_out, frames_ref = refs[N_BACKWARD_INS : N_BACKWARD_INS + 3]
    scratch = refs[N_BACKWARD_INS + 3 :]
    scratch, links = scratch[:N_BACKWARD_SCRATCH], scratch[N_BACKWARD_SCRATCH:]
    grads, rows_ref, gb1, grad_one = scratch[0], scratch[1], scratch[8], scratch[10]
    core_in, first_in, second_in, z_in, rows_in, mate_in = links[:6]
    send, recv, z_send, z_recv, t_send, t_recv, m_send, m_recv = links[6:]
    at = Place()
    at.hello(True)
    scatter = Scatter(at, grads, core_in, first_in, second_in, z_in, out_ref, send, recv, z_send, z_recv)
    totals = Totals(at, rows_ref, rows_in, t_send, t_recv)
    piece = gb1.shape[0] // 4
    swaps = [
        remote(
            gb1.at[pl.ds(i * piece, piece)], mate_in.at[pl.ds(i * piece, piece)], m_send.at[i], m_recv.at[i], at.mate
        )
        for i in range(4)
    ]
    backward_compute(*ins, *scratch, ScatterHooks(at, scatter, swaps))
    totals.start(0)
    scatter.run(second=(9,), first=(11,))
    totals.finish(0)
    scatter.run(third=(8,), z_one=(7,))
    scatter.run(second=(10,))
    scatter.run(third=(9,), z_one=(8,), z_two=(7,))
    scatter.run(second=(11,))
    totals.start(1)
    scatter.run(third=(10,))
    scatter.run(z_one=(9,), z_two=(8,))
    scatter.run(third=(11,))
    totals.finish(1)
    totals.start(2)
    scatter.finish(DOWN)
    scatter.finish(UP)
    totals.finish(2)
    totals.start(3)
    scatter.run(z_one=(10, 11), z_two=(9,))
    totals.finish(3)
    totals.start(4)
    for swap in swaps:
        swap.wait()
    finish_frames(grad_one, mate_in, scratch[31], frames_ref)
    totals.finish(4)
    rows_out[...] = rows_ref[5]
    scatter.drain()
    scatter.finish(ATT)


def backward_alone(*refs):
    ins = refs[:N_BACKWARD_INS]
    grads_out, rows_out, mate_out, grad_one_out = refs[N_BACKWARD_INS : N_BACKWARD_INS + 4]
    scratch = refs[N_BACKWARD_INS + 4 :]
    *scratch, keep_sem = scratch
    grads, rows_ref, gb1, grad_one = scratch[0], scratch[1], scratch[8], scratch[10]
    backward_compute(*ins, *scratch, NoScatter())
    keep = pltpu.make_async_copy(grads, grads_out, keep_sem)
    keep.start()
    rows_out[...] = rows_ref[0]
    mate_out[...] = gb1[...]
    grad_one_out[...] = grad_one[...]
    keep.wait()


def backward_scratch(rows):
    return [
        pltpu.VMEM(BLOCKS, BF16),
        pltpu.VMEM((6, 16, 768), F32),
        pltpu.VMEM((4, *BLOCKS[2:]), BF16),
        pltpu.SemaphoreType.DMA((4,)),
        pltpu.VMEM((2, 2, rows, 768), BF16),
        pltpu.SemaphoreType.DMA((2, 2)),
        pltpu.VMEM((2, 3, rows, rows), BF16),
        pltpu.SemaphoreType.DMA((2, 3)),
        pltpu.VMEM((rows, 768), BF16),
        pltpu.VMEM((768, rows), BF16),
        pltpu.VMEM((rows, 768), F32),
        pltpu.VMEM((8, 8, 768), F32),
        pltpu.VMEM((rows, 768), F32),
        pltpu.SemaphoreType.DMA((6,)),
        pltpu.VMEM((rows, 768), BF16),
        pltpu.VMEM((768, rows), BF16),
        pltpu.VMEM((768, rows), BF16),
        pltpu.VMEM((2, 768, rows), BF16),
        pltpu.VMEM((2, 3, 2, 64, rows), F32),
        pltpu.VMEM((2, 3, rows, 128), BF16),
        pltpu.VMEM((2, 2, 128, rows), BF16),
        pltpu.VMEM((2, 2, rows, 128), BF16),
        pltpu.VMEM((2, rows, 256), BF16),
        pltpu.SemaphoreType.DMA((2, 5)),
        pltpu.VMEM((rows, PROJ), BF16),
        pltpu.VMEM((12, 64, rows), BF16),
        pltpu.VMEM((12, 8, rows), F32),
        pltpu.VMEM((12, 64, rows), F32),
        pltpu.VMEM((12, 8, rows), F32),
        pltpu.VMEM((rows, 1), F32),
        pltpu.VMEM((8, 768), F32),
        pltpu.VMEM((2, rows, 1), F32),
        pltpu.SemaphoreType.DMA((4,)),
    ]


def run_backward(linked, blocks, probs, kept, masked, gain):
    recip, headout, xt, qm, kt, v, att, acted, slope, n1t, n1, rs1, gb2, gb2t, g2, sums = kept
    rows = gb2.shape[0]
    ins = (
        blocks, probs, acted, slope, recip, headout, xt, qm, kt, v, att, n1t, n1, rs1, gb2, gb2t, g2, sums, masked, gain
    )
    in_specs = [vmem() if i == 19 else hbm() for i in range(20)]
    if linked:
        return pl.pallas_call(
            backward_linked,
            name="backward",
            out_shape=[
                jax.ShapeDtypeStruct((3, 96, 768), F32),
                jax.ShapeDtypeStruct((16, 768), F32),
                jax.ShapeDtypeStruct((rows, 768), BF16),
            ],
            in_specs=in_specs,
            out_specs=[vmem()] * 3,
            scratch_shapes=[
                *backward_scratch(rows),
                pltpu.VMEM((3, 4, 2, 2, 96, 768), BF16),
                pltpu.VMEM((3, 4, 2, 2, 48, 768), BF16),
                pltpu.VMEM((3, 4, 2, 48, 768), BF16),
                pltpu.VMEM((3, 5, 96, 768), BF16),
                pltpu.VMEM((5, 16, 768), F32),
                pltpu.VMEM((rows, 768), BF16),
                pltpu.SemaphoreType.DMA((3, 4, 5)),
                pltpu.SemaphoreType.DMA((3, 4, 5)),
                pltpu.SemaphoreType.DMA((3, 4)),
                pltpu.SemaphoreType.DMA((3, 5)),
                pltpu.SemaphoreType.DMA((5,)),
                pltpu.SemaphoreType.DMA((5,)),
                pltpu.SemaphoreType.DMA((4,)),
                pltpu.SemaphoreType.DMA((4,)),
            ],
            compiler_params=pltpu.CompilerParams(
                collective_id=1, has_side_effects=True, vmem_limit_bytes=VMEM_LIMIT
            ),
        )(*ins)
    return pl.pallas_call(
        backward_alone,
        name="backward",
        out_shape=[
            jax.ShapeDtypeStruct(BLOCKS, BF16),
            jax.ShapeDtypeStruct((16, 768), F32),
            jax.ShapeDtypeStruct((rows, 768), BF16),
            jax.ShapeDtypeStruct((rows, 768), F32),
        ],
        in_specs=in_specs,
        out_specs=[hbm()] + [vmem()] * 3,
        scratch_shapes=[*backward_scratch(rows), pltpu.SemaphoreType.DMA],
        compiler_params=pltpu.CompilerParams(vmem_limit_bytes=VMEM_LIMIT),
    )(*ins)


def finish_kernel(parts, grads, totals, out_in, frames_in, out, frames, *outs):
    n_dp, n_mp = parts
    query, key, value, out_w, up, down, query_bias, value_bias, up_bias, *vectors = outs
    out[...] = out_in[...]
    frames[...] = frames_in[...]
    att = grads[0]
    query[...] = jnp.concatenate([att[:, 0:128], att[:, 384:448]], axis=1)
    key[...] = jnp.concatenate([att[:, 128:256], att[:, 448:512]], axis=1)
    value[...] = jnp.concatenate([att[:, 256:384], att[:, 512:576]], axis=1)
    out_w[...] = jnp.concatenate([att[:, 640:768], att[:, 576:640]], axis=1).T
    up[...] = grads[1]
    down[...] = grads[2]
    dp, z = lax.axis_index("dp"), lax.axis_index("mp")
    rows = totals[...]
    row_at = lax.broadcasted_iota(jnp.int32, rows.shape, 0)

    def shifted(block, by):
        return pltpu.roll(block, lax.rem(768 - by, 768), 1)

    def row_of(index):
        return jnp.broadcast_to(jnp.sum(jnp.where(row_at == index, rows, 0.0), axis=0, keepdims=True), (8, 768))

    part = 768 // (n_dp * n_mp)
    mine = shifted(rows[0:8], (dp * n_mp + z) * part)
    for i, ref in enumerate(vectors):
        ref[...] = mine[i : i + 1, :part]
    step = HEAD_DIM // n_dp
    heads = shifted(row_of(12 + z), dp * step)
    for head, (q_lane, v_lane) in enumerate(((0, 256), (64, 320), (384, 512))):
        query_bias[head : head + 1, :] = heads[0:1, q_lane : q_lane + step]
        value_bias[head : head + 1, :] = heads[0:1, v_lane : v_lane + step]
    ups = shifted(row_of(8 + z), dp * 2 * step)
    for i in range(6):
        up_bias[i : i + 1, :] = ups[0:1, 128 * i : 128 * i + 2 * step]


def run_finish(n_dp, n_mp, grads, totals, out, frames):
    def of(shape, dtype=F32):
        return jax.ShapeDtypeStruct(shape, dtype)

    d, step, part = grads.shape[1], HEAD_DIM // n_dp, 768 // (n_dp * n_mp)
    *outs, = pl.pallas_call(
        functools.partial(finish_kernel, (n_dp, n_mp)),
        name="finish",
        out_shape=[
            of(out.shape, BF16), of(frames.shape, BF16), of((d, 192)), of((d, 192)), of((d, 192)), of((192, d)),
            of((d, 768)), of((d, 768)), of((3, step)), of((3, step)), of((6, 2 * step)), *[of((1, part))] * 7,
        ],
        in_specs=[vmem()] * 4,
        out_specs=[vmem()] * 18,
        compiler_params=pltpu.CompilerParams(vmem_limit_bytes=VMEM_LIMIT),
    )(grads, totals, out, frames)
    return (*outs[:7], outs[7].T, *outs[8:11], *(row.reshape(part) for row in outs[11:]))


def shards(
    linked,
    frames,
    lengths,
    span_starts,
    cotangent,
    query_weight,
    key_weight,
    value_weight,
    out_weight,
    up_weight,
    down_weight,
    query_bias,
    value_bias,
    up_bias,
    out_bias,
    down_bias,
    first_gain,
    first_shift,
    second_gain,
    second_shift,
    mask_vector,
):
    rows = frames.shape[0]
    n_dp = 768 // query_weight.shape[0]
    n_mp = 768 // query_weight.shape[1]
    vecs = (out_bias, down_bias, first_gain, first_shift, second_gain, second_shift, mask_vector)
    if linked:
        blocks, probs, out, masked, kept = run_forward_linked(
            rows, lengths, span_starts, frames, cotangent, query_weight, key_weight, value_weight, out_weight,
            up_weight, down_weight.T, query_bias, value_bias, up_bias, *vecs,
        )
        grads, totals, grad_frames = run_backward(True, blocks, probs, kept, masked, first_gain)
        return run_finish(n_dp, n_mp, grads, totals, out, grad_frames)
    z = lax.axis_index("mp")
    half = z % 2
    length = lax.dynamic_index_in_dim(lengths, z // 2, keepdims=False)
    starts = lax.dynamic_index_in_dim(span_starts, z // 2, keepdims=False)
    slots = (jnp.arange(LEN, dtype=jnp.int32) + half * rows) % LEN
    valid = slots < length
    masked = jnp.any((slots[:, None] >= starts[None, :]) & (slots[:, None] < starts[None, :] + SPAN), axis=1)
    keybias = jnp.where(
        (jnp.arange(128) == 0)[None, :] & ~valid[:, None], jnp.float32(NEGATIVE), 0.0
    ).astype(BF16)
    valid_rows = valid[:rows].astype(F32)[:, None]
    masked_rows = masked.astype(F32).reshape(2, rows, 1)
    x = jnp.where(masked[:rows, None], mask_vector[None, :], frames)
    pack = jnp.stack(pack_weights(query_weight, key_weight, value_weight, out_weight.T, up_weight, down_weight.T))
    bias = pack_biases(query_bias, value_bias, up_bias)
    mates = [(0, 1), (1, 0), (2, 3), (3, 2)]
    blocks = lax.all_gather(lax.all_gather(pack, "dp", axis=1, tiled=True), "mp", axis=1).reshape(BLOCKS)
    biases = lax.all_gather(bias, "mp", axis=0)
    both = jnp.stack([x, lax.ppermute(x, "mp", mates)])
    probs, out, kept = run_forward_alone(rows, blocks, biases, both, keybias, valid_rows, cotangent, *vecs)
    grads, totals, mate, grad_one = run_backward(False, blocks, probs, kept, masked_rows, first_gain)
    grads = grads.reshape(3, 4, 768, 768).astype(F32)
    grads = lax.psum_scatter(grads, "mp", scatter_dimension=1, tiled=False)
    grads = lax.psum_scatter(grads, "dp", scatter_dimension=1, tiled=True)
    totals = lax.psum(totals, ("dp", "mp"))
    grad_frames = grad_one + lax.ppermute(mate, "mp", mates).astype(F32)
    grad_frames = jnp.where(masked[:rows, None], 0.0, grad_frames).astype(BF16)
    return run_finish(n_dp, n_mp, grads, totals, out, grad_frames)


def solution(mesh):
    linked = mesh.shape["dp"] == 8 and mesh.shape["mp"] == 4
    split = P(("dp", "mp"))
    return jax.shard_map(
        functools.partial(shards, linked),
        mesh=mesh,
        in_specs=(
            P(("dp", "mp"), None),
            P("dp"),
            P("dp", None),
            P(("dp", "mp"), None),
            P("dp", "mp"),
            P("dp", "mp"),
            P("dp", "mp"),
            P("mp", "dp"),
            P("dp", "mp"),
            P("mp", "dp"),
            P("mp", None),
            P("mp", None),
            P("mp", None),
            *([P()] * 7),
        ),
        out_specs=(
            P(("dp", "mp"), None),
            P(("dp", "mp"), None),
            P("dp", "mp"),
            P("dp", "mp"),
            P("dp", "mp"),
            P("mp", "dp"),
            P("dp", "mp"),
            P("mp", "dp"),
            P("mp", "dp"),
            P("mp", "dp"),
            P("mp", "dp"),
            *([split] * 7),
        ),
        check_vma=False,
    )
```

```python
import functools
import math

import jax
import jax.numpy as jnp
from jax import lax
from jax.experimental import pallas as pl
from jax.experimental.pallas import tpu as pltpu
from jax.sharding import PartitionSpec as P

HEAD_DIM = 64
SPAN = 10
LEN = 1024
EPSILON = 1e-05
NEGATIVE = -1e30
SCALE = 1.0 / math.sqrt(HEAD_DIM)

F32 = jnp.float32
BF16 = jnp.bfloat16
MESH = pl.DeviceIdType.MESH
VMEM_LIMIT = 63 * 1024 * 1024

ATT, UP, DOWN = 0, 1, 2
PROJ = 640


def dot(left, right, contract=(1, 0)):
    return lax.dot_general(
        left, right, (((contract[0],), (contract[1],)), ((), ())), preferred_element_type=F32
    )


def hbm():
    return pl.BlockSpec(memory_space=pl.ANY)


def vmem():
    return pl.BlockSpec(memory_space=pltpu.VMEM)


class Place:
    def __init__(self):
        self.dp = lax.axis_index("dp")
        self.z = lax.axis_index("mp")
        self.c = lax.rem(self.dp, 2)
        self.x = lax.rem(self.dp // 2, 2)
        self.y = self.dp // 4
        self.core = (self.dp + 1 - 2 * self.c, self.z)
        self.across_x = (self.dp + 2 - 4 * self.x, self.z)
        self.across_y = (self.dp + 4 - 8 * self.y, self.z)
        self.right = (self.dp, self.z + 1)
        self.left = (self.dp, self.z - 1)
        self.mate = (self.dp, self.z + 1 - 2 * lax.rem(self.z, 2))
        self.far = (self.dp, lax.rem(self.z + 2, 4))

    def hello(self, far):
        barrier = pltpu.get_barrier_semaphore()

        def signal(device):
            pl.semaphore_signal(barrier, inc=1, device_id=device, device_id_type=MESH)

        signal(self.core)
        signal(self.across_x)
        signal(self.across_y)
        if far:
            signal(self.far)
        pl.when(self.z < 3)(lambda: signal(self.right))
        pl.when(self.z > 0)(lambda: signal(self.left))

    def meet(self, far):
        ends = jnp.where((self.z == 0) | (self.z == 3), 1, 2)
        pl.semaphore_wait(pltpu.get_barrier_semaphore(), (4 if far else 3) + ends)


def remote(src, dst, send, recv, device):
    return pltpu.make_async_remote_copy(
        src_ref=src, dst_ref=dst, send_sem=send, recv_sem=recv, device_id=device, device_id_type=MESH
    )


class Gather:
    def __init__(self, at, blocks, biases, z_send, z_recv, p_send, p_recv):
        self.at, self.blocks, self.biases = at, blocks, biases
        self.z_send, self.z_recv, self.p_send, self.p_recv = z_send, z_recv, p_send, p_recv

    def z_copy(self, kind, m, direction, step):
        at = self.at
        if kind == 3:
            ref = self.biases.at[m]
        else:
            ref = self.blocks.at[kind, m, at.y, at.x, at.c]
        device = at.right if direction == 0 else at.left
        return remote(ref, ref, self.z_send.at[kind, direction, step], self.z_recv.at[kind, m], device)

    def z_step(self, kind, step):
        z = self.at.z
        if step == 0:
            pl.when((z > 0) & (z < 2))(lambda: self.z_copy(kind, z, 1, 0).start())
            pl.when(z < 3)(lambda: self.z_copy(kind, z, 0, 0).start())
            pl.when(z >= 2)(lambda: self.z_copy(kind, z, 1, 0).start())
            return

        def from_left():
            @pl.when(z >= step)
            def _():
                self.z_copy(kind, z - step, 0, 0).wait_recv()
                if step < 3:
                    pl.when(z < 3)(lambda: self.z_copy(kind, z - step, 0, step).start())
                self.first(kind, z - step)

        def from_right():
            @pl.when(z + step <= 3)
            def _():
                self.z_copy(kind, z + step, 1, 0).wait_recv()
                if step < 3:
                    pl.when(z > 0)(lambda: self.z_copy(kind, z + step, 1, step).start())
                self.first(kind, z + step)

        pl.when(z < 2)(from_right)
        from_left()
        pl.when(z >= 2)(from_right)

    def plane_copy(self, kind, m, which):
        at, block = self.at, self.blocks.at[kind, m]
        x, y, c = at.x, at.y, at.c
        low, high = pl.ds(0, 48), pl.ds(48, 48)
        ref, device = {
            0: lambda: (block.at[y, x, c, low], at.across_x),
            1: lambda: (block.at[y, x, c, high], at.across_y),
            2: lambda: (block.at[y, :, c, low], at.across_y),
            3: lambda: (block.at[:, x, c, high], at.across_x),
            4: lambda: (block.at[:, :, c], at.core),
        }[which]()
        return remote(ref, ref, self.p_send.at[kind, m, which], self.p_recv.at[kind, m, which], device)

    def at_step(self, step, act):
        z = self.at.z
        if step == 0:
            act(z)
            return
        pl.when(z >= step)(lambda: act(z - step))
        pl.when(z + step <= 3)(lambda: act(z + step))

    def order(self, step):
        z = self.at.z
        from_low = jnp.where(z == 1, jnp.where(step < 2, 1 - step, step), step)
        mirrored = 3 - z
        from_high = jnp.where(mirrored == 1, jnp.where(step < 2, 1 - step, step), step)
        return jnp.where(z < 2, from_low, 3 - from_high)

    def first(self, kind, m):
        if kind < 3:
            self.plane_copy(kind, m, 0).start()
            self.plane_copy(kind, m, 1).start()

    def second(self, kind, step):
        def act(m):
            self.plane_copy(kind, m, 0).wait_recv()
            self.plane_copy(kind, m, 2).start()
            self.plane_copy(kind, m, 1).wait_recv()
            self.plane_copy(kind, m, 3).start()

        self.at_step(step, act)

    def third(self, kind, step):
        def act(m):
            self.plane_copy(kind, m, 2).wait_recv()
            self.plane_copy(kind, m, 3).wait_recv()
            self.plane_copy(kind, m, 4).start()

        self.at_step(step, act)

    def last(self, kind):
        for m in range(4):
            self.plane_copy(kind, m, 4).wait_recv()

    def drain(self):
        z = self.at.z
        for kind in range(4):
            for step in range(3):
                pl.when((z < 3) & (z >= step))(
                    lambda k=kind, s=step: self.z_copy(k, z - s, 0, s).wait_send()
                )
                pl.when((z > 0) & (z + step <= 3))(
                    lambda k=kind, s=step: self.z_copy(k, z + s, 1, s).wait_send()
                )
        for kind in range(3):
            for m in range(4):
                for which in range(5):
                    self.plane_copy(kind, m, which).wait_send()


def block_of(blocks, kind, m, low=0, width=768):
    return blocks[kind, m, :, :, :, :, pl.ds(low, width)].reshape(768, width)


def lane_mask(rows, lower):
    lanes = lax.broadcasted_iota(jnp.int32, (rows, 128), 1)
    return (lanes < 64) if lower else (lanes >= 64)


def forward_compute(
    blocks,
    biases,
    xs,
    keybias_ref,
    valid_ref,
    cot_ref,
    vec_ref,
    probs_hbm,
    out_hbm,
    outs_hbm,
    outs_ref,
    outs_sem,
    k_ref,
    vt_ref,
    probs,
    probs_sem,
    total,
    low,
    stats,
    out_ref,
    out_sem,
    hooks,
):
    rows = xs.shape[1]
    (recip_ref, headout_ref, xt_ref, qm_ref, kt_ref, v_ref, att_ref, acted_ref, slope_ref, n1t_ref, n1_ref, rs1_ref,
     gb2_ref, gb2t_ref, g2_ref, sums_ref) = outs_ref
    keeps = [
        pltpu.make_async_copy(ref, to, outs_sem.at[i]) for i, (ref, to) in enumerate(zip(outs_ref, outs_hbm, strict=True))
    ]

    def keep(*which):
        for i in which:
            keeps[i].start()

    xt_ref[0] = xs[0].T
    ones_lane = jnp.where(lax.broadcasted_iota(jnp.int32, (rows, 128), 1) == 0, 1.0, 0.0).astype(BF16)

    def probs_copy(head, side, slot):
        return pltpu.make_async_copy(
            probs.at[slot], probs_hbm.at[head, pl.ds(side * rows, rows)], probs_sem.at[slot]
        )

    own_rows, other_rows = pl.ds(0, rows), pl.ds(rows, rows)

    def project(m, _):
        bias = biases[m, 0:1, :].astype(F32)[:, :PROJ]
        own = dot(xs[0], block_of(blocks, ATT, m, 0, PROJ)) + bias
        k_ref[2 * m, own_rows] = own[:, 128:256].astype(BF16)
        v_ref[2 * m, own_rows] = own[:, 256:384].astype(BF16)
        k_ref[2 * m + 1, own_rows] = own[:, 384:512].astype(BF16)
        v_ref[2 * m + 1, own_rows] = own[:, 512:640].astype(BF16)
        lower, upper = lane_mask(rows, True), lane_mask(rows, False)
        pair = own[:, 0:128].astype(BF16).astype(F32) * SCALE
        single = pltpu.roll(own[:, 384:512].astype(BF16).astype(F32) * SCALE, 64, 1)
        qm_ref[3 * m] = jnp.where(lower, pair, 0.0).astype(BF16)
        qm_ref[3 * m + 1] = jnp.where(upper, pair, 0.0).astype(BF16)
        qm_ref[3 * m + 2] = jnp.where(upper, single, 0.0).astype(BF16)
        for tile in range(2):
            kt_ref[2 * m + tile, :, own_rows] = k_ref[2 * m + tile, own_rows].T
            vt_ref[2 * m + tile, :, own_rows] = v_ref[2 * m + tile, own_rows].T
        hooks.after("project", m)
        return 0

    def project_other(m, _):
        bias = biases[m, 0:1, :].astype(F32)[:, 128:PROJ]
        other = dot(xs[1], block_of(blocks, ATT, m, 128, 512)) + bias
        k_ref[2 * m, other_rows] = other[:, 0:128].astype(BF16)
        v_ref[2 * m, other_rows] = other[:, 128:256].astype(BF16)
        k_ref[2 * m + 1, other_rows] = other[:, 256:384].astype(BF16)
        v_ref[2 * m + 1, other_rows] = other[:, 384:512].astype(BF16)
        for tile in range(2):
            kt_ref[2 * m + tile, :, other_rows] = k_ref[2 * m + tile, other_rows].T
            vt_ref[2 * m + tile, :, other_rows] = v_ref[2 * m + tile, other_rows].T
        return 0

    def attend_half(m, side):
        half = own_rows if side == 0 else other_rows

        def free():
            for j in range(3):
                probs_copy(3 * m + j, side, j).wait()

        if side == 0:
            pl.when(m > 0)(free)
        else:
            free()
        scores, tops, sums, outs = [], [], [], []
        for j in range(3):
            keys = jnp.concatenate([k_ref[2 * m + j // 2, half], keybias_ref[half, :]], axis=1)
            queries = jnp.concatenate([qm_ref[3 * m + j], ones_lane], axis=1)
            scores.append(dot(keys, queries, (1, 1)))
        for j in range(3):
            top = jnp.max(scores[j], axis=0, keepdims=True)
            weights = jnp.exp(scores[j] - top)
            tops.append(top)
            sums.append(jnp.sum(weights, axis=0, keepdims=True))
            probs[j] = weights.astype(BF16)
            lane = 64 * (j % 2)
            outs.append(dot(vt_ref[2 * m + j // 2, lane : lane + 64, half], probs[j]))
            headout_ref[3 * m + j, side] = outs[j]
        return tops, sums, outs

    def send_probs(m, side):
        for j in range(3):
            probs_copy(3 * m + j, side, j).start()

    def attend_own(m, _):
        tops, sums, _ = attend_half(m, 0)
        for j in range(3):
            stats[3 * m + j, 0:1, :] = tops[j]
            stats[3 * m + j, 1:2, :] = sums[j]
        send_probs(m, 0)
        hooks.after("own", m)
        return 0

    def attend(m, _):
        tops, sums, outs = attend_half(m, 1)
        pieces = [jnp.zeros((64, rows), BF16), None, None, None]
        for j in range(3):
            head = 3 * m + j
            top_own = stats[head, 0:1, :]
            top_all = jnp.maximum(tops[j], top_own)
            factor, factor_own = jnp.exp(tops[j] - top_all), jnp.exp(top_own - top_all)
            recip = 1.0 / (factor_own * stats[head, 1:2, :] + factor * sums[j])
            factor, factor_own = factor * recip, factor_own * recip
            recip_ref[head] = jnp.concatenate([factor_own, factor, jnp.zeros((6, rows), F32)], axis=0)
            pieces[(2, 3, 1)[j]] = (headout_ref[head, 0] * factor_own + outs[j] * factor).astype(BF16)
        att_ref[m] = jnp.concatenate(pieces, axis=0).T
        send_probs(m, 1)
        hooks.after("other", m)
        return 0

    hooks.before("project")
    lax.fori_loop(0, 4, project, 0)
    lax.fori_loop(0, 4, attend_own, 0)
    hooks.before("other")
    xt_ref[1] = xs[1].T
    lax.fori_loop(0, 4, project_other, 0)
    keep(2, 3, 4, 5)
    hooks.after("swapped")
    lax.fori_loop(0, 4, attend, 0)
    keep(0, 1, 6)
    branch = [dot(att_ref[m], block_of(blocks, ATT, m, 512, 256), (1, 1)) for m in range(4)]
    total[...] = (branch[0] + branch[1]) + (branch[2] + branch[3])
    for j in range(3):
        probs_copy(9 + j, 1, j).wait()

    chunk = 64

    def norm_one(i, _):
        r = pl.ds(pl.multiple_of(i * chunk, chunk), chunk)
        resid = xs[0, r, :].astype(F32) + total[r, :] + vec_ref[0:1, :]
        centered = resid - jnp.mean(resid, axis=1, keepdims=True)
        rstd = lax.rsqrt(jnp.mean(centered * centered, axis=1, keepdims=True) + EPSILON)
        unit = centered * rstd
        n1_ref[r, :] = unit
        rs1_ref[r, :] = rstd
        low[r, :] = (unit * vec_ref[2:3, :] + vec_ref[3:4, :]).astype(BF16)
        return 0

    lax.fori_loop(0, rows // chunk, norm_one, 0, unroll=2)
    n1t_ref[...] = low[...].T
    keep(9, 10, 11)
    hooks.after("norm")
    hooks.before("feed")

    def feed(m, _):
        pre = dot(low[...], block_of(blocks, UP, m)) + biases[m, 1:2, :].astype(F32)
        phi = 0.5 * (1.0 + lax.erf(pre * (1.0 / math.sqrt(2.0))))
        acted_ref[m] = (pre * phi).astype(BF16)
        slope_ref[m] = (phi + pre * jnp.exp(-0.5 * pre * pre) * (1.0 / math.sqrt(2.0 * math.pi))).astype(BF16)
        hooks.after("feed", m)
        return 0

    lax.fori_loop(0, 4, feed, 0)
    keep(7, 8)
    hooks.before("down")

    def down(steps):
        places = [hooks.order(step) for step in steps]
        for m in places:
            hooks.landed(DOWN, m)
        shares = [dot(acted_ref[m], block_of(blocks, DOWN, m), (1, 1)) for m in places]
        return functools.reduce(jnp.add, shares)

    total[...] = down((0, 1, 2))
    total[...] += down((3,))
    hooks.all_landed()

    def norm_two(i, sums):
        r = pl.ds(pl.multiple_of(i * chunk, chunk), chunk)
        normed = n1_ref[r, :] * vec_ref[2:3, :] + vec_ref[3:4, :]
        resid = normed + total[r, :] + vec_ref[1:2, :]
        centered = resid - jnp.mean(resid, axis=1, keepdims=True)
        rstd = lax.rsqrt(jnp.mean(centered * centered, axis=1, keepdims=True) + EPSILON)
        unit = centered * rstd
        valid = valid_ref[r, :]
        out_ref[r, :] = (valid * (unit * vec_ref[4:5, :] + vec_ref[5:6, :])).astype(BF16)
        grad = valid * cot_ref[r, :].astype(F32)
        scaled = grad * vec_ref[4:5, :]
        grad_in = (
            scaled
            - jnp.mean(scaled, axis=1, keepdims=True)
            - unit * jnp.mean(scaled * unit, axis=1, keepdims=True)
        ) * rstd
        g2_ref[r, :] = grad_in
        gb2_ref[r, :] = grad_in.astype(BF16)
        for i, (ref, to) in enumerate(((out_ref, out_hbm), (g2_ref, outs_hbm[14]), (gb2_ref, outs_hbm[12]))):
            pltpu.make_async_copy(ref.at[r], to.at[r], out_sem.at[i]).start()
        return (
            sums[0] + jnp.sum(grad_in, axis=0, keepdims=True),
            sums[1] + jnp.sum(grad * unit, axis=0, keepdims=True),
            sums[2] + jnp.sum(grad, axis=0, keepdims=True),
        )

    zero = jnp.zeros((1, 768), F32)
    sums = lax.fori_loop(0, rows // chunk, norm_two, (zero, zero, zero), unroll=2)
    sums_ref[...] = jnp.concatenate([*sums, jnp.zeros((5, 768), F32)], axis=0)
    keep(15)
    gb2t_ref[...] = gb2_ref[...].T
    keep(13)
    hooks.finish()
    for i, copy in enumerate(keeps):
        if i not in (12, 14):
            copy.wait()
    for i, (ref, to) in enumerate(((out_ref, out_hbm), (g2_ref, outs_hbm[14]), (gb2_ref, outs_hbm[12]))):
        pltpu.make_async_copy(ref, to, out_sem.at[i]).wait()


class NoHooks:
    def after(self, point, m=0):
        pass

    def before(self, point):
        pass

    def order(self, step):
        return step

    def landed(self, kind, m):
        pass

    def all_landed(self):
        pass

    def finish(self):
        pass


class GatherHooks:
    MIDDLE = {
        ("project", 1): (("z_step", DOWN, 1),),
        ("project", 3): (("second", UP, 0), ("second", UP, 1)),
        ("own", 0): (("second", UP, 2),),
        ("own", 1): (("z_step", DOWN, 2), ("second", DOWN, 0), ("third", UP, 0)),
        ("own", 3): (("second", DOWN, 1),),
        ("swapped", 0): (("third", UP, 1),),
        ("other", 0): (("second", DOWN, 2), ("third", UP, 2)),
        ("other", 1): (("third", DOWN, 0),),
        ("other", 3): (("third", DOWN, 1),),
        ("feed", 0): (("third", DOWN, 2),),
    }
    END = {
        ("project", 1): (("second", UP, 0),),
        ("project", 3): (("second", UP, 1),),
        ("own", 0): (("second", DOWN, 0),),
        ("own", 1): (("third", UP, 0),),
        ("own", 2): (("third", UP, 1),),
        ("own", 3): (("z_step", UP, 2),),
        ("swapped", 0): (("z_step", UP, 3), ("third", DOWN, 0)),
        ("other", 0): (("second", UP, 2), ("z_step", DOWN, 1)),
        ("other", 1): (("second", UP, 3), ("z_step", DOWN, 2)),
        ("other", 2): (("second", DOWN, 1), ("third", UP, 2)),
        ("other", 3): (("z_step", DOWN, 3), ("second", DOWN, 2)),
        ("norm", 0): (("third", UP, 3),),
        ("feed", 0): (("second", DOWN, 3),),
        ("feed", 1): (("third", DOWN, 1),),
        ("feed", 3): (("third", DOWN, 2),),
        ("down", 0): (("third", DOWN, 3),),
    }

    def __init__(self, gather, swap, blocks_out, keep_sem):
        self.gather, self.swap = gather, swap
        z = gather.at.z
        self.at_end = (z == 0) | (z == 3)
        self.keep = [
            pltpu.make_async_copy(gather.blocks.at[kind], blocks_out.at[kind], keep_sem.at[kind]) for kind in range(3)
        ]

    def after(self, point, m=0):
        for table, here in ((self.MIDDLE, ~self.at_end), (self.END, self.at_end)):
            for (name, index), events in table.items():
                if name == point:

                    def act(events=events):
                        for step, *which in events:
                            getattr(self.gather, step)(*which)

                    pl.when(here if isinstance(m, int) else here & (m == index))(act)

    def before(self, point):
        if point == "project":
            self.gather.last(ATT)
            self.keep[ATT].start()
        if point == "other":
            self.swap.wait()
        if point == "feed":
            self.gather.last(UP)
            self.keep[UP].start()
        if point == "down":
            self.after("down")

    def order(self, step):
        return self.gather.order(step)

    def landed(self, kind, m):
        self.gather.plane_copy(kind, m, 4).wait_recv()

    def all_landed(self):
        self.keep[DOWN].start()

    def finish(self):
        for copy in self.keep:
            copy.wait()
        self.gather.drain()


N_KEPT = 16


def pack_weights(query, key, value, out_t, up, down_t):
    pair, single = 2 * HEAD_DIM, 3 * HEAD_DIM
    att = jnp.concatenate(
        [
            query[:, :pair], key[:, :pair], value[:, :pair],
            query[:, pair:single], key[:, pair:single],
            value[:, pair:single], out_t[:, pair:single], out_t[:, :pair],
        ],
        axis=1,
    )
    return att, up, down_t


def pack_biases(query_bias, value_bias, up_bias):
    def row(i, bias):
        return bias[i : i + 1, :]

    blank = jnp.zeros((1, HEAD_DIM), BF16)
    pieces = [
        row(0, query_bias), row(1, query_bias), blank, blank, row(0, value_bias), row(1, value_bias),
        row(2, query_bias), blank, row(2, value_bias), blank, blank, blank,
    ]
    ups = jnp.concatenate([row(i, up_bias) for i in range(6)], axis=1)
    return jnp.concatenate([jnp.concatenate(pieces, axis=1), ups, jnp.zeros((14, 768), BF16)], axis=0)


def fill_vectors(vec, vecs):
    for i, ref in enumerate(vecs):
        vec[i : i + 1, :] = ref[...].astype(F32).reshape(1, 768)


def transposed(block):
    wide = jnp.concatenate([block, jnp.zeros((block.shape[0], 128 - block.shape[1]), block.dtype)], axis=1)
    return wide.T[: block.shape[1]]


def forward_linked(*refs):
    (lengths, starts, frames, cot, query, key, value, out_w, up, down, query_bias, value_bias, up_bias) = refs[:13]
    vecs, refs = refs[13:20], refs[20:]
    blocks_hbm, probs_hbm, out_hbm, masked_hbm, *outs = refs[: 4 + N_KEPT]
    blocks, biases, xs, keybias, valid, vec, masked_ref, masked_sem, *scratch = refs[4 + N_KEPT :]
    scratch, links = scratch[:N_FORWARD_SCRATCH], scratch[N_FORWARD_SCRATCH:]
    z_send, z_recv, p_send, p_recv, x_send, x_recv, keep_sem = links
    at = Place()
    at.hello(False)
    at.meet(False)
    gather = Gather(at, blocks, biases, z_send, z_recv, p_send, p_recv)
    packs = pack_weights(
        query[...], key[...], value[...], transposed(out_w[...]), up[...], down[...]
    )
    for kind in range(3):
        blocks[kind, at.z, at.y, at.x, at.c] = packs[kind]
        if kind == 0:
            gather.z_step(ATT, 0)
        gather.first(kind, at.z)
    biases[at.z] = pack_biases(query_bias[...], value_bias[...], up_bias[...])
    gather.z_step(3, 0)
    at_end = (at.z == 0) | (at.z == 3)

    @pl.when(at_end)
    def _():
        gather.z_step(UP, 0)
        gather.z_step(DOWN, 0)

    fill_vectors(vec, vecs)
    rows = frames.shape[0]
    clip, half = at.z // 2, lax.rem(at.z, 2)
    length = lengths[clip]
    start = starts[pl.ds(clip, 1), :]
    for side in range(2):
        first = rows * (half if side == 0 else 1 - half)
        slots = first + lax.broadcasted_iota(jnp.int32, (rows, start.shape[1]), 0)
        covered = jnp.where((slots >= start) & (slots < start + SPAN), 1.0, 0.0)
        masked_ref[side] = jnp.max(covered, axis=1, keepdims=True)
        slots = first + lax.broadcasted_iota(jnp.int32, (rows, 128), 0)
        lanes = lax.broadcasted_iota(jnp.int32, (rows, 128), 1)
        here = pl.ds(side * rows, rows)
        keybias[here, :] = jnp.where((slots >= length) & (lanes == 0), NEGATIVE, 0.0).astype(BF16)
        if side == 0:
            valid[...] = jnp.where(slots[:, 0:1] < length, 1.0, 0.0)
    masked_copy = pltpu.make_async_copy(masked_ref, masked_hbm, masked_sem)
    masked_copy.start()
    xs[0] = jnp.where(masked_ref[0] > 0, vec[6:7, :], frames[...].astype(F32)).astype(BF16)
    swap = remote(xs.at[0], xs.at[1], x_send, x_recv, at.mate)
    pl.when(at_end)(swap.start)
    gather.z_step(ATT, 1)
    gather.z_step(3, 1)
    gather.second(ATT, 0)
    gather.z_step(ATT, 2)
    gather.z_step(3, 2)

    @pl.when(~at_end)
    def _():
        gather.z_step(UP, 0)
        swap.start()

    gather.second(ATT, 1)
    gather.third(ATT, 0)
    gather.z_step(ATT, 3)
    gather.z_step(3, 3)
    gather.second(ATT, 2)
    gather.z_step(UP, 1)
    gather.third(ATT, 1)
    gather.second(ATT, 3)
    gather.third(ATT, 2)

    @pl.when(~at_end)
    def _():
        gather.z_step(UP, 2)
        gather.z_step(DOWN, 0)

    gather.third(ATT, 3)
    hooks = GatherHooks(gather, swap, blocks_hbm, keep_sem)
    forward_compute(blocks, biases, xs, keybias, valid, cot, vec, probs_hbm, out_hbm, outs, *scratch, hooks)
    masked_copy.wait()


def forward_alone(blocks_in, biases, xs, keybias, valid, cot, *refs):
    vecs, (probs_hbm, out_hbm, *outs), scratch = refs[:7], refs[7 : 9 + N_KEPT], refs[9 + N_KEPT :]
    blocks, vec, *scratch, keep_sem = scratch
    fill_vectors(vec, vecs)
    load = pltpu.make_async_copy(blocks_in, blocks, keep_sem)
    load.start()
    load.wait()
    forward_compute(
        blocks, biases, xs, keybias, valid, cot, vec, probs_hbm, out_hbm, outs, *scratch, NoHooks()
    )


BLOCKS = (3, 4, 2, 2, 2, 96, 768)


def forward_outs(rows):
    def of(shape, dtype):
        return jax.ShapeDtypeStruct(shape, dtype)

    return [
        of((12, 8, rows), F32),
        of((12, 2, 64, rows), F32),
        of((2, 768, rows), BF16),
        of((12, rows, 128), BF16),
        of((8, 128, LEN), BF16),
        of((8, LEN, 128), BF16),
        of((4, rows, 256), BF16),
        of((4, rows, 768), BF16),
        of((4, rows, 768), BF16),
        of((768, rows), BF16),
        of((rows, 768), F32),
        of((rows, 1), F32),
        of((rows, 768), BF16),
        of((768, rows), BF16),
        of((rows, 768), F32),
        of((8, 768), F32),
    ]


N_FORWARD_SCRATCH = 11


def forward_scratch(rows):
    return [
        [pltpu.VMEM(out.shape, out.dtype) for out in forward_outs(rows)],
        pltpu.SemaphoreType.DMA((N_KEPT,)),
        pltpu.VMEM((8, LEN, 128), BF16),
        pltpu.VMEM((8, 128, LEN), BF16),
        pltpu.VMEM((3, rows, rows), BF16),
        pltpu.SemaphoreType.DMA((3,)),
        pltpu.VMEM((rows, 768), F32),
        pltpu.VMEM((rows, 768), BF16),
        pltpu.VMEM((12, 8, rows), F32),
        pltpu.VMEM((rows, 768), BF16),
        pltpu.SemaphoreType.DMA((3,)),
    ]


def run_forward_linked(rows, *ins):
    outs = forward_outs(rows)
    probs = jax.ShapeDtypeStruct((12, LEN, rows), BF16)
    frames = jax.ShapeDtypeStruct((rows, 768), BF16)
    masked = jax.ShapeDtypeStruct((2, rows, 1), F32)
    blocks, probs, frames, masked, *kept = pl.pallas_call(
        forward_linked,
        name="forward",
        out_shape=[jax.ShapeDtypeStruct(BLOCKS, BF16), probs, frames, masked, *outs],
        in_specs=[pl.BlockSpec(memory_space=pltpu.SMEM)] + [vmem()] * 19,
        out_specs=[hbm()] * (4 + N_KEPT),
        scratch_shapes=[
            pltpu.VMEM(BLOCKS, BF16),
            pltpu.VMEM((4, 16, 768), BF16),
            pltpu.VMEM((2, rows, 768), BF16),
            pltpu.VMEM((LEN, 128), BF16),
            pltpu.VMEM((rows, 1), F32),
            pltpu.VMEM((8, 768), F32),
            pltpu.VMEM((2, rows, 1), F32),
            pltpu.SemaphoreType.DMA,
            *forward_scratch(rows),
            pltpu.SemaphoreType.DMA((4, 2, 3)),
            pltpu.SemaphoreType.DMA((4, 4)),
            pltpu.SemaphoreType.DMA((3, 4, 5)),
            pltpu.SemaphoreType.DMA((3, 4, 5)),
            pltpu.SemaphoreType.DMA,
            pltpu.SemaphoreType.DMA,
            pltpu.SemaphoreType.DMA((3,)),
        ],
        compiler_params=pltpu.CompilerParams(
            collective_id=0, has_side_effects=True, vmem_limit_bytes=VMEM_LIMIT
        ),
    )(*ins)
    return blocks, probs, frames, masked, kept


def run_forward_alone(rows, *ins):
    probs = jax.ShapeDtypeStruct((12, LEN, rows), BF16)
    frames = jax.ShapeDtypeStruct((rows, 768), BF16)
    probs, frames, *kept = pl.pallas_call(
        forward_alone,
        name="forward",
        out_shape=[probs, frames, *forward_outs(rows)],
        in_specs=[hbm()] + [vmem()] * 12,
        out_specs=[hbm()] * (2 + N_KEPT),
        scratch_shapes=[pltpu.VMEM(BLOCKS, BF16), pltpu.VMEM((8, 768), F32), *forward_scratch(rows), pltpu.SemaphoreType.DMA],
        compiler_params=pltpu.CompilerParams(vmem_limit_bytes=VMEM_LIMIT),
    )(*ins)
    return probs, frames, kept


ATT_ORDER = (0, 3, 1, 2)
DOWN_ORDER = (3, 0, 2, 1)
DEEP = 32


def att_order(place):
    return jnp.where(place == 0, 0, jnp.where(place == 1, 3, place - 1))


def down_order(place):
    return jnp.where(place == 0, 3, jnp.where(place == 1, 0, 4 - place))


def row_parts(kind):
    base = DEEP if kind == DOWN else 0
    half = (96 - base) // 2
    return pl.ds(base, half), pl.ds(base + half, half), pl.ds(base, 2 * half)


def chunk_at(n):
    return (DOWN, DOWN_ORDER[n]) if n < 4 else (UP, n - 4) if n < 8 else (ATT, ATT_ORDER[n - 8])


class Scatter:
    def __init__(self, at, grads, out, buffers, semaphores):
        self.at, self.grads, self.out = at, grads, out
        self.core_in, self.first_in, self.second_in, self.z_in, self.deep_in, self.plane_in = buffers
        self.send, self.recv, self.z_send, self.z_recv, *deep = semaphores
        self.deep_send, self.deep_recv, self.plane_send, self.plane_recv = deep

    def copy(self, kind, m, which):
        at, grads = self.at, self.grads.at[kind, m]
        x, y, c = at.x, at.y, at.c
        low, high, _ = row_parts(kind)
        first, second = self.first_in.at[kind, m], self.second_in.at[kind, m]
        part = pl.ds(0, low.size)
        src, dst, device = {
            0: lambda: (grads.at[:, :, 1 - c], self.core_in.at[kind, m], at.core),
            1: lambda: (grads.at[:, 1 - x, c, low], first.at[0, :, part], at.across_x),
            2: lambda: (grads.at[1 - y, :, c, high], first.at[1, :, part], at.across_y),
            3: lambda: (grads.at[1 - y, x, c, low], second.at[0, part], at.across_y),
            4: lambda: (grads.at[y, 1 - x, c, high], second.at[1, part], at.across_x),
        }[which]()
        return remote(src, dst, self.send.at[kind, m, which], self.recv.at[kind, m, which], device)

    def add(self, ref, got):
        ref[...] = (ref[...].astype(F32) + got[...].astype(F32)).astype(BF16)

    def begin(self, kind, m):
        self.copy(kind, m, 0).start()

    def first(self, kind, m):
        at, grads = self.at, self.grads.at[kind, m]
        self.copy(kind, m, 0).wait_recv()
        for y in range(2):
            for x in range(2):
                self.add(grads.at[y, x, at.c], self.core_in.at[kind, m, y, x])
        self.copy(kind, m, 1).start()
        self.copy(kind, m, 2).start()
        if kind == DOWN:
            self.ends(m, lambda direction: self.deep_copy(m, direction).start())

    def second(self, kind, m):
        at, grads = self.at, self.grads.at[kind, m]
        low, high, _ = row_parts(kind)
        part = pl.ds(0, low.size)
        self.copy(kind, m, 1).wait_recv()
        for y in range(2):
            self.add(grads.at[y, at.x, at.c, low], self.first_in.at[kind, m, 0, y, part])
        self.copy(kind, m, 3).start()
        self.copy(kind, m, 2).wait_recv()
        for x in range(2):
            self.add(grads.at[at.y, x, at.c, high], self.first_in.at[kind, m, 1, x, part])
        self.copy(kind, m, 4).start()

    def third(self, kind, m):
        at = self.at
        grads = self.grads.at[kind, m, at.y, at.x, at.c]
        low, high, _ = row_parts(kind)
        part = pl.ds(0, low.size)
        self.copy(kind, m, 3).wait_recv()
        self.add(grads.at[low], self.second_in.at[kind, m, 0, part])
        self.copy(kind, m, 4).wait_recv()
        self.add(grads.at[high], self.second_in.at[kind, m, 1, part])
        self.z_start(kind, m)

    def ends(self, m, act):
        z = self.at.z
        if m > 0:
            pl.when(z == 0)(lambda: act(0))
        if m < 3:
            pl.when(z == 3)(lambda: act(1))

    def deep_copy(self, m, direction, slot=None):
        at = self.at
        device = at.right if direction == 0 else at.left
        if slot is None:
            slot = m if direction == 0 else jnp.where(m == at.z - 1, 4, m)
        src = self.grads.at[DOWN, m, :, :, at.c, pl.ds(0, DEEP)]
        return remote(src, self.deep_in.at[slot], self.deep_send.at[m], self.deep_recv.at[slot], device)

    def deep_add(self, m, slot, direction):
        self.deep_copy(m, direction, slot).wait_recv()
        for y in range(2):
            for x in range(2):
                self.add(self.grads.at[DOWN, m, y, x, self.at.c, pl.ds(0, DEEP)], self.deep_in.at[slot, y, x])

    def deep_relay(self, m, direction):
        self.deep_add(m, m, direction)
        self.deep_copy(m, direction).start()

    def deep_one(self, kind, m):
        z = self.at.z
        if m > 1:
            pl.when(z == 1)(lambda: self.deep_relay(m, 0))
        else:
            pl.when(z == 2)(lambda: self.deep_relay(m, 1))

    def deep_two(self, kind, m):
        z = self.at.z
        if m == 3:
            pl.when(z == 2)(lambda: self.deep_relay(m, 0))
        if m == 0:
            pl.when(z == 1)(lambda: self.deep_relay(m, 1))

    def deep_plane(self, which):
        at, grads = self.at, self.grads.at[DOWN, self.at.z]
        x, y, c = at.x, at.y, at.c
        half = DEEP // 2
        low, high = pl.ds(0, half), pl.ds(half, half)
        src, dst, device = {
            0: lambda: (grads.at[:, 1 - x, c, low], self.plane_in.at[0], at.across_x),
            1: lambda: (grads.at[1 - y, :, c, high], self.plane_in.at[1], at.across_y),
            2: lambda: (grads.at[1 - y, x, c, low], self.plane_in.at[2, 0], at.across_y),
            3: lambda: (grads.at[y, 1 - x, c, high], self.plane_in.at[2, 1], at.across_x),
        }[which]()
        return remote(src, dst, self.plane_send.at[which], self.plane_recv.at[which], device)

    def deep_first(self):
        z = self.at.z
        pl.when(z > 0)(lambda: self.deep_add(z, z, 0))
        pl.when(z < 3)(lambda: self.deep_add(z, 4, 1))
        self.deep_plane(0).start()
        self.deep_plane(1).start()

    def deep_second(self):
        at, half = self.at, DEEP // 2
        grads = self.grads.at[DOWN, at.z]
        self.deep_plane(0).wait_recv()
        for y in range(2):
            self.add(grads.at[y, at.x, at.c, pl.ds(0, half)], self.plane_in.at[0, y])
        self.deep_plane(2).start()
        self.deep_plane(1).wait_recv()
        for x in range(2):
            self.add(grads.at[at.y, x, at.c, pl.ds(half, half)], self.plane_in.at[1, x])
        self.deep_plane(3).start()

    def deep_third(self):
        at, half = self.at, DEEP // 2
        grads = self.grads.at[DOWN, at.z, at.y, at.x, at.c]
        self.deep_plane(2).wait_recv()
        self.add(grads.at[pl.ds(0, half)], self.plane_in.at[2, 0])
        self.deep_plane(3).wait_recv()
        self.add(grads.at[pl.ds(half, half)], self.plane_in.at[2, 1])

    def z_copy(self, kind, m, direction, slot=None):
        at = self.at
        whole = row_parts(kind)[2]
        device = at.right if direction == 0 else at.left
        if slot is None:
            slot = m if direction == 0 else jnp.where(m == at.z - 1, 4, m)
        src = self.grads.at[kind, m, at.y, at.x, at.c, whole]
        dst = self.z_in.at[kind, slot, whole]
        return remote(src, dst, self.z_send.at[kind, m], self.z_recv.at[kind, slot], device)

    def relay(self, kind, m, direction):
        whole = row_parts(kind)[2]
        self.z_copy(kind, m, direction, m).wait_recv()
        self.add(self.grads.at[kind, m, self.at.y, self.at.x, self.at.c, whole], self.z_in.at[kind, m, whole])
        self.z_copy(kind, m, direction).start()

    def z_start(self, kind, m):
        self.ends(m, lambda direction: self.z_copy(kind, m, direction).start())

    def z_one(self, kind, m):
        z = self.at.z
        if m > 1:
            pl.when(z == 1)(lambda: self.relay(kind, m, 0))
        else:
            pl.when(z == 2)(lambda: self.relay(kind, m, 1))

    def z_two(self, kind, m):
        z = self.at.z
        if m == 3:
            pl.when(z == 2)(lambda: self.relay(kind, m, 0))
        if m == 0:
            pl.when(z == 1)(lambda: self.relay(kind, m, 1))

    def finish(self, kind):
        at, z = self.at, self.at.z
        whole = row_parts(kind)[2]
        self.out[kind] = self.grads[kind, z, at.y, at.x, at.c].astype(F32)

        @pl.when(z > 0)
        def _():
            self.z_copy(kind, z, 0, z).wait_recv()
            self.out[kind, whole] += self.z_in[kind, z, whole].astype(F32)

        @pl.when(z < 3)
        def _():
            self.z_copy(kind, z, 1, 4).wait_recv()
            self.out[kind, whole] += self.z_in[kind, 4, whole].astype(F32)

    def run(self, **steps):
        for name, places in steps.items():
            for n in places:
                getattr(self, name)(*chunk_at(n))

    def drain(self):
        z = self.at.z
        for which in range(4):
            self.deep_plane(which).wait_send()
        for kind in range(3):

            def of_index(m, _, kind=kind):
                for which in range(5):
                    self.copy(kind, m, which).wait_send()

                def along(direction):
                    self.z_copy(kind, m, direction).wait_send()
                    if kind == DOWN:
                        self.deep_copy(m, direction).wait_send()

                pl.when(m > z)(lambda: along(0))
                pl.when(m < z)(lambda: along(1))
                return 0

            lax.fori_loop(0, 4, of_index, 0)


class Totals:
    def __init__(self, at, rows, got, send, recv):
        self.rows, self.got, self.send, self.recv = rows, got, send, recv
        self.partners = (at.core, at.mate, at.far, at.across_x, at.across_y)

    def copy(self, stage):
        return remote(
            self.rows.at[stage], self.got.at[stage], self.send.at[stage], self.recv.at[stage], self.partners[stage]
        )

    def start(self, stage):
        self.copy(stage).start()

    def finish(self, stage):
        self.copy(stage).wait()
        self.rows[stage + 1] = self.rows[stage] + self.got[stage]


def backward_compute(
    blocks_hbm,
    probs_hbm,
    acted_hbm,
    slope_hbm,
    recip_hbm,
    headout_hbm,
    xt_hbm,
    qm_hbm,
    kt_hbm,
    v_hbm,
    att_hbm,
    n1t_hbm,
    n1_hbm,
    rs1_hbm,
    gb2_hbm,
    gb2t_hbm,
    g2_hbm,
    sums_hbm,
    masked_hbm,
    gain_ref,
    grads,
    rows_ref,
    weight,
    weight_sem,
    acts,
    acts_sem,
    probs,
    probs_sem,
    gb1,
    gb1t,
    grad_one,
    parts,
    g2_ref,
    state_sem,
    gb2_ref,
    gb2t_ref,
    n1t_ref,
    xt_ref,
    headout_ref,
    qm_ref,
    kt_ref,
    v_ref,
    att_ref,
    head_sem,
    own,
    sides,
    shifts,
    shares,
    recip_ref,
    rs1_ref,
    sums_ref,
    masked_ref,
    small_sem,
    hooks,
):
    rows = g2_ref.shape[0]
    g2_load = pltpu.make_async_copy(g2_hbm, g2_ref, state_sem.at[0])
    n1_load = pltpu.make_async_copy(n1_hbm, grad_one, state_sem.at[1])
    gb2_load = pltpu.make_async_copy(gb2_hbm, gb2_ref, state_sem.at[2])
    gb2t_load = pltpu.make_async_copy(gb2t_hbm, gb2t_ref, state_sem.at[3])
    n1t_load = pltpu.make_async_copy(n1t_hbm, n1t_ref, state_sem.at[4])
    xt_load = pltpu.make_async_copy(xt_hbm, xt_ref, state_sem.at[5])

    small_loads = [
        pltpu.make_async_copy(src, dst, small_sem.at[i])
        for i, (src, dst) in enumerate(
            ((recip_hbm, recip_ref), (rs1_hbm, rs1_ref), (sums_hbm, sums_ref), (masked_hbm, masked_ref))
        )
    ]

    def head_loads(m, slot, side):
        three, two, half = pl.ds(3 * m, 3), pl.ds(2 * m, 2), pl.ds(side * rows, rows)
        pairs = [
            (qm_hbm.at[three], qm_ref.at[slot]),
            (kt_hbm.at[two, :, half], kt_ref.at[slot]),
            (v_hbm.at[two, half], v_ref.at[slot]),
            (headout_hbm.at[three], headout_ref.at[slot]) if side else (att_hbm.at[m], att_ref.at[slot]),
        ]
        return [
            pltpu.make_async_copy(src, dst, head_sem.at[slot, i if i < 3 else 4 - side])
            for i, (src, dst) in enumerate(pairs)
        ]

    def weight_load(kind, m, slot):
        return pltpu.make_async_copy(blocks_hbm.at[kind, m], weight.at[slot], weight_sem.at[slot])

    def act_load(which, m):
        pair, place = m // 2, lax.rem(m, 2)
        return pltpu.make_async_copy(which.at[m], acts.at[pair, place], acts_sem.at[pair, place])

    def probs_loads(m, slot, side):
        half = pl.ds(side * rows, rows)
        return [
            pltpu.make_async_copy(probs_hbm.at[3 * m + j, half], probs.at[slot, j], probs_sem.at[slot, j])
            for j in range(3)
        ]

    def feed_loads(m, slot):
        return (weight_load(DOWN, m, 2 * slot), weight_load(UP, m, 2 * slot + 1))

    def begin(copies):
        for copy in copies:
            copy.start()

    def finish(copies):
        for copy in copies:
            copy.wait()

    def block(slot, low=0, width=768):
        return weight[slot, :, :, :, :, pl.ds(low, width)].reshape(768, width)

    def put(kind, m, value, low=0):
        width = value.shape[1]
        grads[kind, m, :, :, :, :, pl.ds(low, width)] = value.astype(BF16).reshape(2, 2, 2, 96, width)

    begin([gb2t_load, *(act_load(acted_hbm, m) for m in DOWN_ORDER)])
    parts[...] = jnp.zeros_like(parts)
    hooks.after("start")
    finish((gb2t_load,))

    def feed_down(place, _):
        m = down_order(place)
        act_load(acted_hbm, m).wait()
        put(DOWN, m, dot(gb2t_ref[...], acts[m // 2, lax.rem(m, 2)]))
        hooks.ready(DOWN, m)

        @pl.when(place == 0)
        def _():
            begin((gb2_load, *feed_loads(0, 0)))

        act_load(slope_hbm, m).start()

        @pl.when(place == 1)
        def _():
            begin((n1t_load, g2_load, n1_load, *small_loads, xt_load))
            begin(head_loads(0, 0, 1))
            begin(probs_loads(0, 0, 1))

        hooks.after("down", place)
        return 0

    lax.fori_loop(0, 4, feed_down, 0)
    finish((gb2_load, n1t_load, g2_load))

    def feed(m, _):
        slot = lax.rem(m, 2)
        pl.when(m < 3)(lambda: begin(feed_loads(m + 1, 1 - slot)))
        finish(feed_loads(m, slot))
        act_load(slope_hbm, m).wait()
        grad_acted = dot(gb2_ref[...], block(2 * slot))
        grad_pre = (grad_acted * acts[m // 2, lax.rem(m, 2)].astype(F32)).astype(BF16)
        parts[m, 0:1, :] = jnp.sum(grad_pre.astype(F32), axis=0, keepdims=True)
        put(UP, m, dot(n1t_ref[...], grad_pre))
        g2_ref[...] += dot(grad_pre, block(2 * slot + 1), (1, 1))
        hooks.ready(UP, m)
        hooks.after("feed", m)
        return 0

    lax.fori_loop(0, 4, feed, 0)
    for m in range(4):
        weight_load(ATT, m, m).start()

    chunk = 64

    def norm_back(i, sums):
        r = pl.ds(pl.multiple_of(i * chunk, chunk), chunk)
        grad = g2_ref[r, :]
        unit = grad_one[r, :]
        scaled = grad * gain
        grad_in = (
            scaled
            - jnp.mean(scaled, axis=1, keepdims=True)
            - unit * jnp.mean(scaled * unit, axis=1, keepdims=True)
        ) * rs1_ref[r, :]
        grad_one[r, :] = grad_in
        gb1[r, :] = grad_in.astype(BF16)
        return (
            sums[0] + jnp.sum(grad_in, axis=0, keepdims=True),
            sums[1] + jnp.sum(grad * unit, axis=0, keepdims=True),
            sums[2] + jnp.sum(grad, axis=0, keepdims=True),
        )

    zero = jnp.zeros((1, 768), F32)
    finish((n1_load, xt_load))
    finish(small_loads)
    gain = gain_ref[...].astype(F32).reshape(1, 768)
    sums = lax.fori_loop(0, rows // chunk, norm_back, (zero, zero, zero), unroll=2)
    rows_ref[0, 0:1, :] = sums[0]
    rows_ref[0, 1:2, :] = sums_ref[0:1, :]
    rows_ref[0, 2:3, :] = sums[1]
    rows_ref[0, 3:4, :] = sums[2]
    rows_ref[0, 4:5, :] = sums_ref[1:2, :]
    rows_ref[0, 5:6, :] = sums_ref[2:3, :]
    gb1t[...] = gb1[...].T
    hooks.after("norm")
    g2_ref[...] = jnp.zeros_like(g2_ref)

    def wide(j, side):
        zeros = jnp.zeros((64, rows), BF16)
        return jnp.concatenate([zeros, side] if j == 1 else [side, zeros], axis=0)

    def half_back(slot, sides_here, shifts_here):
        grads_k, grads_v, grads_q = [], [], []
        wides = [wide(j, sides_here[j]) for j in range(3)]
        grad_weights = [dot(v_ref[slot, j // 2], wides[j]) for j in range(3)]
        for j in range(3):
            weights = probs[slot, j]
            grad_scores = (weights.astype(F32) * (grad_weights[j] - shifts_here[j])).astype(BF16)
            grads_v.append(dot(weights, wides[j].T))
            grads_k.append(dot(grad_scores, qm_ref[slot, j]))
            lane = 0 if j == 0 else 64
            grads_q.append(dot(kt_ref[slot, j // 2, lane : lane + 64, :], grad_scores))
        return [grads_k[0] + grads_k[1], grads_k[2]], [grads_v[0] + grads_v[1], grads_v[2]], grads_q

    def back_other(m, _):
        slot = lax.rem(m, 2)
        pl.when(m < 3)(lambda: begin([*head_loads(m + 1, 1 - slot, 1), *probs_loads(m + 1, 1 - slot, 1)]))
        pl.when(m == 3)(lambda: begin([*head_loads(0, 0, 0), *probs_loads(0, 0, 0)]))
        weight_load(ATT, m, m).wait()
        finish(head_loads(m, slot, 1))
        finish(probs_loads(m, slot, 1))
        grad_att_t = dot(gb1[...], block(m, 512, 256)).T
        others, shifts_here = [], []
        for j in range(3):
            head = 3 * m + j
            place = (128, 192, 64)[j]
            grad_att = grad_att_t[place : place + 64, :]
            factor_own, factor = recip_ref[head, 0:1, :], recip_ref[head, 1:2, :]
            own_side = (grad_att * factor_own).astype(BF16)
            others.append((grad_att * factor).astype(BF16))
            row_sum = jnp.sum(
                own_side.astype(F32) * headout_ref[slot, j, 0] + others[j].astype(F32) * headout_ref[slot, j, 1],
                axis=0,
                keepdims=True,
            )
            sides[head] = own_side
            shifts[head, 0:1, :] = row_sum * factor_own
            shifts_here.append(row_sum * factor)
        grads_k, grads_v, grads_q = half_back(slot, others, shifts_here)
        for j in range(3):
            shares[3 * m + j] = grads_q[j]
        tile = acts.at[m // 2, lax.rem(m, 2)]
        tile[:, 128:256] = grads_k[0].astype(BF16)
        tile[:, 256:384] = grads_v[0].astype(BF16)
        tile[:, 384:512] = grads_k[1].astype(BF16)
        tile[:, 512:640] = grads_v[1].astype(BF16)
        parts[4 + m, 0:1, 128:640] = jnp.sum(tile[:, 128:640].astype(F32), axis=0, keepdims=True)
        g2_ref[...] += dot(tile[:, 128:640], block(m, 128, 512), (1, 1))
        hooks.after("other", m)
        return 0

    lax.fori_loop(0, 4, back_other, 0)

    def fill_other(i, total):
        r = pl.ds(pl.multiple_of(i * chunk, chunk), chunk)
        other = g2_ref[r, :]
        gb1[r, :] = other.astype(BF16)
        return total + jnp.sum(other * masked_ref[1, r, :], axis=0, keepdims=True)

    fill = lax.fori_loop(0, rows // chunk, fill_other, zero)
    hooks.after("mate")

    def back_own(place, _):
        slot = lax.rem(place, 2)
        m = att_order(place)

        @pl.when(place < 3)
        def _():
            after = att_order(place + 1)
            begin([*head_loads(after, 1 - slot, 0), *probs_loads(after, 1 - slot, 0)])

        finish(head_loads(m, slot, 0))
        finish(probs_loads(m, slot, 0))
        grads_k, grads_v, grads_q = half_back(
            slot, [sides[3 * m + j] for j in range(3)], [shifts[3 * m + j, 0:1, :] for j in range(3)]
        )
        grads_q = [(grads_q[j] + shares[3 * m + j]) * SCALE for j in range(3)]
        single = jnp.concatenate([grads_q[2], jnp.zeros((64, rows), F32)], axis=0).T
        own[:, 0:128] = jnp.concatenate(grads_q[:2], axis=0).T.astype(BF16)
        own[:, 128:256] = grads_k[0].astype(BF16)
        own[:, 256:384] = grads_v[0].astype(BF16)
        own[:, 384:512] = (grads_k[1] + single).astype(BF16)
        own[:, 512:640] = grads_v[1].astype(BF16)
        parts[4 + m, 0:1, 0:PROJ] += jnp.sum(own[...].astype(F32), axis=0, keepdims=True)
        hooks.after("middle", place)
        other = acts[m // 2, lax.rem(m, 2), :, 128:640]
        grad_proj = dot(xt_ref[0], own[...])
        grad_other = dot(xt_ref[1], other)
        grad_out_w = dot(gb1t[...], att_ref[slot])
        put(ATT, m, grad_proj[:, :128], 0)
        put(ATT, m, grad_proj[:, 128:512] + grad_other[:, :384], 128)
        put(ATT, m, grad_proj[:, 512:] + grad_other[:, 384:] + grad_out_w[:, :128], 512)
        put(ATT, m, grad_out_w[:, 128:], 640)
        grad_one[...] += dot(own[...], block(m, 0, PROJ), (1, 1))
        hooks.ready(ATT, m)
        hooks.after("own", place)
        return 0

    lax.fori_loop(0, 4, back_own, 0)

    def fill_own(i, total):
        r = pl.ds(pl.multiple_of(i * chunk, chunk), chunk)
        return total + jnp.sum(grad_one[r, :] * masked_ref[0, r, :], axis=0, keepdims=True)

    rows_ref[0, 6:7, :] = lax.fori_loop(0, rows // chunk, fill_own, fill)
    rows_ref[0, 7:8, :] = zero
    for row in range(8):
        rows_ref[0, 8 + row : 9 + row, :] = parts[row, 0:1, :]


def finish_frames(grad_one, got, masked_ref, frames_ref):
    chunk = 64

    def body(i, _):
        r = pl.ds(pl.multiple_of(i * chunk, chunk), chunk)
        total = grad_one[r, :] + got[r, :].astype(F32)
        frames_ref[r, :] = jnp.where(masked_ref[0, r, :] > 0, 0.0, total).astype(BF16)
        return 0

    lax.fori_loop(0, grad_one.shape[0] // chunk, body, 0)


class NoScatter:
    def after(self, point, m=0):
        pass

    def ready(self, kind, m):
        pass


class ScatterHooks:
    PLAN = {
        ("down", 2): dict(first=(0,)),
        ("down", 3): dict(first=(1,)),
        ("feed", 0): dict(first=(2, 3)),
        ("feed", 1): dict(second=(0, 1), deep_one=(0,)),
        ("feed", 2): dict(second=(2,), first=(4,), deep_one=(1,)),
        ("feed", 3): dict(second=(3,), first=(5,), third=(0,), deep_one=(2,), deep_two=(0,)),
        ("norm", 0): dict(third=(1,), deep_one=(3,), deep_two=(1,)),
        ("other", 0): dict(second=(4,), first=(6,), third=(2,)),
        ("other", 1): dict(deep=("deep_first",), third=(3,), z_one=(0,)),
        ("other", 2): dict(first=(7,), z_one=(1,)),
        ("other", 3): dict(second=(5,), third=(4,), z_one=(2,), z_two=(0,)),
        ("mate", 0): dict(swap=(0,)),
        ("middle", 0): dict(deep=("deep_second",), swap=(1,)),
        ("own", 0): dict(second=(6,), third=(5,), z_one=(3,), z_two=(1,)),
        ("middle", 1): dict(first=(8,), deep=("deep_third",), swap=(2,)),
        ("own", 1): dict(second=(7,), z_one=(4,)),
        ("middle", 2): dict(first=(9,), third=(6,), swap=(3,)),
        ("own", 2): dict(z_one=(5,)),
        ("middle", 3): dict(second=(8,), first=(10,), third=(7,)),
        ("own", 3): dict(z_one=(6,), z_two=(4,)),
    }

    def __init__(self, at, scatter, swaps):
        self.at, self.scatter, self.swaps = at, scatter, swaps

    def ready(self, kind, m):
        self.scatter.begin(kind, m)

    def run(self, swap=(), deep=(), **steps):
        self.scatter.run(**steps)
        for name in deep:
            getattr(self.scatter, name)()
        for piece in swap:
            self.swaps[piece].start()

    def after(self, point, m=0):
        if point == "start":
            self.at.meet(True)
        for (name, index), steps in self.PLAN.items():
            if name == point:
                if isinstance(m, int):
                    self.run(**steps)
                else:
                    pl.when(m == index)(functools.partial(self.run, **steps))


N_BACKWARD_INS = 20
N_BACKWARD_SCRATCH = 33


def backward_linked(*refs):
    ins = refs[:N_BACKWARD_INS]
    out_ref, rows_out, frames_ref = refs[N_BACKWARD_INS : N_BACKWARD_INS + 3]
    scratch = refs[N_BACKWARD_INS + 3 :]
    scratch, links = scratch[:N_BACKWARD_SCRATCH], scratch[N_BACKWARD_SCRATCH:]
    grads, rows_ref, gb1, grad_one = scratch[0], scratch[1], scratch[8], scratch[10]
    rows_in, mate_in, t_send, t_recv, m_send, m_recv = links[14:]
    at = Place()
    at.hello(True)
    scatter = Scatter(at, grads, out_ref, links[:6], links[6:14])
    totals = Totals(at, rows_ref, rows_in, t_send, t_recv)
    piece = gb1.shape[0] // 4
    swaps = [
        remote(
            gb1.at[pl.ds(i * piece, piece)], mate_in.at[pl.ds(i * piece, piece)], m_send.at[i], m_recv.at[i], at.mate
        )
        for i in range(4)
    ]
    backward_compute(*ins, *scratch, ScatterHooks(at, scatter, swaps))
    totals.start(0)
    scatter.run(second=(9,), first=(11,))
    totals.finish(0)
    totals.start(1)
    scatter.run(third=(8,), z_one=(7,))
    scatter.run(second=(10,))
    scatter.run(third=(9,))
    totals.finish(1)
    totals.start(2)
    scatter.run(second=(11,))
    scatter.run(z_one=(8,), z_two=(7,))
    scatter.run(third=(10,))
    totals.finish(2)
    totals.start(3)
    scatter.run(third=(11,))
    scatter.run(z_one=(9,), z_two=(8,))
    scatter.finish(DOWN)
    scatter.finish(UP)
    totals.finish(3)
    totals.start(4)
    scatter.run(z_one=(10,))
    for swap in swaps:
        swap.wait()
    finish_frames(grad_one, mate_in, scratch[31], frames_ref)
    scatter.run(z_one=(11,), z_two=(9,))
    totals.finish(4)
    rows_out[...] = rows_ref[5]
    scatter.drain()
    scatter.finish(ATT)


def backward_alone(*refs):
    ins = refs[:N_BACKWARD_INS]
    grads_out, rows_out, mate_out, grad_one_out = refs[N_BACKWARD_INS : N_BACKWARD_INS + 4]
    scratch = refs[N_BACKWARD_INS + 4 :]
    *scratch, keep_sem = scratch
    grads, rows_ref, gb1, grad_one = scratch[0], scratch[1], scratch[8], scratch[10]
    backward_compute(*ins, *scratch, NoScatter())
    keep = pltpu.make_async_copy(grads, grads_out, keep_sem)
    keep.start()
    rows_out[...] = rows_ref[0]
    mate_out[...] = gb1[...]
    grad_one_out[...] = grad_one[...]
    keep.wait()


def backward_scratch(rows):
    return [
        pltpu.VMEM(BLOCKS, BF16),
        pltpu.VMEM((6, 16, 768), F32),
        pltpu.VMEM((4, *BLOCKS[2:]), BF16),
        pltpu.SemaphoreType.DMA((4,)),
        pltpu.VMEM((2, 2, rows, 768), BF16),
        pltpu.SemaphoreType.DMA((2, 2)),
        pltpu.VMEM((2, 3, rows, rows), BF16),
        pltpu.SemaphoreType.DMA((2, 3)),
        pltpu.VMEM((rows, 768), BF16),
        pltpu.VMEM((768, rows), BF16),
        pltpu.VMEM((rows, 768), F32),
        pltpu.VMEM((8, 8, 768), F32),
        pltpu.VMEM((rows, 768), F32),
        pltpu.SemaphoreType.DMA((6,)),
        pltpu.VMEM((rows, 768), BF16),
        pltpu.VMEM((768, rows), BF16),
        pltpu.VMEM((768, rows), BF16),
        pltpu.VMEM((2, 768, rows), BF16),
        pltpu.VMEM((2, 3, 2, 64, rows), F32),
        pltpu.VMEM((2, 3, rows, 128), BF16),
        pltpu.VMEM((2, 2, 128, rows), BF16),
        pltpu.VMEM((2, 2, rows, 128), BF16),
        pltpu.VMEM((2, rows, 256), BF16),
        pltpu.SemaphoreType.DMA((2, 5)),
        pltpu.VMEM((rows, PROJ), BF16),
        pltpu.VMEM((12, 64, rows), BF16),
        pltpu.VMEM((12, 8, rows), F32),
        pltpu.VMEM((12, 64, rows), F32),
        pltpu.VMEM((12, 8, rows), F32),
        pltpu.VMEM((rows, 1), F32),
        pltpu.VMEM((8, 768), F32),
        pltpu.VMEM((2, rows, 1), F32),
        pltpu.SemaphoreType.DMA((4,)),
    ]


def run_backward(linked, blocks, probs, kept, masked, gain):
    recip, headout, xt, qm, kt, v, att, acted, slope, n1t, n1, rs1, gb2, gb2t, g2, sums = kept
    rows = gb2.shape[0]
    ins = (
        blocks, probs, acted, slope, recip, headout, xt, qm, kt, v, att, n1t, n1, rs1, gb2, gb2t, g2, sums, masked, gain
    )
    in_specs = [vmem() if i == 19 else hbm() for i in range(20)]
    if linked:
        return pl.pallas_call(
            backward_linked,
            name="backward",
            out_shape=[
                jax.ShapeDtypeStruct((3, 96, 768), F32),
                jax.ShapeDtypeStruct((16, 768), F32),
                jax.ShapeDtypeStruct((rows, 768), BF16),
            ],
            in_specs=in_specs,
            out_specs=[vmem()] * 3,
            scratch_shapes=[
                *backward_scratch(rows),
                pltpu.VMEM((3, 4, 2, 2, 96, 768), BF16),
                pltpu.VMEM((3, 4, 2, 2, 48, 768), BF16),
                pltpu.VMEM((3, 4, 2, 48, 768), BF16),
                pltpu.VMEM((3, 5, 96, 768), BF16),
                pltpu.VMEM((5, 2, 2, DEEP, 768), BF16),
                pltpu.VMEM((3, 2, DEEP // 2, 768), BF16),
                pltpu.SemaphoreType.DMA((3, 4, 5)),
                pltpu.SemaphoreType.DMA((3, 4, 5)),
                pltpu.SemaphoreType.DMA((3, 4)),
                pltpu.SemaphoreType.DMA((3, 5)),
                pltpu.SemaphoreType.DMA((4,)),
                pltpu.SemaphoreType.DMA((5,)),
                pltpu.SemaphoreType.DMA((4,)),
                pltpu.SemaphoreType.DMA((4,)),
                pltpu.VMEM((5, 16, 768), F32),
                pltpu.VMEM((rows, 768), BF16),
                pltpu.SemaphoreType.DMA((5,)),
                pltpu.SemaphoreType.DMA((5,)),
                pltpu.SemaphoreType.DMA((4,)),
                pltpu.SemaphoreType.DMA((4,)),
            ],
            compiler_params=pltpu.CompilerParams(
                collective_id=1, has_side_effects=True, vmem_limit_bytes=VMEM_LIMIT
            ),
        )(*ins)
    return pl.pallas_call(
        backward_alone,
        name="backward",
        out_shape=[
            jax.ShapeDtypeStruct(BLOCKS, BF16),
            jax.ShapeDtypeStruct((16, 768), F32),
            jax.ShapeDtypeStruct((rows, 768), BF16),
            jax.ShapeDtypeStruct((rows, 768), F32),
        ],
        in_specs=in_specs,
        out_specs=[hbm()] + [vmem()] * 3,
        scratch_shapes=[*backward_scratch(rows), pltpu.SemaphoreType.DMA],
        compiler_params=pltpu.CompilerParams(vmem_limit_bytes=VMEM_LIMIT),
    )(*ins)


def finish_kernel(parts, grads, totals, out_in, frames_in, out, frames, *outs):
    n_dp, n_mp = parts
    query, key, value, out_w, up, down, query_bias, value_bias, up_bias, *vectors = outs
    out[...] = out_in[...]
    frames[...] = frames_in[...]
    att = grads[0]
    query[...] = jnp.concatenate([att[:, 0:128], att[:, 384:448]], axis=1)
    key[...] = jnp.concatenate([att[:, 128:256], att[:, 448:512]], axis=1)
    value[...] = jnp.concatenate([att[:, 256:384], att[:, 512:576]], axis=1)
    out_w[...] = jnp.concatenate([att[:, 640:768], att[:, 576:640]], axis=1).T
    up[...] = grads[1]
    down[...] = grads[2]
    dp, z = lax.axis_index("dp"), lax.axis_index("mp")
    rows = totals[...]
    row_at = lax.broadcasted_iota(jnp.int32, rows.shape, 0)

    def shifted(block, by):
        return pltpu.roll(block, lax.rem(768 - by, 768), 1)

    def row_of(index):
        return jnp.broadcast_to(jnp.sum(jnp.where(row_at == index, rows, 0.0), axis=0, keepdims=True), (8, 768))

    part = 768 // (n_dp * n_mp)
    mine = shifted(rows[0:8], (dp * n_mp + z) * part)
    for i, ref in enumerate(vectors):
        ref[...] = mine[i : i + 1, :part]
    step = HEAD_DIM // n_dp
    heads = shifted(row_of(12 + z), dp * step)
    for head, (q_lane, v_lane) in enumerate(((0, 256), (64, 320), (384, 512))):
        query_bias[head : head + 1, :] = heads[0:1, q_lane : q_lane + step]
        value_bias[head : head + 1, :] = heads[0:1, v_lane : v_lane + step]
    ups = shifted(row_of(8 + z), dp * 2 * step)
    for i in range(6):
        up_bias[i : i + 1, :] = ups[0:1, 128 * i : 128 * i + 2 * step]


def run_finish(n_dp, n_mp, grads, totals, out, frames):
    def of(shape, dtype=F32):
        return jax.ShapeDtypeStruct(shape, dtype)

    d, step, part = grads.shape[1], HEAD_DIM // n_dp, 768 // (n_dp * n_mp)
    *outs, = pl.pallas_call(
        functools.partial(finish_kernel, (n_dp, n_mp)),
        name="finish",
        out_shape=[
            of(out.shape, BF16), of(frames.shape, BF16), of((d, 192)), of((d, 192)), of((d, 192)), of((192, d)),
            of((d, 768)), of((d, 768)), of((3, step)), of((3, step)), of((6, 2 * step)), *[of((1, part))] * 7,
        ],
        in_specs=[vmem()] * 4,
        out_specs=[vmem()] * 18,
        compiler_params=pltpu.CompilerParams(vmem_limit_bytes=VMEM_LIMIT),
    )(grads, totals, out, frames)
    return (*outs[:7], outs[7].T, *outs[8:11], *(row.reshape(part) for row in outs[11:]))


def shards(
    linked,
    frames,
    lengths,
    span_starts,
    cotangent,
    query_weight,
    key_weight,
    value_weight,
    out_weight,
    up_weight,
    down_weight,
    query_bias,
    value_bias,
    up_bias,
    out_bias,
    down_bias,
    first_gain,
    first_shift,
    second_gain,
    second_shift,
    mask_vector,
):
    rows = frames.shape[0]
    n_dp = 768 // query_weight.shape[0]
    n_mp = 768 // query_weight.shape[1]
    vecs = (out_bias, down_bias, first_gain, first_shift, second_gain, second_shift, mask_vector)
    if linked:
        blocks, probs, out, masked, kept = run_forward_linked(
            rows, lengths, span_starts, frames, cotangent, query_weight, key_weight, value_weight, out_weight,
            up_weight, down_weight.T, query_bias, value_bias, up_bias, *vecs,
        )
        grads, totals, grad_frames = run_backward(True, blocks, probs, kept, masked, first_gain)
        return run_finish(n_dp, n_mp, grads, totals, out, grad_frames)
    z = lax.axis_index("mp")
    half = z % 2
    length = lax.dynamic_index_in_dim(lengths, z // 2, keepdims=False)
    starts = lax.dynamic_index_in_dim(span_starts, z // 2, keepdims=False)
    slots = (jnp.arange(LEN, dtype=jnp.int32) + half * rows) % LEN
    valid = slots < length
    masked = jnp.any((slots[:, None] >= starts[None, :]) & (slots[:, None] < starts[None, :] + SPAN), axis=1)
    keybias = jnp.where(
        (jnp.arange(128) == 0)[None, :] & ~valid[:, None], jnp.float32(NEGATIVE), 0.0
    ).astype(BF16)
    valid_rows = valid[:rows].astype(F32)[:, None]
    masked_rows = masked.astype(F32).reshape(2, rows, 1)
    x = jnp.where(masked[:rows, None], mask_vector[None, :], frames)
    pack = jnp.stack(pack_weights(query_weight, key_weight, value_weight, out_weight.T, up_weight, down_weight.T))
    bias = pack_biases(query_bias, value_bias, up_bias)
    mates = [(0, 1), (1, 0), (2, 3), (3, 2)]
    blocks = lax.all_gather(lax.all_gather(pack, "dp", axis=1, tiled=True), "mp", axis=1).reshape(BLOCKS)
    biases = lax.all_gather(bias, "mp", axis=0)
    both = jnp.stack([x, lax.ppermute(x, "mp", mates)])
    probs, out, kept = run_forward_alone(rows, blocks, biases, both, keybias, valid_rows, cotangent, *vecs)
    grads, totals, mate, grad_one = run_backward(False, blocks, probs, kept, masked_rows, first_gain)
    grads = grads.reshape(3, 4, 768, 768).astype(F32)
    grads = lax.psum_scatter(grads, "mp", scatter_dimension=1, tiled=False)
    grads = lax.psum_scatter(grads, "dp", scatter_dimension=1, tiled=True)
    totals = lax.psum(totals, ("dp", "mp"))
    grad_frames = grad_one + lax.ppermute(mate, "mp", mates).astype(F32)
    grad_frames = jnp.where(masked[:rows, None], 0.0, grad_frames).astype(BF16)
    return run_finish(n_dp, n_mp, grads, totals, out, grad_frames)


def solution(mesh):
    linked = mesh.shape["dp"] == 8 and mesh.shape["mp"] == 4
    split = P(("dp", "mp"))
    return jax.shard_map(
        functools.partial(shards, linked),
        mesh=mesh,
        in_specs=(
            P(("dp", "mp"), None),
            P("dp"),
            P("dp", None),
            P(("dp", "mp"), None),
            P("dp", "mp"),
            P("dp", "mp"),
            P("dp", "mp"),
            P("mp", "dp"),
            P("dp", "mp"),
            P("mp", "dp"),
            P("mp", None),
            P("mp", None),
            P("mp", None),
            *([P()] * 7),
        ),
        out_specs=(
            P(("dp", "mp"), None),
            P(("dp", "mp"), None),
            P("dp", "mp"),
            P("dp", "mp"),
            P("dp", "mp"),
            P("mp", "dp"),
            P("dp", "mp"),
            P("mp", "dp"),
            P("mp", "dp"),
            P("mp", "dp"),
            P("mp", "dp"),
            *([split] * 7),
        ),
        check_vma=False,
    )
```

```python
import functools
import math

import jax
import jax.numpy as jnp
from jax import lax
from jax.experimental import pallas as pl
from jax.experimental.pallas import tpu as pltpu
from jax.sharding import PartitionSpec as P

HEAD_DIM = 64
SPAN = 10
LEN = 1024
EPSILON = 1e-05
NEGATIVE = -1e30
SCALE = 1.0 / math.sqrt(HEAD_DIM)

F32 = jnp.float32
BF16 = jnp.bfloat16
MESH = pl.DeviceIdType.MESH
VMEM_LIMIT = 63 * 1024 * 1024

ATT, UP, DOWN = 0, 1, 2
PROJ = 640


def dot(left, right, contract=(1, 0)):
    return lax.dot_general(
        left, right, (((contract[0],), (contract[1],)), ((), ())), preferred_element_type=F32
    )


def hbm():
    return pl.BlockSpec(memory_space=pl.ANY)


def vmem():
    return pl.BlockSpec(memory_space=pltpu.VMEM)


class Place:
    def __init__(self):
        self.dp = lax.axis_index("dp")
        self.z = lax.axis_index("mp")
        self.c = lax.rem(self.dp, 2)
        self.x = lax.rem(self.dp // 2, 2)
        self.y = self.dp // 4
        self.core = (self.dp + 1 - 2 * self.c, self.z)
        self.across_x = (self.dp + 2 - 4 * self.x, self.z)
        self.across_y = (self.dp + 4 - 8 * self.y, self.z)
        self.right = (self.dp, self.z + 1)
        self.left = (self.dp, self.z - 1)
        self.mate = (self.dp, self.z + 1 - 2 * lax.rem(self.z, 2))
        self.far = (self.dp, lax.rem(self.z + 2, 4))

    def hello(self, far):
        barrier = pltpu.get_barrier_semaphore()

        def signal(device):
            pl.semaphore_signal(barrier, inc=1, device_id=device, device_id_type=MESH)

        signal(self.core)
        signal(self.across_x)
        signal(self.across_y)
        if far:
            signal(self.far)
        pl.when(self.z < 3)(lambda: signal(self.right))
        pl.when(self.z > 0)(lambda: signal(self.left))

    def meet(self, far):
        ends = jnp.where((self.z == 0) | (self.z == 3), 1, 2)
        pl.semaphore_wait(pltpu.get_barrier_semaphore(), (4 if far else 3) + ends)


def remote(src, dst, send, recv, device):
    return pltpu.make_async_remote_copy(
        src_ref=src, dst_ref=dst, send_sem=send, recv_sem=recv, device_id=device, device_id_type=MESH
    )


class Gather:
    def __init__(self, at, blocks, biases, z_send, z_recv, p_send, p_recv):
        self.at, self.blocks, self.biases = at, blocks, biases
        self.z_send, self.z_recv, self.p_send, self.p_recv = z_send, z_recv, p_send, p_recv

    def z_copy(self, kind, m, direction):
        at = self.at
        if kind == 3:
            ref = self.biases.at[m]
        else:
            ref = self.blocks.at[kind, m, at.y, at.x, at.c]
        device = at.right if direction == 0 else at.left
        return remote(ref, ref, self.z_send.at[kind, direction], self.z_recv.at[kind, m], device)

    def z_step(self, kind, step):
        z = self.at.z
        if step == 0:
            pl.when((z > 0) & (z < 2))(lambda: self.z_copy(kind, z, 1).start())
            pl.when(z < 3)(lambda: self.z_copy(kind, z, 0).start())
            pl.when(z >= 2)(lambda: self.z_copy(kind, z, 1).start())
            return

        def from_left():
            @pl.when(z >= step)
            def _():
                self.z_copy(kind, z - step, 0).wait_recv()
                if step < 3:
                    pl.when(z < 3)(lambda: self.z_copy(kind, z - step, 0).start())
                self.first(kind, z - step)

        def from_right():
            @pl.when(z + step <= 3)
            def _():
                self.z_copy(kind, z + step, 1).wait_recv()
                if step < 3:
                    pl.when(z > 0)(lambda: self.z_copy(kind, z + step, 1).start())
                self.first(kind, z + step)

        pl.when(z < 2)(from_right)
        from_left()
        pl.when(z >= 2)(from_right)

    def plane_copy(self, kind, m, which):
        recv = 0 if m is None else m
        at, block = self.at, self.blocks.at[kind, slice(None) if m is None else m]
        x, y, c = at.x, at.y, at.c
        low, high = pl.ds(0, 48), pl.ds(48, 48)
        every = (slice(None),) if m is None else ()
        ref, device = {
            0: lambda: (block.at[(*every, y, x, c, low)], at.across_x),
            1: lambda: (block.at[(*every, y, x, c, high)], at.across_y),
            2: lambda: (block.at[(*every, y, slice(None), c, low)], at.across_y),
            3: lambda: (block.at[(*every, slice(None), x, c, high)], at.across_x),
            4: lambda: (block.at[(*every, slice(None), slice(None), c)], at.core),
        }[which]()
        return remote(ref, ref, self.p_send.at[kind, which], self.p_recv.at[kind, recv, which], device)

    def at_step(self, step, act):
        z = self.at.z
        if step == 0:
            act(z)
            return
        pl.when(z >= step)(lambda: act(z - step))
        pl.when(z + step <= 3)(lambda: act(z + step))

    def order(self, step):
        z = self.at.z
        from_low = jnp.where(z == 1, jnp.where(step < 2, 1 - step, step), step)
        mirrored = 3 - z
        from_high = jnp.where(mirrored == 1, jnp.where(step < 2, 1 - step, step), step)
        return jnp.where(z < 2, from_low, 3 - from_high)

    def first(self, kind, m):
        if kind < 3:
            self.plane_copy(kind, m, 0).start()
            self.plane_copy(kind, m, 1).start()

    def second(self, kind, step):
        def act(m):
            self.plane_copy(kind, m, 0).wait_recv()
            self.plane_copy(kind, m, 2).start()
            self.plane_copy(kind, m, 1).wait_recv()
            self.plane_copy(kind, m, 3).start()

        self.at_step(step, act)

    def third(self, kind, step):
        def act(m):
            self.plane_copy(kind, m, 2).wait_recv()
            self.plane_copy(kind, m, 3).wait_recv()
            self.plane_copy(kind, m, 4).start()

        self.at_step(step, act)

    def last(self, kind):
        for m in range(4):
            self.plane_copy(kind, m, 4).wait_recv()

    def drain(self):
        z = self.at.z
        for kind in range(4):
            for here in range(4):
                for direction, count in ((0, here + 1), (1, 4 - here)):
                    if (direction == 0 and here < 3) or (direction == 1 and here > 0):
                        pl.when(z == here)(self.z_copy(kind, pl.ds(0, count), direction).wait_send)
        for kind in range(3):
            for which in range(5):
                self.plane_copy(kind, None, which).wait_send()


def block_of(blocks, kind, m, low=0, width=768):
    return blocks[kind, m, :, :, :, :, pl.ds(low, width)].reshape(768, width)


def lane_mask(rows, lower):
    lanes = lax.broadcasted_iota(jnp.int32, (rows, 128), 1)
    return (lanes < 64) if lower else (lanes >= 64)


def forward_compute(
    blocks,
    biases,
    xs,
    keybias_ref,
    valid_ref,
    cot_ref,
    vec_ref,
    probs_hbm,
    out_hbm,
    outs_hbm,
    outs_ref,
    outs_sem,
    k_ref,
    vt_ref,
    probs,
    probs_sem,
    total,
    low,
    stats,
    out_ref,
    out_sem,
    hooks,
):
    rows = xs.shape[1]
    (recip_ref, headout_ref, xt_ref, qm_ref, kt_ref, v_ref, att_ref, acted_ref, slope_ref, n1t_ref, n1_ref, rs1_ref,
     gb2_ref, g2_ref, sums_ref) = outs_ref
    keeps = [
        pltpu.make_async_copy(ref, to, outs_sem.at[i]) for i, (ref, to) in enumerate(zip(outs_ref, outs_hbm, strict=True))
    ]

    def keep(*which):
        for i in which:
            keeps[i].start()

    xt_ref[0] = xs[0].T
    ones_lane = jnp.where(lax.broadcasted_iota(jnp.int32, (rows, 128), 1) == 0, 1.0, 0.0).astype(BF16)

    def probs_copy(head, side, slot):
        return pltpu.make_async_copy(
            probs.at[slot], probs_hbm.at[head, pl.ds(side * rows, rows)], probs_sem.at[slot]
        )

    own_rows, other_rows = pl.ds(0, rows), pl.ds(rows, rows)

    def project(m, _):
        bias = biases[m, 0:1, :].astype(F32)[:, :PROJ]
        own = dot(xs[0], block_of(blocks, ATT, m, 0, PROJ)) + bias
        k_ref[2 * m, own_rows] = own[:, 128:256].astype(BF16)
        v_ref[2 * m, own_rows] = own[:, 256:384].astype(BF16)
        k_ref[2 * m + 1, own_rows] = own[:, 384:512].astype(BF16)
        v_ref[2 * m + 1, own_rows] = own[:, 512:640].astype(BF16)
        lower, upper = lane_mask(rows, True), lane_mask(rows, False)
        pair = own[:, 0:128].astype(BF16).astype(F32) * SCALE
        single = pltpu.roll(own[:, 384:512].astype(BF16).astype(F32) * SCALE, 64, 1)
        qm_ref[3 * m] = jnp.where(lower, pair, 0.0).astype(BF16)
        qm_ref[3 * m + 1] = jnp.where(upper, pair, 0.0).astype(BF16)
        qm_ref[3 * m + 2] = jnp.where(upper, single, 0.0).astype(BF16)
        for tile in range(2):
            kt_ref[2 * m + tile, :, own_rows] = k_ref[2 * m + tile, own_rows].T
            vt_ref[2 * m + tile, :, own_rows] = v_ref[2 * m + tile, own_rows].T
        hooks.after("project", m)
        return 0

    def project_other(m, _):
        bias = biases[m, 0:1, :].astype(F32)[:, 128:PROJ]
        other = dot(xs[1], block_of(blocks, ATT, m, 128, 512)) + bias
        k_ref[2 * m, other_rows] = other[:, 0:128].astype(BF16)
        v_ref[2 * m, other_rows] = other[:, 128:256].astype(BF16)
        k_ref[2 * m + 1, other_rows] = other[:, 256:384].astype(BF16)
        v_ref[2 * m + 1, other_rows] = other[:, 384:512].astype(BF16)
        for tile in range(2):
            kt_ref[2 * m + tile, :, other_rows] = k_ref[2 * m + tile, other_rows].T
            vt_ref[2 * m + tile, :, other_rows] = v_ref[2 * m + tile, other_rows].T
        return 0

    def attend_half(m, side):
        half = own_rows if side == 0 else other_rows

        def free():
            for j in range(3):
                probs_copy(3 * m + j, side, j).wait()

        if side == 0:
            pl.when(m > 0)(free)
        else:
            free()
        scores, tops, sums, outs = [], [], [], []
        for j in range(3):
            keys = jnp.concatenate([k_ref[2 * m + j // 2, half], keybias_ref[half, :]], axis=1)
            queries = jnp.concatenate([qm_ref[3 * m + j], ones_lane], axis=1)
            scores.append(dot(keys, queries, (1, 1)))
        for j in range(3):
            top = jnp.max(scores[j], axis=0, keepdims=True)
            weights = jnp.exp(scores[j] - top)
            tops.append(top)
            sums.append(jnp.sum(weights, axis=0, keepdims=True))
            probs[j] = weights.astype(BF16)
            lane = 64 * (j % 2)
            outs.append(dot(vt_ref[2 * m + j // 2, lane : lane + 64, half], probs[j]))
            headout_ref[3 * m + j, side] = outs[j]
        return tops, sums, outs

    def send_probs(m, side):
        for j in range(3):
            probs_copy(3 * m + j, side, j).start()

    def attend_own(m, _):
        tops, sums, _ = attend_half(m, 0)
        for j in range(3):
            stats[3 * m + j, 0:1, :] = tops[j]
            stats[3 * m + j, 1:2, :] = sums[j]
        send_probs(m, 0)
        hooks.after("own", m)
        return 0

    def attend(m, _):
        tops, sums, outs = attend_half(m, 1)
        pieces = [jnp.zeros((64, rows), BF16), None, None, None]
        for j in range(3):
            head = 3 * m + j
            top_own = stats[head, 0:1, :]
            top_all = jnp.maximum(tops[j], top_own)
            factor, factor_own = jnp.exp(tops[j] - top_all), jnp.exp(top_own - top_all)
            recip = 1.0 / (factor_own * stats[head, 1:2, :] + factor * sums[j])
            factor, factor_own = factor * recip, factor_own * recip
            recip_ref[head] = jnp.concatenate([factor_own, factor, jnp.zeros((6, rows), F32)], axis=0)
            pieces[(2, 3, 1)[j]] = (headout_ref[head, 0] * factor_own + outs[j] * factor).astype(BF16)
        att_ref[m] = jnp.concatenate(pieces, axis=0).T
        send_probs(m, 1)
        hooks.after("other", m)
        return 0

    hooks.before("project")
    lax.fori_loop(0, 4, project, 0)
    lax.fori_loop(0, 4, attend_own, 0)
    hooks.before("other")
    xt_ref[1] = xs[1].T
    lax.fori_loop(0, 4, project_other, 0)
    keep(2, 3, 4, 5)
    hooks.after("swapped")
    lax.fori_loop(0, 4, attend, 0)
    keep(0, 1, 6)
    branch = [dot(att_ref[m], block_of(blocks, ATT, m, 512, 256), (1, 1)) for m in range(4)]
    total[...] = (branch[0] + branch[1]) + (branch[2] + branch[3])
    for j in range(3):
        probs_copy(9 + j, 1, j).wait()

    chunk = 64

    def norm_one(i, _):
        r = pl.ds(pl.multiple_of(i * chunk, chunk), chunk)
        resid = xs[0, r, :].astype(F32) + total[r, :] + vec_ref[0:1, :]
        centered = resid - jnp.mean(resid, axis=1, keepdims=True)
        rstd = lax.rsqrt(jnp.mean(centered * centered, axis=1, keepdims=True) + EPSILON)
        unit = centered * rstd
        n1_ref[r, :] = unit
        rs1_ref[r, :] = rstd
        low[r, :] = (unit * vec_ref[2:3, :] + vec_ref[3:4, :]).astype(BF16)
        return 0

    lax.fori_loop(0, rows // chunk, norm_one, 0, unroll=2)
    n1t_ref[...] = low[...].T
    keep(9, 10, 11)
    hooks.after("norm")
    hooks.before("feed")

    def feed(m, _):
        pre = dot(low[...], block_of(blocks, UP, m)) + biases[m, 1:2, :].astype(F32)
        phi = 0.5 * (1.0 + lax.erf(pre * (1.0 / math.sqrt(2.0))))
        acted_ref[m] = (pre * phi).astype(BF16)
        slope_ref[m] = (phi + pre * jnp.exp(-0.5 * pre * pre) * (1.0 / math.sqrt(2.0 * math.pi))).astype(BF16)
        hooks.after("feed", m)
        return 0

    lax.fori_loop(0, 4, feed, 0)
    keep(7, 8)

    def down(steps):
        places = [hooks.order(step) for step in steps]
        for m in places:
            hooks.landed(DOWN, m)
        shares = [dot(acted_ref[m], block_of(blocks, DOWN, m), (1, 1)) for m in places]
        return functools.reduce(jnp.add, shares)

    hooks.before("down")
    total[...] = down((0, 1, 2))
    total[...] += down((3,))
    hooks.all_landed()

    def norm_two(i, sums):
        r = pl.ds(pl.multiple_of(i * chunk, chunk), chunk)
        normed = n1_ref[r, :] * vec_ref[2:3, :] + vec_ref[3:4, :]
        resid = normed + total[r, :] + vec_ref[1:2, :]
        centered = resid - jnp.mean(resid, axis=1, keepdims=True)
        rstd = lax.rsqrt(jnp.mean(centered * centered, axis=1, keepdims=True) + EPSILON)
        unit = centered * rstd
        valid = valid_ref[r, :]
        out_ref[r, :] = (valid * (unit * vec_ref[4:5, :] + vec_ref[5:6, :])).astype(BF16)
        grad = valid * cot_ref[r, :].astype(F32)
        scaled = grad * vec_ref[4:5, :]
        grad_in = (
            scaled
            - jnp.mean(scaled, axis=1, keepdims=True)
            - unit * jnp.mean(scaled * unit, axis=1, keepdims=True)
        ) * rstd
        g2_ref[r, :] = grad_in
        gb2_ref[r, :] = grad_in.astype(BF16)
        for i, (ref, to) in enumerate(((out_ref, out_hbm), (g2_ref, outs_hbm[13]), (gb2_ref, outs_hbm[12]))):
            pltpu.make_async_copy(ref.at[r], to.at[r], out_sem.at[i]).start()
        return (
            sums[0] + jnp.sum(grad_in, axis=0, keepdims=True),
            sums[1] + jnp.sum(grad * unit, axis=0, keepdims=True),
            sums[2] + jnp.sum(grad, axis=0, keepdims=True),
        )

    zero = jnp.zeros((1, 768), F32)
    sums = lax.fori_loop(0, rows // chunk, norm_two, (zero, zero, zero), unroll=2)
    sums_ref[...] = jnp.concatenate([*sums, jnp.zeros((5, 768), F32)], axis=0)
    keep(14)
    hooks.finish()
    for i, copy in enumerate(keeps):
        if i not in (12, 13):
            copy.wait()
    for i, (ref, to) in enumerate(((out_ref, out_hbm), (g2_ref, outs_hbm[13]), (gb2_ref, outs_hbm[12]))):
        pltpu.make_async_copy(ref, to, out_sem.at[i]).wait()


class NoHooks:
    def after(self, point, m=0):
        pass

    def before(self, point):
        pass

    def order(self, step):
        return step

    def landed(self, kind, m):
        pass

    def all_landed(self):
        pass

    def finish(self):
        pass


class GatherHooks:
    MIDDLE = {
        ("project", 1): (("z_step", DOWN, 1),),
        ("project", 3): (("second", UP, 0), ("second", UP, 1)),
        ("own", 0): (("second", UP, 2),),
        ("own", 1): (("z_step", DOWN, 2), ("second", DOWN, 0), ("third", UP, 0)),
        ("own", 3): (("second", DOWN, 1),),
        ("swapped", 0): (("third", UP, 1),),
        ("other", 0): (("second", DOWN, 2), ("third", UP, 2)),
        ("other", 2): (("third", DOWN, 0),),
        ("norm", 0): (("third", DOWN, 1),),
        ("feed", 1): (("third", DOWN, 2),),
    }
    END = {
        ("project", 1): (("second", UP, 0),),
        ("project", 3): (("second", UP, 1), ("z_step", UP, 2)),
        ("own", 0): (("second", DOWN, 0),),
        ("own", 1): (("third", UP, 0),),
        ("own", 2): (("second", UP, 2), ("third", UP, 1)),
        ("swapped", 0): (("z_step", UP, 3), ("third", DOWN, 0)),
        ("other", 0): (("z_step", DOWN, 1), ("third", UP, 2)),
        ("other", 1): (("second", UP, 3), ("z_step", DOWN, 2)),
        ("other", 2): (("second", DOWN, 1),),
        ("other", 3): (("z_step", DOWN, 3), ("second", DOWN, 2)),
        ("norm", 0): (("third", UP, 3),),
        ("feed", 0): (("second", DOWN, 3),),
        ("feed", 1): (("third", DOWN, 1),),
        ("feed", 3): (("third", DOWN, 2),),
        ("down", 0): (("third", DOWN, 3),),
    }

    def __init__(self, gather, swap, blocks_out, keep_sem):
        self.gather, self.swap = gather, swap
        z = gather.at.z
        self.at_end = (z == 0) | (z == 3)
        self.keep = [
            pltpu.make_async_copy(gather.blocks.at[kind], blocks_out.at[kind], keep_sem.at[kind]) for kind in range(3)
        ]

    def after(self, point, m=0):
        for table, here in ((self.MIDDLE, ~self.at_end), (self.END, self.at_end)):
            for (name, index), events in table.items():
                if name == point:

                    def act(events=events):
                        for step, *which in events:
                            getattr(self.gather, step)(*which)

                    pl.when(here if isinstance(m, int) else here & (m == index))(act)

    def before(self, point):
        if point == "project":
            self.gather.last(ATT)
            self.keep[ATT].start()
        if point == "other":
            self.swap.wait()
        if point == "feed":
            self.gather.last(UP)
            self.keep[UP].start()
        if point == "down":
            self.after("down")

    def order(self, step):
        return self.gather.order(step)

    def landed(self, kind, m):
        self.gather.plane_copy(kind, m, 4).wait_recv()

    def all_landed(self):
        self.keep[DOWN].start()

    def finish(self):
        for copy in self.keep:
            copy.wait()
        self.gather.drain()


N_KEPT = 15


def pack_weights(query, key, value, out_t, up, down_t):
    pair, single = 2 * HEAD_DIM, 3 * HEAD_DIM
    att = jnp.concatenate(
        [
            query[:, :pair], key[:, :pair], value[:, :pair],
            query[:, pair:single], key[:, pair:single],
            value[:, pair:single], out_t[:, pair:single], out_t[:, :pair],
        ],
        axis=1,
    )
    return att, up, down_t


def pack_biases(query_bias, value_bias, up_bias):
    def row(i, bias):
        return bias[i : i + 1, :]

    blank = jnp.zeros((1, HEAD_DIM), BF16)
    pieces = [
        row(0, query_bias), row(1, query_bias), blank, blank, row(0, value_bias), row(1, value_bias),
        row(2, query_bias), blank, row(2, value_bias), blank, blank, blank,
    ]
    ups = jnp.concatenate([row(i, up_bias) for i in range(6)], axis=1)
    return jnp.concatenate([jnp.concatenate(pieces, axis=1), ups, jnp.zeros((14, 768), BF16)], axis=0)


def fill_vectors(vec, vecs):
    for i, ref in enumerate(vecs):
        vec[i : i + 1, :] = ref[...].astype(F32).reshape(1, 768)


def transposed(block):
    wide = jnp.concatenate([block, jnp.zeros((block.shape[0], 128 - block.shape[1]), block.dtype)], axis=1)
    return wide.T[: block.shape[1]]


def forward_linked(*refs):
    (lengths, starts, frames, cot, query, key, value, out_w, up, down, query_bias, value_bias, up_bias) = refs[:13]
    vecs, refs = refs[13:20], refs[20:]
    blocks_hbm, probs_hbm, out_hbm, masked_hbm, *outs = refs[: 4 + N_KEPT]
    blocks, biases, xs, keybias, valid, vec, masked_ref, masked_sem, *scratch = refs[4 + N_KEPT :]
    scratch, links = scratch[:N_FORWARD_SCRATCH], scratch[N_FORWARD_SCRATCH:]
    z_send, z_recv, p_send, p_recv, x_send, x_recv, keep_sem = links
    at = Place()
    at.hello(False)
    at.meet(False)
    gather = Gather(at, blocks, biases, z_send, z_recv, p_send, p_recv)
    packs = pack_weights(
        query[...], key[...], value[...], transposed(out_w[...]), up[...], down[...]
    )
    for kind in range(3):
        blocks[kind, at.z, at.y, at.x, at.c] = packs[kind]
        if kind == 0:
            gather.z_step(ATT, 0)
        gather.first(kind, at.z)
    biases[at.z] = pack_biases(query_bias[...], value_bias[...], up_bias[...])
    gather.z_step(3, 0)
    at_end = (at.z == 0) | (at.z == 3)

    @pl.when(at_end)
    def _():
        gather.z_step(UP, 0)
        gather.z_step(DOWN, 0)

    fill_vectors(vec, vecs)
    rows = frames.shape[0]
    clip, half = at.z // 2, lax.rem(at.z, 2)
    length = lengths[clip]
    start = starts[pl.ds(clip, 1), :]
    for side in range(2):
        first = rows * (half if side == 0 else 1 - half)
        slots = first + lax.broadcasted_iota(jnp.int32, (rows, start.shape[1]), 0)
        covered = jnp.where((slots >= start) & (slots < start + SPAN), 1.0, 0.0)
        masked_ref[side] = jnp.max(covered, axis=1, keepdims=True)
        slots = first + lax.broadcasted_iota(jnp.int32, (rows, 128), 0)
        lanes = lax.broadcasted_iota(jnp.int32, (rows, 128), 1)
        here = pl.ds(side * rows, rows)
        keybias[here, :] = jnp.where((slots >= length) & (lanes == 0), NEGATIVE, 0.0).astype(BF16)
        if side == 0:
            valid[...] = jnp.where(slots[:, 0:1] < length, 1.0, 0.0)
    masked_copy = pltpu.make_async_copy(masked_ref, masked_hbm, masked_sem)
    masked_copy.start()
    xs[0] = jnp.where(masked_ref[0] > 0, vec[6:7, :], frames[...].astype(F32)).astype(BF16)
    swap = remote(xs.at[0], xs.at[1], x_send, x_recv, at.mate)
    pl.when(at_end)(swap.start)
    gather.z_step(ATT, 1)
    gather.z_step(3, 1)
    gather.second(ATT, 0)
    gather.z_step(ATT, 2)
    gather.z_step(3, 2)

    @pl.when(~at_end)
    def _():
        gather.z_step(UP, 0)

    gather.second(ATT, 1)
    gather.third(ATT, 0)
    gather.z_step(ATT, 3)
    gather.z_step(3, 3)
    gather.second(ATT, 2)
    gather.z_step(UP, 1)
    pl.when(~at_end)(swap.start)
    gather.third(ATT, 1)
    gather.second(ATT, 3)
    gather.third(ATT, 2)

    @pl.when(~at_end)
    def _():
        gather.z_step(UP, 2)
        gather.z_step(DOWN, 0)

    gather.third(ATT, 3)
    hooks = GatherHooks(gather, swap, blocks_hbm, keep_sem)
    forward_compute(blocks, biases, xs, keybias, valid, cot, vec, probs_hbm, out_hbm, outs, *scratch, hooks)
    masked_copy.wait()


def forward_alone(blocks_in, biases, xs, keybias, valid, cot, *refs):
    vecs, (probs_hbm, out_hbm, *outs), scratch = refs[:7], refs[7 : 9 + N_KEPT], refs[9 + N_KEPT :]
    blocks, vec, *scratch, keep_sem = scratch
    fill_vectors(vec, vecs)
    load = pltpu.make_async_copy(blocks_in, blocks, keep_sem)
    load.start()
    load.wait()
    forward_compute(
        blocks, biases, xs, keybias, valid, cot, vec, probs_hbm, out_hbm, outs, *scratch, NoHooks()
    )


BLOCKS = (3, 4, 2, 2, 2, 96, 768)


def forward_outs(rows):
    def of(shape, dtype):
        return jax.ShapeDtypeStruct(shape, dtype)

    return [
        of((12, 8, rows), F32),
        of((12, 2, 64, rows), F32),
        of((2, 768, rows), BF16),
        of((12, rows, 128), BF16),
        of((8, 128, LEN), BF16),
        of((8, LEN, 128), BF16),
        of((4, rows, 256), BF16),
        of((4, rows, 768), BF16),
        of((4, rows, 768), BF16),
        of((768, rows), BF16),
        of((rows, 768), F32),
        of((rows, 1), F32),
        of((rows, 768), BF16),
        of((rows, 768), F32),
        of((8, 768), F32),
    ]


N_FORWARD_SCRATCH = 11


def forward_scratch(rows):
    return [
        [pltpu.VMEM(out.shape, out.dtype) for out in forward_outs(rows)],
        pltpu.SemaphoreType.DMA((N_KEPT,)),
        pltpu.VMEM((8, LEN, 128), BF16),
        pltpu.VMEM((8, 128, LEN), BF16),
        pltpu.VMEM((3, rows, rows), BF16),
        pltpu.SemaphoreType.DMA((3,)),
        pltpu.VMEM((rows, 768), F32),
        pltpu.VMEM((rows, 768), BF16),
        pltpu.VMEM((12, 8, rows), F32),
        pltpu.VMEM((rows, 768), BF16),
        pltpu.SemaphoreType.DMA((3,)),
    ]


def run_forward_linked(rows, *ins):
    outs = forward_outs(rows)
    probs = jax.ShapeDtypeStruct((12, LEN, rows), BF16)
    frames = jax.ShapeDtypeStruct((rows, 768), BF16)
    masked = jax.ShapeDtypeStruct((2, rows, 1), F32)
    blocks, probs, frames, masked, *kept = pl.pallas_call(
        forward_linked,
        name="forward",
        out_shape=[jax.ShapeDtypeStruct(BLOCKS, BF16), probs, frames, masked, *outs],
        in_specs=[pl.BlockSpec(memory_space=pltpu.SMEM)] + [vmem()] * 19,
        out_specs=[hbm()] * (4 + N_KEPT),
        scratch_shapes=[
            pltpu.VMEM(BLOCKS, BF16),
            pltpu.VMEM((4, 16, 768), BF16),
            pltpu.VMEM((2, rows, 768), BF16),
            pltpu.VMEM((LEN, 128), BF16),
            pltpu.VMEM((rows, 1), F32),
            pltpu.VMEM((8, 768), F32),
            pltpu.VMEM((2, rows, 1), F32),
            pltpu.SemaphoreType.DMA,
            *forward_scratch(rows),
            pltpu.SemaphoreType.DMA((4, 2)),
            pltpu.SemaphoreType.DMA((4, 4)),
            pltpu.SemaphoreType.DMA((3, 5)),
            pltpu.SemaphoreType.DMA((3, 4, 5)),
            pltpu.SemaphoreType.DMA,
            pltpu.SemaphoreType.DMA,
            pltpu.SemaphoreType.DMA((3,)),
        ],
        compiler_params=pltpu.CompilerParams(
            collective_id=0, has_side_effects=True, vmem_limit_bytes=VMEM_LIMIT
        ),
    )(*ins)
    return blocks, probs, frames, masked, kept


def run_forward_alone(rows, *ins):
    probs = jax.ShapeDtypeStruct((12, LEN, rows), BF16)
    frames = jax.ShapeDtypeStruct((rows, 768), BF16)
    probs, frames, *kept = pl.pallas_call(
        forward_alone,
        name="forward",
        out_shape=[probs, frames, *forward_outs(rows)],
        in_specs=[hbm()] + [vmem()] * 12,
        out_specs=[hbm()] * (2 + N_KEPT),
        scratch_shapes=[pltpu.VMEM(BLOCKS, BF16), pltpu.VMEM((8, 768), F32), *forward_scratch(rows), pltpu.SemaphoreType.DMA],
        compiler_params=pltpu.CompilerParams(vmem_limit_bytes=VMEM_LIMIT),
    )(*ins)
    return probs, frames, kept


ATT_ORDER = (0, 3, 1, 2)
DOWN_ORDER = (3, 0, 2, 1)
DEEP = 32


def att_order(place):
    return jnp.where(place == 0, 0, jnp.where(place == 1, 3, place - 1))


def down_order(place):
    return jnp.where(place == 0, 3, jnp.where(place == 1, 0, 4 - place))


def row_parts(kind):
    base = DEEP if kind == DOWN else 0
    half = (96 - base) // 2
    return pl.ds(base, half), pl.ds(base + half, half), pl.ds(base, 2 * half)


def chunk_at(n):
    return (DOWN, DOWN_ORDER[n]) if n < 4 else (UP, n - 4) if n < 8 else (ATT, ATT_ORDER[n - 8])


ALL = pl.ds(0, 3)


class Scatter:
    def __init__(self, at, grads, out, buffers, semaphores):
        self.at, self.grads, self.out = at, grads, out
        self.core_in, self.first_in, self.second_in, self.z_in, self.deep_in, self.plane_in = buffers
        self.send, self.recv, self.z_send, self.z_recv, *deep = semaphores
        self.deep_send, self.deep_recv, self.plane_send, self.plane_recv = deep

    def copy(self, kind, m, which):
        every, index = ((slice(None),), slice(None)) if m is None else ((), m)
        recv = 0 if m is None else m
        at, grads = self.at, self.grads.at[kind, index]
        x, y, c = at.x, at.y, at.c
        low, high, _ = row_parts(kind)
        core, first, second = self.core_in.at[kind, index], self.first_in.at[kind, index], self.second_in.at[kind, index]
        part, whole = pl.ds(0, low.size), slice(None)
        src, dst, device = {
            0: lambda: (grads.at[(*every, whole, whole, 1 - c)], core, at.core),
            1: lambda: (grads.at[(*every, whole, 1 - x, c, low)], first.at[(*every, 0, whole, part)], at.across_x),
            2: lambda: (grads.at[(*every, 1 - y, whole, c, high)], first.at[(*every, 1, whole, part)], at.across_y),
            3: lambda: (grads.at[(*every, 1 - y, x, c, low)], second.at[(*every, 0, part)], at.across_y),
            4: lambda: (grads.at[(*every, y, 1 - x, c, high)], second.at[(*every, 1, part)], at.across_x),
        }[which]()
        return remote(src, dst, self.send.at[kind, which], self.recv.at[kind, recv, which], device)

    def add(self, ref, got):
        ref[...] = (ref[...].astype(F32) + got[...].astype(F32)).astype(BF16)

    def begin(self, kind, m):
        self.copy(kind, m, 0).start()

    def first(self, kind, m):
        at, grads = self.at, self.grads.at[kind, m]
        self.copy(kind, m, 0).wait_recv()
        for y in range(2):
            for x in range(2):
                self.add(grads.at[y, x, at.c], self.core_in.at[kind, m, y, x])
        self.copy(kind, m, 1).start()
        self.copy(kind, m, 2).start()
        if kind == DOWN:
            self.ends(m, lambda direction: self.deep_copy(m, direction).start())

    def second(self, kind, m):
        at, grads = self.at, self.grads.at[kind, m]
        low, high, _ = row_parts(kind)
        part = pl.ds(0, low.size)
        self.copy(kind, m, 1).wait_recv()
        for y in range(2):
            self.add(grads.at[y, at.x, at.c, low], self.first_in.at[kind, m, 0, y, part])
        self.copy(kind, m, 3).start()
        self.copy(kind, m, 2).wait_recv()
        for x in range(2):
            self.add(grads.at[at.y, x, at.c, high], self.first_in.at[kind, m, 1, x, part])
        self.copy(kind, m, 4).start()

    def third(self, kind, m):
        at = self.at
        grads = self.grads.at[kind, m, at.y, at.x, at.c]
        low, high, _ = row_parts(kind)
        part = pl.ds(0, low.size)
        self.copy(kind, m, 3).wait_recv()
        self.add(grads.at[low], self.second_in.at[kind, m, 0, part])
        self.copy(kind, m, 4).wait_recv()
        self.add(grads.at[high], self.second_in.at[kind, m, 1, part])
        self.z_start(kind, m)

    def ends(self, m, act):
        z = self.at.z
        if m > 0:
            pl.when(z == 0)(lambda: act(0))
        if m < 3:
            pl.when(z == 3)(lambda: act(1))

    def deep_copy(self, m, direction, slot=None):
        at = self.at
        device = at.mate if slot is ALL else at.right if direction == 0 else at.left
        if slot is None:
            slot = m if direction == 0 else jnp.where(m == at.z - 1, 4, m)
        recv = slot if slot is not ALL else 0
        src = self.grads.at[DOWN, m, :, :, at.c, pl.ds(0, DEEP)]
        return remote(src, self.deep_in.at[slot], self.deep_send, self.deep_recv.at[recv], device)

    def deep_add(self, m, slot, direction):
        self.deep_copy(m, direction, slot).wait_recv()
        for y in range(2):
            for x in range(2):
                self.add(self.grads.at[DOWN, m, y, x, self.at.c, pl.ds(0, DEEP)], self.deep_in.at[slot, y, x])

    def deep_relay(self, m, direction):
        self.deep_add(m, m, direction)
        self.deep_copy(m, direction).start()

    def deep_one(self, kind, m):
        z = self.at.z
        if m > 1:
            pl.when(z == 1)(lambda: self.deep_relay(m, 0))
        else:
            pl.when(z == 2)(lambda: self.deep_relay(m, 1))

    def deep_two(self, kind, m):
        z = self.at.z
        if m == 3:
            pl.when(z == 2)(lambda: self.deep_relay(m, 0))
        if m == 0:
            pl.when(z == 1)(lambda: self.deep_relay(m, 1))

    def deep_plane(self, which):
        at, grads = self.at, self.grads.at[DOWN, self.at.z]
        x, y, c = at.x, at.y, at.c
        half = DEEP // 2
        low, high = pl.ds(0, half), pl.ds(half, half)
        src, dst, device = {
            0: lambda: (grads.at[:, 1 - x, c, low], self.plane_in.at[0], at.across_x),
            1: lambda: (grads.at[1 - y, :, c, high], self.plane_in.at[1], at.across_y),
            2: lambda: (grads.at[1 - y, x, c, low], self.plane_in.at[2, 0], at.across_y),
            3: lambda: (grads.at[y, 1 - x, c, high], self.plane_in.at[2, 1], at.across_x),
        }[which]()
        return remote(src, dst, self.plane_send.at[which], self.plane_recv.at[which], device)

    def deep_first(self):
        z = self.at.z
        pl.when(z > 0)(lambda: self.deep_add(z, z, 0))
        pl.when(z < 3)(lambda: self.deep_add(z, 4, 1))
        self.deep_plane(0).start()
        self.deep_plane(1).start()

    def deep_second(self):
        at, half = self.at, DEEP // 2
        grads = self.grads.at[DOWN, at.z]
        self.deep_plane(0).wait_recv()
        for y in range(2):
            self.add(grads.at[y, at.x, at.c, pl.ds(0, half)], self.plane_in.at[0, y])
        self.deep_plane(2).start()
        self.deep_plane(1).wait_recv()
        for x in range(2):
            self.add(grads.at[at.y, x, at.c, pl.ds(half, half)], self.plane_in.at[1, x])
        self.deep_plane(3).start()

    def deep_third(self):
        at, half = self.at, DEEP // 2
        grads = self.grads.at[DOWN, at.z, at.y, at.x, at.c]
        self.deep_plane(2).wait_recv()
        self.add(grads.at[pl.ds(0, half)], self.plane_in.at[2, 0])
        self.deep_plane(3).wait_recv()
        self.add(grads.at[pl.ds(half, half)], self.plane_in.at[2, 1])

    def z_copy(self, kind, m, direction, slot=None):
        at = self.at
        whole = row_parts(kind)[2]
        device = at.mate if slot is ALL else at.right if direction == 0 else at.left
        if slot is None:
            slot = m if direction == 0 else jnp.where(m == at.z - 1, 4, m)
        recv = slot if slot is not ALL else 0
        src = self.grads.at[kind, m, at.y, at.x, at.c, whole]
        dst = self.z_in.at[kind, slot, whole]
        return remote(src, dst, self.z_send.at[kind], self.z_recv.at[kind, recv], device)

    def relay(self, kind, m, direction):
        whole = row_parts(kind)[2]
        self.z_copy(kind, m, direction, m).wait_recv()
        self.add(self.grads.at[kind, m, self.at.y, self.at.x, self.at.c, whole], self.z_in.at[kind, m, whole])
        self.z_copy(kind, m, direction).start()

    def z_start(self, kind, m):
        self.ends(m, lambda direction: self.z_copy(kind, m, direction).start())

    def z_one(self, kind, m):
        z = self.at.z
        if m > 1:
            pl.when(z == 1)(lambda: self.relay(kind, m, 0))
        else:
            pl.when(z == 2)(lambda: self.relay(kind, m, 1))

    def z_two(self, kind, m):
        z = self.at.z
        if m == 3:
            pl.when(z == 2)(lambda: self.relay(kind, m, 0))
        if m == 0:
            pl.when(z == 1)(lambda: self.relay(kind, m, 1))

    def finish(self, kind):
        at, z = self.at, self.at.z
        whole = row_parts(kind)[2]
        self.out[kind] = self.grads[kind, z, at.y, at.x, at.c].astype(F32)

        @pl.when(z > 0)
        def _():
            self.z_copy(kind, z, 0, z).wait_recv()
            self.out[kind, whole] += self.z_in[kind, z, whole].astype(F32)

        @pl.when(z < 3)
        def _():
            self.z_copy(kind, z, 1, 4).wait_recv()
            self.out[kind, whole] += self.z_in[kind, 4, whole].astype(F32)

    def run(self, **steps):
        for name, places in steps.items():
            for n in places:
                getattr(self, name)(*chunk_at(n))

    def drain(self):
        for which in range(4):
            self.deep_plane(which).wait_send()
        self.deep_copy(ALL, 0, ALL).wait_send()
        for kind in range(3):
            for which in range(5):
                self.copy(kind, None, which).wait_send()
            self.z_copy(kind, ALL, 0, ALL).wait_send()


class Totals:
    def __init__(self, at, rows, got, send, recv):
        self.rows, self.got, self.send, self.recv = rows, got, send, recv
        self.partners = (at.core, at.mate, at.far, at.across_x, at.across_y)

    def copy(self, stage):
        return remote(
            self.rows.at[stage], self.got.at[stage], self.send.at[stage], self.recv.at[stage], self.partners[stage]
        )

    def start(self, stage):
        self.copy(stage).start()

    def finish(self, stage):
        self.copy(stage).wait()
        self.rows[stage + 1] = self.rows[stage] + self.got[stage]


def backward_compute(
    blocks_hbm,
    probs_hbm,
    acted_hbm,
    slope_hbm,
    recip_hbm,
    headout_hbm,
    xt_hbm,
    qm_hbm,
    kt_hbm,
    v_hbm,
    att_hbm,
    n1t_hbm,
    n1_hbm,
    rs1_hbm,
    gb2_hbm,
    g2_hbm,
    sums_hbm,
    masked_hbm,
    gain_ref,
    grads,
    rows_ref,
    weight,
    weight_sem,
    acts,
    acts_sem,
    probs,
    probs_sem,
    gb1,
    gb1t,
    grad_one,
    parts,
    g2_ref,
    state_sem,
    gb2_ref,
    gb2t_ref,
    n1t_ref,
    xt_ref,
    headout_ref,
    qm_ref,
    kt_ref,
    v_ref,
    att_ref,
    head_sem,
    own,
    sides,
    shifts,
    shares,
    recip_ref,
    rs1_ref,
    sums_ref,
    masked_ref,
    small_sem,
    hooks,
):
    rows = g2_ref.shape[0]
    g2_load = pltpu.make_async_copy(g2_hbm, g2_ref, state_sem.at[0])
    n1_load = pltpu.make_async_copy(n1_hbm, grad_one, state_sem.at[1])
    gb2_load = pltpu.make_async_copy(gb2_hbm, gb2_ref, state_sem.at[2])
    n1t_load = pltpu.make_async_copy(n1t_hbm, n1t_ref, state_sem.at[4])
    xt_load = pltpu.make_async_copy(xt_hbm, xt_ref, state_sem.at[5])

    small_loads = [
        pltpu.make_async_copy(src, dst, small_sem.at[i])
        for i, (src, dst) in enumerate(
            ((recip_hbm, recip_ref), (rs1_hbm, rs1_ref), (sums_hbm, sums_ref), (masked_hbm, masked_ref))
        )
    ]

    def head_loads(m, slot, side):
        three, two, half = pl.ds(3 * m, 3), pl.ds(2 * m, 2), pl.ds(side * rows, rows)
        pairs = [
            (qm_hbm.at[three], qm_ref.at[slot]),
            (kt_hbm.at[two, :, half], kt_ref.at[slot]),
            (v_hbm.at[two, half], v_ref.at[slot]),
            (headout_hbm.at[three], headout_ref.at[slot]) if side else (att_hbm.at[m], att_ref.at[slot]),
        ]
        return [
            pltpu.make_async_copy(src, dst, head_sem.at[slot, i if i < 3 else 4 - side])
            for i, (src, dst) in enumerate(pairs)
        ]

    def weight_load(kind, m, slot):
        return pltpu.make_async_copy(blocks_hbm.at[kind, m], weight.at[slot], weight_sem.at[slot])

    def act_load(which, m):
        pair, place = m // 2, lax.rem(m, 2)
        return pltpu.make_async_copy(which.at[m], acts.at[pair, place], acts_sem.at[pair, place])

    def probs_loads(m, slot, side):
        half = pl.ds(side * rows, rows)
        return [
            pltpu.make_async_copy(probs_hbm.at[3 * m + j, half], probs.at[slot, j], probs_sem.at[slot, j])
            for j in range(3)
        ]

    def feed_loads(m, slot):
        return (weight_load(DOWN, m, 2 * slot), weight_load(UP, m, 2 * slot + 1))

    def begin(copies):
        for copy in copies:
            copy.start()

    def finish(copies):
        for copy in copies:
            copy.wait()

    def block(slot, low=0, width=768):
        return weight[slot, :, :, :, :, pl.ds(low, width)].reshape(768, width)

    def put(kind, m, value, low=0):
        width = value.shape[1]
        grads[kind, m, :, :, :, :, pl.ds(low, width)] = value.astype(BF16).reshape(2, 2, 2, 96, width)

    begin([gb2_load, *(act_load(acted_hbm, m) for m in DOWN_ORDER)])
    parts[...] = jnp.zeros_like(parts)
    finish((gb2_load,))
    gb2t_ref[...] = gb2_ref[...].T

    def feed_down(m):
        act_load(acted_hbm, m).wait()
        put(DOWN, m, dot(gb2t_ref[...], acts[m // 2, lax.rem(m, 2)]))

    feed_down(DOWN_ORDER[0])
    hooks.after("start")
    hooks.ready(DOWN, DOWN_ORDER[0])
    begin(feed_loads(0, 0))
    act_load(slope_hbm, DOWN_ORDER[0]).start()

    def feed_downs(place, _):
        m = down_order(place)
        feed_down(m)
        hooks.ready(DOWN, m)
        act_load(slope_hbm, m).start()

        @pl.when(place == 1)
        def _():
            begin((n1t_load, g2_load, n1_load, *small_loads, xt_load))
            begin(head_loads(0, 0, 1))
            begin(probs_loads(0, 0, 1))

        hooks.after("down", place)
        return 0

    lax.fori_loop(1, 4, feed_downs, 0)
    finish((n1t_load, g2_load))

    def feed(m, _):
        slot = lax.rem(m, 2)
        pl.when(m < 3)(lambda: begin(feed_loads(m + 1, 1 - slot)))
        finish(feed_loads(m, slot))
        act_load(slope_hbm, m).wait()
        grad_acted = dot(gb2_ref[...], block(2 * slot))
        grad_pre = (grad_acted * acts[m // 2, lax.rem(m, 2)].astype(F32)).astype(BF16)
        parts[m, 0:1, :] = jnp.sum(grad_pre.astype(F32), axis=0, keepdims=True)
        put(UP, m, dot(n1t_ref[...], grad_pre))
        g2_ref[...] += dot(grad_pre, block(2 * slot + 1), (1, 1))
        hooks.ready(UP, m)
        hooks.after("feed", m)
        return 0

    lax.fori_loop(0, 4, feed, 0)
    for m in range(4):
        weight_load(ATT, m, m).start()

    chunk = 64

    def norm_back(i, sums):
        r = pl.ds(pl.multiple_of(i * chunk, chunk), chunk)
        grad = g2_ref[r, :]
        unit = grad_one[r, :]
        scaled = grad * gain
        grad_in = (
            scaled
            - jnp.mean(scaled, axis=1, keepdims=True)
            - unit * jnp.mean(scaled * unit, axis=1, keepdims=True)
        ) * rs1_ref[r, :]
        grad_one[r, :] = grad_in
        gb1[r, :] = grad_in.astype(BF16)
        return (
            sums[0] + jnp.sum(grad_in, axis=0, keepdims=True),
            sums[1] + jnp.sum(grad * unit, axis=0, keepdims=True),
            sums[2] + jnp.sum(grad, axis=0, keepdims=True),
        )

    zero = jnp.zeros((1, 768), F32)
    finish((n1_load, xt_load))
    finish(small_loads)
    gain = gain_ref[...].astype(F32).reshape(1, 768)
    sums = lax.fori_loop(0, rows // chunk, norm_back, (zero, zero, zero), unroll=2)
    rows_ref[0, 0:1, :] = sums[0]
    rows_ref[0, 1:2, :] = sums_ref[0:1, :]
    rows_ref[0, 2:3, :] = sums[1]
    rows_ref[0, 3:4, :] = sums[2]
    rows_ref[0, 4:5, :] = sums_ref[1:2, :]
    rows_ref[0, 5:6, :] = sums_ref[2:3, :]
    gb1t[...] = gb1[...].T
    hooks.after("norm")
    g2_ref[...] = jnp.zeros_like(g2_ref)

    def wide(j, side):
        zeros = jnp.zeros((64, rows), BF16)
        return jnp.concatenate([zeros, side] if j == 1 else [side, zeros], axis=0)

    def half_back(slot, sides_here, shifts_here):
        grads_k, grads_v, grads_q = [], [], []
        wides = [wide(j, sides_here[j]) for j in range(3)]
        grad_weights = [dot(v_ref[slot, j // 2], wides[j]) for j in range(3)]
        for j in range(3):
            weights = probs[slot, j]
            grad_scores = (weights.astype(F32) * (grad_weights[j] - shifts_here[j])).astype(BF16)
            grads_v.append(dot(weights, wides[j].T))
            grads_k.append(dot(grad_scores, qm_ref[slot, j]))
            lane = 0 if j == 0 else 64
            grads_q.append(dot(kt_ref[slot, j // 2, lane : lane + 64, :], grad_scores))
        return [grads_k[0] + grads_k[1], grads_k[2]], [grads_v[0] + grads_v[1], grads_v[2]], grads_q

    def back_other(m, _):
        slot = lax.rem(m, 2)
        pl.when(m < 3)(lambda: begin([*head_loads(m + 1, 1 - slot, 1), *probs_loads(m + 1, 1 - slot, 1)]))
        pl.when(m == 3)(lambda: begin([*head_loads(0, 0, 0), *probs_loads(0, 0, 0)]))
        weight_load(ATT, m, m).wait()
        finish(head_loads(m, slot, 1))
        finish(probs_loads(m, slot, 1))
        grad_att_t = dot(gb1[...], block(m, 512, 256)).T
        others, shifts_here = [], []
        for j in range(3):
            head = 3 * m + j
            place = (128, 192, 64)[j]
            grad_att = grad_att_t[place : place + 64, :]
            factor_own, factor = recip_ref[head, 0:1, :], recip_ref[head, 1:2, :]
            own_side = (grad_att * factor_own).astype(BF16)
            others.append((grad_att * factor).astype(BF16))
            row_sum = jnp.sum(
                own_side.astype(F32) * headout_ref[slot, j, 0] + others[j].astype(F32) * headout_ref[slot, j, 1],
                axis=0,
                keepdims=True,
            )
            sides[head] = own_side
            shifts[head, 0:1, :] = row_sum * factor_own
            shifts_here.append(row_sum * factor)
        grads_k, grads_v, grads_q = half_back(slot, others, shifts_here)
        for j in range(3):
            shares[3 * m + j] = grads_q[j]
        tile = acts.at[m // 2, lax.rem(m, 2)]
        tile[:, 128:256] = grads_k[0].astype(BF16)
        tile[:, 256:384] = grads_v[0].astype(BF16)
        tile[:, 384:512] = grads_k[1].astype(BF16)
        tile[:, 512:640] = grads_v[1].astype(BF16)
        parts[4 + m, 0:1, 128:640] = jnp.sum(tile[:, 128:640].astype(F32), axis=0, keepdims=True)
        g2_ref[...] += dot(tile[:, 128:640], block(m, 128, 512), (1, 1))
        hooks.after("other", m)
        return 0

    lax.fori_loop(0, 4, back_other, 0)

    def fill_other(i, total):
        r = pl.ds(pl.multiple_of(i * chunk, chunk), chunk)
        other = g2_ref[r, :]
        gb1[r, :] = other.astype(BF16)
        return total + jnp.sum(other * masked_ref[1, r, :], axis=0, keepdims=True)

    fill = lax.fori_loop(0, rows // chunk, fill_other, zero)
    hooks.after("mate")

    def back_own(place, _):
        slot = lax.rem(place, 2)
        m = att_order(place)

        @pl.when(place < 3)
        def _():
            after = att_order(place + 1)
            begin([*head_loads(after, 1 - slot, 0), *probs_loads(after, 1 - slot, 0)])

        finish(head_loads(m, slot, 0))
        finish(probs_loads(m, slot, 0))
        grads_k, grads_v, grads_q = half_back(
            slot, [sides[3 * m + j] for j in range(3)], [shifts[3 * m + j, 0:1, :] for j in range(3)]
        )
        grads_q = [(grads_q[j] + shares[3 * m + j]) * SCALE for j in range(3)]
        single = jnp.concatenate([grads_q[2], jnp.zeros((64, rows), F32)], axis=0).T
        own[:, 0:128] = jnp.concatenate(grads_q[:2], axis=0).T.astype(BF16)
        own[:, 128:256] = grads_k[0].astype(BF16)
        own[:, 256:384] = grads_v[0].astype(BF16)
        own[:, 384:512] = (grads_k[1] + single).astype(BF16)
        own[:, 512:640] = grads_v[1].astype(BF16)
        parts[4 + m, 0:1, 0:PROJ] += jnp.sum(own[...].astype(F32), axis=0, keepdims=True)
        hooks.after("middle", place)
        other = acts[m // 2, lax.rem(m, 2), :, 128:640]
        grad_proj = dot(xt_ref[0], own[...])
        grad_other = dot(xt_ref[1], other)
        grad_out_w = dot(gb1t[...], att_ref[slot])
        put(ATT, m, grad_proj[:, :128], 0)
        put(ATT, m, grad_proj[:, 128:512] + grad_other[:, :384], 128)
        put(ATT, m, grad_proj[:, 512:] + grad_other[:, 384:] + grad_out_w[:, :128], 512)
        put(ATT, m, grad_out_w[:, 128:], 640)
        grad_one[...] += dot(own[...], block(m, 0, PROJ), (1, 1))
        hooks.ready(ATT, m)
        hooks.after("own", place)
        return 0

    lax.fori_loop(0, 4, back_own, 0)

    def fill_own(i, total):
        r = pl.ds(pl.multiple_of(i * chunk, chunk), chunk)
        return total + jnp.sum(grad_one[r, :] * masked_ref[0, r, :], axis=0, keepdims=True)

    rows_ref[0, 6:7, :] = lax.fori_loop(0, rows // chunk, fill_own, fill)
    rows_ref[0, 7:8, :] = zero
    for row in range(8):
        rows_ref[0, 8 + row : 9 + row, :] = parts[row, 0:1, :]


def finish_frames(grad_one, got, masked_ref, frames_ref):
    chunk = 64

    def body(i, _):
        r = pl.ds(pl.multiple_of(i * chunk, chunk), chunk)
        total = grad_one[r, :] + got[r, :].astype(F32)
        frames_ref[r, :] = jnp.where(masked_ref[0, r, :] > 0, 0.0, total).astype(BF16)
        return 0

    lax.fori_loop(0, grad_one.shape[0] // chunk, body, 0)


class NoScatter:
    def after(self, point, m=0):
        pass

    def ready(self, kind, m):
        pass


class ScatterHooks:
    PLAN = {
        ("down", 2): dict(first=(0,)),
        ("down", 3): dict(first=(1,)),
        ("feed", 0): dict(first=(2, 3)),
        ("feed", 1): dict(second=(0, 1), deep_one=(0,)),
        ("feed", 2): dict(second=(2,), first=(4,), deep_one=(1,)),
        ("feed", 3): dict(second=(3,), first=(5,), third=(0,), deep_one=(2,), deep_two=(0,)),
        ("norm", 0): dict(third=(1,), deep_one=(3,), deep_two=(1,)),
        ("other", 0): dict(second=(4,), first=(6,), third=(2,)),
        ("other", 1): dict(deep=("deep_first",), third=(3,), z_one=(0,)),
        ("other", 2): dict(first=(7,), z_one=(1,)),
        ("other", 3): dict(second=(5,), third=(4,), z_one=(2,), z_two=(0,)),
        ("mate", 0): dict(swap=(0,)),
        ("middle", 0): dict(deep=("deep_second",), swap=(1,)),
        ("own", 0): dict(second=(6,), third=(5,), z_one=(3,), z_two=(1,)),
        ("middle", 1): dict(first=(8,), deep=("deep_third",), swap=(2,)),
        ("own", 1): dict(second=(7,), z_one=(4,)),
        ("middle", 2): dict(first=(9,), third=(6,), swap=(3,)),
        ("own", 2): dict(z_one=(5,)),
        ("middle", 3): dict(second=(8,), first=(10,), third=(7,)),
        ("own", 3): dict(z_one=(6,), z_two=(4,)),
    }

    def __init__(self, at, scatter, swaps):
        self.at, self.scatter, self.swaps = at, scatter, swaps

    def ready(self, kind, m):
        self.scatter.begin(kind, m)

    def run(self, swap=(), deep=(), **steps):
        self.scatter.run(**steps)
        for name in deep:
            getattr(self.scatter, name)()
        for piece in swap:
            self.swaps[piece].start()

    def after(self, point, m=0):
        if point == "start":
            self.at.meet(True)
        for (name, index), steps in self.PLAN.items():
            if name == point:
                if isinstance(m, int):
                    self.run(**steps)
                else:
                    pl.when(m == index)(functools.partial(self.run, **steps))


N_BACKWARD_INS = 19
N_BACKWARD_SCRATCH = 33


def backward_linked(*refs):
    ins = refs[:N_BACKWARD_INS]
    out_ref, rows_out, frames_ref = refs[N_BACKWARD_INS : N_BACKWARD_INS + 3]
    scratch = refs[N_BACKWARD_INS + 3 :]
    scratch, links = scratch[:N_BACKWARD_SCRATCH], scratch[N_BACKWARD_SCRATCH:]
    grads, rows_ref, gb1, grad_one = scratch[0], scratch[1], scratch[8], scratch[10]
    rows_in, mate_in, t_send, t_recv, m_send, m_recv = links[14:]
    at = Place()
    at.hello(True)
    scatter = Scatter(at, grads, out_ref, links[:6], links[6:14])
    totals = Totals(at, rows_ref, rows_in, t_send, t_recv)
    piece = gb1.shape[0] // 4
    swaps = [
        remote(
            gb1.at[pl.ds(i * piece, piece)], mate_in.at[pl.ds(i * piece, piece)], m_send.at[i], m_recv.at[i], at.mate
        )
        for i in range(4)
    ]
    backward_compute(*ins, *scratch, ScatterHooks(at, scatter, swaps))
    totals.start(0)
    scatter.run(second=(9,), first=(11,))
    totals.finish(0)
    totals.start(1)
    scatter.run(third=(8,), z_one=(7,))
    scatter.run(second=(10,))
    scatter.run(third=(9,))
    totals.finish(1)
    totals.start(2)
    scatter.run(second=(11,))
    scatter.run(z_one=(8,), z_two=(7,))
    scatter.run(third=(10,))
    totals.finish(2)
    totals.start(3)
    scatter.run(third=(11,))
    scatter.run(z_one=(9,), z_two=(8,))
    scatter.finish(DOWN)
    scatter.finish(UP)
    totals.finish(3)
    totals.start(4)
    scatter.run(z_one=(10,))
    for swap in swaps:
        swap.wait()
    finish_frames(grad_one, mate_in, scratch[31], frames_ref)
    scatter.run(z_one=(11,), z_two=(9,))
    totals.finish(4)
    rows_out[...] = rows_ref[5]
    scatter.drain()
    scatter.finish(ATT)


def backward_alone(*refs):
    ins = refs[:N_BACKWARD_INS]
    grads_out, rows_out, mate_out, grad_one_out = refs[N_BACKWARD_INS : N_BACKWARD_INS + 4]
    scratch = refs[N_BACKWARD_INS + 4 :]
    *scratch, keep_sem = scratch
    grads, rows_ref, gb1, grad_one = scratch[0], scratch[1], scratch[8], scratch[10]
    backward_compute(*ins, *scratch, NoScatter())
    keep = pltpu.make_async_copy(grads, grads_out, keep_sem)
    keep.start()
    rows_out[...] = rows_ref[0]
    mate_out[...] = gb1[...]
    grad_one_out[...] = grad_one[...]
    keep.wait()


def backward_scratch(rows):
    return [
        pltpu.VMEM(BLOCKS, BF16),
        pltpu.VMEM((6, 16, 768), F32),
        pltpu.VMEM((4, *BLOCKS[2:]), BF16),
        pltpu.SemaphoreType.DMA((4,)),
        pltpu.VMEM((2, 2, rows, 768), BF16),
        pltpu.SemaphoreType.DMA((2, 2)),
        pltpu.VMEM((2, 3, rows, rows), BF16),
        pltpu.SemaphoreType.DMA((2, 3)),
        pltpu.VMEM((rows, 768), BF16),
        pltpu.VMEM((768, rows), BF16),
        pltpu.VMEM((rows, 768), F32),
        pltpu.VMEM((8, 8, 768), F32),
        pltpu.VMEM((rows, 768), F32),
        pltpu.SemaphoreType.DMA((6,)),
        pltpu.VMEM((rows, 768), BF16),
        pltpu.VMEM((768, rows), BF16),
        pltpu.VMEM((768, rows), BF16),
        pltpu.VMEM((2, 768, rows), BF16),
        pltpu.VMEM((2, 3, 2, 64, rows), F32),
        pltpu.VMEM((2, 3, rows, 128), BF16),
        pltpu.VMEM((2, 2, 128, rows), BF16),
        pltpu.VMEM((2, 2, rows, 128), BF16),
        pltpu.VMEM((2, rows, 256), BF16),
        pltpu.SemaphoreType.DMA((2, 5)),
        pltpu.VMEM((rows, PROJ), BF16),
        pltpu.VMEM((12, 64, rows), BF16),
        pltpu.VMEM((12, 8, rows), F32),
        pltpu.VMEM((12, 64, rows), F32),
        pltpu.VMEM((12, 8, rows), F32),
        pltpu.VMEM((rows, 1), F32),
        pltpu.VMEM((8, 768), F32),
        pltpu.VMEM((2, rows, 1), F32),
        pltpu.SemaphoreType.DMA((4,)),
    ]


def run_backward(linked, blocks, probs, kept, masked, gain):
    recip, headout, xt, qm, kt, v, att, acted, slope, n1t, n1, rs1, gb2, g2, sums = kept
    rows = gb2.shape[0]
    ins = (
        blocks, probs, acted, slope, recip, headout, xt, qm, kt, v, att, n1t, n1, rs1, gb2, g2, sums, masked, gain
    )
    in_specs = [vmem() if i == 18 else hbm() for i in range(19)]
    if linked:
        return pl.pallas_call(
            backward_linked,
            name="backward",
            out_shape=[
                jax.ShapeDtypeStruct((3, 96, 768), F32),
                jax.ShapeDtypeStruct((16, 768), F32),
                jax.ShapeDtypeStruct((rows, 768), BF16),
            ],
            in_specs=in_specs,
            out_specs=[vmem()] * 3,
            scratch_shapes=[
                *backward_scratch(rows),
                pltpu.VMEM((3, 4, 2, 2, 96, 768), BF16),
                pltpu.VMEM((3, 4, 2, 2, 48, 768), BF16),
                pltpu.VMEM((3, 4, 2, 48, 768), BF16),
                pltpu.VMEM((3, 5, 96, 768), BF16),
                pltpu.VMEM((5, 2, 2, DEEP, 768), BF16),
                pltpu.VMEM((3, 2, DEEP // 2, 768), BF16),
                pltpu.SemaphoreType.DMA((3, 5)),
                pltpu.SemaphoreType.DMA((3, 4, 5)),
                pltpu.SemaphoreType.DMA((3,)),
                pltpu.SemaphoreType.DMA((3, 5)),
                pltpu.SemaphoreType.DMA,
                pltpu.SemaphoreType.DMA((5,)),
                pltpu.SemaphoreType.DMA((4,)),
                pltpu.SemaphoreType.DMA((4,)),
                pltpu.VMEM((5, 16, 768), F32),
                pltpu.VMEM((rows, 768), BF16),
                pltpu.SemaphoreType.DMA((5,)),
                pltpu.SemaphoreType.DMA((5,)),
                pltpu.SemaphoreType.DMA((4,)),
                pltpu.SemaphoreType.DMA((4,)),
            ],
            compiler_params=pltpu.CompilerParams(
                collective_id=1, has_side_effects=True, vmem_limit_bytes=VMEM_LIMIT
            ),
        )(*ins)
    return pl.pallas_call(
        backward_alone,
        name="backward",
        out_shape=[
            jax.ShapeDtypeStruct(BLOCKS, BF16),
            jax.ShapeDtypeStruct((16, 768), F32),
            jax.ShapeDtypeStruct((rows, 768), BF16),
            jax.ShapeDtypeStruct((rows, 768), F32),
        ],
        in_specs=in_specs,
        out_specs=[hbm()] + [vmem()] * 3,
        scratch_shapes=[*backward_scratch(rows), pltpu.SemaphoreType.DMA],
        compiler_params=pltpu.CompilerParams(vmem_limit_bytes=VMEM_LIMIT),
    )(*ins)


def finish_kernel(parts, grads, totals, out_in, frames_in, out, frames, *outs):
    n_dp, n_mp = parts
    query, key, value, out_w, up, down, query_bias, value_bias, up_bias, *vectors = outs
    out[...] = out_in[...]
    frames[...] = frames_in[...]
    att = grads[0]
    query[...] = jnp.concatenate([att[:, 0:128], att[:, 384:448]], axis=1)
    key[...] = jnp.concatenate([att[:, 128:256], att[:, 448:512]], axis=1)
    value[...] = jnp.concatenate([att[:, 256:384], att[:, 512:576]], axis=1)
    out_w[...] = jnp.concatenate([att[:, 640:768], att[:, 576:640]], axis=1).T
    up[...] = grads[1]
    down[...] = grads[2]
    dp, z = lax.axis_index("dp"), lax.axis_index("mp")
    rows = totals[...]
    row_at = lax.broadcasted_iota(jnp.int32, rows.shape, 0)

    def shifted(block, by):
        return pltpu.roll(block, lax.rem(768 - by, 768), 1)

    def row_of(index):
        return jnp.broadcast_to(jnp.sum(jnp.where(row_at == index, rows, 0.0), axis=0, keepdims=True), (8, 768))

    part = 768 // (n_dp * n_mp)
    mine = shifted(rows[0:8], (dp * n_mp + z) * part)
    for i, ref in enumerate(vectors):
        ref[...] = mine[i : i + 1, :part]
    step = HEAD_DIM // n_dp
    heads = shifted(row_of(12 + z), dp * step)
    for head, (q_lane, v_lane) in enumerate(((0, 256), (64, 320), (384, 512))):
        query_bias[head : head + 1, :] = heads[0:1, q_lane : q_lane + step]
        value_bias[head : head + 1, :] = heads[0:1, v_lane : v_lane + step]
    ups = shifted(row_of(8 + z), dp * 2 * step)
    for i in range(6):
        up_bias[i : i + 1, :] = ups[0:1, 128 * i : 128 * i + 2 * step]


def run_finish(n_dp, n_mp, grads, totals, out, frames):
    def of(shape, dtype=F32):
        return jax.ShapeDtypeStruct(shape, dtype)

    d, step, part = grads.shape[1], HEAD_DIM // n_dp, 768 // (n_dp * n_mp)
    *outs, = pl.pallas_call(
        functools.partial(finish_kernel, (n_dp, n_mp)),
        name="finish",
        out_shape=[
            of(out.shape, BF16), of(frames.shape, BF16), of((d, 192)), of((d, 192)), of((d, 192)), of((192, d)),
            of((d, 768)), of((d, 768)), of((3, step)), of((3, step)), of((6, 2 * step)), *[of((1, part))] * 7,
        ],
        in_specs=[vmem()] * 4,
        out_specs=[vmem()] * 18,
        compiler_params=pltpu.CompilerParams(vmem_limit_bytes=VMEM_LIMIT),
    )(grads, totals, out, frames)
    return (*outs[:7], outs[7].T, *outs[8:11], *(row.reshape(part) for row in outs[11:]))


def shards(
    linked,
    frames,
    lengths,
    span_starts,
    cotangent,
    query_weight,
    key_weight,
    value_weight,
    out_weight,
    up_weight,
    down_weight,
    query_bias,
    value_bias,
    up_bias,
    out_bias,
    down_bias,
    first_gain,
    first_shift,
    second_gain,
    second_shift,
    mask_vector,
):
    rows = frames.shape[0]
    n_dp = 768 // query_weight.shape[0]
    n_mp = 768 // query_weight.shape[1]
    vecs = (out_bias, down_bias, first_gain, first_shift, second_gain, second_shift, mask_vector)
    if linked:
        blocks, probs, out, masked, kept = run_forward_linked(
            rows, lengths, span_starts, frames, cotangent, query_weight, key_weight, value_weight, out_weight,
            up_weight, down_weight.T, query_bias, value_bias, up_bias, *vecs,
        )
        grads, totals, grad_frames = run_backward(True, blocks, probs, kept, masked, first_gain)
        return run_finish(n_dp, n_mp, grads, totals, out, grad_frames)
    z = lax.axis_index("mp")
    half = z % 2
    length = lax.dynamic_index_in_dim(lengths, z // 2, keepdims=False)
    starts = lax.dynamic_index_in_dim(span_starts, z // 2, keepdims=False)
    slots = (jnp.arange(LEN, dtype=jnp.int32) + half * rows) % LEN
    valid = slots < length
    masked = jnp.any((slots[:, None] >= starts[None, :]) & (slots[:, None] < starts[None, :] + SPAN), axis=1)
    keybias = jnp.where(
        (jnp.arange(128) == 0)[None, :] & ~valid[:, None], jnp.float32(NEGATIVE), 0.0
    ).astype(BF16)
    valid_rows = valid[:rows].astype(F32)[:, None]
    masked_rows = masked.astype(F32).reshape(2, rows, 1)
    x = jnp.where(masked[:rows, None], mask_vector[None, :], frames)
    pack = jnp.stack(pack_weights(query_weight, key_weight, value_weight, out_weight.T, up_weight, down_weight.T))
    bias = pack_biases(query_bias, value_bias, up_bias)
    mates = [(0, 1), (1, 0), (2, 3), (3, 2)]
    blocks = lax.all_gather(lax.all_gather(pack, "dp", axis=1, tiled=True), "mp", axis=1).reshape(BLOCKS)
    biases = lax.all_gather(bias, "mp", axis=0)
    both = jnp.stack([x, lax.ppermute(x, "mp", mates)])
    probs, out, kept = run_forward_alone(rows, blocks, biases, both, keybias, valid_rows, cotangent, *vecs)
    grads, totals, mate, grad_one = run_backward(False, blocks, probs, kept, masked_rows, first_gain)
    grads = grads.reshape(3, 4, 768, 768).astype(F32)
    grads = lax.psum_scatter(grads, "mp", scatter_dimension=1, tiled=False)
    grads = lax.psum_scatter(grads, "dp", scatter_dimension=1, tiled=True)
    totals = lax.psum(totals, ("dp", "mp"))
    grad_frames = grad_one + lax.ppermute(mate, "mp", mates).astype(F32)
    grad_frames = jnp.where(masked[:rows, None], 0.0, grad_frames).astype(BF16)
    return run_finish(n_dp, n_mp, grads, totals, out, grad_frames)


def solution(mesh):
    linked = mesh.shape["dp"] == 8 and mesh.shape["mp"] == 4
    split = P(("dp", "mp"))
    return jax.shard_map(
        functools.partial(shards, linked),
        mesh=mesh,
        in_specs=(
            P(("dp", "mp"), None),
            P("dp"),
            P("dp", None),
            P(("dp", "mp"), None),
            P("dp", "mp"),
            P("dp", "mp"),
            P("dp", "mp"),
            P("mp", "dp"),
            P("dp", "mp"),
            P("mp", "dp"),
            P("mp", None),
            P("mp", None),
            P("mp", None),
            *([P()] * 7),
        ),
        out_specs=(
            P(("dp", "mp"), None),
            P(("dp", "mp"), None),
            P("dp", "mp"),
            P("dp", "mp"),
            P("dp", "mp"),
            P("mp", "dp"),
            P("dp", "mp"),
            P("mp", "dp"),
            P("mp", "dp"),
            P("mp", "dp"),
            P("mp", "dp"),
            *([split] * 7),
        ),
        check_vma=False,
    )
```

```python
import functools
import math

import jax
import jax.numpy as jnp
from jax import lax
from jax.experimental import pallas as pl
from jax.experimental.pallas import tpu as pltpu
from jax.sharding import PartitionSpec as P

HEAD_DIM = 64
SPAN = 10
LEN = 1024
EPSILON = 1e-05
NEGATIVE = -1e30
SCALE = 1.0 / math.sqrt(HEAD_DIM)

F32 = jnp.float32
BF16 = jnp.bfloat16
MESH = pl.DeviceIdType.MESH
VMEM_LIMIT = 63 * 1024 * 1024

ATT, UP, DOWN = 0, 1, 2
PROJ = 640


def dot(left, right, contract=(1, 0)):
    return lax.dot_general(
        left, right, (((contract[0],), (contract[1],)), ((), ())), preferred_element_type=F32
    )


def hbm():
    return pl.BlockSpec(memory_space=pl.ANY)


def vmem():
    return pl.BlockSpec(memory_space=pltpu.VMEM)


class Place:
    def __init__(self):
        self.dp = lax.axis_index("dp")
        self.z = lax.axis_index("mp")
        self.c = lax.rem(self.dp, 2)
        self.x = lax.rem(self.dp // 2, 2)
        self.y = self.dp // 4
        self.core = (self.dp + 1 - 2 * self.c, self.z)
        self.across_x = (self.dp + 2 - 4 * self.x, self.z)
        self.across_y = (self.dp + 4 - 8 * self.y, self.z)
        self.right = (self.dp, self.z + 1)
        self.left = (self.dp, self.z - 1)
        self.mate = (self.dp, self.z + 1 - 2 * lax.rem(self.z, 2))
        self.far = (self.dp, lax.rem(self.z + 2, 4))

    def hello(self, far):
        barrier = pltpu.get_barrier_semaphore()

        def signal(device):
            pl.semaphore_signal(barrier, inc=1, device_id=device, device_id_type=MESH)

        signal(self.core)
        signal(self.across_x)
        signal(self.across_y)
        if far:
            signal(self.far)
        pl.when(self.z < 3)(lambda: signal(self.right))
        pl.when(self.z > 0)(lambda: signal(self.left))

    def meet(self, far):
        ends = jnp.where((self.z == 0) | (self.z == 3), 1, 2)
        pl.semaphore_wait(pltpu.get_barrier_semaphore(), (4 if far else 3) + ends)


def remote(src, dst, send, recv, device):
    return pltpu.make_async_remote_copy(
        src_ref=src, dst_ref=dst, send_sem=send, recv_sem=recv, device_id=device, device_id_type=MESH
    )


class Gather:
    def __init__(self, at, blocks, biases, z_send, z_recv, p_send, p_recv):
        self.at, self.blocks, self.biases = at, blocks, biases
        self.z_send, self.z_recv, self.p_send, self.p_recv = z_send, z_recv, p_send, p_recv

    def z_copy(self, kind, m, direction):
        at = self.at
        if kind == 3:
            ref = self.biases.at[m]
        else:
            ref = self.blocks.at[kind, m, at.y, at.x, at.c]
        device = at.right if direction == 0 else at.left
        return remote(ref, ref, self.z_send.at[kind, direction], self.z_recv.at[kind, m], device)

    def z_step(self, kind, step):
        z = self.at.z
        if step == 0:
            pl.when((z > 0) & (z < 2))(lambda: self.z_copy(kind, z, 1).start())
            pl.when(z < 3)(lambda: self.z_copy(kind, z, 0).start())
            pl.when(z >= 2)(lambda: self.z_copy(kind, z, 1).start())
            return

        def from_left():
            @pl.when(z >= step)
            def _():
                self.z_copy(kind, z - step, 0).wait_recv()
                if step < 3:
                    pl.when(z < 3)(lambda: self.z_copy(kind, z - step, 0).start())
                self.first(kind, z - step)

        def from_right():
            @pl.when(z + step <= 3)
            def _():
                self.z_copy(kind, z + step, 1).wait_recv()
                if step < 3:
                    pl.when(z > 0)(lambda: self.z_copy(kind, z + step, 1).start())
                self.first(kind, z + step)

        pl.when(z < 2)(from_right)
        from_left()
        pl.when(z >= 2)(from_right)

    def plane_copy(self, kind, m, which):
        recv = 0 if m is None else m
        at, block = self.at, self.blocks.at[kind, slice(None) if m is None else m]
        x, y, c = at.x, at.y, at.c
        low, high = pl.ds(0, 48), pl.ds(48, 48)
        every = (slice(None),) if m is None else ()
        ref, device = {
            0: lambda: (block.at[(*every, y, x, c, low)], at.across_x),
            1: lambda: (block.at[(*every, y, x, c, high)], at.across_y),
            2: lambda: (block.at[(*every, y, slice(None), c, low)], at.across_y),
            3: lambda: (block.at[(*every, slice(None), x, c, high)], at.across_x),
            4: lambda: (block.at[(*every, slice(None), slice(None), c)], at.core),
        }[which]()
        return remote(ref, ref, self.p_send.at[kind, which], self.p_recv.at[kind, recv, which], device)

    def at_step(self, step, act):
        z = self.at.z
        if step == 0:
            act(z)
            return
        pl.when(z >= step)(lambda: act(z - step))
        pl.when(z + step <= 3)(lambda: act(z + step))

    def order(self, step):
        z = self.at.z
        from_low = jnp.where(z == 1, jnp.where(step < 2, 1 - step, step), step)
        mirrored = 3 - z
        from_high = jnp.where(mirrored == 1, jnp.where(step < 2, 1 - step, step), step)
        return jnp.where(z < 2, from_low, 3 - from_high)

    def first(self, kind, m):
        if kind < 3:
            self.plane_copy(kind, m, 0).start()
            self.plane_copy(kind, m, 1).start()

    def second(self, kind, step):
        def act(m):
            self.plane_copy(kind, m, 0).wait_recv()
            self.plane_copy(kind, m, 2).start()
            self.plane_copy(kind, m, 1).wait_recv()
            self.plane_copy(kind, m, 3).start()

        self.at_step(step, act)

    def third(self, kind, step):
        def act(m):
            self.plane_copy(kind, m, 2).wait_recv()
            self.plane_copy(kind, m, 3).wait_recv()
            self.plane_copy(kind, m, 4).start()

        self.at_step(step, act)

    def last(self, kind):
        for m in range(4):
            self.plane_copy(kind, m, 4).wait_recv()

    def drain(self):
        z = self.at.z
        for kind in range(4):
            for here in range(4):
                for direction, count in ((0, here + 1), (1, 4 - here)):
                    if (direction == 0 and here < 3) or (direction == 1 and here > 0):
                        pl.when(z == here)(self.z_copy(kind, pl.ds(0, count), direction).wait_send)
        for kind in range(3):
            for which in range(5):
                self.plane_copy(kind, None, which).wait_send()


def block_of(blocks, kind, m, low=0, width=768):
    return blocks[kind, m, :, :, :, :, pl.ds(low, width)].reshape(768, width)


def lane_mask(rows, lower):
    lanes = lax.broadcasted_iota(jnp.int32, (rows, 128), 1)
    return (lanes < 64) if lower else (lanes >= 64)


def forward_compute(
    blocks,
    biases,
    xs,
    keybias_ref,
    valid_ref,
    cot_ref,
    vec_ref,
    probs_hbm,
    out_hbm,
    outs_hbm,
    outs_ref,
    outs_sem,
    k_ref,
    vt_ref,
    probs,
    probs_sem,
    total,
    low,
    stats,
    out_ref,
    out_sem,
    hooks,
):
    rows = xs.shape[1]
    (recip_ref, headout_ref, xt_ref, qm_ref, kt_ref, v_ref, att_ref, acted_ref, slope_ref, n1t_ref, n1_ref, rs1_ref,
     gb2_ref, g2_ref, sums_ref) = outs_ref
    keeps = [
        pltpu.make_async_copy(ref, to, outs_sem.at[i]) for i, (ref, to) in enumerate(zip(outs_ref, outs_hbm, strict=True))
    ]

    def keep(*which):
        for i in which:
            keeps[i].start()

    xt_ref[0] = xs[0].T
    ones_lane = jnp.where(lax.broadcasted_iota(jnp.int32, (rows, 128), 1) == 0, 1.0, 0.0).astype(BF16)

    def probs_copy(head, side, slot):
        return pltpu.make_async_copy(
            probs.at[slot], probs_hbm.at[head, pl.ds(side * rows, rows)], probs_sem.at[slot]
        )

    own_rows, other_rows = pl.ds(0, rows), pl.ds(rows, rows)

    def project(m, _):
        bias = biases[m, 0:1, :].astype(F32)[:, :PROJ]
        own = dot(xs[0], block_of(blocks, ATT, m, 0, PROJ)) + bias
        k_ref[2 * m, own_rows] = own[:, 128:256].astype(BF16)
        v_ref[2 * m, own_rows] = own[:, 256:384].astype(BF16)
        k_ref[2 * m + 1, own_rows] = own[:, 384:512].astype(BF16)
        v_ref[2 * m + 1, own_rows] = own[:, 512:640].astype(BF16)
        lower, upper = lane_mask(rows, True), lane_mask(rows, False)
        pair = own[:, 0:128].astype(BF16).astype(F32) * SCALE
        single = pltpu.roll(own[:, 384:512].astype(BF16).astype(F32) * SCALE, 64, 1)
        qm_ref[3 * m] = jnp.where(lower, pair, 0.0).astype(BF16)
        qm_ref[3 * m + 1] = jnp.where(upper, pair, 0.0).astype(BF16)
        qm_ref[3 * m + 2] = jnp.where(upper, single, 0.0).astype(BF16)
        for tile in range(2):
            kt_ref[2 * m + tile, :, own_rows] = k_ref[2 * m + tile, own_rows].T
            vt_ref[2 * m + tile, :, own_rows] = v_ref[2 * m + tile, own_rows].T
        hooks.after("project", m)
        return 0

    def project_other(m, _):
        bias = biases[m, 0:1, :].astype(F32)[:, 128:PROJ]
        other = dot(xs[1], block_of(blocks, ATT, m, 128, 512)) + bias
        k_ref[2 * m, other_rows] = other[:, 0:128].astype(BF16)
        v_ref[2 * m, other_rows] = other[:, 128:256].astype(BF16)
        k_ref[2 * m + 1, other_rows] = other[:, 256:384].astype(BF16)
        v_ref[2 * m + 1, other_rows] = other[:, 384:512].astype(BF16)
        for tile in range(2):
            kt_ref[2 * m + tile, :, other_rows] = k_ref[2 * m + tile, other_rows].T
            vt_ref[2 * m + tile, :, other_rows] = v_ref[2 * m + tile, other_rows].T
        return 0

    def attend_half(m, side):
        half = own_rows if side == 0 else other_rows

        def free():
            for j in range(3):
                probs_copy(3 * m + j, side, j).wait()

        if side == 0:
            pl.when(m > 0)(free)
        else:
            free()
        scores, tops, sums, outs = [], [], [], []
        for j in range(3):
            keys = jnp.concatenate([k_ref[2 * m + j // 2, half], keybias_ref[half, :]], axis=1)
            queries = jnp.concatenate([qm_ref[3 * m + j], ones_lane], axis=1)
            scores.append(dot(keys, queries, (1, 1)))
        for j in range(3):
            top = jnp.max(scores[j], axis=0, keepdims=True)
            weights = jnp.exp(scores[j] - top)
            tops.append(top)
            sums.append(jnp.sum(weights, axis=0, keepdims=True))
            probs[j] = weights.astype(BF16)
            lane = 64 * (j % 2)
            outs.append(dot(vt_ref[2 * m + j // 2, lane : lane + 64, half], probs[j]))
            headout_ref[3 * m + j, side] = outs[j]
        return tops, sums, outs

    def send_probs(m, side):
        for j in range(3):
            probs_copy(3 * m + j, side, j).start()

    def attend_own(m, _):
        tops, sums, _ = attend_half(m, 0)
        for j in range(3):
            stats[3 * m + j, 0:1, :] = tops[j]
            stats[3 * m + j, 1:2, :] = sums[j]
        send_probs(m, 0)
        hooks.after("own", m)
        return 0

    def attend(m, _):
        tops, sums, outs = attend_half(m, 1)
        pieces = [jnp.zeros((64, rows), BF16), None, None, None]
        for j in range(3):
            head = 3 * m + j
            top_own = stats[head, 0:1, :]
            top_all = jnp.maximum(tops[j], top_own)
            factor, factor_own = jnp.exp(tops[j] - top_all), jnp.exp(top_own - top_all)
            recip = 1.0 / (factor_own * stats[head, 1:2, :] + factor * sums[j])
            factor, factor_own = factor * recip, factor_own * recip
            recip_ref[head] = jnp.concatenate([factor_own, factor, jnp.zeros((6, rows), F32)], axis=0)
            pieces[(2, 3, 1)[j]] = (headout_ref[head, 0] * factor_own + outs[j] * factor).astype(BF16)
        att_ref[m] = jnp.concatenate(pieces, axis=0).T
        send_probs(m, 1)
        hooks.after("other", m)
        return 0

    hooks.before("project")
    lax.fori_loop(0, 4, project, 0)
    lax.fori_loop(0, 4, attend_own, 0)
    hooks.before("other")
    xt_ref[1] = xs[1].T
    lax.fori_loop(0, 4, project_other, 0)
    keep(2, 3, 4, 5)
    hooks.after("swapped")
    lax.fori_loop(0, 4, attend, 0)
    keep(0, 1, 6)
    branch = [dot(att_ref[m], block_of(blocks, ATT, m, 512, 256), (1, 1)) for m in range(4)]
    total[...] = (branch[0] + branch[1]) + (branch[2] + branch[3])
    for j in range(3):
        probs_copy(9 + j, 1, j).wait()

    chunk = 64

    def norm_one(i, _):
        r = pl.ds(pl.multiple_of(i * chunk, chunk), chunk)
        resid = xs[0, r, :].astype(F32) + total[r, :] + vec_ref[0:1, :]
        centered = resid - jnp.mean(resid, axis=1, keepdims=True)
        rstd = lax.rsqrt(jnp.mean(centered * centered, axis=1, keepdims=True) + EPSILON)
        unit = centered * rstd
        n1_ref[r, :] = unit
        rs1_ref[r, :] = rstd
        low[r, :] = (unit * vec_ref[2:3, :] + vec_ref[3:4, :]).astype(BF16)
        return 0

    lax.fori_loop(0, rows // chunk, norm_one, 0, unroll=4)
    n1t_ref[...] = low[...].T
    keep(9, 10, 11)
    hooks.after("norm")
    hooks.before("feed")

    def feed(m, _):
        pre = dot(low[...], block_of(blocks, UP, m)) + biases[m, 1:2, :].astype(F32)
        phi = 0.5 * (1.0 + lax.erf(pre * (1.0 / math.sqrt(2.0))))
        acted_ref[m] = (pre * phi).astype(BF16)
        slope_ref[m] = (phi + pre * jnp.exp(-0.5 * pre * pre) * (1.0 / math.sqrt(2.0 * math.pi))).astype(BF16)
        hooks.after("feed", m)
        return 0

    lax.fori_loop(0, 4, feed, 0)
    keep(7, 8)

    def down(steps):
        places = [hooks.order(step) for step in steps]
        for m in places:
            hooks.landed(DOWN, m)
        shares = [dot(acted_ref[m], block_of(blocks, DOWN, m), (1, 1)) for m in places]
        return functools.reduce(jnp.add, shares)

    hooks.before("down")
    total[...] = down((0, 1, 2))
    total[...] += down((3,))
    hooks.all_landed()

    def norm_two(i, sums):
        r = pl.ds(pl.multiple_of(i * chunk, chunk), chunk)
        normed = n1_ref[r, :] * vec_ref[2:3, :] + vec_ref[3:4, :]
        resid = normed + total[r, :] + vec_ref[1:2, :]
        centered = resid - jnp.mean(resid, axis=1, keepdims=True)
        rstd = lax.rsqrt(jnp.mean(centered * centered, axis=1, keepdims=True) + EPSILON)
        unit = centered * rstd
        valid = valid_ref[r, :]
        out_ref[r, :] = (valid * (unit * vec_ref[4:5, :] + vec_ref[5:6, :])).astype(BF16)
        grad = valid * cot_ref[r, :].astype(F32)
        scaled = grad * vec_ref[4:5, :]
        grad_in = (
            scaled
            - jnp.mean(scaled, axis=1, keepdims=True)
            - unit * jnp.mean(scaled * unit, axis=1, keepdims=True)
        ) * rstd
        g2_ref[r, :] = grad_in
        gb2_ref[r, :] = grad_in.astype(BF16)
        for i, (ref, to) in enumerate(((out_ref, out_hbm), (g2_ref, outs_hbm[13]), (gb2_ref, outs_hbm[12]))):
            pltpu.make_async_copy(ref.at[r], to.at[r], out_sem.at[i]).start()
        return (
            sums[0] + jnp.sum(grad_in, axis=0, keepdims=True),
            sums[1] + jnp.sum(grad * unit, axis=0, keepdims=True),
            sums[2] + jnp.sum(grad, axis=0, keepdims=True),
        )

    zero = jnp.zeros((1, 768), F32)
    sums = lax.fori_loop(0, rows // chunk, norm_two, (zero, zero, zero), unroll=4)
    sums_ref[...] = jnp.concatenate([*sums, jnp.zeros((5, 768), F32)], axis=0)
    keep(14)
    hooks.finish()
    for i, copy in enumerate(keeps):
        if i not in (12, 13):
            copy.wait()
    for i, (ref, to) in enumerate(((out_ref, out_hbm), (g2_ref, outs_hbm[13]), (gb2_ref, outs_hbm[12]))):
        pltpu.make_async_copy(ref, to, out_sem.at[i]).wait()


class NoHooks:
    def after(self, point, m=0):
        pass

    def before(self, point):
        pass

    def order(self, step):
        return step

    def landed(self, kind, m):
        pass

    def all_landed(self):
        pass

    def finish(self):
        pass


class GatherHooks:
    MIDDLE = {
        ("project", 1): (("z_step", DOWN, 1),),
        ("project", 3): (("second", UP, 0), ("second", UP, 1)),
        ("own", 0): (("second", UP, 2),),
        ("own", 1): (("z_step", DOWN, 2), ("second", DOWN, 0), ("third", UP, 0)),
        ("own", 3): (("second", DOWN, 1),),
        ("swapped", 0): (("third", UP, 1),),
        ("other", 0): (("second", DOWN, 2), ("third", UP, 2)),
        ("other", 2): (("third", DOWN, 0),),
        ("norm", 0): (("third", DOWN, 1),),
        ("feed", 1): (("third", DOWN, 2),),
    }
    END = {
        ("project", 1): (("second", UP, 0),),
        ("project", 3): (("second", UP, 1), ("z_step", UP, 2)),
        ("own", 0): (("second", DOWN, 0),),
        ("own", 1): (("third", UP, 0),),
        ("own", 2): (("second", UP, 2), ("third", UP, 1)),
        ("swapped", 0): (("z_step", UP, 3), ("third", DOWN, 0)),
        ("other", 0): (("z_step", DOWN, 1), ("third", UP, 2)),
        ("other", 1): (("second", UP, 3), ("z_step", DOWN, 2)),
        ("other", 2): (("second", DOWN, 1),),
        ("other", 3): (("z_step", DOWN, 3), ("second", DOWN, 2)),
        ("norm", 0): (("third", UP, 3),),
        ("feed", 0): (("second", DOWN, 3),),
        ("feed", 1): (("third", DOWN, 1),),
        ("feed", 3): (("third", DOWN, 2),),
        ("down", 0): (("third", DOWN, 3),),
    }

    def __init__(self, gather, swap, blocks_out, keep_sem):
        self.gather, self.swap = gather, swap
        z = gather.at.z
        self.at_end = (z == 0) | (z == 3)
        self.keep = [
            pltpu.make_async_copy(gather.blocks.at[kind], blocks_out.at[kind], keep_sem.at[kind]) for kind in range(3)
        ]

    def after(self, point, m=0):
        for table, here in ((self.MIDDLE, ~self.at_end), (self.END, self.at_end)):
            for (name, index), events in table.items():
                if name == point:

                    def act(events=events):
                        for step, *which in events:
                            getattr(self.gather, step)(*which)

                    pl.when(here if isinstance(m, int) else here & (m == index))(act)

    def before(self, point):
        if point == "project":
            self.gather.last(ATT)
            self.keep[ATT].start()
        if point == "other":
            self.swap.wait()
        if point == "feed":
            self.gather.last(UP)
            self.keep[UP].start()
        if point == "down":
            self.after("down")

    def order(self, step):
        return self.gather.order(step)

    def landed(self, kind, m):
        self.gather.plane_copy(kind, m, 4).wait_recv()

    def all_landed(self):
        self.keep[DOWN].start()

    def finish(self):
        for copy in self.keep:
            copy.wait()
        self.gather.drain()


N_KEPT = 15


def pack_weights(query, key, value, out_t, up, down_t):
    pair, single = 2 * HEAD_DIM, 3 * HEAD_DIM
    att = jnp.concatenate(
        [
            query[:, :pair], key[:, :pair], value[:, :pair],
            query[:, pair:single], key[:, pair:single],
            value[:, pair:single], out_t[:, pair:single], out_t[:, :pair],
        ],
        axis=1,
    )
    return att, up, down_t


def pack_biases(query_bias, value_bias, up_bias):
    def row(i, bias):
        return bias[i : i + 1, :]

    blank = jnp.zeros((1, HEAD_DIM), BF16)
    pieces = [
        row(0, query_bias), row(1, query_bias), blank, blank, row(0, value_bias), row(1, value_bias),
        row(2, query_bias), blank, row(2, value_bias), blank, blank, blank,
    ]
    ups = jnp.concatenate([row(i, up_bias) for i in range(6)], axis=1)
    return jnp.concatenate([jnp.concatenate(pieces, axis=1), ups, jnp.zeros((14, 768), BF16)], axis=0)


def fill_vectors(vec, vecs):
    for i, ref in enumerate(vecs):
        vec[i : i + 1, :] = ref[...].astype(F32).reshape(1, 768)


def transposed(block):
    wide = jnp.concatenate([block, jnp.zeros((block.shape[0], 128 - block.shape[1]), block.dtype)], axis=1)
    return wide.T[: block.shape[1]]


def forward_linked(*refs):
    (lengths, starts, frames, cot_hbm, query, key, value, out_w, up, down, query_bias, value_bias, up_bias) = refs[:13]
    vecs, refs = refs[13:20], refs[20:]
    blocks_hbm, probs_hbm, out_hbm, masked_hbm, *outs = refs[: 4 + N_KEPT]
    blocks, biases, xs, keybias, valid, vec, masked_ref, masked_sem, cot, cot_sem, *scratch = refs[4 + N_KEPT :]
    scratch, links = scratch[:N_FORWARD_SCRATCH], scratch[N_FORWARD_SCRATCH:]
    z_send, z_recv, p_send, p_recv, x_send, x_recv, keep_sem = links
    at = Place()
    at.hello(False)
    at.meet(False)
    gather = Gather(at, blocks, biases, z_send, z_recv, p_send, p_recv)
    packs = pack_weights(
        query[...], key[...], value[...], transposed(out_w[...]), up[...], down[...]
    )
    for kind in range(3):
        blocks[kind, at.z, at.y, at.x, at.c] = packs[kind]
        if kind == 0:
            gather.z_step(ATT, 0)
        gather.first(kind, at.z)
    biases[at.z] = pack_biases(query_bias[...], value_bias[...], up_bias[...])
    gather.z_step(3, 0)
    at_end = (at.z == 0) | (at.z == 3)

    @pl.when(at_end)
    def _():
        gather.z_step(UP, 0)
        gather.z_step(DOWN, 0)

    fill_vectors(vec, vecs)
    rows = frames.shape[0]
    clip, half = at.z // 2, lax.rem(at.z, 2)
    length = lengths[clip]
    start = starts[pl.ds(clip, 1), :]
    for side in range(2):
        first = rows * (half if side == 0 else 1 - half)
        slots = first + lax.broadcasted_iota(jnp.int32, (rows, start.shape[1]), 0)
        covered = jnp.where((slots >= start) & (slots < start + SPAN), 1.0, 0.0)
        masked_ref[side] = jnp.max(covered, axis=1, keepdims=True)
        slots = first + lax.broadcasted_iota(jnp.int32, (rows, 128), 0)
        lanes = lax.broadcasted_iota(jnp.int32, (rows, 128), 1)
        here = pl.ds(side * rows, rows)
        keybias[here, :] = jnp.where((slots >= length) & (lanes == 0), NEGATIVE, 0.0).astype(BF16)
        if side == 0:
            valid[...] = jnp.where(slots[:, 0:1] < length, 1.0, 0.0)
    masked_copy = pltpu.make_async_copy(masked_ref, masked_hbm, masked_sem)
    cot_load = pltpu.make_async_copy(cot_hbm, cot, cot_sem)
    cot_load.start()
    masked_copy.start()
    xs[0] = jnp.where(masked_ref[0] > 0, vec[6:7, :], frames[...].astype(F32)).astype(BF16)
    swap = remote(xs.at[0], xs.at[1], x_send, x_recv, at.mate)
    pl.when(at_end)(swap.start)
    gather.z_step(ATT, 1)
    gather.z_step(3, 1)
    gather.second(ATT, 0)
    gather.z_step(ATT, 2)
    gather.z_step(3, 2)

    @pl.when(~at_end)
    def _():
        gather.z_step(UP, 0)

    gather.second(ATT, 1)
    gather.third(ATT, 0)
    gather.z_step(ATT, 3)
    gather.z_step(3, 3)
    gather.second(ATT, 2)
    gather.z_step(UP, 1)
    pl.when(~at_end)(swap.start)
    gather.third(ATT, 1)
    gather.second(ATT, 3)
    gather.third(ATT, 2)

    @pl.when(~at_end)
    def _():
        gather.z_step(UP, 2)
        gather.z_step(DOWN, 0)

    gather.third(ATT, 3)
    cot_load.wait()
    hooks = GatherHooks(gather, swap, blocks_hbm, keep_sem)
    forward_compute(blocks, biases, xs, keybias, valid, cot, vec, probs_hbm, out_hbm, outs, *scratch, hooks)
    masked_copy.wait()


def forward_alone(blocks_in, biases, xs, keybias, valid, cot, *refs):
    vecs, (probs_hbm, out_hbm, *outs), scratch = refs[:7], refs[7 : 9 + N_KEPT], refs[9 + N_KEPT :]
    blocks, vec, *scratch, keep_sem = scratch
    fill_vectors(vec, vecs)
    load = pltpu.make_async_copy(blocks_in, blocks, keep_sem)
    load.start()
    load.wait()
    forward_compute(
        blocks, biases, xs, keybias, valid, cot, vec, probs_hbm, out_hbm, outs, *scratch, NoHooks()
    )


BLOCKS = (3, 4, 2, 2, 2, 96, 768)


def forward_outs(rows):
    def of(shape, dtype):
        return jax.ShapeDtypeStruct(shape, dtype)

    return [
        of((12, 8, rows), F32),
        of((12, 2, 64, rows), F32),
        of((2, 768, rows), BF16),
        of((12, rows, 128), BF16),
        of((8, 128, LEN), BF16),
        of((8, LEN, 128), BF16),
        of((4, rows, 256), BF16),
        of((4, rows, 768), BF16),
        of((4, rows, 768), BF16),
        of((768, rows), BF16),
        of((rows, 768), F32),
        of((rows, 1), F32),
        of((rows, 768), BF16),
        of((rows, 768), F32),
        of((8, 768), F32),
    ]


N_FORWARD_SCRATCH = 11


def forward_scratch(rows):
    return [
        [pltpu.VMEM(out.shape, out.dtype) for out in forward_outs(rows)],
        pltpu.SemaphoreType.DMA((N_KEPT,)),
        pltpu.VMEM((8, LEN, 128), BF16),
        pltpu.VMEM((8, 128, LEN), BF16),
        pltpu.VMEM((3, rows, rows), BF16),
        pltpu.SemaphoreType.DMA((3,)),
        pltpu.VMEM((rows, 768), F32),
        pltpu.VMEM((rows, 768), BF16),
        pltpu.VMEM((12, 8, rows), F32),
        pltpu.VMEM((rows, 768), BF16),
        pltpu.SemaphoreType.DMA((3,)),
    ]


def run_forward_linked(rows, *ins):
    outs = forward_outs(rows)
    probs = jax.ShapeDtypeStruct((12, LEN, rows), BF16)
    frames = jax.ShapeDtypeStruct((rows, 768), BF16)
    masked = jax.ShapeDtypeStruct((2, rows, 1), F32)
    blocks, probs, frames, masked, *kept = pl.pallas_call(
        forward_linked,
        name="forward",
        out_shape=[jax.ShapeDtypeStruct(BLOCKS, BF16), probs, frames, masked, *outs],
        in_specs=[pl.BlockSpec(memory_space=pltpu.SMEM), vmem(), vmem(), hbm()] + [vmem()] * 16,
        out_specs=[hbm()] * (4 + N_KEPT),
        scratch_shapes=[
            pltpu.VMEM(BLOCKS, BF16),
            pltpu.VMEM((4, 16, 768), BF16),
            pltpu.VMEM((2, rows, 768), BF16),
            pltpu.VMEM((LEN, 128), BF16),
            pltpu.VMEM((rows, 1), F32),
            pltpu.VMEM((8, 768), F32),
            pltpu.VMEM((2, rows, 1), F32),
            pltpu.SemaphoreType.DMA,
            pltpu.VMEM((rows, 768), BF16),
            pltpu.SemaphoreType.DMA,
            *forward_scratch(rows),
            pltpu.SemaphoreType.DMA((4, 2)),
            pltpu.SemaphoreType.DMA((4, 4)),
            pltpu.SemaphoreType.DMA((3, 5)),
            pltpu.SemaphoreType.DMA((3, 4, 5)),
            pltpu.SemaphoreType.DMA,
            pltpu.SemaphoreType.DMA,
            pltpu.SemaphoreType.DMA((3,)),
        ],
        compiler_params=pltpu.CompilerParams(
            collective_id=0, has_side_effects=True, vmem_limit_bytes=VMEM_LIMIT
        ),
    )(*ins)
    return blocks, probs, frames, masked, kept


def run_forward_alone(rows, *ins):
    probs = jax.ShapeDtypeStruct((12, LEN, rows), BF16)
    frames = jax.ShapeDtypeStruct((rows, 768), BF16)
    probs, frames, *kept = pl.pallas_call(
        forward_alone,
        name="forward",
        out_shape=[probs, frames, *forward_outs(rows)],
        in_specs=[hbm()] + [vmem()] * 12,
        out_specs=[hbm()] * (2 + N_KEPT),
        scratch_shapes=[pltpu.VMEM(BLOCKS, BF16), pltpu.VMEM((8, 768), F32), *forward_scratch(rows), pltpu.SemaphoreType.DMA],
        compiler_params=pltpu.CompilerParams(vmem_limit_bytes=VMEM_LIMIT),
    )(*ins)
    return probs, frames, kept


ATT_ORDER = (0, 3, 1, 2)
DOWN_ORDER = (3, 0, 2, 1)
DEEP = 32


def att_order(place):
    return jnp.where(place == 0, 0, jnp.where(place == 1, 3, place - 1))


def down_order(place):
    return jnp.where(place == 0, 3, jnp.where(place == 1, 0, 4 - place))


def row_parts(kind):
    base = DEEP if kind == DOWN else 0
    half = (96 - base) // 2
    return pl.ds(base, half), pl.ds(base + half, half), pl.ds(base, 2 * half)


def chunk_at(n):
    return (DOWN, DOWN_ORDER[n]) if n < 4 else (UP, n - 4) if n < 8 else (ATT, ATT_ORDER[n - 8])


ALL = pl.ds(0, 3)


class Scatter:
    def __init__(self, at, grads, out, buffers, semaphores):
        self.at, self.grads, self.out = at, grads, out
        self.core_in, self.first_in, self.second_in, self.z_in, self.deep_in, self.plane_in = buffers
        self.send, self.recv, self.z_send, self.z_recv, *deep = semaphores
        self.deep_send, self.deep_recv, self.plane_send, self.plane_recv = deep

    def copy(self, kind, m, which):
        every, index = ((slice(None),), slice(None)) if m is None else ((), m)
        recv = 0 if m is None else m
        at, grads = self.at, self.grads.at[kind, index]
        x, y, c = at.x, at.y, at.c
        low, high, _ = row_parts(kind)
        core, first, second = self.core_in.at[kind, index], self.first_in.at[kind, index], self.second_in.at[kind, index]
        part, whole = pl.ds(0, low.size), slice(None)
        src, dst, device = {
            0: lambda: (grads.at[(*every, whole, whole, 1 - c)], core, at.core),
            1: lambda: (grads.at[(*every, whole, 1 - x, c, low)], first.at[(*every, 0, whole, part)], at.across_x),
            2: lambda: (grads.at[(*every, 1 - y, whole, c, high)], first.at[(*every, 1, whole, part)], at.across_y),
            3: lambda: (grads.at[(*every, 1 - y, x, c, low)], second.at[(*every, 0, part)], at.across_y),
            4: lambda: (grads.at[(*every, y, 1 - x, c, high)], second.at[(*every, 1, part)], at.across_x),
        }[which]()
        return remote(src, dst, self.send.at[kind, which], self.recv.at[kind, recv, which], device)

    def add(self, ref, got):
        ref[...] = (ref[...].astype(F32) + got[...].astype(F32)).astype(BF16)

    def begin(self, kind, m):
        self.copy(kind, m, 0).start()

    def first(self, kind, m):
        at, grads = self.at, self.grads.at[kind, m]
        self.copy(kind, m, 0).wait_recv()
        for y in range(2):
            for x in range(2):
                self.add(grads.at[y, x, at.c], self.core_in.at[kind, m, y, x])
        self.copy(kind, m, 1).start()
        self.copy(kind, m, 2).start()
        if kind == DOWN:
            self.ends(m, lambda direction: self.deep_copy(m, direction).start())

    def second(self, kind, m):
        at, grads = self.at, self.grads.at[kind, m]
        low, high, _ = row_parts(kind)
        part = pl.ds(0, low.size)
        self.copy(kind, m, 1).wait_recv()
        for y in range(2):
            self.add(grads.at[y, at.x, at.c, low], self.first_in.at[kind, m, 0, y, part])
        self.copy(kind, m, 3).start()
        self.copy(kind, m, 2).wait_recv()
        for x in range(2):
            self.add(grads.at[at.y, x, at.c, high], self.first_in.at[kind, m, 1, x, part])
        self.copy(kind, m, 4).start()

    def third(self, kind, m):
        at = self.at
        grads = self.grads.at[kind, m, at.y, at.x, at.c]
        low, high, _ = row_parts(kind)
        part = pl.ds(0, low.size)
        self.copy(kind, m, 3).wait_recv()
        self.add(grads.at[low], self.second_in.at[kind, m, 0, part])
        self.copy(kind, m, 4).wait_recv()
        self.add(grads.at[high], self.second_in.at[kind, m, 1, part])
        self.z_start(kind, m)

    def ends(self, m, act):
        z = self.at.z
        if m > 0:
            pl.when(z == 0)(lambda: act(0))
        if m < 3:
            pl.when(z == 3)(lambda: act(1))

    def deep_copy(self, m, direction, slot=None):
        at = self.at
        device = at.mate if slot is ALL else at.right if direction == 0 else at.left
        if slot is None:
            slot = m if direction == 0 else jnp.where(m == at.z - 1, 4, m)
        recv = slot if slot is not ALL else 0
        src = self.grads.at[DOWN, m, :, :, at.c, pl.ds(0, DEEP)]
        return remote(src, self.deep_in.at[slot], self.deep_send, self.deep_recv.at[recv], device)

    def deep_add(self, m, slot, direction):
        self.deep_copy(m, direction, slot).wait_recv()
        for y in range(2):
            for x in range(2):
                self.add(self.grads.at[DOWN, m, y, x, self.at.c, pl.ds(0, DEEP)], self.deep_in.at[slot, y, x])

    def deep_relay(self, m, direction):
        self.deep_add(m, m, direction)
        self.deep_copy(m, direction).start()

    def deep_one(self, kind, m):
        z = self.at.z
        if m > 1:
            pl.when(z == 1)(lambda: self.deep_relay(m, 0))
        else:
            pl.when(z == 2)(lambda: self.deep_relay(m, 1))

    def deep_two(self, kind, m):
        z = self.at.z
        if m == 3:
            pl.when(z == 2)(lambda: self.deep_relay(m, 0))
        if m == 0:
            pl.when(z == 1)(lambda: self.deep_relay(m, 1))

    def deep_plane(self, which):
        at, grads = self.at, self.grads.at[DOWN, self.at.z]
        x, y, c = at.x, at.y, at.c
        half = DEEP // 2
        low, high = pl.ds(0, half), pl.ds(half, half)
        src, dst, device = {
            0: lambda: (grads.at[:, 1 - x, c, low], self.plane_in.at[0], at.across_x),
            1: lambda: (grads.at[1 - y, :, c, high], self.plane_in.at[1], at.across_y),
            2: lambda: (grads.at[1 - y, x, c, low], self.plane_in.at[2, 0], at.across_y),
            3: lambda: (grads.at[y, 1 - x, c, high], self.plane_in.at[2, 1], at.across_x),
        }[which]()
        return remote(src, dst, self.plane_send.at[which], self.plane_recv.at[which], device)

    def deep_first(self):
        z = self.at.z
        pl.when(z > 0)(lambda: self.deep_add(z, z, 0))
        pl.when(z < 3)(lambda: self.deep_add(z, 4, 1))
        self.deep_plane(0).start()
        self.deep_plane(1).start()

    def deep_second(self):
        at, half = self.at, DEEP // 2
        grads = self.grads.at[DOWN, at.z]
        self.deep_plane(0).wait_recv()
        for y in range(2):
            self.add(grads.at[y, at.x, at.c, pl.ds(0, half)], self.plane_in.at[0, y])
        self.deep_plane(2).start()
        self.deep_plane(1).wait_recv()
        for x in range(2):
            self.add(grads.at[at.y, x, at.c, pl.ds(half, half)], self.plane_in.at[1, x])
        self.deep_plane(3).start()

    def deep_third(self):
        at, half = self.at, DEEP // 2
        grads = self.grads.at[DOWN, at.z, at.y, at.x, at.c]
        self.deep_plane(2).wait_recv()
        self.add(grads.at[pl.ds(0, half)], self.plane_in.at[2, 0])
        self.deep_plane(3).wait_recv()
        self.add(grads.at[pl.ds(half, half)], self.plane_in.at[2, 1])

    def z_copy(self, kind, m, direction, slot=None):
        at = self.at
        whole = row_parts(kind)[2]
        device = at.mate if slot is ALL else at.right if direction == 0 else at.left
        if slot is None:
            slot = m if direction == 0 else jnp.where(m == at.z - 1, 4, m)
        recv = slot if slot is not ALL else 0
        src = self.grads.at[kind, m, at.y, at.x, at.c, whole]
        dst = self.z_in.at[kind, slot, whole]
        return remote(src, dst, self.z_send.at[kind], self.z_recv.at[kind, recv], device)

    def relay(self, kind, m, direction):
        whole = row_parts(kind)[2]
        self.z_copy(kind, m, direction, m).wait_recv()
        self.add(self.grads.at[kind, m, self.at.y, self.at.x, self.at.c, whole], self.z_in.at[kind, m, whole])
        self.z_copy(kind, m, direction).start()

    def z_start(self, kind, m):
        self.ends(m, lambda direction: self.z_copy(kind, m, direction).start())

    def z_one(self, kind, m):
        z = self.at.z
        if m > 1:
            pl.when(z == 1)(lambda: self.relay(kind, m, 0))
        else:
            pl.when(z == 2)(lambda: self.relay(kind, m, 1))

    def z_two(self, kind, m):
        z = self.at.z
        if m == 3:
            pl.when(z == 2)(lambda: self.relay(kind, m, 0))
        if m == 0:
            pl.when(z == 1)(lambda: self.relay(kind, m, 1))

    def finish(self, kind):
        at, z = self.at, self.at.z
        whole = row_parts(kind)[2]
        self.out[kind] = self.grads[kind, z, at.y, at.x, at.c].astype(F32)

        @pl.when(z > 0)
        def _():
            self.z_copy(kind, z, 0, z).wait_recv()
            self.out[kind, whole] += self.z_in[kind, z, whole].astype(F32)

        @pl.when(z < 3)
        def _():
            self.z_copy(kind, z, 1, 4).wait_recv()
            self.out[kind, whole] += self.z_in[kind, 4, whole].astype(F32)

    def run(self, **steps):
        for name, places in steps.items():
            for n in places:
                getattr(self, name)(*chunk_at(n))

    def drain(self):
        for which in range(4):
            self.deep_plane(which).wait_send()
        self.deep_copy(ALL, 0, ALL).wait_send()
        for kind in range(3):
            for which in range(5):
                self.copy(kind, None, which).wait_send()
            self.z_copy(kind, ALL, 0, ALL).wait_send()


class Totals:
    def __init__(self, at, rows, got, send, recv):
        self.rows, self.got, self.send, self.recv = rows, got, send, recv
        self.partners = (at.core, at.mate, at.far, at.across_x, at.across_y)

    def copy(self, stage):
        return remote(
            self.rows.at[stage], self.got.at[stage], self.send.at[stage], self.recv.at[stage], self.partners[stage]
        )

    def start(self, stage):
        self.copy(stage).start()

    def finish(self, stage):
        self.copy(stage).wait()
        self.rows[stage + 1] = self.rows[stage] + self.got[stage]


def backward_compute(
    blocks_hbm,
    probs_hbm,
    acted_hbm,
    slope_hbm,
    recip_hbm,
    headout_hbm,
    xt_hbm,
    qm_hbm,
    kt_hbm,
    v_hbm,
    att_hbm,
    n1t_hbm,
    n1_hbm,
    rs1_hbm,
    gb2_hbm,
    g2_hbm,
    sums_hbm,
    masked_hbm,
    gain_ref,
    grads,
    rows_ref,
    weight,
    weight_sem,
    acts,
    acts_sem,
    probs,
    probs_sem,
    gb1,
    gb1t,
    grad_one,
    parts,
    g2_ref,
    state_sem,
    gb2_ref,
    gb2t_ref,
    n1t_ref,
    xt_ref,
    headout_ref,
    qm_ref,
    kt_ref,
    v_ref,
    att_ref,
    head_sem,
    own,
    sides,
    shifts,
    shares,
    recip_ref,
    rs1_ref,
    sums_ref,
    masked_ref,
    small_sem,
    hooks,
):
    rows = g2_ref.shape[0]
    g2_load = pltpu.make_async_copy(g2_hbm, g2_ref, state_sem.at[0])
    n1_load = pltpu.make_async_copy(n1_hbm, grad_one, state_sem.at[1])
    gb2_load = pltpu.make_async_copy(gb2_hbm, gb2_ref, state_sem.at[2])
    n1t_load = pltpu.make_async_copy(n1t_hbm, n1t_ref, state_sem.at[4])
    xt_load = pltpu.make_async_copy(xt_hbm, xt_ref, state_sem.at[5])

    small_loads = [
        pltpu.make_async_copy(src, dst, small_sem.at[i])
        for i, (src, dst) in enumerate(
            ((recip_hbm, recip_ref), (rs1_hbm, rs1_ref), (sums_hbm, sums_ref), (masked_hbm, masked_ref))
        )
    ]

    def head_loads(m, slot, side):
        three, two, half = pl.ds(3 * m, 3), pl.ds(2 * m, 2), pl.ds(side * rows, rows)
        pairs = [
            (qm_hbm.at[three], qm_ref.at[slot]),
            (kt_hbm.at[two, :, half], kt_ref.at[slot]),
            (v_hbm.at[two, half], v_ref.at[slot]),
            (headout_hbm.at[three], headout_ref.at[slot]) if side else (att_hbm.at[m], att_ref.at[slot]),
        ]
        return [
            pltpu.make_async_copy(src, dst, head_sem.at[slot, i if i < 3 else 4 - side])
            for i, (src, dst) in enumerate(pairs)
        ]

    def weight_load(kind, m, slot):
        return pltpu.make_async_copy(blocks_hbm.at[kind, m], weight.at[slot], weight_sem.at[slot])

    def act_load(which, m):
        pair, place = m // 2, lax.rem(m, 2)
        return pltpu.make_async_copy(which.at[m], acts.at[pair, place], acts_sem.at[pair, place])

    def probs_loads(m, slot, side):
        half = pl.ds(side * rows, rows)
        return [
            pltpu.make_async_copy(probs_hbm.at[3 * m + j, half], probs.at[slot, j], probs_sem.at[slot, j])
            for j in range(3)
        ]

    def feed_loads(m, slot):
        return (weight_load(DOWN, m, 2 * slot), weight_load(UP, m, 2 * slot + 1))

    def begin(copies):
        for copy in copies:
            copy.start()

    def finish(copies):
        for copy in copies:
            copy.wait()

    def block(slot, low=0, width=768):
        return weight[slot, :, :, :, :, pl.ds(low, width)].reshape(768, width)

    def put(kind, m, value, low=0):
        width = value.shape[1]
        grads[kind, m, :, :, :, :, pl.ds(low, width)] = value.astype(BF16).reshape(2, 2, 2, 96, width)

    begin((gb2_load, act_load(acted_hbm, DOWN_ORDER[0])))
    parts[...] = jnp.zeros_like(parts)
    finish((gb2_load,))
    begin([act_load(acted_hbm, m) for m in DOWN_ORDER[1:]])
    gb2t_ref[...] = gb2_ref[...].T

    def feed_down(m):
        act_load(acted_hbm, m).wait()
        put(DOWN, m, dot(gb2t_ref[...], acts[m // 2, lax.rem(m, 2)]))

    feed_down(DOWN_ORDER[0])
    hooks.after("start")
    hooks.ready(DOWN, DOWN_ORDER[0])
    begin(feed_loads(0, 0))
    act_load(slope_hbm, DOWN_ORDER[0]).start()

    def feed_downs(place, _):
        m = down_order(place)
        feed_down(m)
        hooks.ready(DOWN, m)
        act_load(slope_hbm, m).start()

        @pl.when(place == 1)
        def _():
            begin((n1t_load, g2_load, n1_load, *small_loads, xt_load))
            begin(head_loads(0, 0, 1))
            begin(probs_loads(0, 0, 1))

        hooks.after("down", place)
        return 0

    lax.fori_loop(1, 4, feed_downs, 0)
    finish((n1t_load, g2_load))

    def feed(m, _):
        slot = lax.rem(m, 2)
        pl.when(m < 3)(lambda: begin(feed_loads(m + 1, 1 - slot)))
        finish(feed_loads(m, slot))
        act_load(slope_hbm, m).wait()
        grad_acted = dot(gb2_ref[...], block(2 * slot))
        grad_pre = (grad_acted * acts[m // 2, lax.rem(m, 2)].astype(F32)).astype(BF16)
        parts[m, 0:1, :] = jnp.sum(grad_pre.astype(F32), axis=0, keepdims=True)
        put(UP, m, dot(n1t_ref[...], grad_pre))
        g2_ref[...] += dot(grad_pre, block(2 * slot + 1), (1, 1))
        hooks.ready(UP, m)
        hooks.after("feed", m)
        return 0

    lax.fori_loop(0, 4, feed, 0)
    for m in range(4):
        weight_load(ATT, m, m).start()

    chunk = 64

    def norm_back(i, sums):
        r = pl.ds(pl.multiple_of(i * chunk, chunk), chunk)
        grad = g2_ref[r, :]
        unit = grad_one[r, :]
        scaled = grad * gain
        grad_in = (
            scaled
            - jnp.mean(scaled, axis=1, keepdims=True)
            - unit * jnp.mean(scaled * unit, axis=1, keepdims=True)
        ) * rs1_ref[r, :]
        grad_one[r, :] = grad_in
        gb1[r, :] = grad_in.astype(BF16)
        return (
            sums[0] + jnp.sum(grad_in, axis=0, keepdims=True),
            sums[1] + jnp.sum(grad * unit, axis=0, keepdims=True),
            sums[2] + jnp.sum(grad, axis=0, keepdims=True),
        )

    zero = jnp.zeros((1, 768), F32)
    finish((n1_load, xt_load))
    finish(small_loads)
    gain = gain_ref[...].astype(F32).reshape(1, 768)
    sums = lax.fori_loop(0, rows // chunk, norm_back, (zero, zero, zero), unroll=4)
    rows_ref[0, 0:1, :] = sums[0]
    rows_ref[0, 1:2, :] = sums_ref[0:1, :]
    rows_ref[0, 2:3, :] = sums[1]
    rows_ref[0, 3:4, :] = sums[2]
    rows_ref[0, 4:5, :] = sums_ref[1:2, :]
    rows_ref[0, 5:6, :] = sums_ref[2:3, :]
    gb1t[...] = gb1[...].T
    hooks.after("norm")
    g2_ref[...] = jnp.zeros_like(g2_ref)

    def wide(j, side):
        zeros = jnp.zeros((64, rows), BF16)
        return jnp.concatenate([zeros, side] if j == 1 else [side, zeros], axis=0)

    def half_back(slot, sides_here, shifts_here):
        grads_k, grads_v, grads_q = [], [], []
        wides = [wide(j, sides_here[j]) for j in range(3)]
        grad_weights = [dot(v_ref[slot, j // 2], wides[j]) for j in range(3)]
        for j in range(3):
            weights = probs[slot, j]
            grad_scores = (weights.astype(F32) * (grad_weights[j] - shifts_here[j])).astype(BF16)
            grads_v.append(dot(weights, wides[j].T))
            grads_k.append(dot(grad_scores, qm_ref[slot, j]))
            lane = 0 if j == 0 else 64
            grads_q.append(dot(kt_ref[slot, j // 2, lane : lane + 64, :], grad_scores))
        return [grads_k[0] + grads_k[1], grads_k[2]], [grads_v[0] + grads_v[1], grads_v[2]], grads_q

    def back_other(m, _):
        slot = lax.rem(m, 2)
        pl.when(m < 3)(lambda: begin([*head_loads(m + 1, 1 - slot, 1), *probs_loads(m + 1, 1 - slot, 1)]))
        pl.when(m == 3)(lambda: begin([*head_loads(0, 0, 0), *probs_loads(0, 0, 0)]))
        weight_load(ATT, m, m).wait()
        finish(head_loads(m, slot, 1))
        finish(probs_loads(m, slot, 1))
        grad_att_t = dot(gb1[...], block(m, 512, 256)).T
        others, shifts_here = [], []
        for j in range(3):
            head = 3 * m + j
            place = (128, 192, 64)[j]
            grad_att = grad_att_t[place : place + 64, :]
            factor_own, factor = recip_ref[head, 0:1, :], recip_ref[head, 1:2, :]
            own_side = (grad_att * factor_own).astype(BF16)
            others.append((grad_att * factor).astype(BF16))
            row_sum = jnp.sum(
                own_side.astype(F32) * headout_ref[slot, j, 0] + others[j].astype(F32) * headout_ref[slot, j, 1],
                axis=0,
                keepdims=True,
            )
            sides[head] = own_side
            shifts[head, 0:1, :] = row_sum * factor_own
            shifts_here.append(row_sum * factor)
        grads_k, grads_v, grads_q = half_back(slot, others, shifts_here)
        for j in range(3):
            shares[3 * m + j] = grads_q[j]
        tile = acts.at[m // 2, lax.rem(m, 2)]
        tile[:, 128:256] = grads_k[0].astype(BF16)
        tile[:, 256:384] = grads_v[0].astype(BF16)
        tile[:, 384:512] = grads_k[1].astype(BF16)
        tile[:, 512:640] = grads_v[1].astype(BF16)
        parts[4 + m, 0:1, 128:640] = jnp.sum(tile[:, 128:640].astype(F32), axis=0, keepdims=True)
        g2_ref[...] += dot(tile[:, 128:640], block(m, 128, 512), (1, 1))
        hooks.after("other", m)
        return 0

    lax.fori_loop(0, 4, back_other, 0)

    def fill_other(i, total):
        r = pl.ds(pl.multiple_of(i * chunk, chunk), chunk)
        other = g2_ref[r, :]
        gb1[r, :] = other.astype(BF16)
        return total + jnp.sum(other * masked_ref[1, r, :], axis=0, keepdims=True)

    fill = lax.fori_loop(0, rows // chunk, fill_other, zero, unroll=4)
    hooks.after("mate")

    def back_own(place, _):
        slot = lax.rem(place, 2)
        m = att_order(place)

        @pl.when(place < 3)
        def _():
            after = att_order(place + 1)
            begin([*head_loads(after, 1 - slot, 0), *probs_loads(after, 1 - slot, 0)])

        finish(head_loads(m, slot, 0))
        finish(probs_loads(m, slot, 0))
        grads_k, grads_v, grads_q = half_back(
            slot, [sides[3 * m + j] for j in range(3)], [shifts[3 * m + j, 0:1, :] for j in range(3)]
        )
        grads_q = [(grads_q[j] + shares[3 * m + j]) * SCALE for j in range(3)]
        single = jnp.concatenate([grads_q[2], jnp.zeros((64, rows), F32)], axis=0).T
        own[:, 0:128] = jnp.concatenate(grads_q[:2], axis=0).T.astype(BF16)
        own[:, 128:256] = grads_k[0].astype(BF16)
        own[:, 256:384] = grads_v[0].astype(BF16)
        own[:, 384:512] = (grads_k[1] + single).astype(BF16)
        own[:, 512:640] = grads_v[1].astype(BF16)
        parts[4 + m, 0:1, 0:PROJ] += jnp.sum(own[...].astype(F32), axis=0, keepdims=True)
        hooks.after("middle", place)
        other = acts[m // 2, lax.rem(m, 2), :, 128:640]
        grad_proj = dot(xt_ref[0], own[...])
        grad_other = dot(xt_ref[1], other)
        grad_out_w = dot(gb1t[...], att_ref[slot])
        put(ATT, m, grad_proj[:, :128], 0)
        put(ATT, m, grad_proj[:, 128:512] + grad_other[:, :384], 128)
        put(ATT, m, grad_proj[:, 512:] + grad_other[:, 384:] + grad_out_w[:, :128], 512)
        put(ATT, m, grad_out_w[:, 128:], 640)
        grad_one[...] += dot(own[...], block(m, 0, PROJ), (1, 1))
        hooks.ready(ATT, m)
        hooks.after("own", place)
        return 0

    lax.fori_loop(0, 4, back_own, 0)

    def fill_own(i, total):
        r = pl.ds(pl.multiple_of(i * chunk, chunk), chunk)
        return total + jnp.sum(grad_one[r, :] * masked_ref[0, r, :], axis=0, keepdims=True)

    rows_ref[0, 6:7, :] = lax.fori_loop(0, rows // chunk, fill_own, fill, unroll=4)
    rows_ref[0, 7:8, :] = zero
    for row in range(8):
        rows_ref[0, 8 + row : 9 + row, :] = parts[row, 0:1, :]


def finish_frames(grad_one, got, masked_ref, frames_ref):
    chunk = 64

    def body(i, _):
        r = pl.ds(pl.multiple_of(i * chunk, chunk), chunk)
        total = grad_one[r, :] + got[r, :].astype(F32)
        frames_ref[r, :] = jnp.where(masked_ref[0, r, :] > 0, 0.0, total).astype(BF16)
        return 0

    lax.fori_loop(0, grad_one.shape[0] // chunk, body, 0, unroll=4)


class NoScatter:
    def after(self, point, m=0):
        pass

    def ready(self, kind, m):
        pass


class ScatterHooks:
    PLAN = {
        ("down", 2): dict(first=(0,)),
        ("down", 3): dict(first=(1,)),
        ("feed", 0): dict(first=(2, 3)),
        ("feed", 1): dict(second=(0, 1), deep_one=(0,)),
        ("feed", 2): dict(second=(2,), first=(4,), deep_one=(1,)),
        ("feed", 3): dict(second=(3,), first=(5,), third=(0,), deep_one=(2,), deep_two=(0,)),
        ("norm", 0): dict(third=(1,), deep_one=(3,), deep_two=(1,)),
        ("other", 0): dict(second=(4,), first=(6,), third=(2,)),
        ("other", 1): dict(deep=("deep_first",), third=(3,), z_one=(0,)),
        ("other", 2): dict(first=(7,), z_one=(1,)),
        ("other", 3): dict(second=(5,), third=(4,), z_one=(2,), z_two=(0,)),
        ("mate", 0): dict(swap=(0,)),
        ("middle", 0): dict(deep=("deep_second",), swap=(1,)),
        ("own", 0): dict(second=(6,), third=(5,), z_one=(3,), z_two=(1,)),
        ("middle", 1): dict(first=(8,), deep=("deep_third",), swap=(2,)),
        ("own", 1): dict(second=(7,), z_one=(4,)),
        ("middle", 2): dict(first=(9,), third=(6,), swap=(3,)),
        ("own", 2): dict(z_one=(5,)),
        ("middle", 3): dict(second=(8,), first=(10,), third=(7,)),
        ("own", 3): dict(z_one=(6,), z_two=(4,)),
    }

    def __init__(self, at, scatter, swaps):
        self.at, self.scatter, self.swaps = at, scatter, swaps

    def ready(self, kind, m):
        self.scatter.begin(kind, m)

    def run(self, swap=(), deep=(), **steps):
        self.scatter.run(**steps)
        for name in deep:
            getattr(self.scatter, name)()
        for piece in swap:
            self.swaps[piece].start()

    def after(self, point, m=0):
        if point == "start":
            self.at.meet(True)
        for (name, index), steps in self.PLAN.items():
            if name == point:
                if isinstance(m, int):
                    self.run(**steps)
                else:
                    pl.when(m == index)(functools.partial(self.run, **steps))


N_BACKWARD_INS = 19
N_BACKWARD_SCRATCH = 33


def backward_linked(*refs):
    ins = refs[:N_BACKWARD_INS]
    out_ref, rows_out, frames_ref = refs[N_BACKWARD_INS : N_BACKWARD_INS + 3]
    scratch = refs[N_BACKWARD_INS + 3 :]
    scratch, links = scratch[:N_BACKWARD_SCRATCH], scratch[N_BACKWARD_SCRATCH:]
    grads, rows_ref, gb1, grad_one = scratch[0], scratch[1], scratch[8], scratch[10]
    rows_in, mate_in, t_send, t_recv, m_send, m_recv = links[14:]
    at = Place()
    at.hello(True)
    scatter = Scatter(at, grads, out_ref, links[:6], links[6:14])
    totals = Totals(at, rows_ref, rows_in, t_send, t_recv)
    piece = gb1.shape[0] // 4
    swaps = [
        remote(
            gb1.at[pl.ds(i * piece, piece)], mate_in.at[pl.ds(i * piece, piece)], m_send.at[i], m_recv.at[i], at.mate
        )
        for i in range(4)
    ]
    backward_compute(*ins, *scratch, ScatterHooks(at, scatter, swaps))
    totals.start(0)
    scatter.run(second=(9,), first=(11,))
    totals.finish(0)
    totals.start(1)
    scatter.run(third=(8,), z_one=(7,))
    scatter.run(second=(10,))
    scatter.run(third=(9,))
    totals.finish(1)
    totals.start(2)
    scatter.run(second=(11,))
    scatter.run(z_one=(8,), z_two=(7,))
    scatter.run(third=(10,))
    totals.finish(2)
    totals.start(3)
    scatter.run(third=(11,))
    scatter.run(z_one=(9,), z_two=(8,))
    scatter.finish(DOWN)
    scatter.finish(UP)
    totals.finish(3)
    totals.start(4)
    scatter.run(z_one=(10,))
    for swap in swaps:
        swap.wait()
    finish_frames(grad_one, mate_in, scratch[31], frames_ref)
    scatter.run(z_one=(11,), z_two=(9,))
    totals.finish(4)
    rows_out[...] = rows_ref[5]
    scatter.drain()
    scatter.finish(ATT)


def backward_alone(*refs):
    ins = refs[:N_BACKWARD_INS]
    grads_out, rows_out, mate_out, grad_one_out = refs[N_BACKWARD_INS : N_BACKWARD_INS + 4]
    scratch = refs[N_BACKWARD_INS + 4 :]
    *scratch, keep_sem = scratch
    grads, rows_ref, gb1, grad_one = scratch[0], scratch[1], scratch[8], scratch[10]
    backward_compute(*ins, *scratch, NoScatter())
    keep = pltpu.make_async_copy(grads, grads_out, keep_sem)
    keep.start()
    rows_out[...] = rows_ref[0]
    mate_out[...] = gb1[...]
    grad_one_out[...] = grad_one[...]
    keep.wait()


def backward_scratch(rows):
    return [
        pltpu.VMEM(BLOCKS, BF16),
        pltpu.VMEM((6, 16, 768), F32),
        pltpu.VMEM((4, *BLOCKS[2:]), BF16),
        pltpu.SemaphoreType.DMA((4,)),
        pltpu.VMEM((2, 2, rows, 768), BF16),
        pltpu.SemaphoreType.DMA((2, 2)),
        pltpu.VMEM((2, 3, rows, rows), BF16),
        pltpu.SemaphoreType.DMA((2, 3)),
        pltpu.VMEM((rows, 768), BF16),
        pltpu.VMEM((768, rows), BF16),
        pltpu.VMEM((rows, 768), F32),
        pltpu.VMEM((8, 8, 768), F32),
        pltpu.VMEM((rows, 768), F32),
        pltpu.SemaphoreType.DMA((6,)),
        pltpu.VMEM((rows, 768), BF16),
        pltpu.VMEM((768, rows), BF16),
        pltpu.VMEM((768, rows), BF16),
        pltpu.VMEM((2, 768, rows), BF16),
        pltpu.VMEM((2, 3, 2, 64, rows), F32),
        pltpu.VMEM((2, 3, rows, 128), BF16),
        pltpu.VMEM((2, 2, 128, rows), BF16),
        pltpu.VMEM((2, 2, rows, 128), BF16),
        pltpu.VMEM((2, rows, 256), BF16),
        pltpu.SemaphoreType.DMA((2, 5)),
        pltpu.VMEM((rows, PROJ), BF16),
        pltpu.VMEM((12, 64, rows), BF16),
        pltpu.VMEM((12, 8, rows), F32),
        pltpu.VMEM((12, 64, rows), F32),
        pltpu.VMEM((12, 8, rows), F32),
        pltpu.VMEM((rows, 1), F32),
        pltpu.VMEM((8, 768), F32),
        pltpu.VMEM((2, rows, 1), F32),
        pltpu.SemaphoreType.DMA((4,)),
    ]


def run_backward(linked, blocks, probs, kept, masked, gain):
    recip, headout, xt, qm, kt, v, att, acted, slope, n1t, n1, rs1, gb2, g2, sums = kept
    rows = gb2.shape[0]
    ins = (
        blocks, probs, acted, slope, recip, headout, xt, qm, kt, v, att, n1t, n1, rs1, gb2, g2, sums, masked, gain
    )
    in_specs = [vmem() if i == 18 else hbm() for i in range(19)]
    if linked:
        return pl.pallas_call(
            backward_linked,
            name="backward",
            out_shape=[
                jax.ShapeDtypeStruct((3, 96, 768), F32),
                jax.ShapeDtypeStruct((16, 768), F32),
                jax.ShapeDtypeStruct((rows, 768), BF16),
            ],
            in_specs=in_specs,
            out_specs=[vmem()] * 3,
            scratch_shapes=[
                *backward_scratch(rows),
                pltpu.VMEM((3, 4, 2, 2, 96, 768), BF16),
                pltpu.VMEM((3, 4, 2, 2, 48, 768), BF16),
                pltpu.VMEM((3, 4, 2, 48, 768), BF16),
                pltpu.VMEM((3, 5, 96, 768), BF16),
                pltpu.VMEM((5, 2, 2, DEEP, 768), BF16),
                pltpu.VMEM((3, 2, DEEP // 2, 768), BF16),
                pltpu.SemaphoreType.DMA((3, 5)),
                pltpu.SemaphoreType.DMA((3, 4, 5)),
                pltpu.SemaphoreType.DMA((3,)),
                pltpu.SemaphoreType.DMA((3, 5)),
                pltpu.SemaphoreType.DMA,
                pltpu.SemaphoreType.DMA((5,)),
                pltpu.SemaphoreType.DMA((4,)),
                pltpu.SemaphoreType.DMA((4,)),
                pltpu.VMEM((5, 16, 768), F32),
                pltpu.VMEM((rows, 768), BF16),
                pltpu.SemaphoreType.DMA((5,)),
                pltpu.SemaphoreType.DMA((5,)),
                pltpu.SemaphoreType.DMA((4,)),
                pltpu.SemaphoreType.DMA((4,)),
            ],
            compiler_params=pltpu.CompilerParams(
                collective_id=1, has_side_effects=True, vmem_limit_bytes=VMEM_LIMIT
            ),
        )(*ins)
    return pl.pallas_call(
        backward_alone,
        name="backward",
        out_shape=[
            jax.ShapeDtypeStruct(BLOCKS, BF16),
            jax.ShapeDtypeStruct((16, 768), F32),
            jax.ShapeDtypeStruct((rows, 768), BF16),
            jax.ShapeDtypeStruct((rows, 768), F32),
        ],
        in_specs=in_specs,
        out_specs=[hbm()] + [vmem()] * 3,
        scratch_shapes=[*backward_scratch(rows), pltpu.SemaphoreType.DMA],
        compiler_params=pltpu.CompilerParams(vmem_limit_bytes=VMEM_LIMIT),
    )(*ins)


def finish_kernel(parts, grads, totals, out_in, frames_in, out, frames, *outs):
    n_dp, n_mp = parts
    query, key, value, out_w, up, down, query_bias, value_bias, up_bias, *vectors = outs
    out[...] = out_in[...]
    frames[...] = frames_in[...]
    att = grads[0]
    query[...] = jnp.concatenate([att[:, 0:128], att[:, 384:448]], axis=1)
    key[...] = jnp.concatenate([att[:, 128:256], att[:, 448:512]], axis=1)
    value[...] = jnp.concatenate([att[:, 256:384], att[:, 512:576]], axis=1)
    out_w[...] = jnp.concatenate([att[:, 640:768], att[:, 576:640]], axis=1).T
    up[...] = grads[1]
    down[...] = grads[2]
    dp, z = lax.axis_index("dp"), lax.axis_index("mp")
    rows = totals[...]
    row_at = lax.broadcasted_iota(jnp.int32, rows.shape, 0)

    def shifted(block, by):
        return pltpu.roll(block, lax.rem(768 - by, 768), 1)

    def row_of(index):
        return jnp.broadcast_to(jnp.sum(jnp.where(row_at == index, rows, 0.0), axis=0, keepdims=True), (8, 768))

    part = 768 // (n_dp * n_mp)
    mine = shifted(rows[0:8], (dp * n_mp + z) * part)
    for i, ref in enumerate(vectors):
        ref[...] = mine[i : i + 1, :part]
    step = HEAD_DIM // n_dp
    heads = shifted(row_of(12 + z), dp * step)
    for head, (q_lane, v_lane) in enumerate(((0, 256), (64, 320), (384, 512))):
        query_bias[head : head + 1, :] = heads[0:1, q_lane : q_lane + step]
        value_bias[head : head + 1, :] = heads[0:1, v_lane : v_lane + step]
    ups = shifted(row_of(8 + z), dp * 2 * step)
    for i in range(6):
        up_bias[i : i + 1, :] = ups[0:1, 128 * i : 128 * i + 2 * step]


def run_finish(n_dp, n_mp, grads, totals, out, frames):
    def of(shape, dtype=F32):
        return jax.ShapeDtypeStruct(shape, dtype)

    d, step, part = grads.shape[1], HEAD_DIM // n_dp, 768 // (n_dp * n_mp)
    *outs, = pl.pallas_call(
        functools.partial(finish_kernel, (n_dp, n_mp)),
        name="finish",
        out_shape=[
            of(out.shape, BF16), of(frames.shape, BF16), of((d, 192)), of((d, 192)), of((d, 192)), of((192, d)),
            of((d, 768)), of((d, 768)), of((3, step)), of((3, step)), of((6, 2 * step)), *[of((1, part))] * 7,
        ],
        in_specs=[vmem()] * 4,
        out_specs=[vmem()] * 18,
        compiler_params=pltpu.CompilerParams(vmem_limit_bytes=VMEM_LIMIT),
    )(grads, totals, out, frames)
    return (*outs[:7], outs[7].T, *outs[8:11], *(row.reshape(part) for row in outs[11:]))


def shards(
    linked,
    frames,
    lengths,
    span_starts,
    cotangent,
    query_weight,
    key_weight,
    value_weight,
    out_weight,
    up_weight,
    down_weight,
    query_bias,
    value_bias,
    up_bias,
    out_bias,
    down_bias,
    first_gain,
    first_shift,
    second_gain,
    second_shift,
    mask_vector,
):
    rows = frames.shape[0]
    n_dp = 768 // query_weight.shape[0]
    n_mp = 768 // query_weight.shape[1]
    vecs = (out_bias, down_bias, first_gain, first_shift, second_gain, second_shift, mask_vector)
    if linked:
        blocks, probs, out, masked, kept = run_forward_linked(
            rows, lengths, span_starts, frames, cotangent, query_weight, key_weight, value_weight, out_weight,
            up_weight, down_weight.T, query_bias, value_bias, up_bias, *vecs,
        )
        grads, totals, grad_frames = run_backward(True, blocks, probs, kept, masked, first_gain)
        return run_finish(n_dp, n_mp, grads, totals, out, grad_frames)
    z = lax.axis_index("mp")
    half = z % 2
    length = lax.dynamic_index_in_dim(lengths, z // 2, keepdims=False)
    starts = lax.dynamic_index_in_dim(span_starts, z // 2, keepdims=False)
    slots = (jnp.arange(LEN, dtype=jnp.int32) + half * rows) % LEN
    valid = slots < length
    masked = jnp.any((slots[:, None] >= starts[None, :]) & (slots[:, None] < starts[None, :] + SPAN), axis=1)
    keybias = jnp.where(
        (jnp.arange(128) == 0)[None, :] & ~valid[:, None], jnp.float32(NEGATIVE), 0.0
    ).astype(BF16)
    valid_rows = valid[:rows].astype(F32)[:, None]
    masked_rows = masked.astype(F32).reshape(2, rows, 1)
    x = jnp.where(masked[:rows, None], mask_vector[None, :], frames)
    pack = jnp.stack(pack_weights(query_weight, key_weight, value_weight, out_weight.T, up_weight, down_weight.T))
    bias = pack_biases(query_bias, value_bias, up_bias)
    mates = [(0, 1), (1, 0), (2, 3), (3, 2)]
    blocks = lax.all_gather(lax.all_gather(pack, "dp", axis=1, tiled=True), "mp", axis=1).reshape(BLOCKS)
    biases = lax.all_gather(bias, "mp", axis=0)
    both = jnp.stack([x, lax.ppermute(x, "mp", mates)])
    probs, out, kept = run_forward_alone(rows, blocks, biases, both, keybias, valid_rows, cotangent, *vecs)
    grads, totals, mate, grad_one = run_backward(False, blocks, probs, kept, masked_rows, first_gain)
    grads = grads.reshape(3, 4, 768, 768).astype(F32)
    grads = lax.psum_scatter(grads, "mp", scatter_dimension=1, tiled=False)
    grads = lax.psum_scatter(grads, "dp", scatter_dimension=1, tiled=True)
    totals = lax.psum(totals, ("dp", "mp"))
    grad_frames = grad_one + lax.ppermute(mate, "mp", mates).astype(F32)
    grad_frames = jnp.where(masked[:rows, None], 0.0, grad_frames).astype(BF16)
    return run_finish(n_dp, n_mp, grads, totals, out, grad_frames)


def solution(mesh):
    linked = mesh.shape["dp"] == 8 and mesh.shape["mp"] == 4
    split = P(("dp", "mp"))
    return jax.shard_map(
        functools.partial(shards, linked),
        mesh=mesh,
        in_specs=(
            P(("dp", "mp"), None),
            P("dp"),
            P("dp", None),
            P(("dp", "mp"), None),
            P("dp", "mp"),
            P("dp", "mp"),
            P("dp", "mp"),
            P("mp", "dp"),
            P("dp", "mp"),
            P("mp", "dp"),
            P("mp", None),
            P("mp", None),
            P("mp", None),
            *([P()] * 7),
        ),
        out_specs=(
            P(("dp", "mp"), None),
            P(("dp", "mp"), None),
            P("dp", "mp"),
            P("dp", "mp"),
            P("dp", "mp"),
            P("mp", "dp"),
            P("dp", "mp"),
            P("mp", "dp"),
            P("mp", "dp"),
            P("mp", "dp"),
            P("mp", "dp"),
            *([split] * 7),
        ),
        check_vma=False,
    )
```
